32 devices in a mesh: tm: 16 (over z, x, core), head: 2 (over y).
Axes of the slice: x: 2, y: 2, z: 4, core: 2. Of those that a mesh axis runs over, the one named last changes fastest.
Arguments:
- audio_frames: bfloat16 [4096, 1024], P('tm', 'head'), may hold values from -50 to 50
- video_frames: bfloat16 [4096, 1024], P('tm', 'head'), may hold values from -50 to 50
- recording: int32 [4096], P('tm'), may hold values from 0 to 3, never falling along the last dimension, each value on 1 to 2048 neighbouring positions
- audio_query: bfloat16 [1024, 1024], P(None, 'head'), may hold values from -0.1875 to 0.1875
- video_key: bfloat16 [1024, 1024], P(None, 'head'), may hold values from -0.1875 to 0.1875
Outputs:
- audio_attended: bfloat16 [4096, 1024], P('tm', 'head')
- video_attended: bfloat16 [4096, 1024], P('tm', 'head')
The draws below stay inside these ranges and needn't reach their ends.
Inputs may be any that keep to these rules, and one draw needn't show every extreme that they name: Ids never fall along the frames; each recording holds 1 to 2048 frames, and one holds exactly 2048.
All inputs are finite; a program needn't handle non-finite values.
Results may differ from the reference program's by a relative error of at most 0.019.
The reference program's roundings to bfloat16 on the way count: a program that leaves them out, or rounds other values in their place, can miss the bound.
Values may be sent and summed in bfloat16 or wider, within the bound.
No kernel may reach another device: no remote copies, remote signals or barrier semaphores. Data moves between devices by JAX's collectives and lax.ppermute only.
A program may use at most 128 MiB of HBM per device.

```python
import math
import jax
import jax.numpy as jnp
import numpy as np
from jax import lax

D = 1024
HEADS = 16
HEAD = 64
BLK = 256
RADIUS = 3
FRAMES = 4096
N_TM = 16


def drawn_rows(key):
    return jnp.clip(jax.random.normal(key, (FRAMES, D), jnp.float32), -6.0, 6.0).astype(jnp.bfloat16)


def draw_audio_frames(key, part):
    key = jax.random.fold_in(key, 11)
    return drawn_rows(key)


def draw_video_frames(key, part):
    key = jax.random.fold_in(key, 23)
    return drawn_rows(key)


def shard_levels(own_key, dims, cuts, smallest, largest):
    def one(position, parts):
        draws = jax.random.uniform(jax.random.fold_in(jax.random.fold_in(own_key, 6), position), (parts,), jnp.float32, smallest / len(cuts), largest / len(cuts))
        return jnp.repeat(jnp.exp(draws), dims[position] // parts).reshape((-1,) + (1,) * (len(dims) - position - 1))

    level = one(*cuts[0])
    for cut in cuts[1:]:
        level = level * one(*cut)
    return level


def length_profile(count, total, bound, skew):
    portions = [(1 << 20) // math.isqrt(grade ** skew) + 1 for grade in range(2, count + 1)]
    surplus, counts = total - bound - (count - 1), [1] * (count - 1)
    while surplus > 0:
        free = [i for i in range(count - 1) if counts[i] < bound]
        pool, left = sum([portions[i] for i in free]), surplus
        for i in free:
            addition = min(bound - counts[i], max(1, left * portions[i] // pool), surplus)
            counts[i] = counts[i] + addition
            surplus = surplus - addition
    return np.array([bound] + counts)


def uneven(rng, amount, total, most, skew):
    if amount == 2:
        one = jax.random.randint(rng, (), max(1, total - most), min(most, total - 1) + 1)
        return jnp.stack([one, total - one])
    lengths = jnp.asarray(length_profile(amount, total, most, skew), jnp.int32)
    twos = (amount - 1) // 2
    giver, receiver = lengths[1:1 + 2 * twos:2], lengths[2:2 + 2 * twos:2]
    room = jnp.minimum(giver - 1, most - receiver)
    moved = jax.random.randint(jax.random.fold_in(rng, 1), (twos,), 0, 1 << 20) % (room + 1)
    lengths = lengths.at[1:1 + 2 * twos:2].set(giver - moved).at[2:2 + 2 * twos:2].set(receiver + moved)
    return lengths[jax.random.permutation(jax.random.fold_in(rng, 2), amount)]


def noise(own_key, dims, width, reach, pieces=(), held_as=jnp.bfloat16):
    loudness = shard_levels(own_key, dims, pieces, -0.22, 0.18) if pieces else 1.0
    array = jax.random.normal(own_key, dims, jnp.float32) * width * loudness
    return jnp.minimum(jnp.maximum(array, -reach), reach).astype(held_as)


def setup_inputs(seed: int = 0) -> dict:
    splits = jax.random.split(jax.random.key(seed), 6)
    return {
        "audio_frames": draw_audio_frames(jax.random.fold_in(splits[5], 71), 0),
        "video_frames": draw_video_frames(jax.random.fold_in(splits[5], 71), 0),
        "recording": jnp.searchsorted(jnp.cumsum(uneven(splits[2], N_TM // 4, FRAMES, 8 * BLK, 2)), jnp.arange(FRAMES), side="right").astype(jnp.int32),
        "audio_query": noise(splits[3], (D, D), D ** -0.5, 0.1875, ((1, 2),)),
        "video_key": noise(splits[4], (D, D), D ** -0.5, 0.1875, ((1, 2),)),
    }


NEG = -1e30


def rounded(values):
    return lax.optimization_barrier(values.astype(jnp.bfloat16)).astype(jnp.float32)


def masked_weights(scores, allowed, axis):
    peak = jnp.max(jnp.where(allowed, scores, NEG), axis=axis, keepdims=True)
    weights = jnp.where(allowed, jnp.exp(scores - peak), 0.0)
    return rounded(weights), jnp.sum(weights, axis=axis)


def reference(audio_frames, video_frames, recording, audio_query, video_key):
    frames = audio_frames.shape[0]
    blocks = frames // BLK
    window = 2 * RADIUS + 1
    queries = rounded(jnp.dot(audio_frames, audio_query, preferred_element_type=jnp.float32)).reshape(blocks, BLK, HEADS, HEAD)
    key_rows = rounded(jnp.dot(video_frames, video_key, preferred_element_type=jnp.float32)).reshape(blocks, BLK, HEADS, HEAD)
    audio_values = audio_frames.astype(jnp.float32).reshape(blocks, BLK, HEADS, HEAD)
    video_values = video_frames.astype(jnp.float32).reshape(blocks, BLK, HEADS, HEAD)
    block_ids = recording.reshape(blocks, BLK)

    def nearby(table, centre):
        picks = (centre - RADIUS + jnp.arange(window, dtype=jnp.int32)) % blocks
        gathered = jnp.take(table, picks.astype(jnp.int32), axis=0)
        return gathered.reshape((window * BLK,) + table.shape[2:])

    def audio_block(centre):
        scores = jnp.einsum("the,uhe->htu", queries[centre], nearby(key_rows, centre)) * HEAD ** -0.5
        allowed = (block_ids[centre][:, None] == nearby(block_ids, centre)[None, :])[None]
        weights, totals = masked_weights(scores, allowed, 2)
        mixed = jnp.einsum("htu,uhe->the", weights, nearby(video_values, centre))
        return (mixed / totals.T[:, :, None]).reshape(BLK, HEADS * HEAD).astype(jnp.bfloat16)

    def video_block(centre):
        scores = jnp.einsum("the,uhe->htu", nearby(queries, centre), key_rows[centre]) * HEAD ** -0.5
        allowed = (nearby(block_ids, centre)[:, None] == block_ids[centre][None, :])[None]
        weights, totals = masked_weights(scores, allowed, 1)
        mixed = jnp.einsum("htu,the->uhe", weights, nearby(audio_values, centre))
        return (mixed / totals.T[:, :, None]).reshape(BLK, HEADS * HEAD).astype(jnp.bfloat16)

    centres = jnp.arange(blocks, dtype=jnp.int32)
    audio_attended = lax.map(audio_block, centres).reshape(frames, HEADS * HEAD)
    video_attended = lax.map(video_block, centres).reshape(frames, HEADS * HEAD)
    return audio_attended, video_attended
```

```python
import functools

import jax
import jax.numpy as jnp
from jax import lax
from jax.experimental import pallas as pl
from jax.experimental.pallas import tpu as pltpu
from jax.sharding import PartitionSpec as P

HEAD = 64
RADIUS = 3
GROUP = 4
NEG = -1e30
ID_ROWS = 16

VMEM = pl.BlockSpec(memory_space=pltpu.VMEM)


def place():
    return lax.rem(lax.axis_index("tm"), GROUP)


def call(kernel, outs, scratch=(), flops=0, moved=0, exps=0, name=None):
    return pl.pallas_call(
        kernel,
        out_shape=outs,
        scratch_shapes=scratch,
        compiler_params=pltpu.CompilerParams(vmem_limit_bytes=48 * 2**20),
        cost_estimate=pl.CostEstimate(flops=flops, bytes_accessed=moved, transcendentals=exps),
        name=name,
    )


def split_kernel(audio, video, ids, *packs):
    rows, width = audio.shape[0], packs[0].shape[1]
    mine = place()
    id_rows = (ids[...] + 1).astype(jnp.float32).astype(jnp.bfloat16)
    for k in range(GROUP):
        columns = pl.ds(pl.multiple_of((mine ^ k) * width, width), width)
        packs[k][:rows] = audio[:, columns]
        packs[k][rows : 2 * rows] = video[:, columns]
        packs[k][2 * rows :] = id_rows


def project_kernel(scale, own, other, weight, *refs):
    *pieces, full = refs
    half, width = own.shape[1], pieces[0].shape[1]
    side = lax.axis_index("head")
    mine = place()
    first = weight[pl.ds(pl.multiple_of(side * half, half), half), :]
    second = weight[pl.ds(pl.multiple_of((1 - side) * half, half), half), :]
    total = jnp.dot(own[...], first, preferred_element_type=jnp.float32)
    total += jnp.dot(other[...], second, preferred_element_type=jnp.float32)
    rounded = total.astype(jnp.bfloat16)
    full[...] = rounded * jnp.bfloat16(scale) if scale != 1.0 else rounded
    for k in range(GROUP):
        columns = pl.ds(pl.multiple_of((mine ^ k) * width, width), width)
        pieces[k][...] = full[:, columns]


def halo_kernel(*refs):
    pieces, (up, down) = refs[:GROUP], refs[GROUP:]
    rows = pieces[0].shape[0]
    mine = place()
    for k in range(GROUP):
        block = mine ^ k

        @pl.when(block >= GROUP - RADIUS)
        def _():
            up[pl.ds(pl.multiple_of((block - (GROUP - RADIUS)) * rows, 16), rows)] = pieces[k][...]

        @pl.when(block < RADIUS)
        def _():
            down[pl.ds(pl.multiple_of(block * rows, 16), rows)] = pieces[k][...]


def join_kernel(*refs):
    pieces, out = refs[:GROUP], refs[GROUP]
    width = pieces[0].shape[1]
    mine = place()
    for k in range(GROUP):
        out[:, pl.ds(pl.multiple_of((mine ^ k) * width, width), width)] = pieces[k][...]


def attend_kernel(side, *refs):
    refs = list(refs)
    take = lambda count: [refs.pop(0) for _ in range(count)]
    asking = take(GROUP)
    keys, (keys_below, keys_above) = take(GROUP), take(2)
    packs, (packs_below, packs_above) = take(GROUP), take(2)
    outs = take(GROUP)
    ask_all, key_all, value_all, id_lanes, id_column, out_all = refs
    rows, width = asking[0].shape
    window = (2 * RADIUS + 1) * rows
    mine = place()
    pack_rows = packs[0].shape[0]

    def put_pack(pack, at, block):
        value_all[pl.ds(pl.multiple_of(block * rows, rows), rows)] = pack[
            at + side * rows : at + (side + 1) * rows
        ]
        lanes = pack[at + 2 * rows : at + 2 * rows + ID_ROWS].astype(jnp.float32)
        for half in range(rows // width):
            id_lanes[:, pl.ds(pl.multiple_of(block * rows + half * width, width), width)] = (
                jnp.broadcast_to(lanes[half : half + 1], (8, width))
            )
        return lanes

    for k in range(GROUP):
        block = mine ^ k
        at = pl.ds(pl.multiple_of(block * rows, rows), rows)
        ask_all[at] = asking[k][...]
        key_all[pl.ds(pl.multiple_of((block + RADIUS) * rows, rows), rows)] = keys[k][...]
        lanes = put_pack(packs[k], 0, block + RADIUS)
        for half in range(rows // width):
            column = jnp.transpose(jnp.broadcast_to(lanes[half : half + 1], (width, width)))
            id_column[pl.ds(pl.multiple_of(block * rows + half * width, width), width)] = column
    key_all[: RADIUS * rows] = keys_below[...]
    key_all[(RADIUS + GROUP) * rows :] = keys_above[...]
    for i in range(RADIUS):
        put_pack(packs_below, i * pack_rows, i)
        put_pack(packs_above, i * pack_rows, RADIUS + GROUP + i)

    lane = lax.broadcasted_iota(jnp.int32, (rows, width), 1)

    def one(block, _):
        start = pl.multiple_of(block * rows, rows)
        at, near = pl.ds(start, rows), pl.ds(start, window)
        allowed = id_column[at, :1] == id_lanes[:1, near]
        ask, key, value = ask_all[at], key_all[near], value_all[near]
        results = []
        for h in range(width // HEAD):
            mine_lanes = lane // HEAD == h
            only = jnp.where(mine_lanes, ask, jnp.zeros_like(ask))
            scores = lax.dot_general(
                only, key, (((1,), (1,)), ((), ())), preferred_element_type=jnp.float32
            )
            scores = jnp.where(allowed, scores, NEG)
            weights = jnp.exp(scores - jnp.max(scores, axis=1, keepdims=True))
            total = jnp.sum(weights, axis=1, keepdims=True)
            mixed = jnp.dot(weights.astype(jnp.bfloat16), value, preferred_element_type=jnp.float32)
            results.append(mixed / total)
        out = results[0]
        for h in range(1, width // HEAD):
            out = jnp.where(lane // HEAD == h, results[h], out)
        out_all[at] = out.astype(out_all.dtype)
        return _

    lax.fori_loop(0, GROUP, one, 0)
    for k in range(GROUP):
        outs[k][...] = out_all[pl.ds(pl.multiple_of((mine ^ k) * rows, rows), rows)]


def local(audio_frames, video_frames, recording, audio_query, video_key):
    rows, half = audio_frames.shape
    width = half // GROUP
    length = lax.axis_size("tm")
    bf16 = jnp.bfloat16
    pack_rows = 2 * rows + ID_ROWS
    shape = jax.ShapeDtypeStruct

    def swapped(x):
        return lax.ppermute(x, "head", [(0, 1), (1, 0)])

    def traded(pieces):
        pairs = lambda k: [(i, i ^ k) for i in range(length)]
        return [pieces[0]] + [lax.ppermute(pieces[k], "tm", pairs(k)) for k in range(1, GROUP)]

    def halo(pieces):
        size = pieces[0].shape[0]
        edge = shape((RADIUS * size, width), bf16)
        up, down = call(
            halo_kernel, [edge, edge], moved=10 * size * width * 2, name="halo"
        )(*pieces)
        below = lax.ppermute(up, "tm", [(i, i + GROUP) for i in range(length - GROUP)])
        above = lax.ppermute(down, "tm", [(i + GROUP, i) for i in range(length - GROUP)])
        return below, above

    def project(own, other, weight, scale):
        return call(
            functools.partial(project_kernel, scale),
            [shape((rows, width), bf16)] * GROUP,
            [pltpu.VMEM((rows, half), bf16)],
            flops=4 * rows * half * half,
            moved=weight.size * 2 + 3 * rows * half * 2,
            name="project",
        )(own, other, weight)

    def attend(side, asking, keys, key_halo, packs, pack_halo):
        window = (2 * RADIUS + 1) * rows
        reach = (2 * RADIUS + GROUP) * rows
        return call(
            functools.partial(attend_kernel, side),
            [shape((rows, width), bf16)] * GROUP,
            [
                pltpu.VMEM((GROUP * rows, width), bf16),
                pltpu.VMEM((reach, width), bf16),
                pltpu.VMEM((reach, width), bf16),
                pltpu.VMEM((8, reach), jnp.float32),
                pltpu.VMEM((GROUP * rows, width), jnp.float32),
                pltpu.VMEM((GROUP * rows, width), bf16),
            ],
            flops=8 * GROUP * rows * window * width * 4,
            moved=4 * reach * width * 2,
            exps=2 * GROUP * rows * window,
            name="attend",
        )(*asking, *keys, *key_halo, *packs, *pack_halo)

    def join(pieces):
        return call(
            join_kernel, shape((rows, half), bf16), moved=2 * rows * half * 2, name="join"
        )(*traded(pieces))

    other_audio = swapped(audio_frames)
    other_video = swapped(video_frames)
    id_rows = jnp.pad(recording.reshape(rows // width, width), ((0, ID_ROWS - rows // width), (0, 0)))
    packs = call(
        split_kernel,
        [shape((pack_rows, width), bf16)] * GROUP,
        moved=4 * rows * half * 2,
        name="split",
    )(audio_frames, video_frames, id_rows)
    packs = traded(packs)
    pack_halo = halo(packs)
    queries = traded(project(audio_frames, other_audio, audio_query, HEAD**-0.5))
    query_halo = halo(queries)
    key_rows = traded(project(video_frames, other_video, video_key, 1.0))
    key_halo = halo(key_rows)
    video_pieces = attend(0, key_rows, queries, query_halo, packs, pack_halo)
    audio_pieces = attend(1, queries, key_rows, key_halo, packs, pack_halo)
    video_attended = join(video_pieces)
    audio_attended = join(audio_pieces)
    return (audio_attended, video_attended)


def solution(mesh):
    return jax.shard_map(
        local,
        mesh=mesh,
        in_specs=(P("tm", "head"), P("tm", "head"), P("tm"), P(None, "head"), P(None, "head")),
        out_specs=(P("tm", "head"), P("tm", "head")),
        check_vma=False,
    )
```

```python
import functools

import jax
import jax.numpy as jnp
from jax import lax
from jax.experimental import pallas as pl
from jax.experimental.pallas import tpu as pltpu
from jax.sharding import PartitionSpec as P

HEAD = 64
RADIUS = 3
GROUP = 4
NEG = -1e30
ID_ROWS = 16

VMEM = pl.BlockSpec(memory_space=pltpu.VMEM)
ANY = pl.BlockSpec(memory_space=pl.ANY)


def place():
    return lax.rem(lax.axis_index("tm"), GROUP)


def plane():
    return lax.axis_index("tm") // GROUP


def call(kernel, outs, scratch=(), ins=None, flops=0, moved=0, exps=0, name=None):
    return pl.pallas_call(
        kernel,
        out_shape=outs,
        **({"in_specs": ins} if ins else {}),
        scratch_shapes=scratch,
        compiler_params=pltpu.CompilerParams(vmem_limit_bytes=48 * 2**20),
        cost_estimate=pl.CostEstimate(flops=flops, bytes_accessed=moved, transcendentals=exps),
        name=name,
    )


def project_kernel(scale, has_ids, *refs):
    own, other, weight = refs[:3]
    packs, (full, id_rows) = refs[-GROUP - 2 : -2], refs[-2:]
    (rows, half), width = own.shape, packs[0].shape[1]
    side = lax.axis_index("head")
    mine = place()
    first = weight[pl.ds(pl.multiple_of(side * half, half), half), :]
    second = weight[pl.ds(pl.multiple_of((1 - side) * half, half), half), :]
    total = jnp.dot(own[...], first, preferred_element_type=jnp.float32)
    total += jnp.dot(other[...], second, preferred_element_type=jnp.float32)
    rounded = total.astype(jnp.bfloat16)
    full[...] = rounded * jnp.bfloat16(scale) if scale != 1.0 else rounded
    if has_ids:
        ids = refs[3]
        id_rows[...] = jnp.zeros_like(id_rows)
        id_rows[: ids.shape[0]] = (ids[...] + 1).astype(jnp.float32)
    for k in range(GROUP):
        columns = pl.ds(pl.multiple_of((mine ^ k) * width, width), width)
        packs[k][:rows] = own[:, columns]
        packs[k][rows : 2 * rows] = full[:, columns]
        if has_ids:
            packs[k][2 * rows :] = id_rows[...].astype(jnp.bfloat16)


def halo_kernel(has_ids, *refs):
    pieces, (first, second) = refs[:GROUP], refs[-2:]
    rows = pieces[0].shape[0]
    mine = place()
    odd = lax.rem(plane(), 2)
    for k in range(GROUP):
        block = mine ^ k
        for out, skip in ((first, (GROUP - RADIUS) * (1 - odd)), (second, (GROUP - RADIUS) * odd)):
            spot = block - skip

            @pl.when((spot >= 0) & (spot < RADIUS))
            def _():
                out[pl.ds(pl.multiple_of(spot * rows, 16), rows)] = pieces[k][...]

    if has_ids:
        last = lax.axis_size("tm") // GROUP - 1

        @pl.when((plane() == 0) | (plane() == last))
        def _():
            for i in range(RADIUS):
                at = (i + 1) * rows - ID_ROWS
                second[at : at + ID_ROWS] = jnp.zeros((ID_ROWS, second.shape[1]), second.dtype)


def join_kernel(*refs):
    pieces, out = refs[:GROUP], refs[GROUP]
    width = pieces[0].shape[1]
    mine = place()
    for k in range(GROUP):
        out[:, pl.ds(pl.multiple_of((mine ^ k) * width, width), width)] = pieces[k][...]


def attend_kernel(shared, skipped, *refs):
    refs = list(refs)
    take = lambda count: [refs.pop(0) for _ in range(count)]
    asking, sources, source_edges = take(GROUP), take(GROUP), take(2)
    id_packs, id_edges = (sources, source_edges) if shared else (take(GROUP), take(2))
    take(skipped)
    outs = take(GROUP)
    ask_all, key_all, value_all, id_lanes, id_column, out_all = refs
    rows, width = outs[0].shape
    window = (2 * RADIUS + 1) * rows
    mine = place()
    source_rows, id_pack_rows = sources[0].shape[0], id_packs[0].shape[0]

    def block_at(block):
        return pl.ds(pl.multiple_of(block * rows, rows), rows)

    def put(source, at, ids, ids_at, block):
        value_all[block_at(block)] = source[at : at + rows]
        key_all[block_at(block)] = source[at + rows : at + 2 * rows]
        ids_at += 2 * rows
        lanes = ids[ids_at : ids_at + ID_ROWS].astype(jnp.float32)
        for part in range(rows // width):
            id_lanes[:, pl.ds(pl.multiple_of(block * rows + part * width, width), width)] = (
                jnp.broadcast_to(lanes[part : part + 1], (8, width))
            )
        return lanes

    for k in range(GROUP):
        block = mine ^ k
        ask_all[block_at(block)] = asking[k][rows : 2 * rows]
        lanes = put(sources[k], 0, id_packs[k], 0, block + RADIUS)
        for part in range(rows // width):
            column = jnp.transpose(jnp.broadcast_to(lanes[part : part + 1], (width, width)))
            id_column[pl.ds(pl.multiple_of(block * rows + part * width, width), width)] = column
    odd = lax.rem(plane(), 2)
    for edge in range(2):
        spot = (RADIUS + GROUP) * (odd if edge else 1 - odd)
        for i in range(RADIUS):
            put(source_edges[edge], i * source_rows, id_edges[edge], i * id_pack_rows, spot + i)

    lane = lax.broadcasted_iota(jnp.int32, (rows, width), 1)

    def one(block, _):
        start = pl.multiple_of(block * rows, rows)
        at, near = pl.ds(start, rows), pl.ds(start, window)
        allowed = id_column[at, :1] == id_lanes[:1, near]
        ask, key, value = ask_all[at], key_all[near], value_all[near]
        results = []
        for h in range(width // HEAD):
            only = jnp.where(lane // HEAD == h, ask, jnp.zeros_like(ask))
            scores = lax.dot_general(
                only, key, (((1,), (1,)), ((), ())), preferred_element_type=jnp.float32
            )
            scores = jnp.where(allowed, scores, NEG)
            weights = jnp.exp(scores - jnp.max(scores, axis=1, keepdims=True))
            total = jnp.sum(weights, axis=1, keepdims=True)
            mixed = jnp.dot(weights.astype(jnp.bfloat16), value, preferred_element_type=jnp.float32)
            results.append(mixed / total)
        out = results[0]
        for h in range(1, width // HEAD):
            out = jnp.where(lane // HEAD == h, results[h], out)
        out_all[at] = out.astype(out_all.dtype)
        return _

    lax.fori_loop(0, GROUP, one, 0)
    for k in range(GROUP):
        outs[k][...] = out_all[block_at(mine ^ k)]


def local(audio_frames, video_frames, recording, audio_query, video_key):
    rows, half = audio_frames.shape
    width = half // GROUP
    length = lax.axis_size("tm")
    bf16 = jnp.bfloat16
    shape = jax.ShapeDtypeStruct

    def swapped(x):
        return lax.ppermute(x, "head", [(0, 1), (1, 0)])

    def traded(pieces):
        pairs = lambda k: [(i, i ^ k) for i in range(length)]
        return [pieces[0]] + [lax.ppermute(pieces[k], "tm", pairs(k)) for k in range(1, GROUP)]

    def halo(pieces, has_ids, after=()):
        size = pieces[0].shape[0]
        edge = shape((RADIUS * size, width), bf16)
        sent = call(
            functools.partial(halo_kernel, has_ids),
            [edge, edge],
            ins=[VMEM] * GROUP + [ANY] * len(after),
            moved=10 * size * width * 2,
            name="halo",
        )(*pieces, *after)

        def partner(i, second):
            spot, inside = divmod(i, GROUP)
            spot = ((spot + second) ^ 1) - second
            return min(max(spot, 0), length // GROUP - 1) * GROUP + inside

        return [
            lax.ppermute(sent[s], "tm", [(i, partner(i, s)) for i in range(length)])
            for s in range(2)
        ]

    def project(own, other, weight, scale, *ids):
        pack = shape((2 * rows + (ID_ROWS if ids else 0), width), bf16)
        return call(
            functools.partial(project_kernel, scale, bool(ids)),
            [pack] * GROUP,
            [pltpu.VMEM((rows, half), bf16), pltpu.VMEM((ID_ROWS, width), jnp.float32)],
            flops=4 * rows * half * half,
            moved=weight.size * 2 + 3 * rows * half * 2,
            name="project",
        )(own, other, weight, *ids)

    def attend(asking, *sources, after=()):
        window = (2 * RADIUS + 1) * rows
        reach = (2 * RADIUS + GROUP) * rows
        return call(
            functools.partial(attend_kernel, len(sources) == GROUP + 2, len(after)),
            [shape((rows, width), bf16)] * GROUP,
            [
                pltpu.VMEM((GROUP * rows, width), bf16),
                pltpu.VMEM((reach, width), bf16),
                pltpu.VMEM((reach, width), bf16),
                pltpu.VMEM((8, reach), jnp.float32),
                pltpu.VMEM((GROUP * rows, width), jnp.float32),
                pltpu.VMEM((GROUP * rows, width), bf16),
            ],
            flops=8 * GROUP * rows * window * width * 4,
            moved=4 * reach * width * 2,
            exps=2 * GROUP * rows * window,
            ins=[VMEM] * (GROUP + len(sources)) + [ANY] * len(after),
            name="attend",
        )(*asking, *sources, *after)

    def join(pieces):
        return call(
            join_kernel, shape((rows, half), bf16), moved=2 * rows * half * 2, name="join"
        )(*traded(pieces))

    assert length % (2 * GROUP) == 0
    ids = recording.reshape(rows // width, width)
    other_audio = swapped(audio_frames)
    other_video = swapped(video_frames)
    audio_packs = project(audio_frames, other_audio, audio_query, HEAD**-0.5, ids)
    audio_packs = traded(audio_packs)
    video_packs = project(video_frames, other_video, video_key, 1.0)
    audio_edges = halo(audio_packs, True, [video_packs[0]])
    video_packs = traded(video_packs)
    video_edges = halo(video_packs, False)
    video_pieces = attend(video_packs, *audio_packs, *audio_edges)
    audio_pieces = attend(
        audio_packs, *video_packs, *video_edges, *audio_packs, *audio_edges, after=video_pieces[:1]
    )
    video_attended = join(video_pieces)
    audio_attended = join(audio_pieces)
    return (audio_attended, video_attended)


def solution(mesh):
    return jax.shard_map(
        local,
        mesh=mesh,
        in_specs=(P("tm", "head"), P("tm", "head"), P("tm"), P(None, "head"), P(None, "head")),
        out_specs=(P("tm", "head"), P("tm", "head")),
        check_vma=False,
    )
```

```python
import functools

import jax
import jax.numpy as jnp
from jax import lax
from jax.experimental import pallas as pl
from jax.experimental.pallas import tpu as pltpu
from jax.sharding import PartitionSpec as P

HEAD = 64
RADIUS = 3
GROUP = 4
NEG = -1e30
ID_ROWS = 16

VMEM = pl.BlockSpec(memory_space=pltpu.VMEM)
ANY = pl.BlockSpec(memory_space=pl.ANY)
HBM = pl.BlockSpec(memory_space=pltpu.HBM)


def place():
    return lax.rem(lax.axis_index("tm"), GROUP)


def plane():
    return lax.axis_index("tm") // GROUP


def call(kernel, outs, scratch=(), ins=None, flops=0, moved=0, exps=0, name=None, room=48):
    return pl.pallas_call(
        kernel,
        out_shape=outs,
        **({"in_specs": ins} if ins else {}),
        scratch_shapes=scratch,
        compiler_params=pltpu.CompilerParams(vmem_limit_bytes=room * 2**20),
        cost_estimate=pl.CostEstimate(flops=flops, bytes_accessed=moved, transcendentals=exps),
        name=name,
    )


def prepare_kernel(audio, video, query, key, ids, *refs):
    sent, sums, turned, seconds, id_rows = refs[0], refs[1:3], refs[3:5], refs[5:7], refs[7]
    own, firsts, ids_in, ids_wide, sems = refs[8], refs[9:11], refs[11], refs[12], refs[13]
    half = audio.shape[1]
    rows, width = audio.shape[0], turned[0].shape[1]
    side = lax.axis_index("head")
    mine = place()
    copies = []

    def fetch(source, target):
        copies.append(pltpu.make_async_copy(source, target, sems.at[len(copies)]))
        copies[-1].start()
        return copies[-1]

    streams = (own, sent)
    loads = [fetch(audio, own), fetch(video, sent)]
    ours = pl.ds(pl.multiple_of(side * half, half), half)
    theirs = pl.ds(pl.multiple_of((1 - side) * half, half), half)
    weights = [fetch(w.at[ours], f) for w, f in zip((query, key), firsts)]
    others = [fetch(w.at[theirs], f) for w, f in zip((query, key), seconds)]
    others.append(fetch(ids, ids_in))
    for i in range(2):
        loads[i].wait()
        for k in range(GROUP):
            columns = pl.ds(pl.multiple_of((mine ^ k) * width, width), width)
            for at in range(0, rows, width):
                square = streams[i][at : at + width, columns]
                turned[i][k * rows + at : k * rows + at + width] = jnp.transpose(square)
    for i in range(2):
        weights[i].wait()
        sums[i][...] = jnp.dot(
            streams[i][...], firsts[i][...], preferred_element_type=jnp.float32
        )
    for copy in others:
        copy.wait()
    ids_wide[...] = jnp.zeros_like(ids_wide)
    ids_wide[: ids_in.shape[0]] = (ids_in[...] + 1).astype(jnp.float32)
    id_rows[...] = ids_wide[...].astype(id_rows.dtype)


def project_kernel(scale, has_ids, *refs):
    turned, part, other, weight = refs[:4]
    packs, full = refs[-GROUP - 1 : -1], refs[-1]
    rows, width = other.shape[0], packs[0].shape[1]
    mine = place()
    total = part[...] + jnp.dot(other[...], weight[...], preferred_element_type=jnp.float32)
    rounded = total.astype(jnp.bfloat16)
    full[...] = rounded * jnp.bfloat16(scale) if scale != 1.0 else rounded
    for k in range(GROUP):
        columns = pl.ds(pl.multiple_of((mine ^ k) * width, width), width)
        packs[k][:rows] = turned[k * rows : (k + 1) * rows]
        packs[k][rows : 2 * rows] = full[:, columns]
        if has_ids:
            packs[k][2 * rows :] = refs[4][...]


def halo_kernel(has_ids, *refs):
    pieces, (first, second) = refs[:GROUP], refs[-2:]
    rows = pieces[0].shape[0]
    mine = place()
    odd = lax.rem(plane(), 2)
    for k in range(GROUP):
        block = mine ^ k
        for out, skip in ((first, (GROUP - RADIUS) * (1 - odd)), (second, (GROUP - RADIUS) * odd)):
            spot = block - skip

            @pl.when((spot >= 0) & (spot < RADIUS))
            def _():
                out[pl.ds(pl.multiple_of(spot * rows, 16), rows)] = pieces[k][...]

    if has_ids:
        last = lax.axis_size("tm") // GROUP - 1

        @pl.when((plane() == 0) | (plane() == last))
        def _():
            for i in range(RADIUS):
                at = (i + 1) * rows - ID_ROWS
                second[at : at + ID_ROWS] = jnp.zeros((ID_ROWS, second.shape[1]), second.dtype)


def join_kernel(*refs):
    pieces, out = refs[:GROUP], refs[GROUP]
    width = pieces[0].shape[1]
    mine = place()
    for k in range(GROUP):
        out[:, pl.ds(pl.multiple_of((mine ^ k) * width, width), width)] = pieces[k][...]


def attend_kernel(first, *refs):
    refs = list(refs)
    take = lambda count: [refs.pop(0) for _ in range(count)]
    asking, sources, edges, (marks,) = take(GROUP), take(GROUP), take(2), take(1) if not first else (None,)
    outs, (marks_out,) = take(GROUP), take(1) if first else (None,)
    ask_all, key_all, value_all, out_all = refs
    rows, width = outs[0].shape
    window = (2 * RADIUS + 1) * rows
    reach = key_all.shape[0]
    mine = place()
    source_rows = sources[0].shape[0]
    bf16 = jnp.bfloat16

    def block_at(block):
        return pl.ds(pl.multiple_of(block * rows, rows), rows)

    def put(source, at, block):
        key_all[block_at(block), :width] = source[at + rows : at + 2 * rows]
        if first:
            lanes = source[at + 2 * rows : at + 2 * rows + ID_ROWS].astype(jnp.float32)
        for part in range(0, rows, width):
            spot = pl.ds(pl.multiple_of(block * rows + part, width), width)
            value_all[:, spot] = source[at + part : at + part + width]
            if first:
                ids = lanes[part // width : part // width + 1]
                column = jnp.transpose(jnp.broadcast_to(ids, (width, width)))
                lane = lax.broadcasted_iota(jnp.int32, (width, width), 1)
                mark = jnp.where(column == lane.astype(jnp.float32), 1.0, 0.0).astype(bf16)
                key_all[spot, width:] = mark
                marks_out[spot] = mark

    for k in range(GROUP):
        ask_all[block_at(mine ^ k)] = asking[k][rows : 2 * rows]
        put(sources[k], 0, (mine ^ k) + RADIUS)
    odd = lax.rem(plane(), 2)
    for edge in range(2):
        spot = (RADIUS + GROUP) * (odd if edge else 1 - odd)
        for i in range(RADIUS):
            put(edges[edge], i * source_rows, spot + i)
    if not first:
        key_all[:, width:] = marks[...]

    lane = lax.broadcasted_iota(jnp.int32, (rows, width), 1)

    def one(block, _):
        near = pl.ds(pl.multiple_of(block * rows, rows), window)
        ask = ask_all[block_at(block)]
        forbid = (key_all[block_at(block + RADIUS), width:] - bf16(1.0)) * bf16(-NEG)
        results = []
        for h in range(width // HEAD):
            only = jnp.where(lane // HEAD == h, ask, jnp.zeros_like(ask))
            scores = lax.dot_general(
                key_all[near, :],
                jnp.concatenate([only, forbid], axis=1),
                (((1,), (1,)), ((), ())),
                preferred_element_type=jnp.float32,
            )
            weights = jnp.exp(scores - jnp.max(scores, axis=0, keepdims=True))
            total = jnp.sum(weights, axis=0, keepdims=True)
            mixed = jnp.dot(
                value_all[h * HEAD : (h + 1) * HEAD, near],
                weights.astype(bf16),
                preferred_element_type=jnp.float32,
            )
            results.append(mixed / total)
        out_all[block_at(block)] = jnp.transpose(jnp.concatenate(results, axis=0)).astype(bf16)
        return _

    lax.fori_loop(0, GROUP, one, 0)
    for k in range(GROUP):
        outs[k][...] = out_all[block_at(mine ^ k)]


def local(audio_frames, video_frames, recording, audio_query, video_key):
    rows, half = audio_frames.shape
    width = half // GROUP
    length = lax.axis_size("tm")
    bf16 = jnp.bfloat16
    shape = jax.ShapeDtypeStruct

    def swapped(x):
        return lax.ppermute(x, "head", [(0, 1), (1, 0)])

    def traded(pieces):
        pairs = lambda k: [(i, i ^ k) for i in range(length)]
        return [pieces[0]] + [lax.ppermute(pieces[k], "tm", pairs(k)) for k in range(1, GROUP)]

    def halo(pieces, has_ids, after=()):
        size = pieces[0].shape[0]
        edge = shape((RADIUS * size, width), bf16)
        sent = call(
            functools.partial(halo_kernel, has_ids),
            [edge, edge],
            ins=[VMEM] * GROUP + [ANY] * len(after),
            moved=10 * size * width * 2,
            name="halo",
        )(*pieces, *after)

        def partner(i, second):
            spot, inside = divmod(i, GROUP)
            spot = ((spot + second) ^ 1) - second
            return min(max(spot, 0), length // GROUP - 1) * GROUP + inside

        return [
            lax.ppermute(sent[s], "tm", [(i, partner(i, s)) for i in range(length)])
            for s in range(2)
        ]

    def project(turned, part, other, weight, scale, *ids):
        pack = shape((2 * rows + (ID_ROWS if ids else 0), width), bf16)
        return call(
            functools.partial(project_kernel, scale, bool(ids)),
            [pack] * GROUP,
            [pltpu.VMEM((rows, half), bf16)],
            flops=2 * rows * half * half,
            moved=weight.size * 2 + 3 * rows * half * 2,
            name="project",
        )(turned, part, other, weight, *ids)

    def attend(asking, sources, edges, *marks):
        window = (2 * RADIUS + 1) * rows
        reach = (2 * RADIUS + GROUP) * rows
        outs = [shape((rows, width), bf16)] * GROUP
        return call(
            functools.partial(attend_kernel, not marks),
            outs if marks else outs + [shape((reach, width), bf16)],
            [
                pltpu.VMEM((GROUP * rows, width), bf16),
                pltpu.VMEM((reach, 2 * width), bf16),
                pltpu.VMEM((width, reach), bf16),
                pltpu.VMEM((GROUP * rows, width), bf16),
            ],
            flops=8 * GROUP * rows * window * width * 4,
            moved=4 * reach * width * 2,
            exps=2 * GROUP * rows * window,
            name="attend",
        )(*asking, *sources, *edges, *marks)

    def join(pieces):
        return call(
            join_kernel, shape((rows, half), bf16), moved=2 * rows * half * 2, name="join"
        )(*traded(pieces))

    assert length % (2 * GROUP) == 0
    other_audio = swapped(audio_frames)
    part = shape((rows, half), jnp.float32)
    turned = shape((GROUP * rows, width), bf16)
    square = shape((half, half), bf16)
    given = (audio_frames, video_frames, audio_query, video_key, recording.reshape(rows // width, width))
    video_copy, query_part, key_part, audio_turned, video_turned, query_rest, key_rest, ids = call(
        prepare_kernel,
        [shape((rows, half), bf16), part, part, turned, turned, square, square]
        + [shape((ID_ROWS, width), bf16)],
        [pltpu.VMEM((rows, half), bf16)]
        + [pltpu.VMEM((half, half), bf16)] * 2
        + [pltpu.VMEM((rows // width, width), jnp.int32), pltpu.VMEM((ID_ROWS, width), jnp.float32)]
        + [pltpu.SemaphoreType.DMA((7,))],
        ins=[HBM] * 5,
        flops=4 * rows * half * half,
        moved=16 * half * half,
        name="prepare",
    )(*(pltpu.with_memory_space_constraint(x, pltpu.HBM) for x in given))
    other_video = swapped(video_copy)
    audio_packs = traded(
        project(audio_turned, query_part, other_audio, query_rest, HEAD**-0.5, ids)
    )
    video_packs = traded(project(video_turned, key_part, other_video, key_rest, 1.0))
    audio_edges = halo(audio_packs, True, [video_packs[1]])
    video_edges = halo(video_packs, False)
    *video_pieces, marks = attend(video_packs, audio_packs, audio_edges)
    audio_pieces = attend(audio_packs, video_packs, video_edges, marks)
    video_attended = join(video_pieces)
    audio_attended = join(audio_pieces)
    return (audio_attended, video_attended)


def solution(mesh):
    return jax.shard_map(
        local,
        mesh=mesh,
        in_specs=(P("tm", "head"), P("tm", "head"), P("tm"), P(None, "head"), P(None, "head")),
        out_specs=(P("tm", "head"), P("tm", "head")),
        check_vma=False,
    )
```

```python
import functools

import jax
import jax.numpy as jnp
from jax import lax
from jax.experimental import pallas as pl
from jax.experimental.pallas import tpu as pltpu
from jax.sharding import PartitionSpec as P

HEAD = 64
RADIUS = 3
GROUP = 4
NEG = -1e30
ID_ROWS = 16

VMEM = pl.BlockSpec(memory_space=pltpu.VMEM)
ANY = pl.BlockSpec(memory_space=pl.ANY)
HBM = pl.BlockSpec(memory_space=pltpu.HBM)


def plane():
    return lax.axis_index("tm") // GROUP


def call(kernel, outs, scratch=(), ins=None, flops=0, moved=0, exps=0, name=None):
    return pl.pallas_call(
        kernel,
        out_shape=outs,
        **({"in_specs": ins} if ins else {}),
        scratch_shapes=scratch,
        compiler_params=pltpu.CompilerParams(vmem_limit_bytes=48 * 2**20),
        cost_estimate=pl.CostEstimate(flops=flops, bytes_accessed=moved, transcendentals=exps),
        name=name,
    )


def prepare_kernel(audio, video, query, key, ids, *refs):
    sent, sums, seconds, packs = refs[0], refs[1:3], refs[3:5], refs[5]
    own, firsts, ids_in, ids_wide, sems = refs[6], refs[7:9], refs[9], refs[10], refs[11]
    rows, half = audio.shape
    width = packs.shape[2]
    side = lax.axis_index("head")
    copies = []

    def fetch(source, target):
        copies.append(pltpu.make_async_copy(source, target, sems.at[len(copies)]))
        copies[-1].start()
        return copies[-1]

    streams = (own, sent)
    loads = [fetch(audio, own), fetch(video, sent)]
    ours = pl.ds(pl.multiple_of(side * half, half), half)
    theirs = pl.ds(pl.multiple_of((1 - side) * half, half), half)
    weights = [fetch(w.at[ours], f) for w, f in zip((query, key), firsts)]
    others = [fetch(w.at[theirs], f) for w, f in zip((query, key), seconds)]
    others.append(fetch(ids, ids_in))
    for i in range(2):
        loads[i].wait()
        for k in range(GROUP):
            for at in range(0, rows, width):
                square = streams[i][at : at + width, k * width : (k + 1) * width]
                packs[k, i * rows + at : i * rows + at + width] = jnp.transpose(square)
    for i in range(2):
        weights[i].wait()
        sums[i][...] = jnp.dot(
            streams[i][...], firsts[i][...], preferred_element_type=jnp.float32
        )
    for copy in others:
        copy.wait()
    ids_wide[...] = jnp.zeros_like(ids_wide)
    ids_wide[: ids_in.shape[0]] = (ids_in[...] + 1).astype(jnp.float32)
    for k in range(GROUP):
        packs[k, 2 * rows :] = ids_wide[...].astype(packs.dtype)


def project_kernel(scale, part, other, weight, *refs):
    out = refs[-1]
    total = part[...] + jnp.dot(other[...], weight[...], preferred_element_type=jnp.float32)
    rounded = total.astype(jnp.bfloat16)
    rounded = rounded * jnp.bfloat16(scale) if scale != 1.0 else rounded
    rows, width = other.shape[0], out.shape[2]
    before = refs[0] if len(refs) == 2 else None
    for k in range(GROUP):
        if before is None:
            out[k] = rounded[:, k * width : (k + 1) * width]
        else:
            out[k, :rows] = before[k]
            out[k, rows:] = rounded[:, k * width : (k + 1) * width]


def halo_kernel(has_ids, pieces, first, second):
    odd = lax.rem(plane(), 2)
    first[...] = pieces[pl.ds((GROUP - RADIUS) * (1 - odd), RADIUS)]
    second[...] = pieces[pl.ds((GROUP - RADIUS) * odd, RADIUS)]
    if has_ids:
        last = lax.axis_size("tm") // GROUP - 1

        @pl.when((plane() == 0) | (plane() == last))
        def _():
            second[:, second.shape[1] - ID_ROWS :] = jnp.zeros(
                (RADIUS, ID_ROWS, second.shape[2]), second.dtype
            )


def join_kernel(pieces, *outs):
    width = pieces.shape[2]
    rows = outs[0].shape[0]
    for i, out in enumerate(outs):
        for k in range(GROUP):
            out[:, k * width : (k + 1) * width] = pieces[k, i * rows : (i + 1) * rows]


def mark(pack, rows, width, put):
    lanes = pack[2 * rows :].astype(jnp.float32)
    lane = lax.broadcasted_iota(jnp.int32, (width, width), 1).astype(jnp.float32)
    for at in range(0, rows, width):
        ids = lanes[at // width : at // width + 1]
        column = jnp.transpose(jnp.broadcast_to(ids, (width, width)))
        put(at, jnp.where(column == lane, 1.0, 0.0).astype(jnp.bfloat16))


def fold(parts, combine):
    parts = list(parts)
    while len(parts) > 1:
        pairs = [combine(a, b) for a, b in zip(parts[::2], parts[1::2])]
        parts = pairs + ([parts[-1]] if len(parts) % 2 else [])
    x = parts[0]
    while x.shape[0] > 8:
        middle = x.shape[0] // 2
        x = combine(x[:middle], x[middle:])
    return x


def chunk_scores(ask, key_at, count):
    return [
        lax.dot_general(
            key_at(c), ask, (((1,), (1,)), ((), ())), preferred_element_type=jnp.float32
        )
        for c in range(count)
    ]


def peak_of(scores):
    return jnp.max(fold(scores, jnp.maximum), axis=0, keepdims=True)


def weigh(scores, peak, value_at):
    weights = [jnp.exp(s - peak) for s in scores]
    total = jnp.sum(fold(weights, jnp.add), axis=0, keepdims=True)
    mixed = sum(
        jnp.dot(value_at(c), w.astype(jnp.bfloat16), preferred_element_type=jnp.float32)
        for c, w in enumerate(weights)
    )
    return total, mixed


def asks(block, width, forbid):
    lane = lax.broadcasted_iota(jnp.int32, block.shape, 1)
    return [
        jnp.concatenate([jnp.where(lane // HEAD == h, block, jnp.zeros_like(block)), forbid], axis=1)
        for h in range(width // HEAD)
    ]


def plane_kernel(values, projected, peaks, totals, sums, forbids, keys, turned):
    rows = forbids.shape[1]
    width = values.shape[2]
    for b in range(GROUP):
        at = slice(b * rows, (b + 1) * rows)

        def put(spot, marks):
            for i in range(2):
                keys[i, b * rows + spot : b * rows + spot + width, width:] = marks
            forbids[b, spot : spot + width] = (marks - jnp.bfloat16(1.0)) * jnp.bfloat16(-NEG)

        mark(values[b], rows, width, put)
        for i in range(2):
            keys[i, at, :width] = projected[b, (1 - i) * rows : (2 - i) * rows]
            for spot in range(0, rows, width):
                turned[i, :, b * rows + spot : b * rows + spot + width] = values[
                    b, (1 - i) * rows + spot : (1 - i) * rows + spot + width
                ]

    def one(b, _):
        for i in range(2):
            block = projected[b, i * rows : (i + 1) * rows]
            for h, ask in enumerate(asks(block, width, forbids[b])):
                scores = chunk_scores(ask, lambda c: keys[i, c * rows : (c + 1) * rows], GROUP)
                peak = peak_of(scores)
                lanes = slice(h * HEAD, (h + 1) * HEAD)
                total, mixed = weigh(
                    scores, peak, lambda c: turned[i, lanes, c * rows : (c + 1) * rows]
                )
                peaks[i, b, h : h + 1] = peak
                totals[i, b, h : h + 1] = total
                sums[i, b, lanes] = mixed
        return _

    lax.fori_loop(0, GROUP, one, 0)


def edge_kernel(projected, peaks, totals, sums, forbids, *refs):
    value_edges, projected_edges, out, keys, turned = refs[:2], refs[2:4], refs[4], refs[5], refs[6]
    rows = forbids.shape[1]
    width = projected.shape[2]
    odd = lax.rem(plane(), 2)
    for edge in range(2):
        base = RADIUS * (odd if edge else 1 - odd)
        for j in range(RADIUS):

            def spot_at(at, size):
                return pl.ds(pl.multiple_of((base + j) * rows + at, size), size)

            def put(at, marks):
                for i in range(2):
                    keys[i, spot_at(at, width), width:] = marks

            mark(value_edges[edge][j], rows, width, put)
            for i in range(2):
                keys[i, spot_at(0, rows), :width] = projected_edges[edge][
                    j, (1 - i) * rows : (2 - i) * rows
                ]
                for at in range(0, rows, width):
                    turned[i, :, spot_at(at, width)] = value_edges[edge][
                        j, (1 - i) * rows + at : (1 - i) * rows + at + width
                    ]

    def one(b, _):
        def near(c):
            return pl.ds(pl.multiple_of((b + c) * rows, rows), rows)

        for i in range(2):
            block = projected[b, i * rows : (i + 1) * rows]
            results = []
            for h, ask in enumerate(asks(block, width, forbids[b])):
                scores = chunk_scores(ask, lambda c: keys[i, near(c)], RADIUS)
                old = peaks[i, b, h : h + 1]
                peak = jnp.maximum(old, peak_of(scores))
                lanes = slice(h * HEAD, (h + 1) * HEAD)
                total, mixed = weigh(scores, peak, lambda c: turned[i, lanes, near(c)])
                factor = jnp.exp(old - peak)
                total += totals[i, b, h : h + 1] * factor
                results.append((mixed + sums[i, b, lanes] * factor) / total)
            out[b, i * rows : (i + 1) * rows] = jnp.transpose(
                jnp.concatenate(results, axis=0)
            ).astype(out.dtype)
        return _

    lax.fori_loop(0, GROUP, one, 0)


def local(audio_frames, video_frames, recording, audio_query, video_key):
    rows, half = audio_frames.shape
    width = half // GROUP
    heads = width // HEAD
    length = lax.axis_size("tm")
    bf16, f32 = jnp.bfloat16, jnp.float32
    shape = jax.ShapeDtypeStruct
    assert length % (2 * GROUP) == 0

    def swapped(x):
        return lax.ppermute(x, "head", [(0, 1), (1, 0)])

    def traded(pieces):
        groups = [list(range(i, i + GROUP)) for i in range(0, length, GROUP)]
        return lax.all_to_all(pieces, "tm", 0, 0, axis_index_groups=groups)

    def halo(pieces, has_ids, after=()):
        size = pieces.shape[1]
        edge = shape((RADIUS, size, width), bf16)

        def kernel(pieces, *refs):
            halo_kernel(has_ids, pieces, *refs[-2:])

        sent = call(
            kernel,
            [edge, edge],
            ins=[VMEM] + [ANY] * len(after),
            moved=10 * size * width * 2,
            name="halo",
        )(pieces, *after)

        def partner(i, second):
            spot, inside = divmod(i, GROUP)
            spot = ((spot + second) ^ 1) - second
            return min(max(spot, 0), length // GROUP - 1) * GROUP + inside

        return [
            lax.ppermute(sent[s], "tm", [(i, partner(i, s)) for i in range(length)])
            for s in range(2)
        ]

    def project(part, other, weight, scale, *before):
        return call(
            functools.partial(project_kernel, scale),
            shape((GROUP, (1 + len(before)) * rows, width), bf16),
            flops=2 * rows * half * half,
            moved=half * half * 2 + 4 * rows * half * 2,
            name="project",
        )(part, other, weight, *before)

    other_audio = swapped(audio_frames)
    part = shape((rows, half), f32)
    square = shape((half, half), bf16)
    given = (audio_frames, video_frames, audio_query, video_key, recording.reshape(rows // width, width))
    video_copy, query_part, key_part, query_rest, key_rest, values = call(
        prepare_kernel,
        [shape((rows, half), bf16), part, part, square, square]
        + [shape((GROUP, 2 * rows + ID_ROWS, width), bf16)],
        [pltpu.VMEM((rows, half), bf16)]
        + [pltpu.VMEM((half, half), bf16)] * 2
        + [pltpu.VMEM((rows // width, width), jnp.int32), pltpu.VMEM((ID_ROWS, width), f32)]
        + [pltpu.SemaphoreType.DMA((7,))],
        ins=[HBM] * 5,
        flops=4 * rows * half * half,
        moved=16 * half * half,
        name="prepare",
    )(*(pltpu.with_memory_space_constraint(x, pltpu.HBM) for x in given))
    other_video = swapped(video_copy)
    values = traded(values)
    value_edges = halo(values, True)
    queries = project(query_part, other_audio, query_rest, HEAD**-0.5)
    projected = traded(project(key_part, other_video, key_rest, 1.0, queries))
    projected_edges = halo(projected, False)

    stat = shape((2, GROUP, heads, rows), f32)
    sums = shape((2, GROUP, width, rows), f32)
    inside, around = GROUP * rows, 2 * RADIUS * rows
    state = call(
        plane_kernel,
        [stat, stat, sums, shape((GROUP, rows, width), bf16)],
        [pltpu.VMEM((2, inside, 2 * width), bf16), pltpu.VMEM((2, width, inside), bf16)],
        flops=16 * GROUP * rows * inside * width,
        moved=8 * inside * width * 2,
        exps=4 * GROUP * rows * inside,
        name="plane",
    )(values, projected)
    pieces = call(
        edge_kernel,
        shape((GROUP, 2 * rows, width), bf16),
        [pltpu.VMEM((2, around, 2 * width), bf16), pltpu.VMEM((2, width, around), bf16)],
        flops=16 * GROUP * rows * RADIUS * rows * width,
        moved=8 * around * width * 2,
        exps=4 * GROUP * rows * RADIUS * rows,
        name="edge",
    )(projected, *state, *value_edges, *projected_edges)
    out = shape((rows, half), bf16)
    return tuple(
        call(join_kernel, [out, out], moved=4 * rows * half * 2, name="join")(traded(pieces))
    )


def solution(mesh):
    return jax.shard_map(
        local,
        mesh=mesh,
        in_specs=(P("tm", "head"), P("tm", "head"), P("tm"), P(None, "head"), P(None, "head")),
        out_specs=(P("tm", "head"), P("tm", "head")),
        check_vma=False,
    )
```

```python
import functools

import jax
import jax.numpy as jnp
from jax import lax
from jax.experimental import pallas as pl
from jax.experimental.pallas import tpu as pltpu
from jax.sharding import PartitionSpec as P

HEAD = 64
RADIUS = 3
GROUP = 4
NEG = -1e30
ID_ROWS = 16

VMEM = pl.BlockSpec(memory_space=pltpu.VMEM)
ANY = pl.BlockSpec(memory_space=pl.ANY)
HBM = pl.BlockSpec(memory_space=pltpu.HBM)


def place():
    return lax.rem(lax.axis_index("tm"), GROUP)


def plane():
    return lax.axis_index("tm") // GROUP


def call(kernel, outs, scratch=(), ins=None, flops=0, moved=0, exps=0, name=None):
    return pl.pallas_call(
        kernel,
        out_shape=outs,
        **({"in_specs": ins} if ins else {}),
        scratch_shapes=scratch,
        compiler_params=pltpu.CompilerParams(vmem_limit_bytes=48 * 2**20),
        cost_estimate=pl.CostEstimate(flops=flops, bytes_accessed=moved, transcendentals=exps),
        name=name,
    )


def prepare_kernel(audio, video, query, key, ids, *refs):
    sums, seconds, packs = refs[:2], refs[2:4], refs[4 : 4 + GROUP]
    streams, firsts, ids_in, ids_wide, sems = refs[8:10], refs[10:12], refs[12], refs[13], refs[14]
    rows, half = audio.shape
    width = packs[0].shape[1]
    side = lax.axis_index("head")
    mine = place()
    copies = []

    def fetch(source, target):
        copies.append(pltpu.make_async_copy(source, target, sems.at[len(copies)]))
        copies[-1].start()
        return copies[-1]

    pieces = []
    for k in range(GROUP):
        columns = pl.ds(pl.multiple_of((mine ^ k) * width, width), width)
        for i, stream in enumerate((audio, video)):
            pieces.append(fetch(stream.at[:, columns], packs[k].at[i * rows : (i + 1) * rows]))
    pieces.append(fetch(ids, ids_in))
    ours = pl.ds(pl.multiple_of(side * half, half), half)
    theirs = pl.ds(pl.multiple_of((1 - side) * half, half), half)
    loads = [fetch(x, s) for x, s in zip((audio, video), streams)]
    loads += [fetch(w.at[ours], f) for w, f in zip((query, key), firsts)]
    others = [fetch(w.at[theirs], f) for w, f in zip((query, key), seconds)]
    for copy in pieces:
        copy.wait()
    ids_wide[...] = jnp.zeros_like(ids_wide)
    ids_wide[: ids_in.shape[0]] = (ids_in[...] + 1).astype(jnp.float32)
    for k in range(GROUP):
        packs[k][2 * rows :] = ids_wide[...].astype(packs[k].dtype)
    for copy in loads:
        copy.wait()
    for i in range(2):
        sums[i][...] = jnp.dot(
            streams[i][...], firsts[i][...], preferred_element_type=jnp.float32
        )
    for copy in others:
        copy.wait()


def project_kernel(scales, *refs):
    parts, others, weights, packs, full = refs[:2], refs[2:4], refs[4:6], refs[7 : 7 + GROUP], refs[-1]
    rows, width = others[0].shape[0], packs[0].shape[1]
    mine = place()
    for i in range(2):
        total = parts[i][...] + jnp.dot(
            others[i][...], weights[i][...], preferred_element_type=jnp.float32
        )
        full[i] = total.astype(jnp.bfloat16) * jnp.bfloat16(scales[i])
        for k in range(GROUP):
            columns = pl.ds(pl.multiple_of((mine ^ k) * width, width), width)
            packs[k][i * rows : (i + 1) * rows] = full[i, :, columns]


def halo_kernel(has_ids, *refs):
    pieces, (first, second) = refs[:GROUP], refs[-2:]
    mine = place()
    odd = lax.rem(plane(), 2)
    for k in range(GROUP):
        block = mine ^ k
        for out, skip in ((first, (GROUP - RADIUS) * (1 - odd)), (second, (GROUP - RADIUS) * odd)):
            spot = block - skip

            @pl.when((spot >= 0) & (spot < RADIUS))
            def _():
                out[spot] = pieces[k][...]

    if has_ids:
        last = lax.axis_size("tm") // GROUP - 1

        @pl.when((plane() == 0) | (plane() == last))
        def _():
            second[:, second.shape[1] - ID_ROWS :] = jnp.zeros(
                (RADIUS, ID_ROWS, second.shape[2]), second.dtype
            )


def join_kernel(*refs):
    pieces, out = refs[:GROUP], refs[GROUP]
    width = pieces[0].shape[1]
    mine = place()
    for k in range(GROUP):
        out[:, pl.ds(pl.multiple_of((mine ^ k) * width, width), width)] = pieces[k][...]


def mark(lanes, width, put):
    lanes = lanes.astype(jnp.float32)
    lane = lax.broadcasted_iota(jnp.int32, (width, width), 1).astype(jnp.float32)
    for part in range(2):
        column = jnp.transpose(jnp.broadcast_to(lanes[part : part + 1], (width, width)))
        put(part * width, jnp.where(column == lane, 1.0, 0.0).astype(jnp.bfloat16))


def stacked_ask(block, forbid):
    head = lax.broadcasted_iota(jnp.int32, block.shape, 1) // HEAD
    return jnp.concatenate(
        [
            jnp.concatenate([jnp.where(head == h, block, jnp.zeros_like(block)), forbid], axis=1)
            for h in range(block.shape[1] // HEAD)
        ],
        axis=0,
    )


def by_head(stacked, rows):
    out = stacked[:rows]
    head = lax.broadcasted_iota(jnp.int32, out.shape, 1) // HEAD
    for h in range(1, stacked.shape[0] // rows):
        out = jnp.where(head == h, stacked[h * rows : (h + 1) * rows], out)
    return out


def attend(ask, old, key_at, value_at, count):
    scores = [
        lax.dot_general(
            ask, key_at(c), (((1,), (1,)), ((), ())), preferred_element_type=jnp.float32
        )
        for c in range(count)
    ]
    top = scores[0]
    for s in scores[1:]:
        top = jnp.maximum(top, s)
    peak = jnp.max(top, axis=1, keepdims=True)
    if old is not None:
        peak = jnp.maximum(peak, old)
    mixed = None
    for c, s in enumerate(scores):
        part = jnp.dot(
            jnp.exp(s - peak).astype(jnp.bfloat16), value_at(c), preferred_element_type=jnp.float32
        )
        mixed = part if mixed is None else mixed + part
    return peak, mixed


def plane_kernel(*refs):
    values, projected = refs[:GROUP], refs[GROUP : 2 * GROUP]
    peaks, totals, sums, forbids, asked, keys, beside = refs[2 * GROUP :]
    rows, width = projected[0].shape[0] // 2, projected[0].shape[1]
    mine = place()
    beside[:, :, width:] = jnp.ones((2, GROUP * rows, width), beside.dtype)
    for k in range(GROUP):
        b = mine ^ k

        def spot(at, size):
            return pl.ds(pl.multiple_of(b * rows + at, size), size)

        def put(at, marks):
            for i in range(2):
                keys[i, spot(at, width), width:] = marks
            forbids[b, at : at + width] = (marks - jnp.bfloat16(1.0)) * jnp.bfloat16(-NEG)

        mark(values[k][2 * rows :], width, put)
        for i in range(2):
            keys[i, spot(0, rows), :width] = projected[k][(1 - i) * rows : (2 - i) * rows]
            beside[i, spot(0, rows), :width] = values[k][(1 - i) * rows : (2 - i) * rows]
            asked[i, b] = projected[k][i * rows : (i + 1) * rows]

    def one(b, _):
        for i in range(2):
            peak, mixed = attend(
                stacked_ask(asked[i, b], forbids[b]),
                None,
                lambda c: keys[i, c * rows : (c + 1) * rows],
                lambda c: beside[i, c * rows : (c + 1) * rows],
                GROUP,
            )
            peaks[i, b] = by_head(jnp.broadcast_to(peak, (peak.shape[0], width)), rows)
            sums[i, b] = by_head(mixed[:, :width], rows)
            totals[i, b] = by_head(mixed[:, width:], rows)
        return _

    lax.fori_loop(0, GROUP, one, 0)


def edge_kernel(side, peaks, totals, sums, forbids, asked, *refs):
    value_edges, projected_edges = refs[:2], refs[2:4]
    outs, (keys, beside, whole) = refs[-GROUP - 3 : -3], refs[-3:]
    rows, width = forbids.shape[1:]
    mine = place()
    odd = lax.rem(plane(), 2)
    beside[:, width:] = jnp.ones((beside.shape[0], width), beside.dtype)
    theirs = slice((1 - side) * rows, (2 - side) * rows)
    for edge in range(2):
        base = RADIUS * (odd if edge else 1 - odd)
        for j in range(RADIUS):

            def spot(at, size):
                return pl.ds(pl.multiple_of((base + j) * rows + at, size), size)

            def put(at, marks):
                keys[spot(at, width), width:] = marks

            mark(value_edges[edge][j, 2 * rows :], width, put)
            keys[spot(0, rows), :width] = projected_edges[edge][j, theirs]
            beside[spot(0, rows), :width] = value_edges[edge][j, theirs]

    def one(b, _):
        def near(c):
            return pl.ds(pl.multiple_of((b + c) * rows, rows), rows)

        old = peaks[side, b]
        peak, mixed = attend(
            stacked_ask(asked[side, b], forbids[b]),
            jnp.concatenate([old[:, h : h + 1] for h in range(0, width, HEAD)], axis=0),
            lambda c: keys[near(c)],
            lambda c: beside[near(c)],
            RADIUS,
        )
        factor = jnp.exp(old - by_head(jnp.broadcast_to(peak, (peak.shape[0], width)), rows))
        total = by_head(mixed[:, width:], rows) + totals[side, b] * factor
        mean = (by_head(mixed[:, :width], rows) + sums[side, b] * factor) / total
        whole[b] = mean.astype(whole.dtype)
        return _

    lax.fori_loop(0, GROUP, one, 0)
    for k in range(GROUP):
        outs[k][...] = whole[mine ^ k]


def local(audio_frames, video_frames, recording, audio_query, video_key):
    rows, half = audio_frames.shape
    width = half // GROUP
    length = lax.axis_size("tm")
    bf16, f32 = jnp.bfloat16, jnp.float32
    shape = jax.ShapeDtypeStruct
    assert length % (2 * GROUP) == 0

    def swapped(x):
        return lax.ppermute(x, "head", [(0, 1), (1, 0)])

    def traded(pieces):
        pairs = lambda k: [(i, i ^ k) for i in range(length)]
        return [pieces[0]] + [lax.ppermute(pieces[k], "tm", pairs(k)) for k in range(1, GROUP)]

    def halo(pieces, has_ids):
        size = pieces[0].shape[0]
        edge = shape((RADIUS, size, width), bf16)
        sent = call(
            functools.partial(halo_kernel, has_ids),
            [edge, edge],
            moved=10 * size * width * 2,
            name="halo",
        )(*pieces)

        def partner(i, second):
            spot, inside = divmod(i, GROUP)
            spot = ((spot + second) ^ 1) - second
            return min(max(spot, 0), length // GROUP - 1) * GROUP + inside

        return sent, [
            lax.ppermute(sent[s], "tm", [(i, partner(i, s)) for i in range(length)])
            for s in range(2)
        ]

    other_audio = swapped(audio_frames)
    other_video = swapped(video_frames)
    part = shape((rows, half), f32)
    square = shape((half, half), bf16)
    given = (audio_frames, video_frames, audio_query, video_key, recording.reshape(rows // width, width))
    query_part, key_part, query_rest, key_rest, *values = call(
        prepare_kernel,
        [part, part, square, square] + [shape((2 * rows + ID_ROWS, width), bf16)] * GROUP,
        [pltpu.VMEM((rows, half), bf16)] * 2
        + [pltpu.VMEM((half, half), bf16)] * 2
        + [pltpu.VMEM((rows // width, width), jnp.int32), pltpu.VMEM((ID_ROWS, width), f32)]
        + [pltpu.SemaphoreType.DMA((2 * GROUP + 7,))],
        ins=[HBM] * 5,
        flops=4 * rows * half * half,
        moved=16 * half * half,
        name="prepare",
    )(*(pltpu.with_memory_space_constraint(x, pltpu.HBM) for x in given))
    values = traded(values)
    sent, value_edges = halo(values, True)
    projected = call(
        functools.partial(project_kernel, (HEAD**-0.5, 1.0)),
        [shape((2 * rows, width), bf16)] * GROUP,
        [pltpu.VMEM((2, rows, half), bf16)],
        ins=[VMEM] * 6 + [ANY],
        flops=4 * rows * half * half,
        moved=4 * half * half + 8 * rows * half * 2,
        name="project",
    )(query_part, key_part, other_audio, other_video, query_rest, key_rest, sent[0])
    projected = traded(projected)
    _, projected_edges = halo(projected, False)

    stat = shape((2, GROUP, rows, width), f32)
    held = shape((GROUP, rows, width), bf16)
    inside, around = GROUP * rows, 2 * RADIUS * rows
    state = call(
        plane_kernel,
        [stat, stat, stat, held, shape((2, GROUP, rows, width), bf16)],
        [pltpu.VMEM((2, inside, 2 * width), bf16)] * 2,
        flops=96 * GROUP * rows * inside * width,
        moved=8 * inside * width * 2,
        exps=4 * GROUP * rows * inside,
        name="plane",
    )(*values, *projected)

    def edge(side, *after):
        return call(
            functools.partial(edge_kernel, side),
            [shape((rows, width), bf16)] * GROUP,
            [pltpu.VMEM((around, 2 * width), bf16)] * 2 + [pltpu.VMEM((GROUP, rows, width), bf16)],
            ins=[VMEM] * 9 + [ANY] * len(after),
            flops=48 * GROUP * rows * RADIUS * rows * width,
            moved=8 * around * width * 2,
            exps=2 * GROUP * rows * RADIUS * rows,
            name="edge",
        )(*state, *value_edges, *projected_edges, *after)

    def join(pieces):
        return call(
            join_kernel, shape((rows, half), bf16), moved=2 * rows * half * 2, name="join"
        )(*traded(pieces))

    video_pieces = edge(1)
    audio_pieces = edge(0, video_pieces[0])
    video_attended = join(video_pieces)
    audio_attended = join(audio_pieces)
    return (audio_attended, video_attended)


def solution(mesh):
    return jax.shard_map(
        local,
        mesh=mesh,
        in_specs=(P("tm", "head"), P("tm", "head"), P("tm"), P(None, "head"), P(None, "head")),
        out_specs=(P("tm", "head"), P("tm", "head")),
        check_vma=False,
    )
```

```python
import functools

import jax
import jax.numpy as jnp
from jax import lax
from jax.experimental import pallas as pl
from jax.experimental.pallas import tpu as pltpu
from jax.sharding import PartitionSpec as P

HEAD = 64
RADIUS = 3
GROUP = 4
NEG = -1e30
ID_ROWS = 16
STAT_ROWS = 16

VMEM = pl.BlockSpec(memory_space=pltpu.VMEM)
ANY = pl.BlockSpec(memory_space=pl.ANY)
HBM = pl.BlockSpec(memory_space=pltpu.HBM)


def place():
    return lax.rem(lax.axis_index("tm"), GROUP)


def plane():
    return lax.axis_index("tm") // GROUP


def call(kernel, outs, scratch=(), ins=None, flops=0, moved=0, exps=0, name=None):
    return pl.pallas_call(
        kernel,
        out_shape=outs,
        **({"in_specs": ins} if ins else {}),
        scratch_shapes=scratch,
        compiler_params=pltpu.CompilerParams(vmem_limit_bytes=32 * 2**20),
        cost_estimate=pl.CostEstimate(flops=flops, bytes_accessed=moved, transcendentals=exps),
        name=name,
    )


def prepare_kernel(audio, video, query, key, ids, *refs):
    sums, seconds, columns, streams, id_rows = refs[:2], refs[2:4], refs[4:6], refs[6:8], refs[8]
    firsts, ids_in, ids_wide, sems = refs[9:11], refs[11], refs[12], refs[13]
    half = audio.shape[1]
    width = id_rows.shape[1]
    side = lax.axis_index("head")
    mine = place()
    copies = []

    def fetch(source, target):
        copies.append(pltpu.make_async_copy(source, target, sems.at[len(copies)]))
        copies[-1].start()
        return copies[-1]

    ours = pl.ds(pl.multiple_of(side * half, half), half)
    theirs = pl.ds(pl.multiple_of((1 - side) * half, half), half)
    for i, stream in enumerate((audio, video)):
        fetch(stream, streams[i])
    for i, weight in enumerate((query, key)):
        fetch(weight.at[ours], firsts[i])
    fetch(ids, ids_in)
    for i, stream in enumerate((audio, video)):
        for k in range(GROUP):
            at = pl.ds(pl.multiple_of((mine ^ k) * width, width), width)
            fetch(stream.at[:, at], columns[i].at[k])
    for i, weight in enumerate((query, key)):
        fetch(weight.at[theirs], seconds[i])
    for copy in copies[:5]:
        copy.wait()
    for i in range(2):
        sums[i][...] = jnp.dot(
            streams[i][...], firsts[i][...], preferred_element_type=jnp.float32
        )
    ids_wide[...] = jnp.zeros_like(ids_wide)
    ids_wide[: ids_in.shape[0]] = (ids_in[...] + 1).astype(jnp.float32)
    id_rows[...] = ids_wide[...].astype(id_rows.dtype)
    for copy in copies[5:]:
        copy.wait()


def project_kernel(scale, first, part, other, weight, columns, *refs):
    if first:
        ids, passed, *packs, relay, full = refs
        relay[...] = passed[...]
    else:
        *packs, full = refs
    rows, width = other.shape[0], columns.shape[2]
    mine = place()
    total = part[...] + jnp.dot(other[...], weight[...], preferred_element_type=jnp.float32)
    full[...] = total.astype(jnp.bfloat16) * jnp.bfloat16(scale)
    for k in range(GROUP):
        packs[k][:rows] = columns[k]
        at = pl.ds(pl.multiple_of((mine ^ k) * width, width), width)
        packs[k][rows : 2 * rows] = full[:, at]
        if first:
            packs[k][2 * rows :] = ids[...]


def halo_kernel(*refs):
    pieces, (first, second) = refs[:GROUP], refs[-2:]
    mine = place()
    odd = lax.rem(plane(), 2)
    for k in range(GROUP):
        block = mine ^ k
        for out, skip in ((first, (GROUP - RADIUS) * (1 - odd)), (second, (GROUP - RADIUS) * odd)):
            spot = block - skip

            @pl.when((spot >= 0) & (spot < RADIUS))
            def _():
                out[spot] = pieces[k][...]

    last = lax.axis_size("tm") // GROUP - 1

    @pl.when((plane() == 0) | (plane() == last))
    def _():
        second[:, second.shape[1] - ID_ROWS :] = jnp.zeros(
            (RADIUS, ID_ROWS, second.shape[2]), second.dtype
        )


def join_kernel(*refs):
    pieces, out = refs[:GROUP], refs[GROUP]
    width = pieces[0].shape[1]
    mine = place()
    for k in range(GROUP):
        out[:, pl.ds(pl.multiple_of((mine ^ k) * width, width), width)] = pieces[k][...]


def mark(lanes, put):
    lanes = lanes.astype(jnp.float32)
    width = lanes.shape[1]
    row = lax.broadcasted_iota(jnp.int32, (width, width), 0).astype(jnp.float32)
    for part in range(2):
        turned = jnp.where(row == lanes[part : part + 1], 1.0, 0.0).astype(jnp.bfloat16)
        put(part * width, jnp.transpose(turned))


def forbid(marks):
    return (marks - jnp.bfloat16(1.0)) * jnp.bfloat16(-NEG)


def stacked_ask(block, marks):
    head = lax.broadcasted_iota(jnp.int32, block.shape, 1) // HEAD
    beside = forbid(marks)
    return jnp.concatenate(
        [
            jnp.concatenate([jnp.where(head == h, block, jnp.zeros_like(block)), beside], axis=1)
            for h in range(block.shape[1] // HEAD)
        ],
        axis=0,
    )


def by_head(stacked, rows):
    out = stacked[:rows]
    head = lax.broadcasted_iota(jnp.int32, out.shape, 1) // HEAD
    for h in range(1, stacked.shape[0] // rows):
        out = jnp.where(head == h, stacked[h * rows : (h + 1) * rows], out)
    return out


def attend(ask, old, keys, values):
    scores = [
        lax.dot_general(ask, key, (((1,), (1,)), ((), ())), preferred_element_type=jnp.float32)
        for key in keys
    ]
    top = scores[0]
    for s in scores[1:]:
        top = jnp.maximum(top, s)
    middle = top.shape[1] // 2
    top = jnp.maximum(top[:, :middle], top[:, middle:])
    if old is not None:
        top = jnp.maximum(top, old)
    peak = jnp.max(top, axis=1, keepdims=True)
    mixed = None
    for s, value in zip(scores, values):
        part = jnp.dot(
            jnp.exp(s - peak).astype(jnp.bfloat16), value, preferred_element_type=jnp.float32
        )
        mixed = part if mixed is None else mixed + part
    return peak, mixed


def plane_kernel(*refs):
    audio, video = refs[:GROUP], refs[GROUP : 2 * GROUP]
    peaks, sums, keys, beside = refs[2 * GROUP :]
    rows, width = video[0].shape[0] // 2, video[0].shape[1]
    mine = place()
    beside[:, :, width:] = jnp.ones((2, GROUP * rows, width), beside.dtype)
    for k in range(GROUP):
        b = mine ^ k

        def spot(at, size):
            return pl.ds(pl.multiple_of(b * rows + at, size), size)

        def put(at, marks):
            for i in range(2):
                keys[i, spot(at, width), width:] = marks

        mark(audio[k][2 * rows :], put)
        for i, pack in enumerate((video[k], audio[k])):
            keys[i, spot(0, rows), :width] = pack[rows : 2 * rows]
            beside[i, spot(0, rows), :width] = pack[:rows]

    def one(b, _):
        at = pl.ds(pl.multiple_of(b * rows, rows), rows)
        blocks = [slice(c * rows, (c + 1) * rows) for c in range(GROUP)]
        for i in range(2):
            peak, sums[i, b] = attend(
                stacked_ask(keys[1 - i, at, :width], keys[i, at, width:]),
                None,
                [keys[i, c] for c in blocks],
                [beside[i, c] for c in blocks],
            )
            peaks[i, b] = jnp.broadcast_to(peak, (peak.shape[0], width))
        return _

    lax.fori_loop(0, GROUP, one, 0)


def lend_kernel(edge_a, edge_b, plane_keys, plane_beside, first, second, keys, results):
    rows, width = keys.shape[0] // (2 * RADIUS), keys.shape[1] // 2
    odd = lax.rem(plane(), 2)
    for edge, base in ((edge_a, RADIUS * (1 - odd)), (edge_b, RADIUS * odd)):
        for j in range(RADIUS):

            def spot(at, size):
                return pl.ds(pl.multiple_of((base + j) * rows + at, size), size)

            def put(at, marks):
                keys[spot(at, width), width:] = marks

            mark(edge[j, 2 * rows :], put)
            keys[spot(0, rows), :width] = edge[j, rows : 2 * rows]
    lane = lax.broadcasted_iota(jnp.int32, (rows, width), 1)
    for e in range(2 * RADIUS):
        below, j = e < RADIUS, e % RADIUS
        blocks = range(0, j + 1) if below else range(j + 1, GROUP)
        blocks = [slice(c * rows, (c + 1) * rows) for c in blocks]
        at = slice(e * rows, (e + 1) * rows)
        peak, mixed = attend(
            stacked_ask(keys[at, :width], keys[at, width:]),
            None,
            [plane_keys[0, c] for c in blocks],
            [plane_beside[0, c] for c in blocks],
        )
        mean = by_head(mixed[:, :width], rows) / by_head(mixed[:, width:], rows)
        results[e // RADIUS, j, :rows] = mean.astype(results.dtype)
        logs = peak + jnp.log(mixed[:, width:])
        high = logs.astype(jnp.bfloat16)
        rest = logs - high.astype(jnp.float32)
        middle = rest.astype(jnp.bfloat16)
        low = (rest - middle.astype(jnp.float32)).astype(jnp.bfloat16)
        picked = jnp.zeros((rows, width), jnp.bfloat16)
        for h in range(width // HEAD):
            for n, piece in enumerate((high, middle, low)):
                picked = jnp.where(lane == 8 * h + n, piece[h * rows : (h + 1) * rows], picked)
        for part in range(rows // width):
            turned = jnp.transpose(picked[part * width : (part + 1) * width])
            at = rows + part * STAT_ROWS
            results[e // RADIUS, j, at : at + STAT_ROWS] = turned[:STAT_ROWS]
    first[...] = results[1 - odd]
    second[...] = results[odd]


def edge_kernel(edge_a, edge_b, keys, plane_keys, peaks, sums, *refs):
    outs, (beside, whole) = refs[-GROUP - 2 : -2], refs[-2:]
    rows, width = outs[0].shape
    mine = place()
    odd = lax.rem(plane(), 2)
    beside[:, width:] = jnp.ones((beside.shape[0], width), beside.dtype)
    for edge, base in ((edge_a, RADIUS * (1 - odd)), (edge_b, RADIUS * odd)):
        for j in range(RADIUS):
            beside[pl.ds(pl.multiple_of((base + j) * rows, rows), rows), :width] = edge[j, :rows]

    def one(b, _):
        at = pl.ds(pl.multiple_of(b * rows, rows), rows)
        near = [
            pl.ds(pl.multiple_of((b + c) * rows, rows), rows) for c in range(RADIUS)
        ]
        old = peaks[1, b]
        peak, mixed = attend(
            stacked_ask(plane_keys[0, at, :width], plane_keys[0, at, width:]),
            old,
            [keys[c] for c in near],
            [beside[c] for c in near],
        )
        factor = jnp.exp(old - peak)
        mixed += sums[1, b] * jnp.concatenate([factor, factor], axis=1)
        mean = by_head(mixed[:, :width], rows) / by_head(mixed[:, width:], rows)
        whole[b] = mean.astype(whole.dtype)
        return _

    lax.fori_loop(0, GROUP, one, 0)
    for k in range(GROUP):
        outs[k][...] = whole[mine ^ k]


def merge_kernel(back_a, back_b, peaks, sums, *refs):
    outs, (backs, whole) = refs[-GROUP - 2 : -2], refs[-2:]
    rows, width = outs[0].shape
    mine = place()
    odd = lax.rem(plane(), 2)
    backs[1 - odd] = back_a[...]
    backs[odd] = back_b[...]
    lane = lax.broadcasted_iota(jnp.int32, (width, width), 1)

    def logs(side, j):
        squares = []
        for part in range(rows // width):
            at = rows + part * STAT_ROWS
            stats = backs[side, j, at : at + STAT_ROWS].astype(jnp.float32)
            heads = [
                stats[8 * h : 8 * h + 1] + stats[8 * h + 1 : 8 * h + 2] + stats[8 * h + 2 : 8 * h + 3]
                for h in range(width // HEAD)
            ]
            turned = jnp.transpose(
                jnp.concatenate([jnp.broadcast_to(x, (HEAD, width)) for x in heads], axis=0)
            )
            squares.append(turned)
        return jnp.concatenate(squares, axis=0)

    for b in range(GROUP):
        theirs = []
        if b < RADIUS:
            theirs.append((0, b))
        if b >= GROUP - RADIUS:
            theirs.append((1, b - (GROUP - RADIUS)))
        theirs = [(logs(*t), backs[t[0], t[1], :rows].astype(jnp.float32)) for t in theirs]
        old = by_head(peaks[0, b], rows)
        top = old
        for log, _ in theirs:
            top = jnp.maximum(top, log)
        factor = jnp.exp(old - top)
        value = by_head(sums[0, b, :, :width], rows) * factor
        total = by_head(sums[0, b, :, width:], rows) * factor
        for log, mean in theirs:
            weight = jnp.exp(log - top)
            value += weight * mean
            total += weight
        whole[b] = (value / total).astype(whole.dtype)
    for k in range(GROUP):
        outs[k][...] = whole[mine ^ k]


def local(audio_frames, video_frames, recording, audio_query, video_key):
    rows, half = audio_frames.shape
    width = half // GROUP
    heads = width // HEAD
    length = lax.axis_size("tm")
    bf16, f32 = jnp.bfloat16, jnp.float32
    shape = jax.ShapeDtypeStruct
    assert length % (2 * GROUP) == 0

    def swapped(x):
        return lax.ppermute(x, "head", [(0, 1), (1, 0)])

    def traded(pieces):
        pairs = lambda k: [(i, i ^ k) for i in range(length)]
        return [pieces[0]] + [lax.ppermute(pieces[k], "tm", pairs(k)) for k in range(1, GROUP)]

    def partner(i, second):
        spot, inside = divmod(i, GROUP)
        spot = ((spot + second) ^ 1) - second
        return min(max(spot, 0), length // GROUP - 1) * GROUP + inside

    def crossed(sent):
        return [
            lax.ppermute(sent[s], "tm", [(i, partner(i, s)) for i in range(length)])
            for s in range(2)
        ]

    part = shape((rows, half), f32)
    square = shape((half, half), bf16)
    columns = shape((GROUP, rows, width), bf16)
    stream = shape((rows, half), bf16)
    given = (audio_frames, video_frames, audio_query, video_key, recording.reshape(rows // width, width))
    other_audio = swapped(audio_frames)
    query_part, key_part, query_rest, key_rest, audio_columns, video_columns, _, video_copy, ids = call(
        prepare_kernel,
        [part, part, square, square, columns, columns, stream, stream]
        + [shape((ID_ROWS, width), bf16)],
        [pltpu.VMEM((half, half), bf16)] * 2
        + [pltpu.VMEM((rows // width, width), jnp.int32), pltpu.VMEM((ID_ROWS, width), f32)]
        + [pltpu.SemaphoreType.DMA((7 + 2 * GROUP,))],
        ins=[HBM] * 5,
        flops=4 * rows * half * half,
        moved=16 * half * half,
        name="prepare",
    )(*(pltpu.with_memory_space_constraint(x, pltpu.HBM) for x in given))

    def project(scale, pack_rows, *operands):
        first = len(operands) > 4
        return call(
            functools.partial(project_kernel, scale, first),
            [shape((pack_rows, width), bf16)] * GROUP + ([stream] if first else []),
            [pltpu.VMEM((rows, half), bf16)],
            flops=2 * rows * half * half,
            moved=2 * half * half + 6 * rows * half * 2,
            name="project",
        )(*operands)

    *audio, relay = project(
        HEAD**-0.5,
        2 * rows + ID_ROWS,
        query_part,
        other_audio,
        query_rest,
        audio_columns,
        ids,
        video_copy,
    )
    other_video = swapped(relay)
    audio = traded(audio)
    video = traded(project(1.0, 2 * rows, key_part, other_video, key_rest, video_columns))
    edge = shape((RADIUS, 2 * rows + ID_ROWS, width), bf16)
    edges = crossed(
        call(halo_kernel, [edge, edge], moved=20 * rows * width * 2, name="halo")(*audio)
    )

    inside, around = GROUP * rows, 2 * RADIUS * rows
    asked = shape((2, inside, 2 * width), bf16)
    peaks, sums, plane_keys, plane_beside = call(
        plane_kernel,
        [shape((2, GROUP, heads * rows, n * width), f32) for n in (1, 2)] + [asked, asked],
        flops=32 * GROUP * rows * inside * width,
        moved=8 * inside * width * 2,
        exps=4 * GROUP * rows * inside,
        name="plane",
    )(*audio, *video)
    back = shape((RADIUS, rows + rows // width * STAT_ROWS, width), bf16)
    lent_a, lent_b, keys = call(
        lend_kernel,
        [back, back, shape((around, 2 * width), bf16)],
        [pltpu.VMEM((2,) + back.shape, bf16)],
        flops=48 * RADIUS * GROUP * rows * rows * width,
        moved=8 * around * width * 2,
        exps=2 * RADIUS * GROUP * rows * rows,
        name="lend",
    )(*edges, plane_keys, plane_beside)
    backs = crossed([lent_a, lent_b])

    pieces = [shape((rows, width), bf16)] * GROUP
    video_pieces = call(
        edge_kernel,
        pieces,
        [pltpu.VMEM((around, 2 * width), bf16), pltpu.VMEM((GROUP, rows, width), bf16)],
        flops=48 * RADIUS * GROUP * rows * rows * width,
        moved=8 * around * width * 2,
        exps=2 * RADIUS * GROUP * rows * rows,
        name="edge",
    )(*edges, keys, plane_keys, peaks, sums)
    audio_pieces = call(
        merge_kernel,
        pieces,
        [pltpu.VMEM((2,) + back.shape, bf16), pltpu.VMEM((GROUP, rows, width), bf16)],
        moved=16 * inside * width,
        exps=4 * inside * width,
        ins=[VMEM] * 4 + [ANY],
        name="merge",
    )(*backs, peaks, sums, video_pieces[0])

    def join(pieces):
        return call(
            join_kernel, shape((rows, half), bf16), moved=2 * rows * half * 2, name="join"
        )(*traded(pieces))

    video_attended = join(video_pieces)
    audio_attended = join(audio_pieces)
    return (audio_attended, video_attended)


def solution(mesh):
    return jax.shard_map(
        local,
        mesh=mesh,
        in_specs=(P("tm", "head"), P("tm", "head"), P("tm"), P(None, "head"), P(None, "head")),
        out_specs=(P("tm", "head"), P("tm", "head")),
        check_vma=False,
    )
```

```python
import functools

import jax
import jax.numpy as jnp
from jax import lax
from jax.experimental import pallas as pl
from jax.experimental.pallas import tpu as pltpu
from jax.sharding import PartitionSpec as P

HEAD = 64
RADIUS = 3
GROUP = 4
NEG = -1e30
ID_ROWS = 16
STAT_ROWS = 16

VMEM = pl.BlockSpec(memory_space=pltpu.VMEM)
ANY = pl.BlockSpec(memory_space=pl.ANY)
HBM = pl.BlockSpec(memory_space=pltpu.HBM)


def place():
    return lax.rem(lax.axis_index("tm"), GROUP)


def plane():
    return lax.axis_index("tm") // GROUP


def call(kernel, outs, scratch=(), ins=None, flops=0, moved=0, exps=0, name=None):
    return pl.pallas_call(
        kernel,
        out_shape=outs,
        **({"in_specs": ins} if ins else {}),
        scratch_shapes=scratch,
        compiler_params=pltpu.CompilerParams(vmem_limit_bytes=32 * 2**20),
        cost_estimate=pl.CostEstimate(flops=flops, bytes_accessed=moved, transcendentals=exps),
        name=name,
    )


def prepare_kernel(audio, video, query, key, ids, *refs):
    sums, seconds, sent, packs = refs[:2], refs[2:4], refs[4], refs[5 : 5 + GROUP]
    own, firsts, ids_in, ids_wide, sems = refs[9], refs[10:12], refs[12], refs[13], refs[14]
    rows, half = audio.shape
    width = packs[0].shape[1]
    side = lax.axis_index("head")
    mine = place()
    copies = []

    def fetch(source, target):
        copies.append(pltpu.make_async_copy(source, target, sems.at[len(copies)]))
        copies[-1].start()

    ours = pl.ds(pl.multiple_of(side * half, half), half)
    theirs = pl.ds(pl.multiple_of((1 - side) * half, half), half)
    fetch(ids, ids_in)
    fetch(audio, own)
    fetch(video, sent)
    for i, weight in enumerate((query, key)):
        fetch(weight.at[ours], firsts[i])
    for i, stream in enumerate((audio, video)):
        for k in range(GROUP):
            at = pl.ds(pl.multiple_of((mine ^ k) * width, width), width)
            fetch(stream.at[:, at], packs[k].at[i * rows : (i + 1) * rows])
    for i, weight in enumerate((query, key)):
        fetch(weight.at[theirs], seconds[i])
    for copy in copies[:5]:
        copy.wait()
    for i, stream in enumerate((own, sent)):
        sums[i][...] = jnp.dot(stream[...], firsts[i][...], preferred_element_type=jnp.float32)
    ids_wide[...] = jnp.zeros_like(ids_wide)
    ids_wide[: ids_in.shape[0]] = (ids_in[...] + 1).astype(jnp.float32)
    for k in range(GROUP):
        packs[k][2 * rows :] = ids_wide[...].astype(packs[k].dtype)
    for copy in copies[5:]:
        copy.wait()


def project_kernel(scale, part, other, weight, *refs):
    pieces, full = refs[-GROUP - 1 : -1], refs[-1]
    width = pieces[0].shape[1]
    mine = place()
    total = part[...] + jnp.dot(other[...], weight[...], preferred_element_type=jnp.float32)
    full[...] = total.astype(jnp.bfloat16) * jnp.bfloat16(scale)
    for k in range(GROUP):
        pieces[k][...] = full[:, pl.ds(pl.multiple_of((mine ^ k) * width, width), width)]


def halo_kernel(*refs):
    values, queries, (first, second) = refs[:GROUP], refs[GROUP : 2 * GROUP], refs[-2:]
    rows = queries[0].shape[0]
    mine = place()
    odd = lax.rem(plane(), 2)
    for k in range(GROUP):
        block = mine ^ k
        for out, skip in ((first, (GROUP - RADIUS) * (1 - odd)), (second, (GROUP - RADIUS) * odd)):
            spot = block - skip

            @pl.when((spot >= 0) & (spot < RADIUS))
            def _():
                out[spot, :rows] = values[k][:rows]
                out[spot, rows : 2 * rows] = queries[k][...]
                out[spot, 2 * rows :] = values[k][2 * rows :]

    last = lax.axis_size("tm") // GROUP - 1

    @pl.when((plane() == 0) | (plane() == last))
    def _():
        second[:, second.shape[1] - ID_ROWS :] = jnp.zeros(
            (RADIUS, ID_ROWS, second.shape[2]), second.dtype
        )


def join_kernel(*refs):
    pieces, out = refs[:GROUP], refs[GROUP]
    width = pieces[0].shape[1]
    mine = place()
    for k in range(GROUP):
        out[:, pl.ds(pl.multiple_of((mine ^ k) * width, width), width)] = pieces[k][...]


def marks_turned(lanes):
    lanes = lanes.astype(jnp.float32)
    width = lanes.shape[1]
    row = lax.broadcasted_iota(jnp.int32, (width, width), 0).astype(jnp.float32)
    return [
        jnp.where(row == lanes[part : part + 1], 1.0, 0.0).astype(jnp.bfloat16) for part in range(2)
    ]


def stacked_ask(block, turned):
    head = lax.broadcasted_iota(jnp.int32, block.shape, 1) // HEAD
    marks = jnp.concatenate([jnp.transpose(x) for x in turned], axis=0)
    beside = (marks - jnp.bfloat16(1.0)) * jnp.bfloat16(-NEG)
    return jnp.concatenate(
        [
            jnp.concatenate([jnp.where(head == h, block, jnp.zeros_like(block)), beside], axis=1)
            for h in range(block.shape[1] // HEAD)
        ],
        axis=0,
    )


def by_head(stacked, rows):
    out = stacked[:rows]
    head = lax.broadcasted_iota(jnp.int32, out.shape, 1) // HEAD
    for h in range(1, stacked.shape[0] // rows):
        out = jnp.where(head == h, stacked[h * rows : (h + 1) * rows], out)
    return out


def product(a, b):
    return jnp.dot(a, b, preferred_element_type=jnp.float32)


def attend(scores, old, values):
    width = values.shape[1] // 2
    top = old
    for at in range(0, scores.shape[1], width):
        part = scores[:, at : at + width]
        top = part if top is None else jnp.maximum(top, part)
    peak = jnp.max(top, axis=1, keepdims=True)
    return peak, product(jnp.exp(scores - peak).astype(jnp.bfloat16), values)


def plane_kernel(*refs):
    packs, queries, keys = refs[:GROUP], refs[GROUP : 2 * GROUP], refs[2 * GROUP : 3 * GROUP]
    peaks, sums, turned, beside, asks = refs[3 * GROUP :]
    rows, width = keys[0].shape
    mine = place()
    beside[:, :, width:] = jnp.ones((2, GROUP * rows, width), beside.dtype)
    for k in range(GROUP):
        b = mine ^ k

        def spot(at, size):
            return pl.ds(pl.multiple_of(b * rows + at, size), size)

        marks = marks_turned(packs[k][2 * rows :])
        for i, (ask, key) in enumerate(((queries, keys), (keys, queries))):
            asks[i, b] = stacked_ask(ask[k][...], marks)
            beside[i, spot(0, rows), :width] = packs[k][(1 - i) * rows : (2 - i) * rows]
            for part, x in enumerate(marks):
                at = spot(part * width, width)
                turned[i, :width, at] = jnp.transpose(key[k][part * width : (part + 1) * width])
                turned[i, width:, at] = x

    def one(b, _):
        scores = [product(asks[i, b], turned[i]) for i in range(2)]
        for i in range(2):
            peak, sums[i, b] = attend(scores[i], None, beside[i])
            peaks[i, b] = jnp.broadcast_to(peak, (peak.shape[0], width))
        return _

    lax.fori_loop(0, GROUP, one, 0)


def lend_kernel(edge_a, edge_b, plane_turned, plane_beside, first, second, turned, ordered, results):
    rows, width = (ordered.shape[2] - ID_ROWS) // 2, ordered.shape[3]
    odd = lax.rem(plane(), 2)
    ordered[1 - odd] = edge_a[...]
    ordered[odd] = edge_b[...]
    lane = lax.broadcasted_iota(jnp.int32, (rows, width), 1)
    for e in range(2 * RADIUS):
        side, j = e // RADIUS, e % RADIUS
        marks = marks_turned(ordered[side, j, 2 * rows :])
        query = ordered[side, j, rows : 2 * rows]
        for part, x in enumerate(marks):
            at = slice(e * rows + part * width, e * rows + (part + 1) * width)
            turned[:width, at] = jnp.transpose(query[part * width : (part + 1) * width])
            turned[width:, at] = x
        blocks = slice((j + 1) * rows, GROUP * rows) if side else slice(0, (j + 1) * rows)
        scores = product(stacked_ask(query, marks), plane_turned[0, :, blocks])
        peak, mixed = attend(scores, None, plane_beside[0, blocks])
        mean = by_head(mixed[:, :width], rows) / by_head(mixed[:, width:], rows)
        results[side, j, :rows] = mean.astype(results.dtype)
        logs = peak + jnp.log(mixed[:, width:])
        high = logs.astype(jnp.bfloat16)
        rest = logs - high.astype(jnp.float32)
        middle = rest.astype(jnp.bfloat16)
        low = (rest - middle.astype(jnp.float32)).astype(jnp.bfloat16)
        picked = jnp.zeros((rows, width), jnp.bfloat16)
        for h in range(width // HEAD):
            for n, piece in enumerate((high, middle, low)):
                picked = jnp.where(lane == 8 * h + n, piece[h * rows : (h + 1) * rows], picked)
        for part in range(rows // width):
            stats = jnp.transpose(picked[part * width : (part + 1) * width])
            at = rows + part * STAT_ROWS
            results[side, j, at : at + STAT_ROWS] = stats[:STAT_ROWS]
    first[...] = results[1 - odd]
    second[...] = results[odd]


def edge_kernel(edge_a, edge_b, turned, asks, peaks, sums, *refs):
    outs, (beside, whole) = refs[-GROUP - 2 : -2], refs[-2:]
    rows, width = outs[0].shape
    mine = place()
    odd = lax.rem(plane(), 2)
    beside[:, width:] = jnp.ones((beside.shape[0], width), beside.dtype)
    for edge, base in ((edge_a, RADIUS * (1 - odd)), (edge_b, RADIUS * odd)):
        for j in range(RADIUS):
            beside[pl.ds(pl.multiple_of((base + j) * rows, rows), rows), :width] = edge[j, :rows]
    near = [slice(b * rows, (b + RADIUS) * rows) for b in range(GROUP)]
    scores = product(asks[1, 0], turned[:, near[0]])
    for b in range(GROUP):
        following = product(asks[1, b + 1], turned[:, near[b + 1]]) if b + 1 < GROUP else None
        old = peaks[1, b]
        peak, mixed = attend(scores, old, beside[near[b]])
        factor = jnp.exp(old - peak)
        mixed += sums[1, b] * jnp.concatenate([factor, factor], axis=1)
        mean = by_head(mixed[:, :width], rows) / by_head(mixed[:, width:], rows)
        whole[b] = mean.astype(whole.dtype)
        scores = following
    for k in range(GROUP):
        outs[k][...] = whole[mine ^ k]


def merge_kernel(back_a, back_b, peaks, sums, *refs):
    outs, (backs, whole) = refs[-GROUP - 2 : -2], refs[-2:]
    rows, width = outs[0].shape
    mine = place()
    odd = lax.rem(plane(), 2)
    backs[1 - odd] = back_a[...]
    backs[odd] = back_b[...]
    lane = lax.broadcasted_iota(jnp.int32, (width, width), 1)

    def logs(side, j):
        squares = []
        for part in range(rows // width):
            at = rows + part * STAT_ROWS
            stats = backs[side, j, at : at + STAT_ROWS].astype(jnp.float32)
            heads = [
                stats[8 * h : 8 * h + 1] + stats[8 * h + 1 : 8 * h + 2] + stats[8 * h + 2 : 8 * h + 3]
                for h in range(width // HEAD)
            ]
            turned = jnp.transpose(
                jnp.concatenate([jnp.broadcast_to(x, (HEAD, width)) for x in heads], axis=0)
            )
            squares.append(turned)
        return jnp.concatenate(squares, axis=0)

    for b in range(GROUP):
        theirs = []
        if b < RADIUS:
            theirs.append((0, b))
        if b >= GROUP - RADIUS:
            theirs.append((1, b - (GROUP - RADIUS)))
        theirs = [(logs(*t), backs[t[0], t[1], :rows].astype(jnp.float32)) for t in theirs]
        old = by_head(peaks[0, b], rows)
        top = old
        for log, _ in theirs:
            top = jnp.maximum(top, log)
        factor = jnp.exp(old - top)
        value = by_head(sums[0, b, :, :width], rows) * factor
        total = by_head(sums[0, b, :, width:], rows) * factor
        for log, mean in theirs:
            weight = jnp.exp(log - top)
            value += weight * mean
            total += weight
        whole[b] = (value / total).astype(whole.dtype)
    for k in range(GROUP):
        outs[k][...] = whole[mine ^ k]


def local(audio_frames, video_frames, recording, audio_query, video_key):
    rows, half = audio_frames.shape
    width = half // GROUP
    heads = width // HEAD
    length = lax.axis_size("tm")
    bf16, f32 = jnp.bfloat16, jnp.float32
    shape = jax.ShapeDtypeStruct
    assert length % (2 * GROUP) == 0

    def swapped(x):
        return lax.ppermute(x, "head", [(0, 1), (1, 0)])

    def traded(pieces):
        pairs = lambda k: [(i, i ^ k) for i in range(length)]
        return [pieces[0]] + [lax.ppermute(pieces[k], "tm", pairs(k)) for k in range(1, GROUP)]

    def partner(i, second):
        spot, inside = divmod(i, GROUP)
        spot = ((spot + second) ^ 1) - second
        return min(max(spot, 0), length // GROUP - 1) * GROUP + inside

    def crossed(sent):
        return [
            lax.ppermute(sent[s], "tm", [(i, partner(i, s)) for i in range(length)])
            for s in range(2)
        ]

    part = shape((rows, half), f32)
    square = shape((half, half), bf16)
    stream = shape((rows, half), bf16)
    piece = shape((rows, width), bf16)
    given = (audio_frames, video_frames, audio_query, video_key, recording.reshape(rows // width, width))
    other_audio = swapped(audio_frames)
    query_part, key_part, query_rest, key_rest, video_copy, *packs = call(
        prepare_kernel,
        [part, part, square, square, stream] + [shape((2 * rows + ID_ROWS, width), bf16)] * GROUP,
        [pltpu.VMEM((rows, half), bf16)]
        + [pltpu.VMEM((half, half), bf16)] * 2
        + [pltpu.VMEM((rows // width, width), jnp.int32), pltpu.VMEM((ID_ROWS, width), f32)]
        + [pltpu.SemaphoreType.DMA((7 + 2 * GROUP,))],
        ins=[HBM] * 5,
        flops=4 * rows * half * half,
        moved=16 * half * half,
        name="prepare",
    )(*(pltpu.with_memory_space_constraint(x, pltpu.HBM) for x in given))

    def project(scale, *operands):
        return call(
            functools.partial(project_kernel, scale),
            [piece] * GROUP,
            [pltpu.VMEM((rows, half), bf16)],
            ins=[VMEM] * 3 + [ANY] * (len(operands) - 3),
            flops=2 * rows * half * half,
            moved=2 * half * half + 6 * rows * half * 2,
            name="project",
        )(*operands)

    packs = traded(packs)
    other_video = swapped(video_copy)
    queries = project(HEAD**-0.5, query_part, other_audio, query_rest, *packs[1:])
    queries = traded(queries)
    keys = project(1.0, key_part, other_video, key_rest)
    edge = shape((RADIUS, 2 * rows + ID_ROWS, width), bf16)
    edges = crossed(
        call(
            halo_kernel,
            [edge, edge],
            ins=[VMEM] * (2 * GROUP) + [ANY],
            moved=20 * rows * width * 2,
            name="halo",
        )(*packs, *queries, keys[0])
    )
    keys = traded(keys)

    inside, around = GROUP * rows, 2 * RADIUS * rows
    peaks, sums, plane_turned, plane_beside, asks = call(
        plane_kernel,
        [shape((2, GROUP, heads * rows, n * width), f32) for n in (1, 2)]
        + [shape((2, 2 * width, inside), bf16), shape((2, inside, 2 * width), bf16)]
        + [shape((2, GROUP, heads * rows, 2 * width), bf16)],
        flops=32 * GROUP * rows * inside * width,
        moved=8 * inside * width * 2,
        exps=4 * GROUP * rows * inside,
        name="plane",
    )(*packs, *queries, *keys)
    back = shape((RADIUS, rows + rows // width * STAT_ROWS, width), bf16)
    lent_a, lent_b, edge_turned = call(
        lend_kernel,
        [back, back, shape((2 * width, around), bf16)],
        [pltpu.VMEM((2,) + edge.shape, bf16), pltpu.VMEM((2,) + back.shape, bf16)],
        flops=48 * RADIUS * GROUP * rows * rows * width,
        moved=8 * around * width * 2,
        exps=2 * RADIUS * GROUP * rows * rows,
        name="lend",
    )(*edges, plane_turned, plane_beside)
    backs = crossed([lent_a, lent_b])

    video_pieces = call(
        edge_kernel,
        [piece] * GROUP,
        [pltpu.VMEM((around, 2 * width), bf16), pltpu.VMEM((GROUP, rows, width), bf16)],
        flops=48 * RADIUS * GROUP * rows * rows * width,
        moved=8 * around * width * 2,
        exps=2 * RADIUS * GROUP * rows * rows,
        name="edge",
    )(*edges, edge_turned, asks, peaks, sums)
    audio_pieces = call(
        merge_kernel,
        [piece] * GROUP,
        [pltpu.VMEM((2,) + back.shape, bf16), pltpu.VMEM((GROUP, rows, width), bf16)],
        moved=16 * inside * width,
        exps=4 * inside * width,
        ins=[VMEM] * 4 + [ANY],
        name="merge",
    )(*backs, peaks, sums, video_pieces[0])

    def join(pieces):
        return call(
            join_kernel, shape((rows, half), bf16), moved=2 * rows * half * 2, name="join"
        )(*traded(pieces))

    video_attended = join(video_pieces)
    audio_attended = join(audio_pieces)
    return (audio_attended, video_attended)


def solution(mesh):
    return jax.shard_map(
        local,
        mesh=mesh,
        in_specs=(P("tm", "head"), P("tm", "head"), P("tm"), P(None, "head"), P(None, "head")),
        out_specs=(P("tm", "head"), P("tm", "head")),
        check_vma=False,
    )
```

```python
import functools

import jax
import jax.numpy as jnp
from jax import lax
from jax.experimental import pallas as pl
from jax.experimental.pallas import tpu as pltpu
from jax.sharding import PartitionSpec as P

HEAD = 64
RADIUS = 3
GROUP = 4
NEG = -1e30
ID_ROWS = 16
STAT_ROWS = 16

VMEM = pl.BlockSpec(memory_space=pltpu.VMEM)
ANY = pl.BlockSpec(memory_space=pl.ANY)
HBM = pl.BlockSpec(memory_space=pltpu.HBM)


def place():
    return lax.rem(lax.axis_index("tm"), GROUP)


def plane():
    return lax.axis_index("tm") // GROUP


def call(kernel, outs, scratch=(), ins=None, outs_in=None, flops=0, moved=0, exps=0, name=None):
    return pl.pallas_call(
        kernel,
        out_shape=outs,
        **({"in_specs": ins} if ins else {}),
        **({"out_specs": outs_in} if outs_in else {}),
        scratch_shapes=scratch,
        compiler_params=pltpu.CompilerParams(vmem_limit_bytes=32 * 2**20),
        cost_estimate=pl.CostEstimate(flops=flops, bytes_accessed=moved, transcendentals=exps),
        name=name,
    )


def product(a, b):
    return jnp.dot(a, b, preferred_element_type=jnp.float32)


def fetcher(sems):
    copies = []

    def fetch(source, target):
        copies.append(pltpu.make_async_copy(source, target, sems.at[len(copies)]))
        copies[-1].start()

    return copies, fetch


def split_kernel(audio, video, ids, *refs):
    packs, (ids_in, ids_wide, sems) = refs[:GROUP], refs[GROUP:]
    rows, width = audio.shape[0], packs[0].shape[1]
    mine = place()
    copies, fetch = fetcher(sems)
    fetch(ids, ids_in)
    for k in range(GROUP):
        at = pl.ds(pl.multiple_of((mine ^ k) * width, width), width)
        for i, stream in enumerate((audio, video)):
            fetch(stream.at[:, at], packs[k].at[i * rows : (i + 1) * rows])
    copies[0].wait()
    ids_wide[...] = jnp.zeros_like(ids_wide)
    ids_wide[: ids_in.shape[0]] = (ids_in[...] + 1).astype(jnp.float32)
    for k in range(GROUP):
        packs[k][2 * rows :] = ids_wide[...].astype(packs[k].dtype)
    for copy in copies[1:]:
        copy.wait()


def prepare_kernel(audio, video, query, key, *refs):
    sums, seconds, streams, firsts, sems = refs[-9:-7], refs[-7:-5], refs[-5:-3], refs[-3:-1], refs[-1]
    half = audio.shape[1]
    side = lax.axis_index("head")
    ours = pl.ds(pl.multiple_of(side * half, half), half)
    theirs = pl.ds(pl.multiple_of((1 - side) * half, half), half)
    copies, fetch = fetcher(sems)
    for i, (stream, weight) in enumerate(((audio, query), (video, key))):
        fetch(stream, streams[i])
        fetch(weight.at[ours], firsts[i])
    for i, weight in enumerate((query, key)):
        fetch(weight.at[theirs], seconds[i])
    for i in range(2):
        copies[2 * i].wait()
        copies[2 * i + 1].wait()
        sums[i][...] = product(streams[i][...], firsts[i][...])
    for copy in copies[4:]:
        copy.wait()


def project_kernel(scale, part, other, weight, *refs):
    pieces, full = refs[-GROUP - 1 : -1], refs[-1]
    width = pieces[0].shape[1]
    mine = place()
    total = part[...] + product(other[...], weight[...])
    full[...] = total.astype(jnp.bfloat16) * jnp.bfloat16(scale)
    for k in range(GROUP):
        pieces[k][...] = full[:, pl.ds(pl.multiple_of((mine ^ k) * width, width), width)]


def halo_kernel(*refs):
    values, queries, (first, second) = refs[:GROUP], refs[GROUP : 2 * GROUP], refs[-2:]
    rows = queries[0].shape[0]
    mine = place()
    odd = lax.rem(plane(), 2)
    for k in range(GROUP):
        block = mine ^ k
        for out, skip in ((first, (GROUP - RADIUS) * (1 - odd)), (second, (GROUP - RADIUS) * odd)):
            spot = block - skip

            @pl.when((spot >= 0) & (spot < RADIUS))
            def _():
                out[spot, :rows] = values[k][:rows]
                out[spot, rows : 2 * rows] = queries[k][...]
                out[spot, 2 * rows :] = values[k][2 * rows :]

    last = lax.axis_size("tm") // GROUP - 1

    @pl.when((plane() == 0) | (plane() == last))
    def _():
        second[:, second.shape[1] - ID_ROWS :] = jnp.zeros(
            (RADIUS, ID_ROWS, second.shape[2]), second.dtype
        )


def join_kernel(*refs):
    pieces, out, sems = refs[:GROUP], refs[GROUP], refs[GROUP + 1]
    width = pieces[0].shape[1]
    mine = place()
    copies, fetch = fetcher(sems)
    for k in range(GROUP):
        fetch(pieces[k], out.at[:, pl.ds(pl.multiple_of((mine ^ k) * width, width), width)])
    for copy in copies:
        copy.wait()


def marks_turned(lanes):
    lanes = lanes.astype(jnp.float32)
    width = lanes.shape[1]
    row = lax.broadcasted_iota(jnp.int32, (width, width), 0).astype(jnp.float32)
    return [
        jnp.where(row == lanes[part : part + 1], 1.0, 0.0).astype(jnp.bfloat16) for part in range(2)
    ]


def stacked_ask(block, turned):
    head = lax.broadcasted_iota(jnp.int32, block.shape, 1) // HEAD
    marks = jnp.concatenate([jnp.transpose(x) for x in turned], axis=0)
    beside = (marks - jnp.bfloat16(1.0)) * jnp.bfloat16(-NEG)
    return jnp.concatenate(
        [
            jnp.concatenate([jnp.where(head == h, block, jnp.zeros_like(block)), beside], axis=1)
            for h in range(block.shape[1] // HEAD)
        ],
        axis=0,
    )


def by_head(stacked, rows):
    out = stacked[:rows]
    head = lax.broadcasted_iota(jnp.int32, out.shape, 1) // HEAD
    for h in range(1, stacked.shape[0] // rows):
        out = jnp.where(head == h, stacked[h * rows : (h + 1) * rows], out)
    return out


def attend(scores, old, values):
    width = values.shape[1] // 2
    top = old
    for at in range(0, scores.shape[1], width):
        part = scores[:, at : at + width]
        top = part if top is None else jnp.maximum(top, part)
    peak = jnp.max(top, axis=1, keepdims=True)
    return peak, product(jnp.exp(scores - peak).astype(jnp.bfloat16), values)


def plane_kernel(*refs):
    packs, queries, keys = refs[:GROUP], refs[GROUP : 2 * GROUP], refs[2 * GROUP : 3 * GROUP]
    peaks, sums, turned, beside, asks = refs[3 * GROUP :]
    rows, width = keys[0].shape
    mine = place()
    beside[:, :, width:] = jnp.ones((2, GROUP * rows, width), beside.dtype)
    for k in range(GROUP):
        b = mine ^ k

        def spot(at, size):
            return pl.ds(pl.multiple_of(b * rows + at, size), size)

        marks = marks_turned(packs[k][2 * rows :])
        for i, (ask, key) in enumerate(((queries, keys), (keys, queries))):
            asks[i, b] = stacked_ask(ask[k][...], marks)
            beside[i, spot(0, rows), :width] = packs[k][(1 - i) * rows : (2 - i) * rows]
            for part, x in enumerate(marks):
                at = spot(part * width, width)
                turned[i, :width, at] = jnp.transpose(key[k][part * width : (part + 1) * width])
                turned[i, width:, at] = x

    units = [(i, b) for b in range(GROUP) for i in range(2)]
    ahead = product(asks[units[0]], turned[0])
    for n, (i, b) in enumerate(units):
        scores = ahead
        if n + 1 < len(units):
            ahead = product(asks[units[n + 1]], turned[units[n + 1][0]])
        peak, sums[i, b] = attend(scores, None, beside[i])
        peaks[i, b] = jnp.broadcast_to(peak, (peak.shape[0], width))


def lend_kernel(edge_a, edge_b, plane_turned, plane_beside, first, second, turned, ordered, results):
    rows, width = (ordered.shape[2] - ID_ROWS) // 2, ordered.shape[3]
    odd = lax.rem(plane(), 2)
    ordered[1 - odd] = edge_a[...]
    ordered[odd] = edge_b[...]
    lane = lax.broadcasted_iota(jnp.int32, (rows, width), 1)
    blocks = [slice(0, (j + 1) * rows) for j in range(RADIUS)]
    blocks += [slice((j + 1) * rows, GROUP * rows) for j in range(RADIUS)]

    def scores_of(e):
        side, j = e // RADIUS, e % RADIUS
        marks = marks_turned(ordered[side, j, 2 * rows :])
        query = ordered[side, j, rows : 2 * rows]
        for part, x in enumerate(marks):
            at = slice(e * rows + part * width, e * rows + (part + 1) * width)
            turned[:width, at] = jnp.transpose(query[part * width : (part + 1) * width])
            turned[width:, at] = x
        return product(stacked_ask(query, marks), plane_turned[0, :, blocks[e]])

    ahead = scores_of(0)
    for e in range(2 * RADIUS):
        side, j = e // RADIUS, e % RADIUS
        scores = ahead
        if e + 1 < 2 * RADIUS:
            ahead = scores_of(e + 1)
        peak, mixed = attend(scores, None, plane_beside[0, blocks[e]])
        mean = by_head(mixed[:, :width], rows) / by_head(mixed[:, width:], rows)
        results[side, j, :rows] = mean.astype(results.dtype)
        logs = peak + jnp.log(mixed[:, width:])
        high = logs.astype(jnp.bfloat16)
        rest = logs - high.astype(jnp.float32)
        middle = rest.astype(jnp.bfloat16)
        low = (rest - middle.astype(jnp.float32)).astype(jnp.bfloat16)
        picked = jnp.zeros((rows, width), jnp.bfloat16)
        for h in range(width // HEAD):
            for n, piece in enumerate((high, middle, low)):
                picked = jnp.where(lane == 8 * h + n, piece[h * rows : (h + 1) * rows], picked)
        for part in range(rows // width):
            stats = jnp.transpose(picked[part * width : (part + 1) * width])
            at = rows + part * STAT_ROWS
            results[side, j, at : at + STAT_ROWS] = stats[:STAT_ROWS]
    first[...] = results[1 - odd]
    second[...] = results[odd]


def edge_kernel(edge_a, edge_b, turned, asks, peaks, sums, *refs):
    outs, (beside, whole) = refs[-GROUP - 2 : -2], refs[-2:]
    rows, width = outs[0].shape
    mine = place()
    odd = lax.rem(plane(), 2)
    beside[:, width:] = jnp.ones((beside.shape[0], width), beside.dtype)
    for edge, base in ((edge_a, RADIUS * (1 - odd)), (edge_b, RADIUS * odd)):
        for j in range(RADIUS):
            beside[pl.ds(pl.multiple_of((base + j) * rows, rows), rows), :width] = edge[j, :rows]
    near = [slice(b * rows, (b + RADIUS) * rows) for b in range(GROUP)]
    scores = product(asks[1, 0], turned[:, near[0]])
    for b in range(GROUP):
        following = product(asks[1, b + 1], turned[:, near[b + 1]]) if b + 1 < GROUP else None
        old = peaks[1, b]
        peak, mixed = attend(scores, old, beside[near[b]])
        factor = jnp.exp(old - peak)
        mixed += sums[1, b] * jnp.concatenate([factor, factor], axis=1)
        mean = by_head(mixed[:, :width], rows) / by_head(mixed[:, width:], rows)
        whole[b] = mean.astype(whole.dtype)
        scores = following
    for k in range(GROUP):
        outs[k][...] = whole[mine ^ k]


def merge_kernel(back_a, back_b, peaks, sums, *refs):
    outs, (backs, whole) = refs[-GROUP - 2 : -2], refs[-2:]
    rows, width = outs[0].shape
    mine = place()
    odd = lax.rem(plane(), 2)
    backs[1 - odd] = back_a[...]
    backs[odd] = back_b[...]
    lane = lax.broadcasted_iota(jnp.int32, (width, width), 1)

    def logs(side, j):
        squares = []
        for part in range(rows // width):
            at = rows + part * STAT_ROWS
            stats = backs[side, j, at : at + STAT_ROWS].astype(jnp.float32)
            heads = [
                stats[8 * h : 8 * h + 1] + stats[8 * h + 1 : 8 * h + 2] + stats[8 * h + 2 : 8 * h + 3]
                for h in range(width // HEAD)
            ]
            turned = jnp.transpose(
                jnp.concatenate([jnp.broadcast_to(x, (HEAD, width)) for x in heads], axis=0)
            )
            squares.append(turned)
        return jnp.concatenate(squares, axis=0)

    for b in range(GROUP):
        theirs = []
        if b < RADIUS:
            theirs.append((0, b))
        if b >= GROUP - RADIUS:
            theirs.append((1, b - (GROUP - RADIUS)))
        theirs = [(logs(*t), backs[t[0], t[1], :rows].astype(jnp.float32)) for t in theirs]
        old = by_head(peaks[0, b], rows)
        top = old
        for log, _ in theirs:
            top = jnp.maximum(top, log)
        factor = jnp.exp(old - top)
        value = by_head(sums[0, b, :, :width], rows) * factor
        total = by_head(sums[0, b, :, width:], rows) * factor
        for log, mean in theirs:
            weight = jnp.exp(log - top)
            value += weight * mean
            total += weight
        whole[b] = (value / total).astype(whole.dtype)
    for k in range(GROUP):
        outs[k][...] = whole[mine ^ k]


def local(audio_frames, video_frames, recording, audio_query, video_key):
    rows, half = audio_frames.shape
    width = half // GROUP
    heads = width // HEAD
    length = lax.axis_size("tm")
    bf16, f32 = jnp.bfloat16, jnp.float32
    shape = jax.ShapeDtypeStruct
    assert length % (2 * GROUP) == 0

    def swapped(x):
        return lax.ppermute(x, "head", [(0, 1), (1, 0)])

    def traded(pieces):
        pairs = lambda k: [(i, i ^ k) for i in range(length)]
        return [pieces[0]] + [lax.ppermute(pieces[k], "tm", pairs(k)) for k in range(1, GROUP)]

    def partner(i, second):
        spot, inside = divmod(i, GROUP)
        spot = ((spot + second) ^ 1) - second
        return min(max(spot, 0), length // GROUP - 1) * GROUP + inside

    def crossed(sent):
        return [
            lax.ppermute(sent[s], "tm", [(i, partner(i, s)) for i in range(length)])
            for s in range(2)
        ]

    part = shape((rows, half), f32)
    square = shape((half, half), bf16)
    piece = shape((rows, width), bf16)
    given = (audio_frames, video_frames, audio_query, video_key, recording.reshape(rows // width, width))
    audio_in, video_in, query_in, key_in, ids_in = (
        pltpu.with_memory_space_constraint(x, pltpu.HBM) for x in given
    )
    other_audio = swapped(audio_frames)
    other_video = swapped(video_frames)
    packs = call(
        split_kernel,
        [shape((2 * rows + ID_ROWS, width), bf16)] * GROUP,
        [pltpu.VMEM((rows // width, width), jnp.int32), pltpu.VMEM((ID_ROWS, width), f32)]
        + [pltpu.SemaphoreType.DMA((1 + 2 * GROUP,))],
        ins=[HBM] * 3,
        moved=8 * rows * half,
        name="split",
    )(audio_in, video_in, ids_in)
    packs = traded(packs)
    query_part, key_part, query_rest, key_rest = call(
        prepare_kernel,
        [part, part, square, square],
        [pltpu.VMEM((rows, half), bf16)] * 2
        + [pltpu.VMEM((half, half), bf16)] * 2
        + [pltpu.SemaphoreType.DMA((6,))],
        ins=[HBM] * 4 + [ANY],
        flops=4 * rows * half * half,
        moved=16 * half * half,
        name="prepare",
    )(audio_in, video_in, query_in, key_in, packs[1])

    def project(scale, *operands):
        return call(
            functools.partial(project_kernel, scale),
            [piece] * GROUP,
            [pltpu.VMEM((rows, half), bf16)],
            ins=[VMEM] * 3 + [ANY] * (len(operands) - 3),
            flops=2 * rows * half * half,
            moved=2 * half * half + 6 * rows * half * 2,
            name="project",
        )(*operands)

    queries = project(HEAD**-0.5, query_part, other_audio, query_rest, *packs[1:])
    queries = traded(queries)
    keys = project(1.0, key_part, other_video, key_rest)
    edge = shape((RADIUS, 2 * rows + ID_ROWS, width), bf16)
    edges = crossed(
        call(
            halo_kernel,
            [edge, edge],
            ins=[VMEM] * (2 * GROUP) + [ANY],
            moved=20 * rows * width * 2,
            name="halo",
        )(*packs, *queries, keys[0])
    )
    keys = traded(keys)

    inside, around = GROUP * rows, 2 * RADIUS * rows
    peaks, sums, plane_turned, plane_beside, asks = call(
        plane_kernel,
        [shape((2, GROUP, heads * rows, n * width), f32) for n in (1, 2)]
        + [shape((2, 2 * width, inside), bf16), shape((2, inside, 2 * width), bf16)]
        + [shape((2, GROUP, heads * rows, 2 * width), bf16)],
        flops=32 * GROUP * rows * inside * width,
        moved=8 * inside * width * 2,
        exps=4 * GROUP * rows * inside,
        name="plane",
    )(*packs, *queries, *keys)
    back = shape((RADIUS, rows + rows // width * STAT_ROWS, width), bf16)
    lent_a, lent_b, edge_turned = call(
        lend_kernel,
        [back, back, shape((2 * width, around), bf16)],
        [pltpu.VMEM((2,) + edge.shape, bf16), pltpu.VMEM((2,) + back.shape, bf16)],
        flops=48 * RADIUS * GROUP * rows * rows * width,
        moved=8 * around * width * 2,
        exps=2 * RADIUS * GROUP * rows * rows,
        name="lend",
    )(*edges, plane_turned, plane_beside)
    backs = crossed([lent_a, lent_b])

    video_pieces = call(
        edge_kernel,
        [piece] * GROUP,
        [pltpu.VMEM((around, 2 * width), bf16), pltpu.VMEM((GROUP, rows, width), bf16)],
        flops=48 * RADIUS * GROUP * rows * rows * width,
        moved=8 * around * width * 2,
        exps=2 * RADIUS * GROUP * rows * rows,
        name="edge",
    )(*edges, edge_turned, asks, peaks, sums)
    audio_pieces = call(
        merge_kernel,
        [piece] * GROUP,
        [pltpu.VMEM((2,) + back.shape, bf16), pltpu.VMEM((GROUP, rows, width), bf16)],
        moved=16 * inside * width,
        exps=4 * inside * width,
        ins=[VMEM] * 4 + [ANY],
        name="merge",
    )(*backs, peaks, sums, video_pieces[0])

    def join(pieces):
        return call(
            join_kernel,
            shape((rows, half), bf16),
            [pltpu.SemaphoreType.DMA((GROUP,))],
            outs_in=HBM,
            moved=2 * rows * half * 2,
            name="join",
        )(*traded(pieces))

    video_attended = join(video_pieces)
    audio_attended = join(audio_pieces)
    return (audio_attended, video_attended)


def solution(mesh):
    return jax.shard_map(
        local,
        mesh=mesh,
        in_specs=(P("tm", "head"), P("tm", "head"), P("tm"), P(None, "head"), P(None, "head")),
        out_specs=(P("tm", "head"), P("tm", "head")),
        check_vma=False,
    )
```

```python
import functools

import jax
import jax.numpy as jnp
from jax import lax
from jax.experimental import pallas as pl
from jax.experimental.pallas import tpu as pltpu
from jax.sharding import PartitionSpec as P

HEAD = 64
RADIUS = 3
GROUP = 4
NEG = -1e30
ID_ROWS = 16
STAT_ROWS = 16

VMEM = pl.BlockSpec(memory_space=pltpu.VMEM)
ANY = pl.BlockSpec(memory_space=pl.ANY)
HBM = pl.BlockSpec(memory_space=pltpu.HBM)


def place():
    return lax.rem(lax.axis_index("tm"), GROUP)


def plane():
    return lax.axis_index("tm") // GROUP


def call(kernel, outs, scratch=(), ins=None, outs_in=None, flops=0, moved=0, exps=0, name=None):
    return pl.pallas_call(
        kernel,
        out_shape=outs,
        **({"in_specs": ins} if ins else {}),
        **({"out_specs": outs_in} if outs_in else {}),
        scratch_shapes=scratch,
        compiler_params=pltpu.CompilerParams(vmem_limit_bytes=32 * 2**20),
        cost_estimate=pl.CostEstimate(flops=flops, bytes_accessed=moved, transcendentals=exps),
        name=name,
    )


def product(a, b):
    return jnp.dot(a, b, preferred_element_type=jnp.float32)


def fetcher(sems):
    copies = []

    def fetch(source, target):
        copies.append(pltpu.make_async_copy(source, target, sems.at[len(copies)]))
        copies[-1].start()

    return copies, fetch


def split_kernel(audio, ids, *refs):
    packs, (ids_in, ids_wide, sems) = refs[:GROUP], refs[GROUP:]
    rows, width = audio.shape[0], packs[0].shape[1]
    mine = place()
    copies, fetch = fetcher(sems)
    fetch(ids, ids_in)
    for k in range(GROUP):
        at = pl.ds(pl.multiple_of((mine ^ k) * width, width), width)
        fetch(audio.at[:, at], packs[k].at[:rows])
    copies[0].wait()
    ids_wide[...] = jnp.zeros_like(ids_wide)
    ids_wide[: ids_in.shape[0]] = (ids_in[...] + 1).astype(jnp.float32)
    for k in range(GROUP):
        packs[k][rows:] = ids_wide[...].astype(packs[k].dtype)
    for copy in copies[1:]:
        copy.wait()


def prepare_kernel(audio, video, query, key, *refs):
    sums, seconds, sent, own, firsts, sems = refs[-9:-7], refs[-7:-5], refs[-5], refs[-4], refs[-3:-1], refs[-1]
    half = audio.shape[1]
    side = lax.axis_index("head")
    ours = pl.ds(pl.multiple_of(side * half, half), half)
    theirs = pl.ds(pl.multiple_of((1 - side) * half, half), half)
    streams = (own, sent)
    copies, fetch = fetcher(sems)
    for i, (stream, weight) in enumerate(((audio, query), (video, key))):
        fetch(stream, streams[i])
        fetch(weight.at[ours], firsts[i])
    for i, weight in enumerate((query, key)):
        fetch(weight.at[theirs], seconds[i])
    for i in range(2):
        copies[2 * i].wait()
        copies[2 * i + 1].wait()
        sums[i][...] = product(streams[i][...], firsts[i][...])
    for copy in copies[4:]:
        copy.wait()


def project_kernel(scale, stream, part, other, weight, *refs):
    pieces, full = refs[-GROUP - 1 : -1], refs[-1]
    rows, width = other.shape[0], pieces[0].shape[1]
    mine = place()
    full[...] = (part[...] + product(other[...], weight[...])).astype(jnp.bfloat16) * jnp.bfloat16(scale)
    for k in range(GROUP):
        at = pl.ds(pl.multiple_of((mine ^ k) * width, width), width)
        if stream:
            pieces[k][:rows] = refs[0][:, at]
        pieces[k][stream * rows :] = full[:, at]


def halo_kernel(*refs):
    values, queries, (first, second) = refs[:GROUP], refs[GROUP : 2 * GROUP], refs[-2:]
    rows = queries[0].shape[0]
    mine = place()
    odd = lax.rem(plane(), 2)
    for k in range(GROUP):
        block = mine ^ k
        for out, skip in ((first, (GROUP - RADIUS) * (1 - odd)), (second, (GROUP - RADIUS) * odd)):
            spot = block - skip

            @pl.when((spot >= 0) & (spot < RADIUS))
            def _():
                out[spot, :rows] = values[k][:rows]
                out[spot, rows : 2 * rows] = queries[k][...]
                out[spot, 2 * rows :] = values[k][rows:]

    last = lax.axis_size("tm") // GROUP - 1

    @pl.when((plane() == 0) | (plane() == last))
    def _():
        second[:, second.shape[1] - ID_ROWS :] = jnp.zeros(
            (RADIUS, ID_ROWS, second.shape[2]), second.dtype
        )


def join_kernel(*refs):
    pieces, out, sems = refs[:GROUP], refs[GROUP], refs[GROUP + 1]
    width = pieces[0].shape[1]
    mine = place()
    copies, fetch = fetcher(sems)
    for k in range(GROUP):
        fetch(pieces[k], out.at[:, pl.ds(pl.multiple_of((mine ^ k) * width, width), width)])
    for copy in copies:
        copy.wait()


def marks_turned(lanes):
    lanes = lanes.astype(jnp.float32)
    width = lanes.shape[1]
    row = lax.broadcasted_iota(jnp.int32, (width, width), 0).astype(jnp.float32)
    return [
        jnp.where(row == lanes[part : part + 1], 1.0, 0.0).astype(jnp.bfloat16) for part in range(2)
    ]


def stacked_ask(block, turned):
    head = lax.broadcasted_iota(jnp.int32, block.shape, 1) // HEAD
    marks = jnp.concatenate([jnp.transpose(x) for x in turned], axis=0)
    beside = (marks - jnp.bfloat16(1.0)) * jnp.bfloat16(-NEG)
    return jnp.concatenate(
        [
            jnp.concatenate([jnp.where(head == h, block, jnp.zeros_like(block)), beside], axis=1)
            for h in range(block.shape[1] // HEAD)
        ],
        axis=0,
    )


def by_head(stacked, rows):
    out = stacked[:rows]
    head = lax.broadcasted_iota(jnp.int32, out.shape, 1) // HEAD
    for h in range(1, stacked.shape[0] // rows):
        out = jnp.where(head == h, stacked[h * rows : (h + 1) * rows], out)
    return out


def attend(scores, old, values):
    width = values.shape[1] // 2
    top = old
    for at in range(0, scores.shape[1], width):
        part = scores[:, at : at + width]
        top = part if top is None else jnp.maximum(top, part)
    peak = jnp.max(top, axis=1, keepdims=True)
    return peak, product(jnp.exp(scores - peak).astype(jnp.bfloat16), values)


def plane_kernel(*refs):
    audio, queries, video = refs[:GROUP], refs[GROUP : 2 * GROUP], refs[2 * GROUP : 3 * GROUP]
    peaks, sums, turned, beside, asks = refs[3 * GROUP :]
    rows, width = queries[0].shape
    mine = place()
    beside[:, :, width:] = jnp.ones((2, GROUP * rows, width), beside.dtype)
    for k in range(GROUP):
        b = mine ^ k

        def spot(at, size):
            return pl.ds(pl.multiple_of(b * rows + at, size), size)

        marks = marks_turned(audio[k][rows:])
        projections = (queries[k][...], video[k][rows:])
        for i in range(2):
            key = projections[1 - i]
            asks[i, b] = stacked_ask(projections[i], marks)
            beside[i, spot(0, rows), :width] = (audio if i else video)[k][:rows]
            for part, x in enumerate(marks):
                at = spot(part * width, width)
                turned[i, :width, at] = jnp.transpose(key[part * width : (part + 1) * width])
                turned[i, width:, at] = x

    units = [(i, b) for b in range(GROUP) for i in range(2)]
    ahead = product(asks[units[0]], turned[0])
    for n, (i, b) in enumerate(units):
        scores = ahead
        if n + 1 < len(units):
            ahead = product(asks[units[n + 1]], turned[units[n + 1][0]])
        peak, sums[i, b] = attend(scores, None, beside[i])
        peaks[i, b] = jnp.broadcast_to(peak, (peak.shape[0], width))


def lend_kernel(edge_a, edge_b, plane_turned, plane_beside, first, second, turned, ordered, results):
    rows, width = (ordered.shape[2] - ID_ROWS) // 2, ordered.shape[3]
    odd = lax.rem(plane(), 2)
    ordered[1 - odd] = edge_a[...]
    ordered[odd] = edge_b[...]
    lane = lax.broadcasted_iota(jnp.int32, (rows, width), 1)
    blocks = [slice(0, (j + 1) * rows) for j in range(RADIUS)]
    blocks += [slice((j + 1) * rows, GROUP * rows) for j in range(RADIUS)]

    def scores_of(e):
        side, j = e // RADIUS, e % RADIUS
        marks = marks_turned(ordered[side, j, 2 * rows :])
        query = ordered[side, j, rows : 2 * rows]
        for part, x in enumerate(marks):
            at = slice(e * rows + part * width, e * rows + (part + 1) * width)
            turned[:width, at] = jnp.transpose(query[part * width : (part + 1) * width])
            turned[width:, at] = x
        return product(stacked_ask(query, marks), plane_turned[0, :, blocks[e]])

    ahead = scores_of(0)
    for e in range(2 * RADIUS):
        side, j = e // RADIUS, e % RADIUS
        scores = ahead
        if e + 1 < 2 * RADIUS:
            ahead = scores_of(e + 1)
        peak, mixed = attend(scores, None, plane_beside[0, blocks[e]])
        mean = by_head(mixed[:, :width], rows) / by_head(mixed[:, width:], rows)
        results[side, j, :rows] = mean.astype(results.dtype)
        logs = peak + jnp.log(mixed[:, width:])
        high = logs.astype(jnp.bfloat16)
        rest = logs - high.astype(jnp.float32)
        middle = rest.astype(jnp.bfloat16)
        low = (rest - middle.astype(jnp.float32)).astype(jnp.bfloat16)
        picked = jnp.zeros((rows, width), jnp.bfloat16)
        for h in range(width // HEAD):
            for n, piece in enumerate((high, middle, low)):
                picked = jnp.where(lane == 8 * h + n, piece[h * rows : (h + 1) * rows], picked)
        for part in range(rows // width):
            stats = jnp.transpose(picked[part * width : (part + 1) * width])
            at = rows + part * STAT_ROWS
            results[side, j, at : at + STAT_ROWS] = stats[:STAT_ROWS]
    first[...] = results[1 - odd]
    second[...] = results[odd]


def edge_kernel(edge_a, edge_b, turned, asks, peaks, sums, *refs):
    outs, (beside, whole) = refs[-GROUP - 2 : -2], refs[-2:]
    rows, width = outs[0].shape
    mine = place()
    odd = lax.rem(plane(), 2)
    beside[:, width:] = jnp.ones((beside.shape[0], width), beside.dtype)
    for edge, base in ((edge_a, RADIUS * (1 - odd)), (edge_b, RADIUS * odd)):
        for j in range(RADIUS):
            beside[pl.ds(pl.multiple_of((base + j) * rows, rows), rows), :width] = edge[j, :rows]
    near = [slice(b * rows, (b + RADIUS) * rows) for b in range(GROUP)]
    scores = product(asks[1, 0], turned[:, near[0]])
    for b in range(GROUP):
        following = product(asks[1, b + 1], turned[:, near[b + 1]]) if b + 1 < GROUP else None
        old = peaks[1, b]
        peak, mixed = attend(scores, old, beside[near[b]])
        factor = jnp.exp(old - peak)
        mixed += sums[1, b] * jnp.concatenate([factor, factor], axis=1)
        mean = by_head(mixed[:, :width], rows) / by_head(mixed[:, width:], rows)
        whole[b] = mean.astype(whole.dtype)
        scores = following
    for k in range(GROUP):
        outs[k][...] = whole[mine ^ k]


def merge_kernel(back_a, back_b, peaks, sums, *refs):
    outs, (backs, whole) = refs[-GROUP - 2 : -2], refs[-2:]
    rows, width = outs[0].shape
    mine = place()
    odd = lax.rem(plane(), 2)
    backs[1 - odd] = back_a[...]
    backs[odd] = back_b[...]
    lane = lax.broadcasted_iota(jnp.int32, (width, width), 1)

    def logs(side, j):
        squares = []
        for part in range(rows // width):
            at = rows + part * STAT_ROWS
            stats = backs[side, j, at : at + STAT_ROWS].astype(jnp.float32)
            heads = [
                stats[8 * h : 8 * h + 1] + stats[8 * h + 1 : 8 * h + 2] + stats[8 * h + 2 : 8 * h + 3]
                for h in range(width // HEAD)
            ]
            turned = jnp.transpose(
                jnp.concatenate([jnp.broadcast_to(x, (HEAD, width)) for x in heads], axis=0)
            )
            squares.append(turned)
        return jnp.concatenate(squares, axis=0)

    for b in range(GROUP):
        theirs = []
        if b < RADIUS:
            theirs.append((0, b))
        if b >= GROUP - RADIUS:
            theirs.append((1, b - (GROUP - RADIUS)))
        theirs = [(logs(*t), backs[t[0], t[1], :rows].astype(jnp.float32)) for t in theirs]
        old = by_head(peaks[0, b], rows)
        top = old
        for log, _ in theirs:
            top = jnp.maximum(top, log)
        factor = jnp.exp(old - top)
        value = by_head(sums[0, b, :, :width], rows) * factor
        total = by_head(sums[0, b, :, width:], rows) * factor
        for log, mean in theirs:
            weight = jnp.exp(log - top)
            value += weight * mean
            total += weight
        whole[b] = (value / total).astype(whole.dtype)
    for k in range(GROUP):
        outs[k][...] = whole[mine ^ k]


def local(audio_frames, video_frames, recording, audio_query, video_key):
    rows, half = audio_frames.shape
    width = half // GROUP
    heads = width // HEAD
    length = lax.axis_size("tm")
    bf16, f32 = jnp.bfloat16, jnp.float32
    shape = jax.ShapeDtypeStruct
    assert length % (2 * GROUP) == 0

    def swapped(x):
        return lax.ppermute(x, "head", [(0, 1), (1, 0)])

    def traded(pieces):
        pairs = lambda k: [(i, i ^ k) for i in range(length)]
        return [pieces[0]] + [lax.ppermute(pieces[k], "tm", pairs(k)) for k in range(1, GROUP)]

    def partner(i, second):
        spot, inside = divmod(i, GROUP)
        spot = ((spot + second) ^ 1) - second
        return min(max(spot, 0), length // GROUP - 1) * GROUP + inside

    def crossed(sent):
        return [
            lax.ppermute(sent[s], "tm", [(i, partner(i, s)) for i in range(length)])
            for s in range(2)
        ]

    part = shape((rows, half), f32)
    square = shape((half, half), bf16)
    piece = shape((rows, width), bf16)
    given = (audio_frames, video_frames, audio_query, video_key, recording.reshape(rows // width, width))
    audio_in, video_in, query_in, key_in, ids_in = (
        pltpu.with_memory_space_constraint(x, pltpu.HBM) for x in given
    )
    other_audio = swapped(audio_frames)
    other_video = swapped(video_frames)
    packs = call(
        split_kernel,
        [shape((rows + ID_ROWS, width), bf16)] * GROUP,
        [pltpu.VMEM((rows // width, width), jnp.int32), pltpu.VMEM((ID_ROWS, width), f32)]
        + [pltpu.SemaphoreType.DMA((1 + GROUP,))],
        ins=[HBM] * 2,
        moved=4 * rows * half,
        name="split",
    )(audio_in, ids_in)
    packs = traded(packs)
    query_part, key_part, query_rest, key_rest, video_copy = call(
        prepare_kernel,
        [part, part, square, square, shape((rows, half), bf16)],
        [pltpu.VMEM((rows, half), bf16)]
        + [pltpu.VMEM((half, half), bf16)] * 2
        + [pltpu.SemaphoreType.DMA((6,))],
        ins=[HBM] * 4 + [ANY],
        flops=4 * rows * half * half,
        moved=16 * half * half,
        name="prepare",
    )(audio_in, video_in, query_in, key_in, packs[1])

    def project(scale, *operands, stream=(), after=()):
        return call(
            functools.partial(project_kernel, scale, len(stream)),
            [shape(((1 + len(stream)) * rows, width), bf16)] * GROUP,
            [pltpu.VMEM((rows, half), bf16)],
            ins=[VMEM] * (3 + len(stream)) + [ANY] * len(after),
            flops=2 * rows * half * half,
            moved=2 * half * half + 6 * rows * half * 2,
            name="project",
        )(*operands, *stream, *after)

    queries = project(HEAD**-0.5, query_part, other_audio, query_rest, after=packs[1:])
    queries = traded(queries)
    video = project(1.0, key_part, other_video, key_rest, stream=[video_copy], after=queries[1:])
    edge = shape((RADIUS, 2 * rows + ID_ROWS, width), bf16)
    edges = crossed(
        call(
            halo_kernel,
            [edge, edge],
            ins=[VMEM] * (2 * GROUP) + [ANY],
            moved=20 * rows * width * 2,
            name="halo",
        )(*packs, *queries, video[0])
    )
    video = traded(video)

    inside, around = GROUP * rows, 2 * RADIUS * rows
    peaks, sums, plane_turned, plane_beside, asks = call(
        plane_kernel,
        [shape((2, GROUP, heads * rows, n * width), f32) for n in (1, 2)]
        + [shape((2, 2 * width, inside), bf16), shape((2, inside, 2 * width), bf16)]
        + [shape((2, GROUP, heads * rows, 2 * width), bf16)],
        flops=32 * GROUP * rows * inside * width,
        moved=8 * inside * width * 2,
        exps=4 * GROUP * rows * inside,
        name="plane",
    )(*packs, *queries, *video)
    back = shape((RADIUS, rows + rows // width * STAT_ROWS, width), bf16)
    lent_a, lent_b, edge_turned = call(
        lend_kernel,
        [back, back, shape((2 * width, around), bf16)],
        [pltpu.VMEM((2,) + edge.shape, bf16), pltpu.VMEM((2,) + back.shape, bf16)],
        flops=48 * RADIUS * GROUP * rows * rows * width,
        moved=8 * around * width * 2,
        exps=2 * RADIUS * GROUP * rows * rows,
        name="lend",
    )(*edges, plane_turned, plane_beside)
    backs = crossed([lent_a, lent_b])

    video_pieces = call(
        edge_kernel,
        [piece] * GROUP,
        [pltpu.VMEM((around, 2 * width), bf16), pltpu.VMEM((GROUP, rows, width), bf16)],
        flops=48 * RADIUS * GROUP * rows * rows * width,
        moved=8 * around * width * 2,
        exps=2 * RADIUS * GROUP * rows * rows,
        name="edge",
    )(*edges, edge_turned, asks, peaks, sums)
    audio_pieces = call(
        merge_kernel,
        [piece] * GROUP,
        [pltpu.VMEM((2,) + back.shape, bf16), pltpu.VMEM((GROUP, rows, width), bf16)],
        moved=16 * inside * width,
        exps=4 * inside * width,
        ins=[VMEM] * 4 + [ANY],
        name="merge",
    )(*backs, peaks, sums, video_pieces[0])

    def join(pieces):
        return call(
            join_kernel,
            shape((rows, half), bf16),
            [pltpu.SemaphoreType.DMA((GROUP,))],
            outs_in=HBM,
            moved=2 * rows * half * 2,
            name="join",
        )(*traded(pieces))

    video_attended = join(video_pieces)
    audio_attended = join(audio_pieces)
    return (audio_attended, video_attended)


def solution(mesh):
    return jax.shard_map(
        local,
        mesh=mesh,
        in_specs=(P("tm", "head"), P("tm", "head"), P("tm"), P(None, "head"), P(None, "head")),
        out_specs=(P("tm", "head"), P("tm", "head")),
        check_vma=False,
    )
```

```python
import functools

import jax
import jax.numpy as jnp
from jax import lax
from jax.experimental import pallas as pl
from jax.experimental.pallas import tpu as pltpu
from jax.sharding import PartitionSpec as P

HEAD = 64
RADIUS = 3
GROUP = 4
NEG = -1e30
ID_ROWS = 16
STAT_ROWS = 16

VMEM = pl.BlockSpec(memory_space=pltpu.VMEM)
ANY = pl.BlockSpec(memory_space=pl.ANY)
HBM = pl.BlockSpec(memory_space=pltpu.HBM)


def place():
    return lax.rem(lax.axis_index("tm"), GROUP)


def plane():
    return lax.axis_index("tm") // GROUP


def call(kernel, outs, scratch=(), ins=None, outs_in=None, flops=0, moved=0, exps=0, name=None):
    return pl.pallas_call(
        kernel,
        out_shape=outs,
        **({"in_specs": ins} if ins else {}),
        **({"out_specs": outs_in} if outs_in else {}),
        scratch_shapes=scratch,
        compiler_params=pltpu.CompilerParams(vmem_limit_bytes=32 * 2**20),
        cost_estimate=pl.CostEstimate(flops=flops, bytes_accessed=moved, transcendentals=exps),
        name=name,
    )


def product(a, b):
    return jnp.dot(a, b, preferred_element_type=jnp.float32)


def fetcher(sems):
    copies = []

    def fetch(source, target):
        copies.append(pltpu.make_async_copy(source, target, sems.at[len(copies)]))
        copies[-1].start()

    return copies, fetch


def split_kernel(audio, ids, *refs):
    packs, (ids_in, ids_wide, sems) = refs[:GROUP], refs[GROUP:]
    rows, width = audio.shape[0], packs[0].shape[1]
    mine = place()
    copies, fetch = fetcher(sems)
    fetch(ids, ids_in)
    for k in range(GROUP):
        at = pl.ds(pl.multiple_of((mine ^ k) * width, width), width)
        fetch(audio.at[:, at], packs[k].at[:rows])
    copies[0].wait()
    ids_wide[...] = jnp.zeros_like(ids_wide)
    ids_wide[: ids_in.shape[0]] = (ids_in[...] + 1).astype(jnp.float32)
    for k in range(GROUP):
        packs[k][rows:] = ids_wide[...].astype(packs[k].dtype)
    for copy in copies[1:]:
        copy.wait()


def prepare_kernel(audio, video, query, key, *refs):
    sums, seconds, sent, own, firsts, sems = refs[-9:-7], refs[-7:-5], refs[-5], refs[-4], refs[-3:-1], refs[-1]
    half = audio.shape[1]
    side = lax.axis_index("head")
    ours = pl.ds(pl.multiple_of(side * half, half), half)
    theirs = pl.ds(pl.multiple_of((1 - side) * half, half), half)
    streams = (own, sent)
    copies, fetch = fetcher(sems)
    for i, (stream, weight) in enumerate(((audio, query), (video, key))):
        fetch(stream, streams[i])
        fetch(weight.at[ours], firsts[i])
    for i, weight in enumerate((query, key)):
        fetch(weight.at[theirs], seconds[i])
    for i in range(2):
        copies[2 * i].wait()
        copies[2 * i + 1].wait()
        sums[i][...] = product(streams[i][...], firsts[i][...])
    for copy in copies[4:]:
        copy.wait()


def project_kernel(scale, stream, part, other, weight, *refs):
    pieces, full = refs[-GROUP - 1 : -1], refs[-1]
    rows, width = other.shape[0], pieces[0].shape[1]
    mine = place()
    full[...] = (part[...] + product(other[...], weight[...])).astype(jnp.bfloat16) * jnp.bfloat16(scale)
    for k in range(GROUP):
        at = pl.ds(pl.multiple_of((mine ^ k) * width, width), width)
        if stream:
            pieces[k][:rows] = refs[0][:, at]
        pieces[k][stream * rows :] = full[:, at]


def halo_kernel(*refs):
    values, queries, (first, second) = refs[:GROUP], refs[GROUP : 2 * GROUP], refs[-2:]
    rows = queries[0].shape[0]
    mine = place()
    odd = lax.rem(plane(), 2)
    for k in range(GROUP):
        block = mine ^ k
        for out, skip in ((first, (GROUP - RADIUS) * (1 - odd)), (second, (GROUP - RADIUS) * odd)):
            spot = block - skip

            @pl.when((spot >= 0) & (spot < RADIUS))
            def _():
                out[spot, :rows] = values[k][:rows]
                out[spot, rows : 2 * rows] = queries[k][...]
                out[spot, 2 * rows :] = values[k][rows:]


def join_kernel(*refs):
    pieces, out, sems = refs[:GROUP], refs[GROUP], refs[GROUP + 1]
    width = pieces[0].shape[1]
    mine = place()
    copies, fetch = fetcher(sems)
    for k in range(GROUP):
        fetch(pieces[k], out.at[:, pl.ds(pl.multiple_of((mine ^ k) * width, width), width)])
    for copy in copies:
        copy.wait()


def marks_turned(lanes):
    lanes = lanes.astype(jnp.float32)
    width = lanes.shape[1]
    row = lax.broadcasted_iota(jnp.int32, (width, width), 0).astype(jnp.float32)
    return [
        jnp.where(row == lanes[part : part + 1], 1.0, 0.0).astype(jnp.bfloat16) for part in range(2)
    ]


def stacked_ask(block, turned):
    head = lax.broadcasted_iota(jnp.int32, block.shape, 1) // HEAD
    marks = jnp.concatenate([jnp.transpose(x) for x in turned], axis=0)
    beside = (marks - jnp.bfloat16(1.0)) * jnp.bfloat16(-NEG)
    return jnp.concatenate(
        [
            jnp.concatenate([jnp.where(head == h, block, jnp.zeros_like(block)), beside], axis=1)
            for h in range(block.shape[1] // HEAD)
        ],
        axis=0,
    )


def by_head(stacked, rows):
    out = stacked[:rows]
    head = lax.broadcasted_iota(jnp.int32, out.shape, 1) // HEAD
    for h in range(1, stacked.shape[0] // rows):
        out = jnp.where(head == h, stacked[h * rows : (h + 1) * rows], out)
    return out


def attend(scores, old, values):
    width = values.shape[1] // 2
    top = old
    for at in range(0, scores.shape[1], width):
        part = scores[:, at : at + width]
        top = part if top is None else jnp.maximum(top, part)
    peak = jnp.max(top, axis=1, keepdims=True)
    return peak, product(jnp.exp(scores - peak).astype(jnp.bfloat16), values)


def plane_kernel(*refs):
    audio, queries, video = refs[:GROUP], refs[GROUP : 2 * GROUP], refs[2 * GROUP : 3 * GROUP]
    peaks, sums, turned, beside, asks = refs[3 * GROUP :]
    rows, width = queries[0].shape
    mine = place()
    beside[:, :, width:] = jnp.ones((2, GROUP * rows, width), beside.dtype)
    for k in range(GROUP):
        b = mine ^ k

        def spot(at, size):
            return pl.ds(pl.multiple_of(b * rows + at, size), size)

        marks = marks_turned(audio[k][rows:])
        projections = (queries[k][...], video[k][rows:])
        for i in range(2):
            key = projections[1 - i]
            asks[i, b] = stacked_ask(projections[i], marks)
            beside[i, spot(0, rows), :width] = (audio if i else video)[k][:rows]
            for part, x in enumerate(marks):
                at = spot(part * width, width)
                turned[i, :width, at] = jnp.transpose(key[part * width : (part + 1) * width])
                turned[i, width:, at] = x

    units = [(i, b) for b in range(GROUP) for i in range(2)]
    ahead = product(asks[units[0]], turned[0])
    for n, (i, b) in enumerate(units):
        scores = ahead
        if n + 1 < len(units):
            ahead = product(asks[units[n + 1]], turned[units[n + 1][0]])
        peak, sums[i, b] = attend(scores, None, beside[i])
        peaks[i, b] = jnp.broadcast_to(peak, (peak.shape[0], width))


def lend_kernel(second, edge, plane_turned, plane_beside, result, turned):
    rows, width = (edge.shape[1] - ID_ROWS) // 2, edge.shape[2]
    above = lax.rem(plane() + 1 + second, 2)
    lane = lax.broadcasted_iota(jnp.int32, (rows, width), 1)

    def place_of(n):
        return n + above * (RADIUS - 1 - 2 * n), above * (GROUP - 1 - n)

    def near(n):
        return pl.ds(pl.multiple_of(place_of(n)[1] * rows, rows), (n + 1) * rows)

    def scores_of(n):
        j = place_of(n)[0]
        marks = marks_turned(edge[j, 2 * rows :])
        query = edge[j, rows : 2 * rows]
        for part, x in enumerate(marks):
            at = pl.ds(pl.multiple_of(j * rows + part * width, width), width)
            turned[:width, at] = jnp.transpose(query[part * width : (part + 1) * width])
            turned[width:, at] = x
        return product(stacked_ask(query, marks), plane_turned[0, :, near(n)])

    ahead = scores_of(0)
    for n in range(RADIUS):
        j = place_of(n)[0]
        scores = ahead
        if n + 1 < RADIUS:
            ahead = scores_of(n + 1)
        peak, mixed = attend(scores, None, plane_beside[0, near(n)])
        mean = by_head(mixed[:, :width], rows) / by_head(mixed[:, width:], rows)
        result[j, :rows] = mean.astype(result.dtype)
        logs = peak + jnp.log(mixed[:, width:])
        high = logs.astype(jnp.bfloat16)
        rest = logs - high.astype(jnp.float32)
        middle = rest.astype(jnp.bfloat16)
        low = (rest - middle.astype(jnp.float32)).astype(jnp.bfloat16)
        picked = jnp.zeros((rows, width), jnp.bfloat16)
        for h in range(width // HEAD):
            for m, piece in enumerate((high, middle, low)):
                picked = jnp.where(lane == 8 * h + m, piece[h * rows : (h + 1) * rows], picked)
        for part in range(rows // width):
            stats = jnp.transpose(picked[part * width : (part + 1) * width])
            at = rows + part * STAT_ROWS
            result[j, at : at + STAT_ROWS] = stats[:STAT_ROWS]


def edge_kernel(edge_a, edge_b, turned_a, turned_b, asks, peaks, sums, *refs):
    outs, (turned, beside, whole) = refs[-GROUP - 3 : -3], refs[-3:]
    rows, width = outs[0].shape
    mine = place()
    odd = lax.rem(plane(), 2)
    for half, base in ((turned_a, RADIUS * (1 - odd)), (turned_b, RADIUS * odd)):
        turned[:, pl.ds(pl.multiple_of(base * rows, rows), RADIUS * rows)] = half[...]
    beside[:, width:] = jnp.ones((beside.shape[0], width), beside.dtype)
    for edge, base in ((edge_a, RADIUS * (1 - odd)), (edge_b, RADIUS * odd)):
        for j in range(RADIUS):
            beside[pl.ds(pl.multiple_of((base + j) * rows, rows), rows), :width] = edge[j, :rows]
    near = [slice(b * rows, (b + RADIUS) * rows) for b in range(GROUP)]
    scores = product(asks[1, 0], turned[:, near[0]])
    for b in range(GROUP):
        following = product(asks[1, b + 1], turned[:, near[b + 1]]) if b + 1 < GROUP else None
        old = peaks[1, b]
        peak, mixed = attend(scores, old, beside[near[b]])
        factor = jnp.exp(old - peak)
        mixed += sums[1, b] * jnp.concatenate([factor, factor], axis=1)
        mean = by_head(mixed[:, :width], rows) / by_head(mixed[:, width:], rows)
        whole[b] = mean.astype(whole.dtype)
        scores = following
    for k in range(GROUP):
        outs[k][...] = whole[mine ^ k]


def merge_kernel(back_a, back_b, peaks, sums, *refs):
    outs, (backs, whole) = refs[-GROUP - 2 : -2], refs[-2:]
    rows, width = outs[0].shape
    mine = place()
    odd = lax.rem(plane(), 2)
    backs[1 - odd] = back_a[...]
    backs[odd] = back_b[...]
    last = lax.axis_size("tm") // GROUP - 1
    absent = [jnp.where(plane() == end, NEG, 0.0) for end in (0, last)]

    def logs(side, j):
        squares = []
        for part in range(rows // width):
            at = rows + part * STAT_ROWS
            stats = backs[side, j, at : at + STAT_ROWS].astype(jnp.float32)
            heads = [
                stats[8 * h : 8 * h + 1] + stats[8 * h + 1 : 8 * h + 2] + stats[8 * h + 2 : 8 * h + 3]
                for h in range(width // HEAD)
            ]
            turned = jnp.transpose(
                jnp.concatenate([jnp.broadcast_to(x, (HEAD, width)) for x in heads], axis=0)
            )
            squares.append(turned)
        return jnp.concatenate(squares, axis=0) + absent[side]

    for b in range(GROUP):
        theirs = []
        if b < RADIUS:
            theirs.append((0, b))
        if b >= GROUP - RADIUS:
            theirs.append((1, b - (GROUP - RADIUS)))
        theirs = [(logs(*t), backs[t[0], t[1], :rows].astype(jnp.float32)) for t in theirs]
        old = by_head(peaks[0, b], rows)
        top = old
        for log, _ in theirs:
            top = jnp.maximum(top, log)
        factor = jnp.exp(old - top)
        value = by_head(sums[0, b, :, :width], rows) * factor
        total = by_head(sums[0, b, :, width:], rows) * factor
        for log, mean in theirs:
            weight = jnp.exp(log - top)
            value += weight * mean
            total += weight
        whole[b] = (value / total).astype(whole.dtype)
    for k in range(GROUP):
        outs[k][...] = whole[mine ^ k]


def local(audio_frames, video_frames, recording, audio_query, video_key):
    rows, half = audio_frames.shape
    width = half // GROUP
    heads = width // HEAD
    length = lax.axis_size("tm")
    bf16, f32 = jnp.bfloat16, jnp.float32
    shape = jax.ShapeDtypeStruct
    assert length % (2 * GROUP) == 0

    def swapped(x):
        return lax.ppermute(x, "head", [(0, 1), (1, 0)])

    def traded(pieces):
        pairs = lambda k: [(i, i ^ k) for i in range(length)]
        return [pieces[0]] + [lax.ppermute(pieces[k], "tm", pairs(k)) for k in range(1, GROUP)]

    def crossed(sent, second):
        planes = range(second, length // GROUP - second)
        pairs = [(p, ((p + second) ^ 1) - second) for p in planes]
        return lax.ppermute(
            sent, "tm", [(p * GROUP + i, q * GROUP + i) for p, q in pairs for i in range(GROUP)]
        )

    part = shape((rows, half), f32)
    square = shape((half, half), bf16)
    piece = shape((rows, width), bf16)
    given = (audio_frames, video_frames, audio_query, video_key, recording.reshape(rows // width, width))
    audio_in, video_in, query_in, key_in, ids_in = (
        pltpu.with_memory_space_constraint(x, pltpu.HBM) for x in given
    )
    other_audio = swapped(audio_frames)
    other_video = swapped(video_frames)
    packs = call(
        split_kernel,
        [shape((rows + ID_ROWS, width), bf16)] * GROUP,
        [pltpu.VMEM((rows // width, width), jnp.int32), pltpu.VMEM((ID_ROWS, width), f32)]
        + [pltpu.SemaphoreType.DMA((1 + GROUP,))],
        ins=[HBM] * 2,
        moved=4 * rows * half,
        name="split",
    )(audio_in, ids_in)
    packs = traded(packs)
    query_part, key_part, query_rest, key_rest, video_copy = call(
        prepare_kernel,
        [part, part, square, square, shape((rows, half), bf16)],
        [pltpu.VMEM((rows, half), bf16)]
        + [pltpu.VMEM((half, half), bf16)] * 2
        + [pltpu.SemaphoreType.DMA((6,))],
        ins=[HBM] * 4 + [ANY],
        flops=4 * rows * half * half,
        moved=16 * half * half,
        name="prepare",
    )(audio_in, video_in, query_in, key_in, packs[1])

    def project(scale, *operands, stream=(), after=()):
        return call(
            functools.partial(project_kernel, scale, len(stream)),
            [shape(((1 + len(stream)) * rows, width), bf16)] * GROUP,
            [pltpu.VMEM((rows, half), bf16)],
            ins=[VMEM] * (3 + len(stream)) + [ANY] * len(after),
            flops=2 * rows * half * half,
            moved=2 * half * half + 6 * rows * half * 2,
            name="project",
        )(*operands, *stream, *after)

    queries = project(HEAD**-0.5, query_part, other_audio, query_rest, after=packs[1:])
    queries = traded(queries)
    video = project(1.0, key_part, other_video, key_rest, stream=[video_copy], after=queries[1:])
    edge = shape((RADIUS, 2 * rows + ID_ROWS, width), bf16)
    sent = call(
        halo_kernel,
        [edge, edge],
        ins=[VMEM] * (2 * GROUP) + [ANY],
        moved=20 * rows * width * 2,
        name="halo",
    )(*packs, *queries, video[0])
    edges = [crossed(sent[i], i) for i in range(2)]
    video = traded(video)

    inside, around = GROUP * rows, 2 * RADIUS * rows
    peaks, sums, plane_turned, plane_beside, asks = call(
        plane_kernel,
        [shape((2, GROUP, heads * rows, n * width), f32) for n in (1, 2)]
        + [shape((2, 2 * width, inside), bf16), shape((2, inside, 2 * width), bf16)]
        + [shape((2, GROUP, heads * rows, 2 * width), bf16)],
        flops=32 * GROUP * rows * inside * width,
        moved=8 * inside * width * 2,
        exps=4 * GROUP * rows * inside,
        name="plane",
    )(*packs, *queries, *video)
    back = shape((RADIUS, rows + rows // width * STAT_ROWS, width), bf16)
    backs, edge_turned = [], []
    for i in range(2):
        lent, edge_keys = call(
            functools.partial(lend_kernel, i),
            [back, shape((2 * width, RADIUS * rows), bf16)],
            flops=24 * RADIUS * GROUP * rows * rows * width,
            moved=4 * around * width * 2,
            exps=RADIUS * GROUP * rows * rows,
            name="lend",
        )(edges[i], plane_turned, plane_beside)
        backs.append(crossed(lent, i))
        edge_turned.append(edge_keys)

    video_pieces = call(
        edge_kernel,
        [piece] * GROUP,
        [pltpu.VMEM((2 * width, around), bf16), pltpu.VMEM((around, 2 * width), bf16)]
        + [pltpu.VMEM((GROUP, rows, width), bf16)],
        flops=48 * RADIUS * GROUP * rows * rows * width,
        moved=8 * around * width * 2,
        exps=2 * RADIUS * GROUP * rows * rows,
        name="edge",
    )(*edges, *edge_turned, asks, peaks, sums)
    audio_pieces = call(
        merge_kernel,
        [piece] * GROUP,
        [pltpu.VMEM((2,) + back.shape, bf16), pltpu.VMEM((GROUP, rows, width), bf16)],
        moved=16 * inside * width,
        exps=4 * inside * width,
        ins=[VMEM] * 4 + [ANY],
        name="merge",
    )(*backs, peaks, sums, video_pieces[0])

    def join(pieces):
        return call(
            join_kernel,
            shape((rows, half), bf16),
            [pltpu.SemaphoreType.DMA((GROUP,))],
            outs_in=HBM,
            moved=2 * rows * half * 2,
            name="join",
        )(*traded(pieces))

    video_attended = join(video_pieces)
    audio_attended = join(audio_pieces)
    return (audio_attended, video_attended)


def solution(mesh):
    return jax.shard_map(
        local,
        mesh=mesh,
        in_specs=(P("tm", "head"), P("tm", "head"), P("tm"), P(None, "head"), P(None, "head")),
        out_specs=(P("tm", "head"), P("tm", "head")),
        check_vma=False,
    )
```

```python
import functools

import jax
import jax.numpy as jnp
from jax import lax
from jax.experimental import pallas as pl
from jax.experimental.pallas import tpu as pltpu
from jax.sharding import PartitionSpec as P

HEAD = 64
RADIUS = 3
GROUP = 4
NEG = -1e30
ID_ROWS = 16
STAT_ROWS = 16

VMEM = pl.BlockSpec(memory_space=pltpu.VMEM)
ANY = pl.BlockSpec(memory_space=pl.ANY)
HBM = pl.BlockSpec(memory_space=pltpu.HBM)


def place():
    return lax.rem(lax.axis_index("tm"), GROUP)


def plane():
    return lax.axis_index("tm") // GROUP


def call(kernel, outs, scratch=(), ins=None, outs_in=None, flops=0, moved=0, exps=0, name=None):
    return pl.pallas_call(
        kernel,
        out_shape=outs,
        **({"in_specs": ins} if ins else {}),
        **({"out_specs": outs_in} if outs_in else {}),
        scratch_shapes=scratch,
        compiler_params=pltpu.CompilerParams(vmem_limit_bytes=32 * 2**20),
        cost_estimate=pl.CostEstimate(flops=flops, bytes_accessed=moved, transcendentals=exps),
        name=name,
    )


def product(a, b):
    return jnp.dot(a, b, preferred_element_type=jnp.float32)


def fetcher(sems):
    copies = []

    def fetch(source, target):
        copies.append(pltpu.make_async_copy(source, target, sems.at[len(copies)]))
        copies[-1].start()

    return copies, fetch


def split_kernel(audio, video, ids, *refs):
    packs, (ids_in, ids_wide, sems) = refs[:GROUP], refs[GROUP:]
    rows, width = audio.shape[0], packs[0].shape[1]
    mine = place()
    copies, fetch = fetcher(sems)
    fetch(ids, ids_in)
    for k in range(GROUP):
        at = pl.ds(pl.multiple_of((mine ^ k) * width, width), width)
        for i, stream in enumerate((audio, video)):
            fetch(stream.at[:, at], packs[k].at[i * rows : (i + 1) * rows])
    copies[0].wait()
    ids_wide[...] = jnp.zeros_like(ids_wide)
    ids_wide[: ids_in.shape[0]] = (ids_in[...] + 1).astype(jnp.float32)
    for k in range(GROUP):
        packs[k][2 * rows :] = ids_wide[...].astype(packs[k].dtype)
    for copy in copies[1:]:
        copy.wait()


def prepare_kernel(audio, video, query, key, *refs):
    sums, seconds, streams, firsts, sems = refs[-9:-7], refs[-7:-5], refs[-5:-3], refs[-3:-1], refs[-1]
    half = audio.shape[1]
    side = lax.axis_index("head")
    ours = pl.ds(pl.multiple_of(side * half, half), half)
    theirs = pl.ds(pl.multiple_of((1 - side) * half, half), half)
    copies, fetch = fetcher(sems)
    for i, (stream, weight) in enumerate(((audio, query), (video, key))):
        fetch(stream, streams[i])
        fetch(weight.at[ours], firsts[i])
    for i, weight in enumerate((query, key)):
        fetch(weight.at[theirs], seconds[i])
    for i in range(2):
        copies[2 * i].wait()
        copies[2 * i + 1].wait()
        sums[i][...] = product(streams[i][...], firsts[i][...])
    for copy in copies[4:]:
        copy.wait()


def project_kernel(scale, part, other, weight, *refs):
    pieces, full = refs[-GROUP - 1 : -1], refs[-1]
    width = pieces[0].shape[1]
    mine = place()
    total = part[...] + product(other[...], weight[...])
    full[...] = total.astype(jnp.bfloat16) * jnp.bfloat16(scale)
    for k in range(GROUP):
        pieces[k][...] = full[:, pl.ds(pl.multiple_of((mine ^ k) * width, width), width)]


def halo_kernel(ids_at, *refs):
    pieces, id_packs, outs = refs[:GROUP], refs[GROUP : 2 * GROUP], refs[-2:]
    rows = outs[0].shape[1] - (ID_ROWS if ids_at else 0)
    mine = place()
    odd = lax.rem(plane(), 2)
    for k in range(GROUP):
        block = mine ^ k
        for out, skip in zip(outs, ((GROUP - RADIUS) * (1 - odd), (GROUP - RADIUS) * odd)):
            spot = block - skip

            @pl.when((spot >= 0) & (spot < RADIUS))
            def _():
                out[spot, :rows] = pieces[k][:rows]
                if ids_at:
                    out[spot, rows:] = id_packs[k][ids_at:]


def join_kernel(*refs):
    pieces, out, sems = refs[:GROUP], refs[GROUP], refs[GROUP + 1]
    width = pieces[0].shape[1]
    mine = place()
    copies, fetch = fetcher(sems)
    for k in range(GROUP):
        fetch(pieces[k], out.at[:, pl.ds(pl.multiple_of((mine ^ k) * width, width), width)])
    for copy in copies:
        copy.wait()


def marks_turned(lanes):
    lanes = lanes.astype(jnp.float32)
    width = lanes.shape[1]
    row = lax.broadcasted_iota(jnp.int32, (width, width), 0).astype(jnp.float32)
    return [
        jnp.where(row == lanes[part : part + 1], 1.0, 0.0).astype(jnp.bfloat16) for part in range(2)
    ]


def stacked_ask(block, turned):
    head = lax.broadcasted_iota(jnp.int32, block.shape, 1) // HEAD
    marks = jnp.concatenate([jnp.transpose(x) for x in turned], axis=0)
    beside = (marks - jnp.bfloat16(1.0)) * jnp.bfloat16(-NEG)
    return jnp.concatenate(
        [
            jnp.concatenate([jnp.where(head == h, block, jnp.zeros_like(block)), beside], axis=1)
            for h in range(block.shape[1] // HEAD)
        ],
        axis=0,
    )


def by_head(stacked, rows):
    out = stacked[:rows]
    head = lax.broadcasted_iota(jnp.int32, out.shape, 1) // HEAD
    for h in range(1, stacked.shape[0] // rows):
        out = jnp.where(head == h, stacked[h * rows : (h + 1) * rows], out)
    return out


def attend(scores, old, values):
    width = values.shape[1] // 2
    top = old
    for at in range(0, scores.shape[1], width):
        part = scores[:, at : at + width]
        top = part if top is None else jnp.maximum(top, part)
    peak = jnp.max(top, axis=1, keepdims=True)
    return peak, product(jnp.exp(scores - peak).astype(jnp.bfloat16), values)


def plane_kernel(*refs):
    packs, queries, keys = refs[:GROUP], refs[GROUP : 2 * GROUP], refs[2 * GROUP : 3 * GROUP]
    peaks, sums, turned, beside, asks = refs[3 * GROUP :]
    rows, width = keys[0].shape
    mine = place()
    beside[:, :, width:] = jnp.ones((2, GROUP * rows, width), beside.dtype)
    for k in range(GROUP):
        b = mine ^ k

        def spot(at, size):
            return pl.ds(pl.multiple_of(b * rows + at, size), size)

        marks = marks_turned(packs[k][2 * rows :])
        for i, (ask, key) in enumerate(((queries, keys), (keys, queries))):
            asks[i, b] = stacked_ask(ask[k][...], marks)
            beside[i, spot(0, rows), :width] = packs[k][(1 - i) * rows : (2 - i) * rows]
            for part, x in enumerate(marks):
                at = spot(part * width, width)
                turned[i, :width, at] = jnp.transpose(key[k][part * width : (part + 1) * width])
                turned[i, width:, at] = x

    units = [(i, b) for b in range(GROUP) for i in range(2)]
    ahead = product(asks[units[0]], turned[0])
    for n, (i, b) in enumerate(units):
        scores = ahead
        if n + 1 < len(units):
            ahead = product(asks[units[n + 1]], turned[units[n + 1][0]])
        peak, sums[i, b] = attend(scores, None, beside[i])
        peaks[i, b] = jnp.broadcast_to(peak, (peak.shape[0], width))


def lend_kernel(edge_b, edge_a, plane_turned, plane_beside, first, second, turned, ordered, results):
    rows, width = ordered.shape[2] - ID_ROWS, ordered.shape[3]
    odd = lax.rem(plane(), 2)
    ordered[1 - odd] = edge_a[...]
    ordered[odd] = edge_b[...]
    lane = lax.broadcasted_iota(jnp.int32, (rows, width), 1)
    blocks = [slice(0, (j + 1) * rows) for j in range(RADIUS)]
    blocks += [slice((j + 1) * rows, GROUP * rows) for j in range(RADIUS)]

    def scores_of(e):
        side, j = e // RADIUS, e % RADIUS
        marks = marks_turned(ordered[side, j, rows:])
        query = ordered[side, j, :rows]
        for part, x in enumerate(marks):
            at = slice(e * rows + part * width, e * rows + (part + 1) * width)
            turned[:width, at] = jnp.transpose(query[part * width : (part + 1) * width])
            turned[width:, at] = x
        return product(stacked_ask(query, marks), plane_turned[0, :, blocks[e]])

    ahead = scores_of(0)
    for e in range(2 * RADIUS):
        side, j = e // RADIUS, e % RADIUS
        scores = ahead
        if e + 1 < 2 * RADIUS:
            ahead = scores_of(e + 1)
        peak, mixed = attend(scores, None, plane_beside[0, blocks[e]])
        mean = by_head(mixed[:, :width], rows) / by_head(mixed[:, width:], rows)
        results[side, j, :rows] = mean.astype(results.dtype)
        logs = peak + jnp.log(mixed[:, width:])
        high = logs.astype(jnp.bfloat16)
        rest = logs - high.astype(jnp.float32)
        middle = rest.astype(jnp.bfloat16)
        low = (rest - middle.astype(jnp.float32)).astype(jnp.bfloat16)
        picked = jnp.zeros((rows, width), jnp.bfloat16)
        for h in range(width // HEAD):
            for n, piece in enumerate((high, middle, low)):
                picked = jnp.where(lane == 8 * h + n, piece[h * rows : (h + 1) * rows], picked)
        for part in range(rows // width):
            stats = jnp.transpose(picked[part * width : (part + 1) * width])
            at = rows + part * STAT_ROWS
            results[side, j, at : at + STAT_ROWS] = stats[:STAT_ROWS]
    first[...] = results[1 - odd]
    second[...] = results[odd]


def edge_kernel(edge_b, edge_a, turned, asks, peaks, sums, *refs):
    outs, (beside, whole) = refs[-GROUP - 2 : -2], refs[-2:]
    rows, width = outs[0].shape
    mine = place()
    odd = lax.rem(plane(), 2)
    beside[:, width:] = jnp.ones((beside.shape[0], width), beside.dtype)
    for edge, base in ((edge_a, RADIUS * (1 - odd)), (edge_b, RADIUS * odd)):
        for j in range(RADIUS):
            beside[pl.ds(pl.multiple_of((base + j) * rows, rows), rows), :width] = edge[j]
    near = [slice(b * rows, (b + RADIUS) * rows) for b in range(GROUP)]
    scores = product(asks[1, 0], turned[:, near[0]])
    for b in range(GROUP):
        following = product(asks[1, b + 1], turned[:, near[b + 1]]) if b + 1 < GROUP else None
        old = peaks[1, b]
        peak, mixed = attend(scores, old, beside[near[b]])
        factor = jnp.exp(old - peak)
        mixed += sums[1, b] * jnp.concatenate([factor, factor], axis=1)
        mean = by_head(mixed[:, :width], rows) / by_head(mixed[:, width:], rows)
        whole[b] = mean.astype(whole.dtype)
        scores = following
    for k in range(GROUP):
        outs[k][...] = whole[mine ^ k]


def merge_kernel(back_a, back_b, peaks, sums, *refs):
    outs, (backs, whole) = refs[-GROUP - 2 : -2], refs[-2:]
    rows, width = outs[0].shape
    mine = place()
    odd = lax.rem(plane(), 2)
    backs[1 - odd] = back_a[...]
    backs[odd] = back_b[...]
    last = lax.axis_size("tm") // GROUP - 1
    absent = [jnp.where(plane() == end, NEG, 0.0) for end in (0, last)]

    def logs(side, j):
        squares = []
        for part in range(rows // width):
            at = rows + part * STAT_ROWS
            stats = backs[side, j, at : at + STAT_ROWS].astype(jnp.float32)
            heads = [
                stats[8 * h : 8 * h + 1] + stats[8 * h + 1 : 8 * h + 2] + stats[8 * h + 2 : 8 * h + 3]
                for h in range(width // HEAD)
            ]
            turned = jnp.transpose(
                jnp.concatenate([jnp.broadcast_to(x, (HEAD, width)) for x in heads], axis=0)
            )
            squares.append(turned)
        return jnp.concatenate(squares, axis=0) + absent[side]

    for b in range(GROUP):
        theirs = []
        if b < RADIUS:
            theirs.append((0, b))
        if b >= GROUP - RADIUS:
            theirs.append((1, b - (GROUP - RADIUS)))
        theirs = [(logs(*t), backs[t[0], t[1], :rows].astype(jnp.float32)) for t in theirs]
        old = by_head(peaks[0, b], rows)
        top = old
        for log, _ in theirs:
            top = jnp.maximum(top, log)
        factor = jnp.exp(old - top)
        value = by_head(sums[0, b, :, :width], rows) * factor
        total = by_head(sums[0, b, :, width:], rows) * factor
        for log, mean in theirs:
            weight = jnp.exp(log - top)
            value += weight * mean
            total += weight
        whole[b] = (value / total).astype(whole.dtype)
    for k in range(GROUP):
        outs[k][...] = whole[mine ^ k]


def local(audio_frames, video_frames, recording, audio_query, video_key):
    rows, half = audio_frames.shape
    width = half // GROUP
    heads = width // HEAD
    length = lax.axis_size("tm")
    bf16, f32 = jnp.bfloat16, jnp.float32
    shape = jax.ShapeDtypeStruct
    assert length % (2 * GROUP) == 0

    def swapped(x):
        return lax.ppermute(x, "head", [(0, 1), (1, 0)])

    def traded(pieces):
        pairs = lambda k: [(i, i ^ k) for i in range(length)]
        return [pieces[0]] + [lax.ppermute(pieces[k], "tm", pairs(k)) for k in range(1, GROUP)]

    def crossed(sent, second):
        planes = range(second, length // GROUP - second)
        pairs = [(p, ((p + second) ^ 1) - second) for p in planes]
        return lax.ppermute(
            sent, "tm", [(p * GROUP + i, q * GROUP + i) for p, q in pairs for i in range(GROUP)]
        )

    part = shape((rows, half), f32)
    square = shape((half, half), bf16)
    piece = shape((rows, width), bf16)
    given = (audio_frames, video_frames, audio_query, video_key, recording.reshape(rows // width, width))
    audio_in, video_in, query_in, key_in, ids_in = (
        pltpu.with_memory_space_constraint(x, pltpu.HBM) for x in given
    )
    other_audio = swapped(audio_frames)
    other_video = swapped(video_frames)
    packs = call(
        split_kernel,
        [shape((2 * rows + ID_ROWS, width), bf16)] * GROUP,
        [pltpu.VMEM((rows // width, width), jnp.int32), pltpu.VMEM((ID_ROWS, width), f32)]
        + [pltpu.SemaphoreType.DMA((1 + 2 * GROUP,))],
        ins=[HBM] * 3,
        moved=8 * rows * half,
        name="split",
    )(audio_in, video_in, ids_in)
    packs = traded(packs)
    query_part, key_part, query_rest, key_rest = call(
        prepare_kernel,
        [part, part, square, square],
        [pltpu.VMEM((rows, half), bf16)] * 2
        + [pltpu.VMEM((half, half), bf16)] * 2
        + [pltpu.SemaphoreType.DMA((6,))],
        ins=[HBM] * 4 + [ANY],
        flops=4 * rows * half * half,
        moved=16 * half * half,
        name="prepare",
    )(audio_in, video_in, query_in, key_in, packs[1])

    def project(scale, *operands):
        return call(
            functools.partial(project_kernel, scale),
            [piece] * GROUP,
            [pltpu.VMEM((rows, half), bf16)],
            ins=[VMEM] * 3 + [ANY] * (len(operands) - 3),
            flops=2 * rows * half * half,
            moved=2 * half * half + 6 * rows * half * 2,
            name="project",
        )(*operands)

    queries = project(HEAD**-0.5, query_part, other_audio, query_rest, *packs[1:])
    queries = traded(queries)
    keys = project(1.0, key_part, other_video, key_rest, *queries[1:])

    def halo(pieces, id_packs, *after):
        edge = shape((RADIUS, rows + (ID_ROWS if id_packs else 0), width), bf16)
        sent = call(
            functools.partial(halo_kernel, 2 * rows if id_packs else 0),
            [edge, edge],
            ins=[VMEM] * (GROUP + len(id_packs)) + [ANY] * len(after),
            moved=10 * rows * width * 2,
            name="halo",
        )(*pieces, *id_packs, *after)
        return [crossed(sent[i], i) for i in range(2)]

    query_edges = halo(queries, packs, keys[0])
    keys = traded(keys)
    audio_edges = halo(packs, [], *keys[1:])

    inside, around = GROUP * rows, 2 * RADIUS * rows
    peaks, sums, plane_turned, plane_beside, asks = call(
        plane_kernel,
        [shape((2, GROUP, heads * rows, n * width), f32) for n in (1, 2)]
        + [shape((2, 2 * width, inside), bf16), shape((2, inside, 2 * width), bf16)]
        + [shape((2, GROUP, heads * rows, 2 * width), bf16)],
        flops=32 * GROUP * rows * inside * width,
        moved=8 * inside * width * 2,
        exps=4 * GROUP * rows * inside,
        name="plane",
    )(*packs, *queries, *keys)
    back = shape((RADIUS, rows + rows // width * STAT_ROWS, width), bf16)
    lent_a, lent_b, edge_turned = call(
        lend_kernel,
        [back, back, shape((2 * width, around), bf16)],
        [pltpu.VMEM((2, RADIUS, rows + ID_ROWS, width), bf16), pltpu.VMEM((2,) + back.shape, bf16)],
        flops=48 * RADIUS * GROUP * rows * rows * width,
        moved=8 * around * width * 2,
        exps=2 * RADIUS * GROUP * rows * rows,
        name="lend",
    )(*query_edges[::-1], plane_turned, plane_beside)
    backs = [crossed(x, i) for i, x in enumerate((lent_a, lent_b))]

    video_pieces = call(
        edge_kernel,
        [piece] * GROUP,
        [pltpu.VMEM((around, 2 * width), bf16), pltpu.VMEM((GROUP, rows, width), bf16)],
        flops=48 * RADIUS * GROUP * rows * rows * width,
        moved=8 * around * width * 2,
        exps=2 * RADIUS * GROUP * rows * rows,
        name="edge",
    )(*audio_edges[::-1], edge_turned, asks, peaks, sums)
    audio_pieces = call(
        merge_kernel,
        [piece] * GROUP,
        [pltpu.VMEM((2,) + back.shape, bf16), pltpu.VMEM((GROUP, rows, width), bf16)],
        moved=16 * inside * width,
        exps=4 * inside * width,
        ins=[VMEM] * 4 + [ANY],
        name="merge",
    )(*backs, peaks, sums, video_pieces[0])

    def join(pieces):
        return call(
            join_kernel,
            shape((rows, half), bf16),
            [pltpu.SemaphoreType.DMA((GROUP,))],
            outs_in=HBM,
            moved=2 * rows * half * 2,
            name="join",
        )(*traded(pieces))

    video_attended = join(video_pieces)
    audio_attended = join(audio_pieces)
    return (audio_attended, video_attended)


def solution(mesh):
    return jax.shard_map(
        local,
        mesh=mesh,
        in_specs=(P("tm", "head"), P("tm", "head"), P("tm"), P(None, "head"), P(None, "head")),
        out_specs=(P("tm", "head"), P("tm", "head")),
        check_vma=False,
    )
```

```python
import functools

import jax
import jax.numpy as jnp
from jax import lax
from jax.experimental import pallas as pl
from jax.experimental.pallas import tpu as pltpu
from jax.sharding import PartitionSpec as P

HEAD = 64
RADIUS = 3
GROUP = 4
NEG = -1e30
ID_ROWS = 16
STAT_ROWS = 16

VMEM = pl.BlockSpec(memory_space=pltpu.VMEM)
ANY = pl.BlockSpec(memory_space=pl.ANY)
HBM = pl.BlockSpec(memory_space=pltpu.HBM)


def place():
    return lax.rem(lax.axis_index("tm"), GROUP)


def plane():
    return lax.axis_index("tm") // GROUP


def call(kernel, outs, scratch=(), ins=None, outs_in=None, flops=0, moved=0, exps=0, name=None):
    return pl.pallas_call(
        kernel,
        out_shape=outs,
        **({"in_specs": ins} if ins else {}),
        **({"out_specs": outs_in} if outs_in else {}),
        scratch_shapes=scratch,
        compiler_params=pltpu.CompilerParams(vmem_limit_bytes=32 * 2**20),
        cost_estimate=pl.CostEstimate(flops=flops, bytes_accessed=moved, transcendentals=exps),
        name=name,
    )


def product(a, b):
    return jnp.dot(a, b, preferred_element_type=jnp.float32)


def fetcher(sems):
    copies = []

    def fetch(source, target):
        copies.append(pltpu.make_async_copy(source, target, sems.at[len(copies)]))
        copies[-1].start()

    return copies, fetch


def split_kernel(audio, ids, *refs):
    packs, (ids_in, ids_wide, sems) = refs[:GROUP], refs[GROUP:]
    rows, width = audio.shape[0], packs[0].shape[1]
    mine = place()
    copies, fetch = fetcher(sems)
    fetch(ids, ids_in)
    for k in range(GROUP):
        at = pl.ds(pl.multiple_of((mine ^ k) * width, width), width)
        fetch(audio.at[:, at], packs[k].at[:rows])
    copies[0].wait()
    ids_wide[...] = jnp.zeros_like(ids_wide)
    ids_wide[: ids_in.shape[0]] = (ids_in[...] + 1).astype(jnp.float32)
    for k in range(GROUP):
        packs[k][rows:] = ids_wide[...].astype(packs[k].dtype)
    for copy in copies[1:]:
        copy.wait()


def prepare_kernel(audio, video, query, key, *refs):
    sums, seconds, sent, own, firsts, sems = refs[-9:-7], refs[-7:-5], refs[-5], refs[-4], refs[-3:-1], refs[-1]
    half = audio.shape[1]
    side = lax.axis_index("head")
    ours = pl.ds(pl.multiple_of(side * half, half), half)
    theirs = pl.ds(pl.multiple_of((1 - side) * half, half), half)
    streams = (own, sent)
    copies, fetch = fetcher(sems)
    for i, (stream, weight) in enumerate(((audio, query), (video, key))):
        fetch(stream, streams[i])
        fetch(weight.at[ours], firsts[i])
    for i, weight in enumerate((query, key)):
        fetch(weight.at[theirs], seconds[i])
    for i in range(2):
        copies[2 * i].wait()
        copies[2 * i + 1].wait()
        sums[i][...] = product(streams[i][...], firsts[i][...])
    for copy in copies[4:]:
        copy.wait()


def project_kernel(scale, stream, part, other, weight, *refs):
    pieces, full = refs[-GROUP - 1 : -1], refs[-1]
    rows, width = other.shape[0], pieces[0].shape[1]
    mine = place()
    full[...] = (part[...] + product(other[...], weight[...])).astype(jnp.bfloat16) * jnp.bfloat16(scale)
    for k in range(GROUP):
        at = pl.ds(pl.multiple_of((mine ^ k) * width, width), width)
        if stream:
            pieces[k][:rows] = refs[0][:, at]
        pieces[k][stream * rows :] = full[:, at]


def halo_kernel(ids_at, *refs):
    pieces, id_packs, outs = refs[:GROUP], refs[GROUP : 2 * GROUP], refs[-2:]
    rows = outs[0].shape[1] - (ID_ROWS if ids_at else 0)
    mine = place()
    odd = lax.rem(plane(), 2)
    for k in range(GROUP):
        block = mine ^ k
        for out, skip in zip(outs, ((GROUP - RADIUS) * (1 - odd), (GROUP - RADIUS) * odd)):
            spot = block - skip

            @pl.when((spot >= 0) & (spot < RADIUS))
            def _():
                out[spot, :rows] = pieces[k][:rows]
                if ids_at:
                    out[spot, rows:] = id_packs[k][ids_at:]


def join_kernel(*refs):
    pieces, out, sems = refs[:GROUP], refs[GROUP], refs[GROUP + 1]
    width = pieces[0].shape[1]
    mine = place()
    copies, fetch = fetcher(sems)
    for k in range(GROUP):
        fetch(pieces[k], out.at[:, pl.ds(pl.multiple_of((mine ^ k) * width, width), width)])
    for copy in copies:
        copy.wait()


def marks_turned(lanes):
    lanes = lanes.astype(jnp.float32)
    width = lanes.shape[1]
    row = lax.broadcasted_iota(jnp.int32, (width, width), 0).astype(jnp.float32)
    return [
        jnp.where(row == lanes[part : part + 1], 1.0, 0.0).astype(jnp.bfloat16) for part in range(2)
    ]


def stacked_ask(block, turned):
    head = lax.broadcasted_iota(jnp.int32, block.shape, 1) // HEAD
    marks = jnp.concatenate([jnp.transpose(x) for x in turned], axis=0)
    beside = (marks - jnp.bfloat16(1.0)) * jnp.bfloat16(-NEG)
    return jnp.concatenate(
        [
            jnp.concatenate([jnp.where(head == h, block, jnp.zeros_like(block)), beside], axis=1)
            for h in range(block.shape[1] // HEAD)
        ],
        axis=0,
    )


def by_head(stacked, rows):
    out = stacked[:rows]
    head = lax.broadcasted_iota(jnp.int32, out.shape, 1) // HEAD
    for h in range(1, stacked.shape[0] // rows):
        out = jnp.where(head == h, stacked[h * rows : (h + 1) * rows], out)
    return out


def attend(scores, old, values):
    width = values.shape[1] // 2
    top = old
    for at in range(0, scores.shape[1], width):
        part = scores[:, at : at + width]
        top = part if top is None else jnp.maximum(top, part)
    peak = jnp.max(top, axis=1, keepdims=True)
    return peak, product(jnp.exp(scores - peak).astype(jnp.bfloat16), values)


def plane_kernel(*refs):
    audio, queries, video = refs[:GROUP], refs[GROUP : 2 * GROUP], refs[2 * GROUP : 3 * GROUP]
    peaks, sums, turned, beside, asks = refs[3 * GROUP :]
    rows, width = queries[0].shape
    mine = place()
    beside[:, :, width:] = jnp.ones((2, GROUP * rows, width), beside.dtype)
    for k in range(GROUP):
        b = mine ^ k

        def spot(at, size):
            return pl.ds(pl.multiple_of(b * rows + at, size), size)

        marks = marks_turned(audio[k][rows:])
        projections = (queries[k][...], video[k][rows:])
        for i in range(2):
            key = projections[1 - i]
            asks[i, b] = stacked_ask(projections[i], marks)
            beside[i, spot(0, rows), :width] = (audio if i else video)[k][:rows]
            for part, x in enumerate(marks):
                at = spot(part * width, width)
                turned[i, :width, at] = jnp.transpose(key[part * width : (part + 1) * width])
                turned[i, width:, at] = x

    units = [(i, b) for b in range(GROUP) for i in range(2)]
    ahead = product(asks[units[0]], turned[0])
    for n, (i, b) in enumerate(units):
        scores = ahead
        if n + 1 < len(units):
            ahead = product(asks[units[n + 1]], turned[units[n + 1][0]])
        peak, sums[i, b] = attend(scores, None, beside[i])
        peaks[i, b] = jnp.broadcast_to(peak, (peak.shape[0], width))


def lend_kernel(edge_b, edge_a, plane_turned, plane_beside, first, second, turned, ordered, results):
    rows, width = ordered.shape[2] - ID_ROWS, ordered.shape[3]
    odd = lax.rem(plane(), 2)
    ordered[1 - odd] = edge_a[...]
    ordered[odd] = edge_b[...]
    lane = lax.broadcasted_iota(jnp.int32, (rows, width), 1)
    blocks = [slice(0, (j + 1) * rows) for j in range(RADIUS)]
    blocks += [slice((j + 1) * rows, GROUP * rows) for j in range(RADIUS)]

    def scores_of(e):
        side, j = e // RADIUS, e % RADIUS
        marks = marks_turned(ordered[side, j, rows:])
        query = ordered[side, j, :rows]
        for part, x in enumerate(marks):
            at = slice(e * rows + part * width, e * rows + (part + 1) * width)
            turned[:width, at] = jnp.transpose(query[part * width : (part + 1) * width])
            turned[width:, at] = x
        return product(stacked_ask(query, marks), plane_turned[0, :, blocks[e]])

    ahead = scores_of(0)
    for e in range(2 * RADIUS):
        side, j = e // RADIUS, e % RADIUS
        scores = ahead
        if e + 1 < 2 * RADIUS:
            ahead = scores_of(e + 1)
        peak, mixed = attend(scores, None, plane_beside[0, blocks[e]])
        mean = by_head(mixed[:, :width], rows) / by_head(mixed[:, width:], rows)
        results[side, j, :rows] = mean.astype(results.dtype)
        logs = peak + jnp.log(mixed[:, width:])
        high = logs.astype(jnp.bfloat16)
        rest = logs - high.astype(jnp.float32)
        middle = rest.astype(jnp.bfloat16)
        low = (rest - middle.astype(jnp.float32)).astype(jnp.bfloat16)
        picked = jnp.zeros((rows, width), jnp.bfloat16)
        for h in range(width // HEAD):
            for n, piece in enumerate((high, middle, low)):
                picked = jnp.where(lane == 8 * h + n, piece[h * rows : (h + 1) * rows], picked)
        for part in range(rows // width):
            stats = jnp.transpose(picked[part * width : (part + 1) * width])
            at = rows + part * STAT_ROWS
            results[side, j, at : at + STAT_ROWS] = stats[:STAT_ROWS]
    first[...] = results[1 - odd]
    second[...] = results[odd]


def edge_kernel(edge_b, edge_a, turned, asks, peaks, sums, *refs):
    outs, (beside, whole) = refs[-GROUP - 2 : -2], refs[-2:]
    rows, width = outs[0].shape
    mine = place()
    odd = lax.rem(plane(), 2)
    beside[:, width:] = jnp.ones((beside.shape[0], width), beside.dtype)
    for edge, base in ((edge_a, RADIUS * (1 - odd)), (edge_b, RADIUS * odd)):
        for j in range(RADIUS):
            beside[pl.ds(pl.multiple_of((base + j) * rows, rows), rows), :width] = edge[j]
    near = [slice(b * rows, (b + RADIUS) * rows) for b in range(GROUP)]
    scores = product(asks[1, 0], turned[:, near[0]])
    for b in range(GROUP):
        following = product(asks[1, b + 1], turned[:, near[b + 1]]) if b + 1 < GROUP else None
        old = peaks[1, b]
        peak, mixed = attend(scores, old, beside[near[b]])
        factor = jnp.exp(old - peak)
        mixed += sums[1, b] * jnp.concatenate([factor, factor], axis=1)
        mean = by_head(mixed[:, :width], rows) / by_head(mixed[:, width:], rows)
        whole[b] = mean.astype(whole.dtype)
        scores = following
    for k in range(GROUP):
        outs[k][...] = whole[mine ^ k]


def merge_kernel(back_a, back_b, peaks, sums, *refs):
    outs, (backs, whole) = refs[-GROUP - 2 : -2], refs[-2:]
    rows, width = outs[0].shape
    mine = place()
    odd = lax.rem(plane(), 2)
    backs[1 - odd] = back_a[...]
    backs[odd] = back_b[...]
    last = lax.axis_size("tm") // GROUP - 1
    absent = [jnp.where(plane() == end, NEG, 0.0) for end in (0, last)]

    def logs(side, j):
        squares = []
        for part in range(rows // width):
            at = rows + part * STAT_ROWS
            stats = backs[side, j, at : at + STAT_ROWS].astype(jnp.float32)
            heads = [
                stats[8 * h : 8 * h + 1] + stats[8 * h + 1 : 8 * h + 2] + stats[8 * h + 2 : 8 * h + 3]
                for h in range(width // HEAD)
            ]
            turned = jnp.transpose(
                jnp.concatenate([jnp.broadcast_to(x, (HEAD, width)) for x in heads], axis=0)
            )
            squares.append(turned)
        return jnp.concatenate(squares, axis=0) + absent[side]

    for b in range(GROUP):
        theirs = []
        if b < RADIUS:
            theirs.append((0, b))
        if b >= GROUP - RADIUS:
            theirs.append((1, b - (GROUP - RADIUS)))
        theirs = [(logs(*t), backs[t[0], t[1], :rows].astype(jnp.float32)) for t in theirs]
        old = by_head(peaks[0, b], rows)
        top = old
        for log, _ in theirs:
            top = jnp.maximum(top, log)
        factor = jnp.exp(old - top)
        value = by_head(sums[0, b, :, :width], rows) * factor
        total = by_head(sums[0, b, :, width:], rows) * factor
        for log, mean in theirs:
            weight = jnp.exp(log - top)
            value += weight * mean
            total += weight
        whole[b] = (value / total).astype(whole.dtype)
    for k in range(GROUP):
        outs[k][...] = whole[mine ^ k]


def local(audio_frames, video_frames, recording, audio_query, video_key):
    rows, half = audio_frames.shape
    width = half // GROUP
    heads = width // HEAD
    length = lax.axis_size("tm")
    bf16, f32 = jnp.bfloat16, jnp.float32
    shape = jax.ShapeDtypeStruct
    assert length % (2 * GROUP) == 0

    def swapped(x):
        return lax.ppermute(x, "head", [(0, 1), (1, 0)])

    def traded(pieces):
        pairs = lambda k: [(i, i ^ k) for i in range(length)]
        return [pieces[0]] + [lax.ppermute(pieces[k], "tm", pairs(k)) for k in range(1, GROUP)]

    def crossed(sent, second):
        planes = range(second, length // GROUP - second)
        pairs = [(p, ((p + second) ^ 1) - second) for p in planes]
        return lax.ppermute(
            sent, "tm", [(p * GROUP + i, q * GROUP + i) for p, q in pairs for i in range(GROUP)]
        )

    part = shape((rows, half), f32)
    square = shape((half, half), bf16)
    piece = shape((rows, width), bf16)
    given = (audio_frames, video_frames, audio_query, video_key, recording.reshape(rows // width, width))
    audio_in, video_in, query_in, key_in, ids_in = (
        pltpu.with_memory_space_constraint(x, pltpu.HBM) for x in given
    )
    other_audio = swapped(audio_frames)
    other_video = swapped(video_frames)
    packs = call(
        split_kernel,
        [shape((rows + ID_ROWS, width), bf16)] * GROUP,
        [pltpu.VMEM((rows // width, width), jnp.int32), pltpu.VMEM((ID_ROWS, width), f32)]
        + [pltpu.SemaphoreType.DMA((1 + GROUP,))],
        ins=[HBM] * 2,
        moved=4 * rows * half,
        name="split",
    )(audio_in, ids_in)
    packs = traded(packs)
    query_part, key_part, query_rest, key_rest, video_copy = call(
        prepare_kernel,
        [part, part, square, square, shape((rows, half), bf16)],
        [pltpu.VMEM((rows, half), bf16)]
        + [pltpu.VMEM((half, half), bf16)] * 2
        + [pltpu.SemaphoreType.DMA((6,))],
        ins=[HBM] * 4 + [ANY],
        flops=4 * rows * half * half,
        moved=16 * half * half,
        name="prepare",
    )(audio_in, video_in, query_in, key_in, packs[1])

    def project(scale, *operands, stream=(), after=()):
        return call(
            functools.partial(project_kernel, scale, len(stream)),
            [shape(((1 + len(stream)) * rows, width), bf16)] * GROUP,
            [pltpu.VMEM((rows, half), bf16)],
            ins=[VMEM] * (3 + len(stream)) + [ANY] * len(after),
            flops=2 * rows * half * half,
            moved=2 * half * half + 6 * rows * half * 2,
            name="project",
        )(*operands, *stream, *after)

    def halo(pieces, id_packs, *after):
        edge = shape((RADIUS, rows + (ID_ROWS if id_packs else 0), width), bf16)
        sent = call(
            functools.partial(halo_kernel, rows if id_packs else 0),
            [edge, edge],
            ins=[VMEM] * (GROUP + len(id_packs)) + [ANY] * len(after),
            moved=10 * rows * width * 2,
            name="halo",
        )(*pieces, *id_packs, *after)
        return [crossed(sent[i], i) for i in range(2)]

    audio_edges = halo(packs, [])
    queries = project(HEAD**-0.5, query_part, other_audio, query_rest, after=packs[1:])
    queries = traded(queries)
    video = project(1.0, key_part, other_video, key_rest, stream=[video_copy], after=queries[1:])
    query_edges = halo(queries, packs, *audio_edges[::-1])
    video = traded(video)

    inside, around = GROUP * rows, 2 * RADIUS * rows
    peaks, sums, plane_turned, plane_beside, asks = call(
        plane_kernel,
        [shape((2, GROUP, heads * rows, n * width), f32) for n in (1, 2)]
        + [shape((2, 2 * width, inside), bf16), shape((2, inside, 2 * width), bf16)]
        + [shape((2, GROUP, heads * rows, 2 * width), bf16)],
        flops=32 * GROUP * rows * inside * width,
        moved=8 * inside * width * 2,
        exps=4 * GROUP * rows * inside,
        name="plane",
    )(*packs, *queries, *video)
    back = shape((RADIUS, rows + rows // width * STAT_ROWS, width), bf16)
    lent_a, lent_b, edge_turned = call(
        lend_kernel,
        [back, back, shape((2 * width, around), bf16)],
        [pltpu.VMEM((2, RADIUS, rows + ID_ROWS, width), bf16), pltpu.VMEM((2,) + back.shape, bf16)],
        flops=48 * RADIUS * GROUP * rows * rows * width,
        moved=8 * around * width * 2,
        exps=2 * RADIUS * GROUP * rows * rows,
        name="lend",
    )(*query_edges[::-1], plane_turned, plane_beside)
    backs = [crossed(x, i) for i, x in enumerate((lent_a, lent_b))]

    video_pieces = call(
        edge_kernel,
        [piece] * GROUP,
        [pltpu.VMEM((around, 2 * width), bf16), pltpu.VMEM((GROUP, rows, width), bf16)],
        flops=48 * RADIUS * GROUP * rows * rows * width,
        moved=8 * around * width * 2,
        exps=2 * RADIUS * GROUP * rows * rows,
        name="edge",
    )(*audio_edges[::-1], edge_turned, asks, peaks, sums)
    audio_pieces = call(
        merge_kernel,
        [piece] * GROUP,
        [pltpu.VMEM((2,) + back.shape, bf16), pltpu.VMEM((GROUP, rows, width), bf16)],
        moved=16 * inside * width,
        exps=4 * inside * width,
        ins=[VMEM] * 4 + [ANY],
        name="merge",
    )(*backs, peaks, sums, video_pieces[0])

    def join(pieces):
        return call(
            join_kernel,
            shape((rows, half), bf16),
            [pltpu.SemaphoreType.DMA((GROUP,))],
            outs_in=HBM,
            moved=2 * rows * half * 2,
            name="join",
        )(*traded(pieces))

    video_attended = join(video_pieces)
    audio_attended = join(audio_pieces)
    return (audio_attended, video_attended)


def solution(mesh):
    return jax.shard_map(
        local,
        mesh=mesh,
        in_specs=(P("tm", "head"), P("tm", "head"), P("tm"), P(None, "head"), P(None, "head")),
        out_specs=(P("tm", "head"), P("tm", "head")),
        check_vma=False,
    )
```

```python
import functools

import jax
import jax.numpy as jnp
from jax import lax
from jax.experimental import pallas as pl
from jax.experimental.pallas import tpu as pltpu
from jax.sharding import PartitionSpec as P

HEAD = 64
RADIUS = 3
GROUP = 4
NEG = -1e30
ID_ROWS = 16
STAT_ROWS = 16

VMEM = pl.BlockSpec(memory_space=pltpu.VMEM)
ANY = pl.BlockSpec(memory_space=pl.ANY)
HBM = pl.BlockSpec(memory_space=pltpu.HBM)


def place():
    return lax.rem(lax.axis_index("tm"), GROUP)


def plane():
    return lax.axis_index("tm") // GROUP


def call(kernel, outs, scratch=(), ins=None, outs_in=None, flops=0, moved=0, exps=0, name=None):
    return pl.pallas_call(
        kernel,
        out_shape=outs,
        **({"in_specs": ins} if ins else {}),
        **({"out_specs": outs_in} if outs_in else {}),
        scratch_shapes=scratch,
        compiler_params=pltpu.CompilerParams(vmem_limit_bytes=32 * 2**20),
        cost_estimate=pl.CostEstimate(flops=flops, bytes_accessed=moved, transcendentals=exps),
        name=name,
    )


def product(a, b):
    return jnp.dot(a, b, preferred_element_type=jnp.float32)


def fetcher(sems):
    copies = []

    def fetch(source, target):
        copies.append(pltpu.make_async_copy(source, target, sems.at[len(copies)]))
        copies[-1].start()

    return copies, fetch


def split_kernel(audio, ids, *refs):
    packs, (ids_in, ids_wide, sems) = refs[:GROUP], refs[GROUP:]
    rows, width = audio.shape[0], packs[0].shape[1]
    mine = place()
    copies, fetch = fetcher(sems)
    fetch(ids, ids_in)
    for k in range(GROUP):
        at = pl.ds(pl.multiple_of((mine ^ k) * width, width), width)
        fetch(audio.at[:, at], packs[k].at[:rows])
    copies[0].wait()
    ids_wide[...] = jnp.zeros_like(ids_wide)
    ids_wide[: ids_in.shape[0]] = (ids_in[...] + 1).astype(jnp.float32)
    for k in range(GROUP):
        packs[k][rows:] = ids_wide[...].astype(packs[k].dtype)
    for copy in copies[1:]:
        copy.wait()


def prepare_kernel(audio, video, query, key, *refs):
    sums, seconds, sent, own, firsts, sems = refs[-9:-7], refs[-7:-5], refs[-5], refs[-4], refs[-3:-1], refs[-1]
    half = audio.shape[1]
    side = lax.axis_index("head")
    ours = pl.ds(pl.multiple_of(side * half, half), half)
    theirs = pl.ds(pl.multiple_of((1 - side) * half, half), half)
    streams = (own, sent)
    copies, fetch = fetcher(sems)
    for i, (stream, weight) in enumerate(((audio, query), (video, key))):
        fetch(stream, streams[i])
        fetch(weight.at[ours], firsts[i])
    for i, weight in enumerate((query, key)):
        fetch(weight.at[theirs], seconds[i])
    for i in range(2):
        copies[2 * i].wait()
        copies[2 * i + 1].wait()
        sums[i][...] = product(streams[i][...], firsts[i][...])
    for copy in copies[4:]:
        copy.wait()


def project_kernel(scale, stream, part, other, weight, *refs):
    pieces, full = refs[-GROUP - 1 : -1], refs[-1]
    rows, width = other.shape[0], pieces[0].shape[1]
    mine = place()
    full[...] = (part[...] + product(other[...], weight[...])).astype(jnp.bfloat16) * jnp.bfloat16(scale)
    for k in range(GROUP):
        at = pl.ds(pl.multiple_of((mine ^ k) * width, width), width)
        if stream:
            pieces[k][:rows] = refs[0][:, at]
        pieces[k][stream * rows :] = full[:, at]


def halo_kernel(ids_at, *refs):
    pieces, id_packs, outs = refs[:GROUP], refs[GROUP : 2 * GROUP], refs[-2:]
    rows = outs[0].shape[1] - (ID_ROWS if ids_at else 0)
    mine = place()
    odd = lax.rem(plane(), 2)
    for k in range(GROUP):
        block = mine ^ k
        for out, skip in zip(outs, ((GROUP - RADIUS) * (1 - odd), (GROUP - RADIUS) * odd)):
            spot = block - skip

            @pl.when((spot >= 0) & (spot < RADIUS))
            def _():
                out[spot, :rows] = pieces[k][:rows]
                if ids_at:
                    out[spot, rows:] = id_packs[k][ids_at:]


def join_kernel(*refs):
    pieces, out, sems = refs[:GROUP], refs[GROUP], refs[GROUP + 1]
    width = pieces[0].shape[1]
    mine = place()
    copies, fetch = fetcher(sems)
    for k in range(GROUP):
        fetch(pieces[k], out.at[:, pl.ds(pl.multiple_of((mine ^ k) * width, width), width)])
    for copy in copies:
        copy.wait()


def marks_turned(lanes):
    lanes = lanes.astype(jnp.float32)
    width = lanes.shape[1]
    row = lax.broadcasted_iota(jnp.int32, (width, width), 0).astype(jnp.float32)
    return [
        jnp.where(row == lanes[part : part + 1], 1.0, 0.0).astype(jnp.bfloat16) for part in range(2)
    ]


def stacked_ask(block, turned):
    head = lax.broadcasted_iota(jnp.int32, block.shape, 1) // HEAD
    marks = jnp.concatenate([jnp.transpose(x) for x in turned], axis=0)
    beside = (marks - jnp.bfloat16(1.0)) * jnp.bfloat16(-NEG)
    return jnp.concatenate(
        [
            jnp.concatenate([jnp.where(head == h, block, jnp.zeros_like(block)), beside], axis=1)
            for h in range(block.shape[1] // HEAD)
        ],
        axis=0,
    )


def by_head(stacked, rows):
    out = stacked[:rows]
    head = lax.broadcasted_iota(jnp.int32, out.shape, 1) // HEAD
    for h in range(1, stacked.shape[0] // rows):
        out = jnp.where(head == h, stacked[h * rows : (h + 1) * rows], out)
    return out


def attend(scores, values):
    top = None
    for s in scores:
        for at in range(0, s.shape[1], values[0].shape[1] // 2):
            part = s[:, at : at + values[0].shape[1] // 2]
            top = part if top is None else jnp.maximum(top, part)
    peak = jnp.max(top, axis=1, keepdims=True)
    mixed = None
    for s, value in zip(scores, values):
        part = product(jnp.exp(s - peak).astype(jnp.bfloat16), value)
        mixed = part if mixed is None else mixed + part
    return peak, mixed


def set_up(audio, asked, keys, values, turned, beside, asks):
    rows, width = asks.shape[1] // 2, asks.shape[2] // 2
    mine = place()
    beside[:, width:] = jnp.ones((GROUP * rows, width), beside.dtype)
    for k in range(GROUP):
        b = mine ^ k

        def spot(at, size):
            return pl.ds(pl.multiple_of(b * rows + at, size), size)

        marks = marks_turned(audio[k][rows:])
        asks[b] = stacked_ask(asked(k), marks)
        beside[spot(0, rows), :width] = values(k)
        key = keys(k)
        for part, x in enumerate(marks):
            at = spot(part * width, width)
            turned[:width, at] = jnp.transpose(key[part * width : (part + 1) * width])
            turned[width:, at] = x


def rows_kernel(*refs):
    audio, queries, video = refs[:GROUP], refs[GROUP : 2 * GROUP], refs[2 * GROUP : 3 * GROUP]
    peaks, sums, turned, beside, asks = refs[-5:]
    rows, width = queries[0].shape
    set_up(
        audio,
        lambda k: queries[k][...],
        lambda k: video[k][rows:],
        lambda k: video[k][:rows],
        turned,
        beside,
        asks,
    )
    ahead = product(asks[0], turned[...])
    for b in range(GROUP):
        scores = ahead
        if b + 1 < GROUP:
            ahead = product(asks[b + 1], turned[...])
        peak, sums[b] = attend([scores], [beside[...]])
        peaks[b] = jnp.broadcast_to(peak, (peak.shape[0], width))


def lend_kernel(edge_b, edge_a, plane_turned, plane_beside, first, second, turned, ordered, results):
    rows, width = ordered.shape[2] - ID_ROWS, ordered.shape[3]
    odd = lax.rem(plane(), 2)
    ordered[1 - odd] = edge_a[...]
    ordered[odd] = edge_b[...]
    lane = lax.broadcasted_iota(jnp.int32, (rows, width), 1)
    blocks = [slice(0, (j + 1) * rows) for j in range(RADIUS)]
    blocks += [slice((j + 1) * rows, GROUP * rows) for j in range(RADIUS)]

    def scores_of(e):
        side, j = e // RADIUS, e % RADIUS
        marks = marks_turned(ordered[side, j, rows:])
        query = ordered[side, j, :rows]
        for part, x in enumerate(marks):
            at = slice(e * rows + part * width, e * rows + (part + 1) * width)
            turned[:width, at] = jnp.transpose(query[part * width : (part + 1) * width])
            turned[width:, at] = x
        return product(stacked_ask(query, marks), plane_turned[:, blocks[e]])

    ahead = scores_of(0)
    for e in range(2 * RADIUS):
        side, j = e // RADIUS, e % RADIUS
        scores = ahead
        if e + 1 < 2 * RADIUS:
            ahead = scores_of(e + 1)
        peak, mixed = attend([scores], [plane_beside[blocks[e]]])
        mean = by_head(mixed[:, :width], rows) / by_head(mixed[:, width:], rows)
        results[side, j, :rows] = mean.astype(results.dtype)
        logs = peak + jnp.log(mixed[:, width:])
        high = logs.astype(jnp.bfloat16)
        rest = logs - high.astype(jnp.float32)
        middle = rest.astype(jnp.bfloat16)
        low = (rest - middle.astype(jnp.float32)).astype(jnp.bfloat16)
        picked = jnp.zeros((rows, width), jnp.bfloat16)
        for h in range(width // HEAD):
            for n, piece in enumerate((high, middle, low)):
                picked = jnp.where(lane == 8 * h + n, piece[h * rows : (h + 1) * rows], picked)
        for part in range(rows // width):
            stats = jnp.transpose(picked[part * width : (part + 1) * width])
            at = rows + part * STAT_ROWS
            results[side, j, at : at + STAT_ROWS] = stats[:STAT_ROWS]
    first[...] = results[1 - odd]
    second[...] = results[odd]


def columns_kernel(*refs):
    audio, queries, video = refs[:GROUP], refs[GROUP : 2 * GROUP], refs[2 * GROUP : 3 * GROUP]
    (edge_b, edge_a, edge_turned), outs = refs[3 * GROUP : 3 * GROUP + 3], refs[-GROUP - 5 : -5]
    edge_beside, turned, beside, asks, whole = refs[-5:]
    rows, width = outs[0].shape
    mine = place()
    odd = lax.rem(plane(), 2)
    set_up(
        audio,
        lambda k: video[k][rows:],
        lambda k: queries[k][...],
        lambda k: audio[k][:rows],
        turned,
        beside,
        asks,
    )
    edge_beside[:, width:] = jnp.ones((edge_beside.shape[0], width), beside.dtype)
    for edge, base in ((edge_a, RADIUS * (1 - odd)), (edge_b, RADIUS * odd)):
        for j in range(RADIUS):
            at = pl.ds(pl.multiple_of((base + j) * rows, rows), rows)
            edge_beside[at, :width] = edge[j]
    near = [slice(b * rows, (b + RADIUS) * rows) for b in range(GROUP)]

    def scores_of(b):
        return [product(asks[b], turned[...]), product(asks[b], edge_turned[:, near[b]])]

    ahead = scores_of(0)
    for b in range(GROUP):
        scores = ahead
        if b + 1 < GROUP:
            ahead = scores_of(b + 1)
        _, mixed = attend(scores, [beside[...], edge_beside[near[b]]])
        mean = by_head(mixed[:, :width], rows) / by_head(mixed[:, width:], rows)
        whole[b] = mean.astype(whole.dtype)
    for k in range(GROUP):
        outs[k][...] = whole[mine ^ k]


def merge_kernel(back_a, back_b, peaks, sums, *refs):
    outs, (backs, whole) = refs[-GROUP - 2 : -2], refs[-2:]
    rows, width = outs[0].shape
    mine = place()
    odd = lax.rem(plane(), 2)
    backs[1 - odd] = back_a[...]
    backs[odd] = back_b[...]
    last = lax.axis_size("tm") // GROUP - 1
    absent = [jnp.where(plane() == end, NEG, 0.0) for end in (0, last)]

    def logs(side, j):
        squares = []
        for part in range(rows // width):
            at = rows + part * STAT_ROWS
            stats = backs[side, j, at : at + STAT_ROWS].astype(jnp.float32)
            heads = [
                stats[8 * h : 8 * h + 1] + stats[8 * h + 1 : 8 * h + 2] + stats[8 * h + 2 : 8 * h + 3]
                for h in range(width // HEAD)
            ]
            turned = jnp.transpose(
                jnp.concatenate([jnp.broadcast_to(x, (HEAD, width)) for x in heads], axis=0)
            )
            squares.append(turned)
        return jnp.concatenate(squares, axis=0) + absent[side]

    for b in range(GROUP):
        theirs = []
        if b < RADIUS:
            theirs.append((0, b))
        if b >= GROUP - RADIUS:
            theirs.append((1, b - (GROUP - RADIUS)))
        theirs = [(logs(*t), backs[t[0], t[1], :rows].astype(jnp.float32)) for t in theirs]
        old = by_head(peaks[b], rows)
        top = old
        for log, _ in theirs:
            top = jnp.maximum(top, log)
        factor = jnp.exp(old - top)
        value = by_head(sums[b, :, :width], rows) * factor
        total = by_head(sums[b, :, width:], rows) * factor
        for log, mean in theirs:
            weight = jnp.exp(log - top)
            value += weight * mean
            total += weight
        whole[b] = (value / total).astype(whole.dtype)
    for k in range(GROUP):
        outs[k][...] = whole[mine ^ k]


def local(audio_frames, video_frames, recording, audio_query, video_key):
    rows, half = audio_frames.shape
    width = half // GROUP
    heads = width // HEAD
    length = lax.axis_size("tm")
    bf16, f32 = jnp.bfloat16, jnp.float32
    shape = jax.ShapeDtypeStruct
    assert length % (2 * GROUP) == 0

    def swapped(x):
        return lax.ppermute(x, "head", [(0, 1), (1, 0)])

    def traded(pieces):
        pairs = lambda k: [(i, i ^ k) for i in range(length)]
        return [pieces[0]] + [lax.ppermute(pieces[k], "tm", pairs(k)) for k in range(1, GROUP)]

    def crossed(sent, second):
        planes = range(second, length // GROUP - second)
        pairs = [(p, ((p + second) ^ 1) - second) for p in planes]
        return lax.ppermute(
            sent, "tm", [(p * GROUP + i, q * GROUP + i) for p, q in pairs for i in range(GROUP)]
        )

    part = shape((rows, half), f32)
    square = shape((half, half), bf16)
    piece = shape((rows, width), bf16)
    given = (audio_frames, video_frames, audio_query, video_key, recording.reshape(rows // width, width))
    audio_in, video_in, query_in, key_in, ids_in = (
        pltpu.with_memory_space_constraint(x, pltpu.HBM) for x in given
    )
    other_audio = swapped(audio_frames)
    other_video = swapped(video_frames)
    packs = call(
        split_kernel,
        [shape((rows + ID_ROWS, width), bf16)] * GROUP,
        [pltpu.VMEM((rows // width, width), jnp.int32), pltpu.VMEM((ID_ROWS, width), f32)]
        + [pltpu.SemaphoreType.DMA((1 + GROUP,))],
        ins=[HBM] * 2,
        moved=4 * rows * half,
        name="split",
    )(audio_in, ids_in)
    packs = traded(packs)
    query_part, key_part, query_rest, key_rest, video_copy = call(
        prepare_kernel,
        [part, part, square, square, shape((rows, half), bf16)],
        [pltpu.VMEM((rows, half), bf16)]
        + [pltpu.VMEM((half, half), bf16)] * 2
        + [pltpu.SemaphoreType.DMA((6,))],
        ins=[HBM] * 4 + [ANY],
        flops=4 * rows * half * half,
        moved=16 * half * half,
        name="prepare",
    )(audio_in, video_in, query_in, key_in, packs[1])

    def project(scale, *operands, stream=(), after=()):
        return call(
            functools.partial(project_kernel, scale, len(stream)),
            [shape(((1 + len(stream)) * rows, width), bf16)] * GROUP,
            [pltpu.VMEM((rows, half), bf16)],
            ins=[VMEM] * (3 + len(stream)) + [ANY] * len(after),
            flops=2 * rows * half * half,
            moved=2 * half * half + 6 * rows * half * 2,
            name="project",
        )(*operands, *stream, *after)

    def halo(pieces, id_packs, *after):
        edge = shape((RADIUS, rows + (ID_ROWS if id_packs else 0), width), bf16)
        sent = call(
            functools.partial(halo_kernel, rows if id_packs else 0),
            [edge, edge],
            ins=[VMEM] * (GROUP + len(id_packs)) + [ANY] * len(after),
            moved=10 * rows * width * 2,
            name="halo",
        )(*pieces, *id_packs, *after)
        return [crossed(sent[i], i) for i in range(2)]

    audio_edges = halo(packs, [])
    queries = project(HEAD**-0.5, query_part, other_audio, query_rest, after=packs[1:])
    queries = traded(queries)
    video = project(1.0, key_part, other_video, key_rest, stream=[video_copy], after=queries[1:])
    query_edges = halo(queries, packs, video[0])
    video = traded(video)

    inside, around = GROUP * rows, 2 * RADIUS * rows
    turned, beside = shape((2 * width, inside), bf16), shape((inside, 2 * width), bf16)
    asks = shape((GROUP, heads * rows, 2 * width), bf16)
    peaks, sums, plane_turned, plane_beside = call(
        rows_kernel,
        [shape((GROUP, heads * rows, n * width), f32) for n in (1, 2)] + [turned, beside],
        [pltpu.VMEM(asks.shape, bf16)],
        flops=16 * GROUP * rows * inside * width,
        moved=8 * inside * width * 2,
        exps=2 * GROUP * rows * inside,
        name="rows",
    )(*packs, *queries, *video)
    back = shape((RADIUS, rows + rows // width * STAT_ROWS, width), bf16)
    lent_a, lent_b, edge_turned = call(
        lend_kernel,
        [back, back, shape((2 * width, around), bf16)],
        [pltpu.VMEM((2, RADIUS, rows + ID_ROWS, width), bf16), pltpu.VMEM((2,) + back.shape, bf16)],
        flops=48 * RADIUS * GROUP * rows * rows * width,
        moved=8 * around * width * 2,
        exps=2 * RADIUS * GROUP * rows * rows,
        name="lend",
    )(*query_edges[::-1], plane_turned, plane_beside)
    backs = [crossed(x, i) for i, x in enumerate((lent_a, lent_b))]

    video_pieces = call(
        columns_kernel,
        [piece] * GROUP,
        [pltpu.VMEM((around, 2 * width), bf16)]
        + [pltpu.VMEM(x.shape, bf16) for x in (turned, beside, asks)]
        + [pltpu.VMEM((GROUP, rows, width), bf16)],
        flops=112 * GROUP * rows * rows * width,
        moved=8 * around * width * 2,
        exps=14 * GROUP * rows * rows,
        name="columns",
    )(*packs, *queries, *video, *audio_edges[::-1], edge_turned)
    audio_pieces = call(
        merge_kernel,
        [piece] * GROUP,
        [pltpu.VMEM((2,) + back.shape, bf16), pltpu.VMEM((GROUP, rows, width), bf16)],
        moved=16 * inside * width,
        exps=4 * inside * width,
        ins=[VMEM] * 4 + [ANY],
        name="merge",
    )(*backs, peaks, sums, video_pieces[0])

    def join(pieces):
        return call(
            join_kernel,
            shape((rows, half), bf16),
            [pltpu.SemaphoreType.DMA((GROUP,))],
            outs_in=HBM,
            moved=2 * rows * half * 2,
            name="join",
        )(*traded(pieces))

    video_attended = join(video_pieces)
    audio_attended = join(audio_pieces)
    return (audio_attended, video_attended)


def solution(mesh):
    return jax.shard_map(
        local,
        mesh=mesh,
        in_specs=(P("tm", "head"), P("tm", "head"), P("tm"), P(None, "head"), P(None, "head")),
        out_specs=(P("tm", "head"), P("tm", "head")),
        check_vma=False,
    )
```

```python
import functools

import jax
import jax.numpy as jnp
from jax import lax
from jax.experimental import pallas as pl
from jax.experimental.pallas import tpu as pltpu
from jax.sharding import PartitionSpec as P

HEAD = 64
RADIUS = 3
GROUP = 4
NEG = -1e30
ID_ROWS = 16
STAT_ROWS = 16

VMEM = pl.BlockSpec(memory_space=pltpu.VMEM)
ANY = pl.BlockSpec(memory_space=pl.ANY)
HBM = pl.BlockSpec(memory_space=pltpu.HBM)


def place():
    return lax.rem(lax.axis_index("tm"), GROUP)


def plane():
    return lax.axis_index("tm") // GROUP


def call(kernel, outs, scratch=(), ins=None, outs_in=None, flops=0, moved=0, exps=0, name=None):
    return pl.pallas_call(
        kernel,
        out_shape=outs,
        **({"in_specs": ins} if ins else {}),
        **({"out_specs": outs_in} if outs_in else {}),
        scratch_shapes=scratch,
        compiler_params=pltpu.CompilerParams(vmem_limit_bytes=32 * 2**20),
        cost_estimate=pl.CostEstimate(flops=flops, bytes_accessed=moved, transcendentals=exps),
        name=name,
    )


def product(a, b):
    return jnp.dot(a, b, preferred_element_type=jnp.float32)


def fetcher(sems):
    copies = []

    def fetch(source, target):
        copies.append(pltpu.make_async_copy(source, target, sems.at[len(copies)]))
        copies[-1].start()

    return copies, fetch


def split_kernel(audio, ids, *refs):
    packs, (ids_in, ids_wide, sems) = refs[:GROUP], refs[GROUP:]
    rows, width = audio.shape[0], packs[0].shape[1]
    mine = place()
    copies, fetch = fetcher(sems)
    fetch(ids, ids_in)
    for k in range(GROUP):
        at = pl.ds(pl.multiple_of((mine ^ k) * width, width), width)
        fetch(audio.at[:, at], packs[k].at[:rows])
    copies[0].wait()
    ids_wide[...] = jnp.zeros_like(ids_wide)
    ids_wide[: ids_in.shape[0]] = (ids_in[...] + 1).astype(jnp.float32)
    for k in range(GROUP):
        packs[k][rows:] = ids_wide[...].astype(packs[k].dtype)
    for copy in copies[1:]:
        copy.wait()


def prepare_kernel(audio, video, query, key, *refs):
    sums, seconds, sent, own, firsts, sems = refs[-9:-7], refs[-7:-5], refs[-5], refs[-4], refs[-3:-1], refs[-1]
    half = audio.shape[1]
    side = lax.axis_index("head")
    ours = pl.ds(pl.multiple_of(side * half, half), half)
    theirs = pl.ds(pl.multiple_of((1 - side) * half, half), half)
    streams = (own, sent)
    copies, fetch = fetcher(sems)
    for i, (stream, weight) in enumerate(((audio, query), (video, key))):
        fetch(stream, streams[i])
        fetch(weight.at[ours], firsts[i])
    for i, weight in enumerate((query, key)):
        fetch(weight.at[theirs], seconds[i])
    for i in range(2):
        copies[2 * i].wait()
        copies[2 * i + 1].wait()
        sums[i][...] = product(streams[i][...], firsts[i][...])
    for copy in copies[4:]:
        copy.wait()


def project_kernel(scale, stream, part, other, weight, *refs):
    pieces, full = refs[-GROUP - 1 : -1], refs[-1]
    rows, width = other.shape[0], pieces[0].shape[1]
    mine = place()
    full[...] = (part[...] + product(other[...], weight[...])).astype(jnp.bfloat16) * jnp.bfloat16(scale)
    for k in range(GROUP):
        at = pl.ds(pl.multiple_of((mine ^ k) * width, width), width)
        if stream:
            pieces[k][:rows] = refs[0][:, at]
        pieces[k][stream * rows :] = full[:, at]


def halo_kernel(at, ids_at, *refs):
    pieces, id_packs, outs = refs[:GROUP], refs[GROUP : 2 * GROUP], refs[-2:]
    rows = outs[0].shape[1] - (ID_ROWS if ids_at else 0)
    mine = place()
    odd = lax.rem(plane(), 2)
    for k in range(GROUP):
        block = mine ^ k
        for out, skip in zip(outs, ((GROUP - RADIUS) * (1 - odd), (GROUP - RADIUS) * odd)):
            spot = block - skip

            @pl.when((spot >= 0) & (spot < RADIUS))
            def _():
                out[spot, :rows] = pieces[k][at : at + rows]
                if ids_at:
                    out[spot, rows:] = id_packs[k][ids_at:]


def join_kernel(*refs):
    pieces, out, sems = refs[:GROUP], refs[GROUP], refs[GROUP + 1]
    width = pieces[0].shape[1]
    mine = place()
    copies, fetch = fetcher(sems)
    for k in range(GROUP):
        fetch(pieces[k], out.at[:, pl.ds(pl.multiple_of((mine ^ k) * width, width), width)])
    for copy in copies:
        copy.wait()


def marks_turned(lanes):
    lanes = lanes.astype(jnp.float32)
    width = lanes.shape[1]
    row = lax.broadcasted_iota(jnp.int32, (width, width), 0).astype(jnp.float32)
    return [
        jnp.where(row == lanes[part : part + 1], 1.0, 0.0).astype(jnp.bfloat16) for part in range(2)
    ]


def stacked_ask(block, turned):
    head = lax.broadcasted_iota(jnp.int32, block.shape, 1) // HEAD
    marks = jnp.concatenate([jnp.transpose(x) for x in turned], axis=0)
    beside = (marks - jnp.bfloat16(1.0)) * jnp.bfloat16(-NEG)
    return jnp.concatenate(
        [
            jnp.concatenate([jnp.where(head == h, block, jnp.zeros_like(block)), beside], axis=1)
            for h in range(block.shape[1] // HEAD)
        ],
        axis=0,
    )


def by_head(stacked, rows):
    out = stacked[:rows]
    head = lax.broadcasted_iota(jnp.int32, out.shape, 1) // HEAD
    for h in range(1, stacked.shape[0] // rows):
        out = jnp.where(head == h, stacked[h * rows : (h + 1) * rows], out)
    return out


def attend(scores, values):
    top = None
    for s in scores:
        for at in range(0, s.shape[1], values[0].shape[1] // 2):
            part = s[:, at : at + values[0].shape[1] // 2]
            top = part if top is None else jnp.maximum(top, part)
    peak = jnp.max(top, axis=1, keepdims=True)
    mixed = None
    for s, value in zip(scores, values):
        part = product(jnp.exp(s - peak).astype(jnp.bfloat16), value)
        mixed = part if mixed is None else mixed + part
    return peak, mixed


def set_up(audio, asked, keys, values, turned, beside, asks):
    rows, width = asks.shape[1] // 2, asks.shape[2] // 2
    mine = place()
    beside[:, width:] = jnp.ones((GROUP * rows, width), beside.dtype)
    for k in range(GROUP):
        b = mine ^ k

        def spot(at, size):
            return pl.ds(pl.multiple_of(b * rows + at, size), size)

        marks = marks_turned(audio[k][rows:])
        asks[b] = stacked_ask(asked(k), marks)
        beside[spot(0, rows), :width] = values(k)
        key = keys(k)
        for part, x in enumerate(marks):
            at = spot(part * width, width)
            turned[:width, at] = jnp.transpose(key[part * width : (part + 1) * width])
            turned[width:, at] = x


def rows_kernel(*refs):
    audio, queries, keys = refs[:GROUP], refs[GROUP : 2 * GROUP], refs[2 * GROUP : 3 * GROUP]
    peaks, sums, turned, beside, asks = refs[-5:]
    rows, width = keys[0].shape
    set_up(
        audio,
        lambda k: queries[k][rows:],
        lambda k: keys[k][...],
        lambda k: queries[k][:rows],
        turned,
        beside,
        asks,
    )
    ahead = product(asks[0], turned[...])
    for b in range(GROUP):
        scores = ahead
        if b + 1 < GROUP:
            ahead = product(asks[b + 1], turned[...])
        peak, sums[b] = attend([scores], [beside[...]])
        peaks[b] = jnp.broadcast_to(peak, (peak.shape[0], width))


def lend_kernel(edge_b, edge_a, plane_turned, plane_beside, first, second, turned, ordered, results):
    rows, width = ordered.shape[2] - ID_ROWS, ordered.shape[3]
    odd = lax.rem(plane(), 2)
    ordered[1 - odd] = edge_a[...]
    ordered[odd] = edge_b[...]
    lane = lax.broadcasted_iota(jnp.int32, (rows, width), 1)
    blocks = [slice(0, (j + 1) * rows) for j in range(RADIUS)]
    blocks += [slice((j + 1) * rows, GROUP * rows) for j in range(RADIUS)]

    def scores_of(e):
        side, j = e // RADIUS, e % RADIUS
        marks = marks_turned(ordered[side, j, rows:])
        query = ordered[side, j, :rows]
        for part, x in enumerate(marks):
            at = slice(e * rows + part * width, e * rows + (part + 1) * width)
            turned[:width, at] = jnp.transpose(query[part * width : (part + 1) * width])
            turned[width:, at] = x
        return product(stacked_ask(query, marks), plane_turned[:, blocks[e]])

    ahead = scores_of(0)
    for e in range(2 * RADIUS):
        side, j = e // RADIUS, e % RADIUS
        scores = ahead
        if e + 1 < 2 * RADIUS:
            ahead = scores_of(e + 1)
        peak, mixed = attend([scores], [plane_beside[blocks[e]]])
        mean = by_head(mixed[:, :width], rows) / by_head(mixed[:, width:], rows)
        results[side, j, :rows] = mean.astype(results.dtype)
        logs = peak + jnp.log(mixed[:, width:])
        high = logs.astype(jnp.bfloat16)
        rest = logs - high.astype(jnp.float32)
        middle = rest.astype(jnp.bfloat16)
        low = (rest - middle.astype(jnp.float32)).astype(jnp.bfloat16)
        picked = jnp.zeros((rows, width), jnp.bfloat16)
        for h in range(width // HEAD):
            for n, piece in enumerate((high, middle, low)):
                picked = jnp.where(lane == 8 * h + n, piece[h * rows : (h + 1) * rows], picked)
        for part in range(rows // width):
            stats = jnp.transpose(picked[part * width : (part + 1) * width])
            at = rows + part * STAT_ROWS
            results[side, j, at : at + STAT_ROWS] = stats[:STAT_ROWS]
    first[...] = results[1 - odd]
    second[...] = results[odd]


def columns_kernel(receivers, *refs):
    refs = list(refs)
    take = lambda count: [refs.pop(0) for _ in range(count)]
    first = 0 not in receivers
    if first:
        audio, queries, keys, (edge_b, edge_a) = take(GROUP), take(GROUP), take(GROUP), take(2)
    (edge_turned,) = take(1)
    if not first:
        shared, _ = take(4), take(1)
    outs = take(len(receivers))
    turned, beside, asks, edge_beside = take(4) if first else shared
    rows, width = outs[0].shape
    mine = place()
    if first:
        odd = lax.rem(plane(), 2)
        set_up(
            audio,
            lambda k: keys[k][...],
            lambda k: queries[k][rows:],
            lambda k: audio[k][:rows],
            turned,
            beside,
            asks,
        )
        edge_beside[:, width:] = jnp.ones((edge_beside.shape[0], width), beside.dtype)
        for edge, base in ((edge_a, RADIUS * (1 - odd)), (edge_b, RADIUS * odd)):
            for j in range(RADIUS):
                at = pl.ds(pl.multiple_of((base + j) * rows, rows), rows)
                edge_beside[at, :width] = edge[j]
    near = [pl.ds(pl.multiple_of((mine ^ k) * rows, rows), RADIUS * rows) for k in receivers]

    def scores_of(n):
        ask = asks[mine ^ receivers[n]]
        return [product(ask, turned[...]), product(ask, edge_turned[:, near[n]])]

    ahead = scores_of(0)
    for n in range(len(receivers)):
        scores = ahead
        if n + 1 < len(receivers):
            ahead = scores_of(n + 1)
        _, mixed = attend(scores, [beside[...], edge_beside[near[n]]])
        mean = by_head(mixed[:, :width], rows) / by_head(mixed[:, width:], rows)
        outs[n][...] = mean.astype(outs[n].dtype)


def merge_kernel(back_a, back_b, peaks, sums, *refs):
    outs, (backs, whole) = refs[-GROUP - 2 : -2], refs[-2:]
    rows, width = outs[0].shape
    mine = place()
    odd = lax.rem(plane(), 2)
    backs[1 - odd] = back_a[...]
    backs[odd] = back_b[...]
    last = lax.axis_size("tm") // GROUP - 1
    absent = [jnp.where(plane() == end, NEG, 0.0) for end in (0, last)]

    def logs(side, j):
        squares = []
        for part in range(rows // width):
            at = rows + part * STAT_ROWS
            stats = backs[side, j, at : at + STAT_ROWS].astype(jnp.float32)
            heads = [
                stats[8 * h : 8 * h + 1] + stats[8 * h + 1 : 8 * h + 2] + stats[8 * h + 2 : 8 * h + 3]
                for h in range(width // HEAD)
            ]
            turned = jnp.transpose(
                jnp.concatenate([jnp.broadcast_to(x, (HEAD, width)) for x in heads], axis=0)
            )
            squares.append(turned)
        return jnp.concatenate(squares, axis=0) + absent[side]

    for b in range(GROUP):
        theirs = []
        if b < RADIUS:
            theirs.append((0, b))
        if b >= GROUP - RADIUS:
            theirs.append((1, b - (GROUP - RADIUS)))
        theirs = [(logs(*t), backs[t[0], t[1], :rows].astype(jnp.float32)) for t in theirs]
        old = by_head(peaks[b], rows)
        top = old
        for log, _ in theirs:
            top = jnp.maximum(top, log)
        factor = jnp.exp(old - top)
        value = by_head(sums[b, :, :width], rows) * factor
        total = by_head(sums[b, :, width:], rows) * factor
        for log, mean in theirs:
            weight = jnp.exp(log - top)
            value += weight * mean
            total += weight
        whole[b] = (value / total).astype(whole.dtype)
    for k in range(GROUP):
        outs[k][...] = whole[mine ^ k]


def local(audio_frames, video_frames, recording, audio_query, video_key):
    rows, half = audio_frames.shape
    width = half // GROUP
    heads = width // HEAD
    length = lax.axis_size("tm")
    bf16, f32 = jnp.bfloat16, jnp.float32
    shape = jax.ShapeDtypeStruct
    assert length % (2 * GROUP) == 0

    def swapped(x):
        return lax.ppermute(x, "head", [(0, 1), (1, 0)])

    def traded(pieces):
        pairs = lambda k: [(i, i ^ k) for i in range(length)]
        return [pieces[0]] + [lax.ppermute(pieces[k], "tm", pairs(k)) for k in range(1, GROUP)]

    def crossed(sent, second):
        planes = range(second, length // GROUP - second)
        pairs = [(p, ((p + second) ^ 1) - second) for p in planes]
        return lax.ppermute(
            sent, "tm", [(p * GROUP + i, q * GROUP + i) for p, q in pairs for i in range(GROUP)]
        )

    part = shape((rows, half), f32)
    square = shape((half, half), bf16)
    piece = shape((rows, width), bf16)
    given = (audio_frames, video_frames, audio_query, video_key, recording.reshape(rows // width, width))
    audio_in, video_in, query_in, key_in, ids_in = (
        pltpu.with_memory_space_constraint(x, pltpu.HBM) for x in given
    )
    other_audio = swapped(audio_frames)
    other_video = swapped(video_frames)
    packs = call(
        split_kernel,
        [shape((rows + ID_ROWS, width), bf16)] * GROUP,
        [pltpu.VMEM((rows // width, width), jnp.int32), pltpu.VMEM((ID_ROWS, width), f32)]
        + [pltpu.SemaphoreType.DMA((1 + GROUP,))],
        ins=[HBM] * 2,
        moved=4 * rows * half,
        name="split",
    )(audio_in, ids_in)
    packs = traded(packs)
    query_part, key_part, query_rest, key_rest, video_copy = call(
        prepare_kernel,
        [part, part, square, square, shape((rows, half), bf16)],
        [pltpu.VMEM((rows, half), bf16)]
        + [pltpu.VMEM((half, half), bf16)] * 2
        + [pltpu.SemaphoreType.DMA((6,))],
        ins=[HBM] * 4 + [ANY],
        flops=4 * rows * half * half,
        moved=16 * half * half,
        name="prepare",
    )(audio_in, video_in, query_in, key_in, packs[1])

    def project(scale, *operands, stream=(), after=()):
        return call(
            functools.partial(project_kernel, scale, len(stream)),
            [shape(((1 + len(stream)) * rows, width), bf16)] * GROUP,
            [pltpu.VMEM((rows, half), bf16)],
            ins=[VMEM] * (3 + len(stream)) + [ANY] * len(after),
            flops=2 * rows * half * half,
            moved=2 * half * half + 6 * rows * half * 2,
            name="project",
        )(*operands, *stream, *after)

    def halo(at, pieces, id_packs, *after):
        edge = shape((RADIUS, rows + (ID_ROWS if id_packs else 0), width), bf16)
        sent = call(
            functools.partial(halo_kernel, at, rows if id_packs else 0),
            [edge, edge],
            ins=[VMEM] * (GROUP + len(id_packs)) + [ANY] * len(after),
            moved=10 * rows * width * 2,
            name="halo",
        )(*pieces, *id_packs, *after)
        return [crossed(sent[i], i) for i in range(2)]

    queries = project(
        HEAD**-0.5, query_part, other_audio, query_rest, stream=[video_copy], after=packs[1:]
    )
    queries = traded(queries)
    keys = project(1.0, key_part, other_video, key_rest, after=())
    query_edges = halo(rows, queries, packs, keys[0])
    keys = traded(keys)

    inside, around = GROUP * rows, 2 * RADIUS * rows
    turned, beside = shape((2 * width, inside), bf16), shape((inside, 2 * width), bf16)
    asks = shape((GROUP, heads * rows, 2 * width), bf16)
    peaks, sums, plane_turned, plane_beside = call(
        rows_kernel,
        [shape((GROUP, heads * rows, n * width), f32) for n in (1, 2)] + [turned, beside],
        [pltpu.VMEM(asks.shape, bf16)],
        flops=16 * GROUP * rows * inside * width,
        moved=8 * inside * width * 2,
        exps=2 * GROUP * rows * inside,
        name="rows",
    )(*packs, *queries, *keys)
    audio_edges = halo(0, packs, [], peaks)
    back = shape((RADIUS, rows + rows // width * STAT_ROWS, width), bf16)
    lent_a, lent_b, edge_turned = call(
        lend_kernel,
        [back, back, shape((2 * width, around), bf16)],
        [pltpu.VMEM((2, RADIUS, rows + ID_ROWS, width), bf16), pltpu.VMEM((2,) + back.shape, bf16)],
        flops=48 * RADIUS * GROUP * rows * rows * width,
        moved=8 * around * width * 2,
        exps=2 * RADIUS * GROUP * rows * rows,
        name="lend",
    )(*query_edges[::-1], plane_turned, plane_beside)
    backs = [crossed(x, i) for i, x in enumerate((lent_a, lent_b))]

    half_columns = dict(
        flops=56 * GROUP * rows * rows * width,
        moved=4 * around * width * 2,
        exps=7 * GROUP * rows * rows,
        name="columns",
    )
    shared = [turned, beside, asks, shape((around, 2 * width), bf16)]
    near, far = range(GROUP // 2), range(GROUP // 2, GROUP)
    *far_pieces, turned, beside, asks, edge_beside = call(
        functools.partial(columns_kernel, far), [piece] * len(far) + shared, **half_columns
    )(*packs, *queries, *keys, *audio_edges[::-1], edge_turned)
    audio_pieces = call(
        merge_kernel,
        [piece] * GROUP,
        [pltpu.VMEM((2,) + back.shape, bf16), pltpu.VMEM((GROUP, rows, width), bf16)],
        moved=16 * inside * width,
        exps=4 * inside * width,
        ins=[VMEM] * 4 + [ANY],
        name="merge",
    )(*backs, peaks, sums, far_pieces[0])
    audio_pieces = traded(audio_pieces)
    near_pieces = call(
        functools.partial(columns_kernel, near),
        [piece] * len(near),
        ins=[VMEM] * 5 + [ANY],
        **half_columns,
    )(edge_turned, turned, beside, asks, edge_beside, audio_pieces[0])
    video_pieces = traded([*near_pieces, *far_pieces])

    def join(pieces):
        return call(
            join_kernel,
            shape((rows, half), bf16),
            [pltpu.SemaphoreType.DMA((GROUP,))],
            outs_in=HBM,
            moved=2 * rows * half * 2,
            name="join",
        )(*pieces)

    video_attended = join(video_pieces)
    audio_attended = join(audio_pieces)
    return (audio_attended, video_attended)


def solution(mesh):
    return jax.shard_map(
        local,
        mesh=mesh,
        in_specs=(P("tm", "head"), P("tm", "head"), P("tm"), P(None, "head"), P(None, "head")),
        out_specs=(P("tm", "head"), P("tm", "head")),
        check_vma=False,
    )
```

```python
import functools

import jax
import jax.numpy as jnp
from jax import lax
from jax.experimental import pallas as pl
from jax.experimental.pallas import tpu as pltpu
from jax.sharding import PartitionSpec as P

HEAD = 64
RADIUS = 3
GROUP = 4
NEG = -1e30
ID_ROWS = 16
STAT_ROWS = 16

VMEM = pl.BlockSpec(memory_space=pltpu.VMEM)
ANY = pl.BlockSpec(memory_space=pl.ANY)
HBM = pl.BlockSpec(memory_space=pltpu.HBM)


def place():
    return lax.rem(lax.axis_index("tm"), GROUP)


def plane():
    return lax.axis_index("tm") // GROUP


def call(kernel, outs, scratch=(), ins=None, outs_in=None, flops=0, moved=0, exps=0, name=None):
    return pl.pallas_call(
        kernel,
        out_shape=outs,
        **({"in_specs": ins} if ins else {}),
        **({"out_specs": outs_in} if outs_in else {}),
        scratch_shapes=scratch,
        compiler_params=pltpu.CompilerParams(vmem_limit_bytes=32 * 2**20),
        cost_estimate=pl.CostEstimate(flops=flops, bytes_accessed=moved, transcendentals=exps),
        name=name,
    )


def product(a, b):
    return jnp.dot(a, b, preferred_element_type=jnp.float32)


def fetcher(sems):
    copies = []

    def fetch(source, target):
        copies.append(pltpu.make_async_copy(source, target, sems.at[len(copies)]))
        copies[-1].start()

    return copies, fetch


def split_kernel(audio, video, ids, *refs):
    packs, (ids_in, ids_wide, sems) = refs[:GROUP], refs[GROUP:]
    rows, width = audio.shape[0], packs[0].shape[1]
    mine = place()
    copies, fetch = fetcher(sems)
    fetch(ids, ids_in)
    for k in range(GROUP):
        at = pl.ds(pl.multiple_of((mine ^ k) * width, width), width)
        for i, stream in enumerate((audio, video)):
            fetch(stream.at[:, at], packs[k].at[i * rows : (i + 1) * rows])
    copies[0].wait()
    ids_wide[...] = jnp.zeros_like(ids_wide)
    ids_wide[: ids_in.shape[0]] = (ids_in[...] + 1).astype(jnp.float32)
    for k in range(GROUP):
        packs[k][2 * rows :] = ids_wide[...].astype(packs[k].dtype)
    for copy in copies[1:]:
        copy.wait()


def prepare_kernel(audio, video, query, key, *refs):
    sums, seconds, streams, firsts, sems = refs[-9:-7], refs[-7:-5], refs[-5:-3], refs[-3:-1], refs[-1]
    half = audio.shape[1]
    side = lax.axis_index("head")
    ours = pl.ds(pl.multiple_of(side * half, half), half)
    theirs = pl.ds(pl.multiple_of((1 - side) * half, half), half)
    copies, fetch = fetcher(sems)
    for i, (stream, weight) in enumerate(((audio, query), (video, key))):
        fetch(stream, streams[i])
        fetch(weight.at[ours], firsts[i])
    for i, weight in enumerate((query, key)):
        fetch(weight.at[theirs], seconds[i])
    for i in range(2):
        copies[2 * i].wait()
        copies[2 * i + 1].wait()
        sums[i][...] = product(streams[i][...], firsts[i][...])
    for copy in copies[4:]:
        copy.wait()


def project_kernel(scale, part, other, weight, *refs):
    pieces, full = refs[-GROUP - 1 : -1], refs[-1]
    width = pieces[0].shape[1]
    mine = place()
    full[...] = (part[...] + product(other[...], weight[...])).astype(jnp.bfloat16) * jnp.bfloat16(scale)
    for k in range(GROUP):
        pieces[k][...] = full[:, pl.ds(pl.multiple_of((mine ^ k) * width, width), width)]


def halo_kernel(ids_at, *refs):
    pieces, id_packs, outs = refs[:GROUP], refs[GROUP : 2 * GROUP], refs[-2:]
    rows = outs[0].shape[1] - (ID_ROWS if ids_at else 0)
    mine = place()
    odd = lax.rem(plane(), 2)
    for k in range(GROUP):
        block = mine ^ k
        for out, skip in zip(outs, ((GROUP - RADIUS) * (1 - odd), (GROUP - RADIUS) * odd)):
            spot = block - skip

            @pl.when((spot >= 0) & (spot < RADIUS))
            def _():
                out[spot, :rows] = pieces[k][:rows]
                if ids_at:
                    out[spot, rows:] = id_packs[k][ids_at:]


def join_kernel(*refs):
    pieces, out, sems = refs[:GROUP], refs[GROUP], refs[GROUP + 1]
    width = pieces[0].shape[1]
    mine = place()
    copies, fetch = fetcher(sems)
    for k in range(GROUP):
        fetch(pieces[k], out.at[:, pl.ds(pl.multiple_of((mine ^ k) * width, width), width)])
    for copy in copies:
        copy.wait()


def marks_turned(lanes):
    lanes = lanes.astype(jnp.float32)
    width = lanes.shape[1]
    row = lax.broadcasted_iota(jnp.int32, (width, width), 0).astype(jnp.float32)
    return [
        jnp.where(row == lanes[part : part + 1], 1.0, 0.0).astype(jnp.bfloat16) for part in range(2)
    ]


def stacked_ask(block, turned):
    head = lax.broadcasted_iota(jnp.int32, block.shape, 1) // HEAD
    marks = jnp.concatenate([jnp.transpose(x) for x in turned], axis=0)
    beside = (marks - jnp.bfloat16(1.0)) * jnp.bfloat16(-NEG)
    return jnp.concatenate(
        [
            jnp.concatenate([jnp.where(head == h, block, jnp.zeros_like(block)), beside], axis=1)
            for h in range(block.shape[1] // HEAD)
        ],
        axis=0,
    )


def by_head(stacked, rows):
    out = stacked[:rows]
    head = lax.broadcasted_iota(jnp.int32, out.shape, 1) // HEAD
    for h in range(1, stacked.shape[0] // rows):
        out = jnp.where(head == h, stacked[h * rows : (h + 1) * rows], out)
    return out


def attend(scores, values):
    top = None
    for s in scores:
        for at in range(0, s.shape[1], values[0].shape[1] // 2):
            part = s[:, at : at + values[0].shape[1] // 2]
            top = part if top is None else jnp.maximum(top, part)
    peak = jnp.max(top, axis=1, keepdims=True)
    mixed = None
    for s, value in zip(scores, values):
        part = product(jnp.exp(s - peak).astype(jnp.bfloat16), value)
        mixed = part if mixed is None else mixed + part
    return peak, mixed


def set_up(packs, asked, keys, values, turned, beside, asks):
    rows, width = asks.shape[1] // 2, asks.shape[2] // 2
    mine = place()
    beside[:, width:] = jnp.ones((GROUP * rows, width), beside.dtype)
    for k in range(GROUP):
        b = mine ^ k

        def spot(at, size):
            return pl.ds(pl.multiple_of(b * rows + at, size), size)

        marks = marks_turned(packs[k][2 * rows :])
        asks[b] = stacked_ask(asked(k), marks)
        beside[spot(0, rows), :width] = values(k)
        key = keys(k)
        for part, x in enumerate(marks):
            at = spot(part * width, width)
            turned[:width, at] = jnp.transpose(key[part * width : (part + 1) * width])
            turned[width:, at] = x


def rows_kernel(*refs):
    packs, queries, keys = refs[:GROUP], refs[GROUP : 2 * GROUP], refs[2 * GROUP : 3 * GROUP]
    peaks, sums, turned, beside, asks = refs[-5:]
    rows, width = keys[0].shape
    set_up(
        packs,
        lambda k: queries[k][...],
        lambda k: keys[k][...],
        lambda k: packs[k][rows : 2 * rows],
        turned,
        beside,
        asks,
    )
    ahead = product(asks[0], turned[...])
    for b in range(GROUP):
        scores = ahead
        if b + 1 < GROUP:
            ahead = product(asks[b + 1], turned[...])
        peak, sums[b] = attend([scores], [beside[...]])
        peaks[b] = jnp.broadcast_to(peak, (peak.shape[0], width))


def lend_kernel(edge_b, edge_a, plane_turned, plane_beside, first, second, turned, ordered, results):
    rows, width = ordered.shape[2] - ID_ROWS, ordered.shape[3]
    odd = lax.rem(plane(), 2)
    ordered[1 - odd] = edge_a[...]
    ordered[odd] = edge_b[...]
    lane = lax.broadcasted_iota(jnp.int32, (rows, width), 1)
    blocks = [slice(0, (j + 1) * rows) for j in range(RADIUS)]
    blocks += [slice((j + 1) * rows, GROUP * rows) for j in range(RADIUS)]

    def scores_of(e):
        side, j = e // RADIUS, e % RADIUS
        marks = marks_turned(ordered[side, j, rows:])
        query = ordered[side, j, :rows]
        for part, x in enumerate(marks):
            at = slice(e * rows + part * width, e * rows + (part + 1) * width)
            turned[:width, at] = jnp.transpose(query[part * width : (part + 1) * width])
            turned[width:, at] = x
        return product(stacked_ask(query, marks), plane_turned[:, blocks[e]])

    ahead = scores_of(0)
    for e in range(2 * RADIUS):
        side, j = e // RADIUS, e % RADIUS
        scores = ahead
        if e + 1 < 2 * RADIUS:
            ahead = scores_of(e + 1)
        peak, mixed = attend([scores], [plane_beside[blocks[e]]])
        mean = by_head(mixed[:, :width], rows) / by_head(mixed[:, width:], rows)
        results[side, j, :rows] = mean.astype(results.dtype)
        logs = peak + jnp.log(mixed[:, width:])
        high = logs.astype(jnp.bfloat16)
        rest = logs - high.astype(jnp.float32)
        middle = rest.astype(jnp.bfloat16)
        low = (rest - middle.astype(jnp.float32)).astype(jnp.bfloat16)
        picked = jnp.zeros((rows, width), jnp.bfloat16)
        for h in range(width // HEAD):
            for n, piece in enumerate((high, middle, low)):
                picked = jnp.where(lane == 8 * h + n, piece[h * rows : (h + 1) * rows], picked)
        for part in range(rows // width):
            stats = jnp.transpose(picked[part * width : (part + 1) * width])
            at = rows + part * STAT_ROWS
            results[side, j, at : at + STAT_ROWS] = stats[:STAT_ROWS]
    first[...] = results[1 - odd]
    second[...] = results[odd]


def columns_kernel(receivers, *refs):
    refs = list(refs)
    take = lambda count: [refs.pop(0) for _ in range(count)]
    first = 0 not in receivers
    if first:
        packs, queries, keys, (edge_b, edge_a) = take(GROUP), take(GROUP), take(GROUP), take(2)
    (edge_turned,) = take(1)
    if not first:
        shared, _ = take(4), take(1)
    outs = take(len(receivers))
    turned, beside, asks, edge_beside = take(4) if first else shared
    rows, width = outs[0].shape
    mine = place()
    if first:
        odd = lax.rem(plane(), 2)
        set_up(
            packs,
            lambda k: keys[k][...],
            lambda k: queries[k][...],
            lambda k: packs[k][:rows],
            turned,
            beside,
            asks,
        )
        edge_beside[:, width:] = jnp.ones((edge_beside.shape[0], width), beside.dtype)
        for edge, base in ((edge_a, RADIUS * (1 - odd)), (edge_b, RADIUS * odd)):
            for j in range(RADIUS):
                at = pl.ds(pl.multiple_of((base + j) * rows, rows), rows)
                edge_beside[at, :width] = edge[j]
    near = [pl.ds(pl.multiple_of((mine ^ k) * rows, rows), RADIUS * rows) for k in receivers]

    def scores_of(n):
        ask = asks[mine ^ receivers[n]]
        return [product(ask, turned[...]), product(ask, edge_turned[:, near[n]])]

    ahead = scores_of(0)
    for n in range(len(receivers)):
        scores = ahead
        if n + 1 < len(receivers):
            ahead = scores_of(n + 1)
        _, mixed = attend(scores, [beside[...], edge_beside[near[n]]])
        mean = by_head(mixed[:, :width], rows) / by_head(mixed[:, width:], rows)
        outs[n][...] = mean.astype(outs[n].dtype)


def merge_kernel(back_a, back_b, peaks, sums, *refs):
    outs, (backs, whole) = refs[-GROUP - 2 : -2], refs[-2:]
    rows, width = outs[0].shape
    mine = place()
    odd = lax.rem(plane(), 2)
    backs[1 - odd] = back_a[...]
    backs[odd] = back_b[...]
    last = lax.axis_size("tm") // GROUP - 1
    absent = [jnp.where(plane() == end, NEG, 0.0) for end in (0, last)]

    def logs(side, j):
        squares = []
        for part in range(rows // width):
            at = rows + part * STAT_ROWS
            stats = backs[side, j, at : at + STAT_ROWS].astype(jnp.float32)
            heads = [
                stats[8 * h : 8 * h + 1] + stats[8 * h + 1 : 8 * h + 2] + stats[8 * h + 2 : 8 * h + 3]
                for h in range(width // HEAD)
            ]
            turned = jnp.transpose(
                jnp.concatenate([jnp.broadcast_to(x, (HEAD, width)) for x in heads], axis=0)
            )
            squares.append(turned)
        return jnp.concatenate(squares, axis=0) + absent[side]

    for b in range(GROUP):
        theirs = []
        if b < RADIUS:
            theirs.append((0, b))
        if b >= GROUP - RADIUS:
            theirs.append((1, b - (GROUP - RADIUS)))
        theirs = [(logs(*t), backs[t[0], t[1], :rows].astype(jnp.float32)) for t in theirs]
        old = by_head(peaks[b], rows)
        top = old
        for log, _ in theirs:
            top = jnp.maximum(top, log)
        factor = jnp.exp(old - top)
        value = by_head(sums[b, :, :width], rows) * factor
        total = by_head(sums[b, :, width:], rows) * factor
        for log, mean in theirs:
            weight = jnp.exp(log - top)
            value += weight * mean
            total += weight
        whole[b] = (value / total).astype(whole.dtype)
    for k in range(GROUP):
        outs[k][...] = whole[mine ^ k]


def local(audio_frames, video_frames, recording, audio_query, video_key):
    rows, half = audio_frames.shape
    width = half // GROUP
    heads = width // HEAD
    length = lax.axis_size("tm")
    bf16, f32 = jnp.bfloat16, jnp.float32
    shape = jax.ShapeDtypeStruct
    assert length % (2 * GROUP) == 0

    def swapped(x):
        return lax.ppermute(x, "head", [(0, 1), (1, 0)])

    def traded(pieces):
        pairs = lambda k: [(i, i ^ k) for i in range(length)]
        return [pieces[0]] + [lax.ppermute(pieces[k], "tm", pairs(k)) for k in range(1, GROUP)]

    def crossed(sent, second):
        planes = range(second, length // GROUP - second)
        pairs = [(p, ((p + second) ^ 1) - second) for p in planes]
        return lax.ppermute(
            sent, "tm", [(p * GROUP + i, q * GROUP + i) for p, q in pairs for i in range(GROUP)]
        )

    part = shape((rows, half), f32)
    square = shape((half, half), bf16)
    piece = shape((rows, width), bf16)
    given = (audio_frames, video_frames, audio_query, video_key, recording.reshape(rows // width, width))
    audio_in, video_in, query_in, key_in, ids_in = (
        pltpu.with_memory_space_constraint(x, pltpu.HBM) for x in given
    )
    other_audio = swapped(audio_frames)
    other_video = swapped(video_frames)
    packs = call(
        split_kernel,
        [shape((2 * rows + ID_ROWS, width), bf16)] * GROUP,
        [pltpu.VMEM((rows // width, width), jnp.int32), pltpu.VMEM((ID_ROWS, width), f32)]
        + [pltpu.SemaphoreType.DMA((1 + 2 * GROUP,))],
        ins=[HBM] * 3,
        moved=8 * rows * half,
        name="split",
    )(audio_in, video_in, ids_in)
    packs = traded(packs)
    query_part, key_part, query_rest, key_rest = call(
        prepare_kernel,
        [part, part, square, square],
        [pltpu.VMEM((rows, half), bf16)] * 2
        + [pltpu.VMEM((half, half), bf16)] * 2
        + [pltpu.SemaphoreType.DMA((6,))],
        ins=[HBM] * 4 + [ANY],
        flops=4 * rows * half * half,
        moved=16 * half * half,
        name="prepare",
    )(audio_in, video_in, query_in, key_in, packs[1])

    def project(scale, *operands, after=()):
        return call(
            functools.partial(project_kernel, scale),
            [piece] * GROUP,
            [pltpu.VMEM((rows, half), bf16)],
            ins=[VMEM] * 3 + [ANY] * len(after),
            flops=2 * rows * half * half,
            moved=2 * half * half + 6 * rows * half * 2,
            name="project",
        )(*operands, *after)

    def halo(pieces, id_packs, *after):
        edge = shape((RADIUS, rows + (ID_ROWS if id_packs else 0), width), bf16)
        sent = call(
            functools.partial(halo_kernel, 2 * rows if id_packs else 0),
            [edge, edge],
            ins=[VMEM] * (GROUP + len(id_packs)) + [ANY] * len(after),
            moved=10 * rows * width * 2,
            name="halo",
        )(*pieces, *id_packs, *after)
        return [crossed(sent[i], i) for i in range(2)]

    queries = traded(project(HEAD**-0.5, query_part, other_audio, query_rest, after=packs[1:3]))
    keys = project(1.0, key_part, other_video, key_rest, after=())
    query_edges = halo(queries, packs, keys[0])
    keys = traded(keys)

    inside, around = GROUP * rows, 2 * RADIUS * rows
    turned, beside = shape((2 * width, inside), bf16), shape((inside, 2 * width), bf16)
    asks = shape((GROUP, heads * rows, 2 * width), bf16)
    peaks, sums, plane_turned, plane_beside = call(
        rows_kernel,
        [shape((GROUP, heads * rows, n * width), f32) for n in (1, 2)] + [turned, beside],
        [pltpu.VMEM(asks.shape, bf16)],
        flops=16 * GROUP * rows * inside * width,
        moved=8 * inside * width * 2,
        exps=2 * GROUP * rows * inside,
        name="rows",
    )(*packs, *queries, *keys)
    audio_edges = halo(packs, [], peaks)
    back = shape((RADIUS, rows + rows // width * STAT_ROWS, width), bf16)
    lent_a, lent_b, edge_turned = call(
        lend_kernel,
        [back, back, shape((2 * width, around), bf16)],
        [pltpu.VMEM((2, RADIUS, rows + ID_ROWS, width), bf16), pltpu.VMEM((2,) + back.shape, bf16)],
        flops=48 * RADIUS * GROUP * rows * rows * width,
        moved=8 * around * width * 2,
        exps=2 * RADIUS * GROUP * rows * rows,
        name="lend",
    )(*query_edges[::-1], plane_turned, plane_beside)
    backs = [crossed(x, i) for i, x in enumerate((lent_a, lent_b))]

    half_columns = dict(
        flops=56 * GROUP * rows * rows * width,
        moved=4 * around * width * 2,
        exps=7 * GROUP * rows * rows,
        name="columns",
    )
    shared = [turned, beside, asks, shape((around, 2 * width), bf16)]
    near, far = range(GROUP // 2), range(GROUP // 2, GROUP)
    *far_pieces, turned, beside, asks, edge_beside = call(
        functools.partial(columns_kernel, far), [piece] * len(far) + shared, **half_columns
    )(*packs, *queries, *keys, *audio_edges[::-1], edge_turned)
    audio_pieces = call(
        merge_kernel,
        [piece] * GROUP,
        [pltpu.VMEM((2,) + back.shape, bf16), pltpu.VMEM((GROUP, rows, width), bf16)],
        moved=16 * inside * width,
        exps=4 * inside * width,
        ins=[VMEM] * 4 + [ANY],
        name="merge",
    )(*backs, peaks, sums, far_pieces[0])
    audio_pieces = traded(audio_pieces)
    near_pieces = call(
        functools.partial(columns_kernel, near),
        [piece] * len(near),
        ins=[VMEM] * 5 + [ANY],
        **half_columns,
    )(edge_turned, turned, beside, asks, edge_beside, audio_pieces[0])
    video_pieces = traded([*near_pieces, *far_pieces])

    def join(pieces):
        return call(
            join_kernel,
            shape((rows, half), bf16),
            [pltpu.SemaphoreType.DMA((GROUP,))],
            outs_in=HBM,
            moved=2 * rows * half * 2,
            name="join",
        )(*pieces)

    video_attended = join(video_pieces)
    audio_attended = join(audio_pieces)
    return (audio_attended, video_attended)


def solution(mesh):
    return jax.shard_map(
        local,
        mesh=mesh,
        in_specs=(P("tm", "head"), P("tm", "head"), P("tm"), P(None, "head"), P(None, "head")),
        out_specs=(P("tm", "head"), P("tm", "head")),
        check_vma=False,
    )
```

```python
import functools

import jax
import jax.numpy as jnp
from jax import lax
from jax.experimental import pallas as pl
from jax.experimental.pallas import tpu as pltpu
from jax.sharding import PartitionSpec as P

HEAD = 64
RADIUS = 3
GROUP = 4
NEG = -1e30
ID_ROWS = 16
STAT_ROWS = 16

VMEM = pl.BlockSpec(memory_space=pltpu.VMEM)
ANY = pl.BlockSpec(memory_space=pl.ANY)
HBM = pl.BlockSpec(memory_space=pltpu.HBM)


def place():
    return lax.rem(lax.axis_index("tm"), GROUP)


def plane():
    return lax.axis_index("tm") // GROUP


def call(kernel, outs, scratch=(), ins=None, outs_in=None, flops=0, moved=0, exps=0, name=None):
    return pl.pallas_call(
        kernel,
        out_shape=outs,
        **({"in_specs": ins} if ins else {}),
        **({"out_specs": outs_in} if outs_in else {}),
        scratch_shapes=scratch,
        compiler_params=pltpu.CompilerParams(vmem_limit_bytes=32 * 2**20),
        cost_estimate=pl.CostEstimate(flops=flops, bytes_accessed=moved, transcendentals=exps),
        name=name,
    )


def product(a, b):
    return jnp.dot(a, b, preferred_element_type=jnp.float32)


def fetcher(sems):
    copies = []

    def fetch(source, target):
        copies.append(pltpu.make_async_copy(source, target, sems.at[len(copies)]))
        copies[-1].start()

    return copies, fetch


def split_kernel(audio, video, ids, *refs):
    packs, (ids_in, ids_wide, sems) = refs[:GROUP], refs[GROUP:]
    rows, width = audio.shape[0], packs[0].shape[1]
    mine = place()
    copies, fetch = fetcher(sems)
    fetch(ids, ids_in)
    for k in range(GROUP):
        at = pl.ds(pl.multiple_of((mine ^ k) * width, width), width)
        for i, stream in enumerate((audio, video)):
            fetch(stream.at[:, at], packs[k].at[i * rows : (i + 1) * rows])
    copies[0].wait()
    ids_wide[...] = jnp.zeros_like(ids_wide)
    ids_wide[: ids_in.shape[0]] = (ids_in[...] + 1).astype(jnp.float32)
    for k in range(GROUP):
        packs[k][2 * rows :] = ids_wide[...].astype(packs[k].dtype)
    for copy in copies[1:]:
        copy.wait()


def prepare_kernel(audio, video, query, key, *refs):
    sums, seconds, streams, firsts, sems = refs[-9:-7], refs[-7:-5], refs[-5:-3], refs[-3:-1], refs[-1]
    half = audio.shape[1]
    side = lax.axis_index("head")
    ours = pl.ds(pl.multiple_of(side * half, half), half)
    theirs = pl.ds(pl.multiple_of((1 - side) * half, half), half)
    copies, fetch = fetcher(sems)
    for i, (stream, weight) in enumerate(((audio, query), (video, key))):
        fetch(stream, streams[i])
        fetch(weight.at[ours], firsts[i])
    for i, weight in enumerate((query, key)):
        fetch(weight.at[theirs], seconds[i])
    for i in range(2):
        copies[2 * i].wait()
        copies[2 * i + 1].wait()
        sums[i][...] = product(streams[i][...], firsts[i][...])
    for copy in copies[4:]:
        copy.wait()


def project_kernel(scale, part, other, weight, *refs):
    pieces, full = refs[-GROUP - 1 : -1], refs[-1]
    width = pieces[0].shape[1]
    mine = place()
    full[...] = (part[...] + product(other[...], weight[...])).astype(jnp.bfloat16) * jnp.bfloat16(scale)
    for k in range(GROUP):
        pieces[k][...] = full[:, pl.ds(pl.multiple_of((mine ^ k) * width, width), width)]


def halo_kernel(ids_at, *refs):
    pieces, id_packs, outs = refs[:GROUP], refs[GROUP : 2 * GROUP], refs[-2:]
    rows = outs[0].shape[1] - (ID_ROWS if ids_at else 0)
    mine = place()
    odd = lax.rem(plane(), 2)
    for k in range(GROUP):
        block = mine ^ k
        for out, skip in zip(outs, ((GROUP - RADIUS) * (1 - odd), (GROUP - RADIUS) * odd)):
            spot = block - skip

            @pl.when((spot >= 0) & (spot < RADIUS))
            def _():
                out[spot, :rows] = pieces[k][:rows]
                if ids_at:
                    out[spot, rows:] = id_packs[k][ids_at:]


def join_kernel(*refs):
    pieces, out, sems = refs[:GROUP], refs[GROUP], refs[GROUP + 1]
    width = pieces[0].shape[1]
    mine = place()
    copies, fetch = fetcher(sems)
    for k in range(GROUP):
        fetch(pieces[k], out.at[:, pl.ds(pl.multiple_of((mine ^ k) * width, width), width)])
    for copy in copies:
        copy.wait()


def marks_turned(lanes):
    lanes = lanes.astype(jnp.float32)
    width = lanes.shape[1]
    row = lax.broadcasted_iota(jnp.int32, (width, width), 0).astype(jnp.float32)
    return [
        jnp.where(row == lanes[part : part + 1], 1.0, 0.0).astype(jnp.bfloat16) for part in range(2)
    ]


def stacked_ask(block, turned):
    head = lax.broadcasted_iota(jnp.int32, block.shape, 1) // HEAD
    marks = jnp.concatenate([jnp.transpose(x) for x in turned], axis=0)
    beside = (marks - jnp.bfloat16(1.0)) * jnp.bfloat16(-NEG)
    return jnp.concatenate(
        [
            jnp.concatenate([jnp.where(head == h, block, jnp.zeros_like(block)), beside], axis=1)
            for h in range(block.shape[1] // HEAD)
        ],
        axis=0,
    )


def by_head(stacked, rows):
    out = stacked[:rows]
    head = lax.broadcasted_iota(jnp.int32, out.shape, 1) // HEAD
    for h in range(1, stacked.shape[0] // rows):
        out = jnp.where(head == h, stacked[h * rows : (h + 1) * rows], out)
    return out


def attend(scores, values):
    top = None
    for s in scores:
        for at in range(0, s.shape[1], values[0].shape[1] // 2):
            part = s[:, at : at + values[0].shape[1] // 2]
            top = part if top is None else jnp.maximum(top, part)
    peak = jnp.max(top, axis=1, keepdims=True)
    mixed = None
    for s, value in zip(scores, values):
        part = product(jnp.exp(s - peak).astype(jnp.bfloat16), value)
        mixed = part if mixed is None else mixed + part
    return peak, mixed


def set_up(packs, asked, keys, values, turned, beside, asks):
    rows, width = asks.shape[1] // 2, asks.shape[2] // 2
    mine = place()
    beside[:, width:] = jnp.ones((GROUP * rows, width), beside.dtype)
    for k in range(GROUP):
        b = mine ^ k

        def spot(at, size):
            return pl.ds(pl.multiple_of(b * rows + at, size), size)

        marks = marks_turned(packs[k][2 * rows :])
        asks[b] = stacked_ask(asked(k), marks)
        beside[spot(0, rows), :width] = values(k)
        key = keys(k)
        for part, x in enumerate(marks):
            at = spot(part * width, width)
            turned[:width, at] = jnp.transpose(key[part * width : (part + 1) * width])
            turned[width:, at] = x


def rows_kernel(*refs):
    packs, queries, keys = refs[:GROUP], refs[GROUP : 2 * GROUP], refs[2 * GROUP : 3 * GROUP]
    peaks, sums, turned, beside, asks = refs[-5:]
    rows, width = keys[0].shape
    set_up(
        packs,
        lambda k: queries[k][...],
        lambda k: keys[k][...],
        lambda k: packs[k][rows : 2 * rows],
        turned,
        beside,
        asks,
    )
    ahead = product(asks[0], turned[...])
    for b in range(GROUP):
        scores = ahead
        if b + 1 < GROUP:
            ahead = product(asks[b + 1], turned[...])
        peak, sums[b] = attend([scores], [beside[...]])
        peaks[b] = jnp.broadcast_to(peak, (peak.shape[0], width))


def lend_kernel(edge_b, edge_a, plane_turned, plane_beside, first, second, turned, ordered, results):
    rows, width = ordered.shape[2] - ID_ROWS, ordered.shape[3]
    odd = lax.rem(plane(), 2)
    ordered[1 - odd] = edge_a[...]
    ordered[odd] = edge_b[...]
    lane = lax.broadcasted_iota(jnp.int32, (rows, width), 1)
    blocks = [slice(0, (j + 1) * rows) for j in range(RADIUS)]
    blocks += [slice((j + 1) * rows, GROUP * rows) for j in range(RADIUS)]

    def scores_of(e):
        side, j = e // RADIUS, e % RADIUS
        marks = marks_turned(ordered[side, j, rows:])
        query = ordered[side, j, :rows]
        for part, x in enumerate(marks):
            at = slice(e * rows + part * width, e * rows + (part + 1) * width)
            turned[:width, at] = jnp.transpose(query[part * width : (part + 1) * width])
            turned[width:, at] = x
        return product(stacked_ask(query, marks), plane_turned[:, blocks[e]])

    ahead = scores_of(0)
    for e in range(2 * RADIUS):
        side, j = e // RADIUS, e % RADIUS
        scores = ahead
        if e + 1 < 2 * RADIUS:
            ahead = scores_of(e + 1)
        peak, mixed = attend([scores], [plane_beside[blocks[e]]])
        mean = by_head(mixed[:, :width], rows) / by_head(mixed[:, width:], rows)
        results[side, j, :rows] = mean.astype(results.dtype)
        logs = peak + jnp.log(mixed[:, width:])
        high = logs.astype(jnp.bfloat16)
        rest = logs - high.astype(jnp.float32)
        middle = rest.astype(jnp.bfloat16)
        low = (rest - middle.astype(jnp.float32)).astype(jnp.bfloat16)
        picked = jnp.zeros((rows, width), jnp.bfloat16)
        for h in range(width // HEAD):
            for n, piece in enumerate((high, middle, low)):
                picked = jnp.where(lane == 8 * h + n, piece[h * rows : (h + 1) * rows], picked)
        for part in range(rows // width):
            stats = jnp.transpose(picked[part * width : (part + 1) * width])
            at = rows + part * STAT_ROWS
            results[side, j, at : at + STAT_ROWS] = stats[:STAT_ROWS]
    first[...] = results[1 - odd]
    second[...] = results[odd]


def columns_kernel(receivers, *refs):
    refs = list(refs)
    take = lambda count: [refs.pop(0) for _ in range(count)]
    first = 0 not in receivers
    if first:
        packs, queries, keys, (edge_b, edge_a) = take(GROUP), take(GROUP), take(GROUP), take(2)
    (edge_turned,) = take(1)
    if not first:
        shared, received, _ = take(4), take(GROUP - 1), take(1)
    outs = take(len(receivers) if first else 1)
    turned, beside, asks, edge_beside = take(4) if first else shared
    rows, width = beside.shape[0] // GROUP, beside.shape[1] // 2
    mine = place()
    if not first:
        own, sems = refs
        copies, fetch = fetcher(sems)
        columns = [pl.ds(pl.multiple_of((mine ^ k) * width, width), width) for k in range(GROUP)]
        for k in range(1, GROUP):
            fetch(received[k - 1], outs[0].at[:, columns[k]])
    if first:
        odd = lax.rem(plane(), 2)
        set_up(
            packs,
            lambda k: keys[k][...],
            lambda k: queries[k][...],
            lambda k: packs[k][:rows],
            turned,
            beside,
            asks,
        )
        edge_beside[:, width:] = jnp.ones((edge_beside.shape[0], width), beside.dtype)
        for edge, base in ((edge_a, RADIUS * (1 - odd)), (edge_b, RADIUS * odd)):
            for j in range(RADIUS):
                at = pl.ds(pl.multiple_of((base + j) * rows, rows), rows)
                edge_beside[at, :width] = edge[j]
    near = [pl.ds(pl.multiple_of((mine ^ k) * rows, rows), RADIUS * rows) for k in receivers]

    def scores_of(n):
        ask = asks[mine ^ receivers[n]]
        return [product(ask, turned[...]), product(ask, edge_turned[:, near[n]])]

    ahead = scores_of(0)
    for n in range(len(receivers)):
        scores = ahead
        if n + 1 < len(receivers):
            ahead = scores_of(n + 1)
        _, mixed = attend(scores, [beside[...], edge_beside[near[n]]])
        mean = by_head(mixed[:, :width], rows) / by_head(mixed[:, width:], rows)
        (outs[n] if first else own)[...] = mean.astype(outs[0].dtype)
    if not first:
        fetch(own, outs[0].at[:, columns[0]])
        for copy in copies:
            copy.wait()


def merge_kernel(back_a, back_b, peaks, sums, *refs):
    outs, (backs, whole) = refs[-GROUP - 2 : -2], refs[-2:]
    rows, width = outs[0].shape
    mine = place()
    odd = lax.rem(plane(), 2)
    backs[1 - odd] = back_a[...]
    backs[odd] = back_b[...]
    last = lax.axis_size("tm") // GROUP - 1
    absent = [jnp.where(plane() == end, NEG, 0.0) for end in (0, last)]

    def logs(side, j):
        squares = []
        for part in range(rows // width):
            at = rows + part * STAT_ROWS
            stats = backs[side, j, at : at + STAT_ROWS].astype(jnp.float32)
            heads = [
                stats[8 * h : 8 * h + 1] + stats[8 * h + 1 : 8 * h + 2] + stats[8 * h + 2 : 8 * h + 3]
                for h in range(width // HEAD)
            ]
            turned = jnp.transpose(
                jnp.concatenate([jnp.broadcast_to(x, (HEAD, width)) for x in heads], axis=0)
            )
            squares.append(turned)
        return jnp.concatenate(squares, axis=0) + absent[side]

    for b in range(GROUP):
        theirs = []
        if b < RADIUS:
            theirs.append((0, b))
        if b >= GROUP - RADIUS:
            theirs.append((1, b - (GROUP - RADIUS)))
        theirs = [(logs(*t), backs[t[0], t[1], :rows].astype(jnp.float32)) for t in theirs]
        old = by_head(peaks[b], rows)
        top = old
        for log, _ in theirs:
            top = jnp.maximum(top, log)
        factor = jnp.exp(old - top)
        value = by_head(sums[b, :, :width], rows) * factor
        total = by_head(sums[b, :, width:], rows) * factor
        for log, mean in theirs:
            weight = jnp.exp(log - top)
            value += weight * mean
            total += weight
        whole[b] = (value / total).astype(whole.dtype)
    for k in range(GROUP):
        outs[k][...] = whole[mine ^ k]


def local(audio_frames, video_frames, recording, audio_query, video_key):
    rows, half = audio_frames.shape
    width = half // GROUP
    heads = width // HEAD
    length = lax.axis_size("tm")
    bf16, f32 = jnp.bfloat16, jnp.float32
    shape = jax.ShapeDtypeStruct
    assert length % (2 * GROUP) == 0

    def swapped(x):
        return lax.ppermute(x, "head", [(0, 1), (1, 0)])

    def traded(pieces):
        pairs = lambda k: [(i, i ^ k) for i in range(length)]
        return [pieces[0]] + [lax.ppermute(pieces[k], "tm", pairs(k)) for k in range(1, GROUP)]

    def crossed(sent, second):
        planes = range(second, length // GROUP - second)
        pairs = [(p, ((p + second) ^ 1) - second) for p in planes]
        return lax.ppermute(
            sent, "tm", [(p * GROUP + i, q * GROUP + i) for p, q in pairs for i in range(GROUP)]
        )

    part = shape((rows, half), f32)
    square = shape((half, half), bf16)
    piece = shape((rows, width), bf16)
    given = (audio_frames, video_frames, audio_query, video_key, recording.reshape(rows // width, width))
    audio_in, video_in, query_in, key_in, ids_in = (
        pltpu.with_memory_space_constraint(x, pltpu.HBM) for x in given
    )
    other_audio = swapped(audio_frames)
    other_video = swapped(video_frames)
    packs = call(
        split_kernel,
        [shape((2 * rows + ID_ROWS, width), bf16)] * GROUP,
        [pltpu.VMEM((rows // width, width), jnp.int32), pltpu.VMEM((ID_ROWS, width), f32)]
        + [pltpu.SemaphoreType.DMA((1 + 2 * GROUP,))],
        ins=[HBM] * 3,
        moved=8 * rows * half,
        name="split",
    )(audio_in, video_in, ids_in)
    packs = traded(packs)
    query_part, key_part, query_rest, key_rest = call(
        prepare_kernel,
        [part, part, square, square],
        [pltpu.VMEM((rows, half), bf16)] * 2
        + [pltpu.VMEM((half, half), bf16)] * 2
        + [pltpu.SemaphoreType.DMA((6,))],
        ins=[HBM] * 4 + [ANY],
        flops=4 * rows * half * half,
        moved=16 * half * half,
        name="prepare",
    )(audio_in, video_in, query_in, key_in, packs[1])

    def project(scale, *operands, after=()):
        return call(
            functools.partial(project_kernel, scale),
            [piece] * GROUP,
            [pltpu.VMEM((rows, half), bf16)],
            ins=[VMEM] * 3 + [ANY] * len(after),
            flops=2 * rows * half * half,
            moved=2 * half * half + 6 * rows * half * 2,
            name="project",
        )(*operands, *after)

    def halo(pieces, id_packs, *after):
        edge = shape((RADIUS, rows + (ID_ROWS if id_packs else 0), width), bf16)
        sent = call(
            functools.partial(halo_kernel, 2 * rows if id_packs else 0),
            [edge, edge],
            ins=[VMEM] * (GROUP + len(id_packs)) + [ANY] * len(after),
            moved=10 * rows * width * 2,
            name="halo",
        )(*pieces, *id_packs, *after)
        return [crossed(sent[i], i) for i in range(2)]

    queries = traded(project(HEAD**-0.5, query_part, other_audio, query_rest, after=packs[1:3]))
    keys = project(1.0, key_part, other_video, key_rest, after=())
    query_edges = halo(queries, packs, keys[0])
    keys = traded(keys)

    inside, around = GROUP * rows, 2 * RADIUS * rows
    turned, beside = shape((2 * width, inside), bf16), shape((inside, 2 * width), bf16)
    asks = shape((GROUP, heads * rows, 2 * width), bf16)
    peaks, sums, plane_turned, plane_beside = call(
        rows_kernel,
        [shape((GROUP, heads * rows, n * width), f32) for n in (1, 2)] + [turned, beside],
        [pltpu.VMEM(asks.shape, bf16)],
        flops=16 * GROUP * rows * inside * width,
        moved=8 * inside * width * 2,
        exps=2 * GROUP * rows * inside,
        name="rows",
    )(*packs, *queries, *keys)
    audio_edges = halo(packs, [], peaks)
    back = shape((RADIUS, rows + rows // width * STAT_ROWS, width), bf16)
    lent_a, lent_b, edge_turned = call(
        lend_kernel,
        [back, back, shape((2 * width, around), bf16)],
        [pltpu.VMEM((2, RADIUS, rows + ID_ROWS, width), bf16), pltpu.VMEM((2,) + back.shape, bf16)],
        flops=48 * RADIUS * GROUP * rows * rows * width,
        moved=8 * around * width * 2,
        exps=2 * RADIUS * GROUP * rows * rows,
        name="lend",
    )(*query_edges[::-1], plane_turned, plane_beside)
    backs = [crossed(x, i) for i, x in enumerate((lent_a, lent_b))]

    half_columns = dict(
        flops=56 * GROUP * rows * rows * width,
        moved=4 * around * width * 2,
        exps=7 * GROUP * rows * rows,
        name="columns",
    )
    shared = [turned, beside, asks, shape((around, 2 * width), bf16)]
    far = range(1, GROUP)
    *far_pieces, turned, beside, asks, edge_beside = call(
        functools.partial(columns_kernel, far), [piece] * len(far) + shared, **half_columns
    )(*packs, *queries, *keys, *audio_edges[::-1], edge_turned)
    audio_pieces = call(
        merge_kernel,
        [piece] * GROUP,
        [pltpu.VMEM((2,) + back.shape, bf16), pltpu.VMEM((GROUP, rows, width), bf16)],
        moved=16 * inside * width,
        exps=4 * inside * width,
        ins=[VMEM] * 4 + [ANY],
        name="merge",
    )(*backs, peaks, sums, far_pieces[0])
    audio_pieces = traded(audio_pieces)
    video_pieces = traded([None, *far_pieces])[1:]
    video_attended = call(
        functools.partial(columns_kernel, range(1)),
        shape((rows, half), bf16),
        [pltpu.VMEM((rows, width), bf16), pltpu.SemaphoreType.DMA((GROUP,))],
        ins=[VMEM] * (5 + GROUP - 1) + [ANY],
        outs_in=HBM,
        **half_columns,
    )(edge_turned, turned, beside, asks, edge_beside, *video_pieces, audio_pieces[0])

    def join(pieces):
        return call(
            join_kernel,
            shape((rows, half), bf16),
            [pltpu.SemaphoreType.DMA((GROUP,))],
            outs_in=HBM,
            moved=2 * rows * half * 2,
            name="join",
        )(*pieces)

    audio_attended = join(audio_pieces)
    return (audio_attended, video_attended)


def solution(mesh):
    return jax.shard_map(
        local,
        mesh=mesh,
        in_specs=(P("tm", "head"), P("tm", "head"), P("tm"), P(None, "head"), P(None, "head")),
        out_specs=(P("tm", "head"), P("tm", "head")),
        check_vma=False,
    )
```

```python
import functools

import jax
import jax.numpy as jnp
from jax import lax
from jax.experimental import pallas as pl
from jax.experimental.pallas import tpu as pltpu
from jax.sharding import PartitionSpec as P

HEAD = 64
RADIUS = 3
GROUP = 4
NEG = -1e30
ID_ROWS = 16
STAT_ROWS = 16

VMEM = pl.BlockSpec(memory_space=pltpu.VMEM)
ANY = pl.BlockSpec(memory_space=pl.ANY)
HBM = pl.BlockSpec(memory_space=pltpu.HBM)


def place():
    return lax.rem(lax.axis_index("tm"), GROUP)


def plane():
    return lax.axis_index("tm") // GROUP


def call(kernel, outs, scratch=(), ins=None, outs_in=None, aliases=None, flops=0, moved=0, exps=0, name=None):
    return pl.pallas_call(
        kernel,
        out_shape=outs,
        **({"in_specs": ins} if ins else {}),
        **({"out_specs": outs_in} if outs_in else {}),
        input_output_aliases=aliases or {},
        scratch_shapes=scratch,
        compiler_params=pltpu.CompilerParams(vmem_limit_bytes=32 * 2**20),
        cost_estimate=pl.CostEstimate(flops=flops, bytes_accessed=moved, transcendentals=exps),
        name=name,
    )


def product(a, b):
    return jnp.dot(a, b, preferred_element_type=jnp.float32)


def fetcher(sems):
    copies = []

    def fetch(source, target):
        copies.append(pltpu.make_async_copy(source, target, sems.at[len(copies)]))
        copies[-1].start()

    return copies, fetch


def split_kernel(audio, video, ids, *refs):
    packs, (ids_in, ids_wide, sems) = refs[:GROUP], refs[GROUP:]
    rows, width = audio.shape[0], packs[0].shape[1]
    mine = place()
    copies, fetch = fetcher(sems)
    fetch(ids, ids_in)
    for k in range(GROUP):
        at = pl.ds(pl.multiple_of((mine ^ k) * width, width), width)
        for i, stream in enumerate((audio, video)):
            fetch(stream.at[:, at], packs[k].at[i * rows : (i + 1) * rows])
    copies[0].wait()
    ids_wide[...] = jnp.zeros_like(ids_wide)
    ids_wide[: ids_in.shape[0]] = (ids_in[...] + 1).astype(jnp.float32)
    for k in range(GROUP):
        packs[k][2 * rows :] = ids_wide[...].astype(packs[k].dtype)
    for copy in copies[1:]:
        copy.wait()


def prepare_kernel(audio, video, query, key, *refs):
    sums, seconds, streams, firsts, sems = refs[-9:-7], refs[-7:-5], refs[-5:-3], refs[-3:-1], refs[-1]
    half = audio.shape[1]
    side = lax.axis_index("head")
    ours = pl.ds(pl.multiple_of(side * half, half), half)
    theirs = pl.ds(pl.multiple_of((1 - side) * half, half), half)
    copies, fetch = fetcher(sems)
    for i, (stream, weight) in enumerate(((audio, query), (video, key))):
        fetch(stream, streams[i])
        fetch(weight.at[ours], firsts[i])
    for i, weight in enumerate((query, key)):
        fetch(weight.at[theirs], seconds[i])
    for i in range(2):
        copies[2 * i].wait()
        copies[2 * i + 1].wait()
        sums[i][...] = product(streams[i][...], firsts[i][...])
    for copy in copies[4:]:
        copy.wait()


def project_kernel(scale, part, other, weight, *refs):
    pieces, full = refs[-GROUP - 1 : -1], refs[-1]
    width = pieces[0].shape[1]
    mine = place()
    full[...] = (part[...] + product(other[...], weight[...])).astype(jnp.bfloat16) * jnp.bfloat16(scale)
    for k in range(GROUP):
        pieces[k][...] = full[:, pl.ds(pl.multiple_of((mine ^ k) * width, width), width)]


def halo_kernel(ids_at, *refs):
    pieces, id_packs, outs = refs[:GROUP], refs[GROUP : 2 * GROUP], refs[-2:]
    rows = outs[0].shape[1] - (ID_ROWS if ids_at else 0)
    mine = place()
    odd = lax.rem(plane(), 2)
    for k in range(GROUP):
        block = mine ^ k
        for out, skip in zip(outs, ((GROUP - RADIUS) * (1 - odd), (GROUP - RADIUS) * odd)):
            spot = block - skip

            @pl.when((spot >= 0) & (spot < RADIUS))
            def _():
                out[spot, :rows] = pieces[k][:rows]
                if ids_at:
                    out[spot, rows:] = id_packs[k][ids_at:]


def join_kernel(*refs):
    audio, video, (_, audio_out, video_out, sems) = refs[:GROUP], refs[GROUP:-4], refs[-4:]
    width = audio[0].shape[1]
    mine = place()
    copies, fetch = fetcher(sems)
    for pieces, out in ((audio, audio_out), (video, video_out)):
        for k, piece in enumerate(pieces):
            fetch(piece, out.at[:, pl.ds(pl.multiple_of((mine ^ k) * width, width), width)])
    for copy in copies:
        copy.wait()


def marks_turned(lanes):
    lanes = lanes.astype(jnp.float32)
    width = lanes.shape[1]
    row = lax.broadcasted_iota(jnp.int32, (width, width), 0).astype(jnp.float32)
    return [
        jnp.where(row == lanes[part : part + 1], 1.0, 0.0).astype(jnp.bfloat16) for part in range(2)
    ]


def stacked_ask(block, turned):
    head = lax.broadcasted_iota(jnp.int32, block.shape, 1) // HEAD
    marks = jnp.concatenate([jnp.transpose(x) for x in turned], axis=0)
    beside = (marks - jnp.bfloat16(1.0)) * jnp.bfloat16(-NEG)
    return jnp.concatenate(
        [
            jnp.concatenate([jnp.where(head == h, block, jnp.zeros_like(block)), beside], axis=1)
            for h in range(block.shape[1] // HEAD)
        ],
        axis=0,
    )


def by_head(stacked, rows):
    out = stacked[:rows]
    head = lax.broadcasted_iota(jnp.int32, out.shape, 1) // HEAD
    for h in range(1, stacked.shape[0] // rows):
        out = jnp.where(head == h, stacked[h * rows : (h + 1) * rows], out)
    return out


def attend(scores, values):
    top = None
    for s in scores:
        for at in range(0, s.shape[1], values[0].shape[1] // 2):
            part = s[:, at : at + values[0].shape[1] // 2]
            top = part if top is None else jnp.maximum(top, part)
    peak = jnp.max(top, axis=1, keepdims=True)
    mixed = None
    for s, value in zip(scores, values):
        part = product(jnp.exp(s - peak).astype(jnp.bfloat16), value)
        mixed = part if mixed is None else mixed + part
    return peak, mixed


def set_up(packs, asked, keys, values, turned, beside, asks):
    rows, width = asks.shape[1] // 2, asks.shape[2] // 2
    mine = place()
    beside[:, width:] = jnp.ones((GROUP * rows, width), beside.dtype)
    for k in range(GROUP):
        b = mine ^ k

        def spot(at, size):
            return pl.ds(pl.multiple_of(b * rows + at, size), size)

        marks = marks_turned(packs[k][2 * rows :])
        asks[b] = stacked_ask(asked(k), marks)
        beside[spot(0, rows), :width] = values(k)
        key = keys(k)
        for part, x in enumerate(marks):
            at = spot(part * width, width)
            turned[:width, at] = jnp.transpose(key[part * width : (part + 1) * width])
            turned[width:, at] = x


def rows_kernel(*refs):
    packs, queries, keys = refs[:GROUP], refs[GROUP : 2 * GROUP], refs[2 * GROUP : 3 * GROUP]
    peaks, sums, turned, beside, asks = refs[-5:]
    rows, width = keys[0].shape
    set_up(
        packs,
        lambda k: queries[k][...],
        lambda k: keys[k][...],
        lambda k: packs[k][rows : 2 * rows],
        turned,
        beside,
        asks,
    )
    ahead = product(asks[0], turned[...])
    for b in range(GROUP):
        scores = ahead
        if b + 1 < GROUP:
            ahead = product(asks[b + 1], turned[...])
        peak, sums[b] = attend([scores], [beside[...]])
        peaks[b] = jnp.broadcast_to(peak, (peak.shape[0], width))


def lend_kernel(edge_b, edge_a, plane_turned, plane_beside, first, second, ordered, results):
    rows, width = ordered.shape[2] - ID_ROWS, ordered.shape[3]
    odd = lax.rem(plane(), 2)
    ordered[1 - odd] = edge_a[...]
    ordered[odd] = edge_b[...]
    lane = lax.broadcasted_iota(jnp.int32, (rows, width), 1)
    blocks = [slice(0, (j + 1) * rows) for j in range(RADIUS)]
    blocks += [slice((j + 1) * rows, GROUP * rows) for j in range(RADIUS)]

    def scores_of(e):
        side, j = e // RADIUS, e % RADIUS
        marks = marks_turned(ordered[side, j, rows:])
        query = ordered[side, j, :rows]
        return product(stacked_ask(query, marks), plane_turned[:, blocks[e]])

    ahead = scores_of(0)
    for e in range(2 * RADIUS):
        side, j = e // RADIUS, e % RADIUS
        scores = ahead
        if e + 1 < 2 * RADIUS:
            ahead = scores_of(e + 1)
        peak, mixed = attend([scores], [plane_beside[blocks[e]]])
        mean = by_head(mixed[:, :width], rows) / by_head(mixed[:, width:], rows)
        results[side, j, :rows] = mean.astype(results.dtype)
        logs = peak + jnp.log(mixed[:, width:])
        high = logs.astype(jnp.bfloat16)
        rest = logs - high.astype(jnp.float32)
        middle = rest.astype(jnp.bfloat16)
        low = (rest - middle.astype(jnp.float32)).astype(jnp.bfloat16)
        picked = jnp.zeros((rows, width), jnp.bfloat16)
        for h in range(width // HEAD):
            for n, piece in enumerate((high, middle, low)):
                picked = jnp.where(lane == 8 * h + n, piece[h * rows : (h + 1) * rows], picked)
        for part in range(rows // width):
            stats = jnp.transpose(picked[part * width : (part + 1) * width])
            at = rows + part * STAT_ROWS
            results[side, j, at : at + STAT_ROWS] = stats[:STAT_ROWS]
    first[...] = results[1 - odd]
    second[...] = results[odd]


def columns_kernel(receivers, *refs):
    refs = list(refs)
    take = lambda count: [refs.pop(0) for _ in range(count)]
    first = 0 not in receivers
    if first:
        packs, queries, keys = take(GROUP), take(GROUP), take(GROUP)
        (ask_b, ask_a), (edge_b, edge_a) = take(2), take(2)
        outs = take(len(receivers))
        turned, beside, asks, edge_beside, edge_turned = take(5)
    else:
        turned, beside, asks, edge_beside, edge_turned = take(5)
        received, _, outs, (whole,), (sems,) = take(len(receivers)), take(1), take(len(receivers)), take(1), take(1)
    rows, width = outs[0].shape
    mine = place()
    if first:
        odd = lax.rem(plane(), 2)
        set_up(
            packs,
            lambda k: keys[k][...],
            lambda k: queries[k][...],
            lambda k: packs[k][:rows],
            turned,
            beside,
            asks,
        )
        edge_beside[:, width:] = jnp.ones((edge_beside.shape[0], width), beside.dtype)
        for ask, edge, base in ((ask_a, edge_a, RADIUS * (1 - odd)), (ask_b, edge_b, RADIUS * odd)):
            for j in range(RADIUS):

                def spot(at, size):
                    return pl.ds(pl.multiple_of((base + j) * rows + at, size), size)

                edge_beside[spot(0, rows), :width] = edge[j]
                for part, x in enumerate(marks_turned(ask[j, rows:])):
                    at = spot(part * width, width)
                    edge_turned[:width, at] = jnp.transpose(
                        ask[j, part * width : (part + 1) * width]
                    )
                    edge_turned[width:, at] = x
    else:
        copies, fetch = fetcher(sems)
        for n, k in enumerate(range(GROUP - len(receivers), GROUP)):
            at = pl.ds(pl.multiple_of((mine ^ k) * width, width), width)
            fetch(received[n], whole.at[:, at])
    near = [pl.ds(pl.multiple_of((mine ^ k) * rows, rows), RADIUS * rows) for k in receivers]

    def scores_of(n):
        ask = asks[mine ^ receivers[n]]
        return [product(ask, turned[...]), product(ask, edge_turned[:, near[n]])]

    ahead = scores_of(0)
    for n in range(len(receivers)):
        scores = ahead
        if n + 1 < len(receivers):
            ahead = scores_of(n + 1)
        _, mixed = attend(scores, [beside[...], edge_beside[near[n]]])
        mean = by_head(mixed[:, :width], rows) / by_head(mixed[:, width:], rows)
        outs[n][...] = mean.astype(outs[n].dtype)
    if not first:
        for copy in copies:
            copy.wait()


def merge_kernel(back_a, back_b, peaks, sums, *refs):
    outs, (backs, whole) = refs[-GROUP - 2 : -2], refs[-2:]
    rows, width = outs[0].shape
    mine = place()
    odd = lax.rem(plane(), 2)
    backs[1 - odd] = back_a[...]
    backs[odd] = back_b[...]
    last = lax.axis_size("tm") // GROUP - 1
    absent = [jnp.where(plane() == end, NEG, 0.0) for end in (0, last)]

    def logs(side, j):
        squares = []
        for part in range(rows // width):
            at = rows + part * STAT_ROWS
            stats = backs[side, j, at : at + STAT_ROWS].astype(jnp.float32)
            heads = [
                stats[8 * h : 8 * h + 1] + stats[8 * h + 1 : 8 * h + 2] + stats[8 * h + 2 : 8 * h + 3]
                for h in range(width // HEAD)
            ]
            turned = jnp.transpose(
                jnp.concatenate([jnp.broadcast_to(x, (HEAD, width)) for x in heads], axis=0)
            )
            squares.append(turned)
        return jnp.concatenate(squares, axis=0) + absent[side]

    for b in range(GROUP):
        theirs = []
        if b < RADIUS:
            theirs.append((0, b))
        if b >= GROUP - RADIUS:
            theirs.append((1, b - (GROUP - RADIUS)))
        theirs = [(logs(*t), backs[t[0], t[1], :rows].astype(jnp.float32)) for t in theirs]
        old = by_head(peaks[b], rows)
        top = old
        for log, _ in theirs:
            top = jnp.maximum(top, log)
        factor = jnp.exp(old - top)
        value = by_head(sums[b, :, :width], rows) * factor
        total = by_head(sums[b, :, width:], rows) * factor
        for log, mean in theirs:
            weight = jnp.exp(log - top)
            value += weight * mean
            total += weight
        whole[b] = (value / total).astype(whole.dtype)
    for k in range(GROUP):
        outs[k][...] = whole[mine ^ k]


def local(audio_frames, video_frames, recording, audio_query, video_key):
    rows, half = audio_frames.shape
    width = half // GROUP
    heads = width // HEAD
    length = lax.axis_size("tm")
    bf16, f32 = jnp.bfloat16, jnp.float32
    shape = jax.ShapeDtypeStruct
    assert length % (2 * GROUP) == 0

    def swapped(x):
        return lax.ppermute(x, "head", [(0, 1), (1, 0)])

    def traded(pieces):
        pairs = lambda k: [(i, i ^ k) for i in range(length)]
        return [
            lax.ppermute(x, "tm", pairs(k)) if k and x is not None else x for k, x in enumerate(pieces)
        ]

    def crossed(sent, second):
        planes = range(second, length // GROUP - second)
        pairs = [(p, ((p + second) ^ 1) - second) for p in planes]
        return lax.ppermute(
            sent, "tm", [(p * GROUP + i, q * GROUP + i) for p, q in pairs for i in range(GROUP)]
        )

    part = shape((rows, half), f32)
    square = shape((half, half), bf16)
    piece = shape((rows, width), bf16)
    given = (audio_frames, video_frames, audio_query, video_key, recording.reshape(rows // width, width))
    audio_in, video_in, query_in, key_in, ids_in = (
        pltpu.with_memory_space_constraint(x, pltpu.HBM) for x in given
    )
    other_audio = swapped(audio_frames)
    other_video = swapped(video_frames)
    packs = call(
        split_kernel,
        [shape((2 * rows + ID_ROWS, width), bf16)] * GROUP,
        [pltpu.VMEM((rows // width, width), jnp.int32), pltpu.VMEM((ID_ROWS, width), f32)]
        + [pltpu.SemaphoreType.DMA((1 + 2 * GROUP,))],
        ins=[HBM] * 3,
        moved=8 * rows * half,
        name="split",
    )(audio_in, video_in, ids_in)
    packs = traded(packs)
    query_part, key_part, query_rest, key_rest = call(
        prepare_kernel,
        [part, part, square, square],
        [pltpu.VMEM((rows, half), bf16)] * 2
        + [pltpu.VMEM((half, half), bf16)] * 2
        + [pltpu.SemaphoreType.DMA((6,))],
        ins=[HBM] * 4 + [ANY],
        flops=4 * rows * half * half,
        moved=16 * half * half,
        name="prepare",
    )(audio_in, video_in, query_in, key_in, packs[1])

    def project(scale, *operands, after=()):
        return call(
            functools.partial(project_kernel, scale),
            [piece] * GROUP,
            [pltpu.VMEM((rows, half), bf16)],
            ins=[VMEM] * 3 + [ANY] * len(after),
            flops=2 * rows * half * half,
            moved=2 * half * half + 6 * rows * half * 2,
            name="project",
        )(*operands, *after)

    def halo(pieces, id_packs, *after):
        edge = shape((RADIUS, rows + (ID_ROWS if id_packs else 0), width), bf16)
        sent = call(
            functools.partial(halo_kernel, 2 * rows if id_packs else 0),
            [edge, edge],
            ins=[VMEM] * (GROUP + len(id_packs)) + [ANY] * len(after),
            moved=10 * rows * width * 2,
            name="halo",
        )(*pieces, *id_packs, *after)
        return [crossed(sent[i], i) for i in range(2)]

    queries = traded(project(HEAD**-0.5, query_part, other_audio, query_rest, after=packs[1:3]))
    keys = project(1.0, key_part, other_video, key_rest, after=())
    query_edges = halo(queries, packs, keys[0])
    keys = traded(keys)

    inside, around = GROUP * rows, 2 * RADIUS * rows
    turned, beside = shape((2 * width, inside), bf16), shape((inside, 2 * width), bf16)
    asks = shape((GROUP, heads * rows, 2 * width), bf16)
    peaks, sums, plane_turned, plane_beside = call(
        rows_kernel,
        [shape((GROUP, heads * rows, n * width), f32) for n in (1, 2)] + [turned, beside],
        [pltpu.VMEM(asks.shape, bf16)],
        flops=16 * GROUP * rows * inside * width,
        moved=8 * inside * width * 2,
        exps=2 * GROUP * rows * inside,
        name="rows",
    )(*packs, *queries, *keys)
    audio_edges = halo(packs, [], peaks)
    back = shape((RADIUS, rows + rows // width * STAT_ROWS, width), bf16)
    lent_a, lent_b = call(
        lend_kernel,
        [back, back],
        [pltpu.VMEM((2, RADIUS, rows + ID_ROWS, width), bf16), pltpu.VMEM((2,) + back.shape, bf16)],
        flops=48 * RADIUS * GROUP * rows * rows * width,
        moved=8 * around * width * 2,
        exps=2 * RADIUS * GROUP * rows * rows,
        name="lend",
    )(*query_edges[::-1], plane_turned, plane_beside)
    backs = [crossed(x, i) for i, x in enumerate((lent_a, lent_b))]

    half_columns = dict(
        flops=56 * GROUP * rows * rows * width,
        moved=4 * around * width * 2,
        exps=7 * GROUP * rows * rows,
        name="columns",
    )
    shared = [turned, beside, asks, shape((around, 2 * width), bf16), shape((2 * width, around), bf16)]
    near, far = range(GROUP // 2), range(GROUP // 2, GROUP)
    *far_pieces, turned, beside, asks, edge_beside, edge_turned = call(
        functools.partial(columns_kernel, far), [piece] * len(far) + shared, **half_columns
    )(*packs, *queries, *keys, *query_edges[::-1], *audio_edges[::-1])
    audio_pieces = call(
        merge_kernel,
        [piece] * GROUP,
        [pltpu.VMEM((2,) + back.shape, bf16), pltpu.VMEM((GROUP, rows, width), bf16)],
        moved=16 * inside * width,
        exps=4 * inside * width,
        ins=[VMEM] * 4 + [ANY],
        name="merge",
    )(*backs, peaks, sums, far_pieces[0])
    audio_pieces = traded(audio_pieces)
    received = traded([None, None, *far_pieces])[2:]
    whole = shape((rows, half), bf16)
    *near_pieces, partial = call(
        functools.partial(columns_kernel, near),
        [piece] * len(near) + [whole],
        [pltpu.SemaphoreType.DMA((len(far),))],
        ins=[VMEM] * (5 + len(far)) + [ANY],
        outs_in=[VMEM] * len(near) + [HBM],
        **half_columns,
    )(turned, beside, asks, edge_beside, edge_turned, *received, audio_pieces[0])
    near_pieces = traded(near_pieces)
    audio_attended, video_attended = call(
        join_kernel,
        [whole, whole],
        [pltpu.SemaphoreType.DMA((GROUP + len(near),))],
        ins=[VMEM] * (GROUP + len(near)) + [HBM],
        outs_in=[HBM, HBM],
        aliases={GROUP + len(near): 1},
        moved=4 * rows * half * 2,
        name="join",
    )(*audio_pieces, *near_pieces, partial)
    return (audio_attended, video_attended)


def solution(mesh):
    return jax.shard_map(
        local,
        mesh=mesh,
        in_specs=(P("tm", "head"), P("tm", "head"), P("tm"), P(None, "head"), P(None, "head")),
        out_specs=(P("tm", "head"), P("tm", "head")),
        check_vma=False,
    )
```

```python
import functools

import jax
import jax.numpy as jnp
from jax import lax
from jax.experimental import pallas as pl
from jax.experimental.pallas import tpu as pltpu
from jax.sharding import PartitionSpec as P

HEAD = 64
RADIUS = 3
GROUP = 4
NEG = -1e30
ID_ROWS = 16
STAT_ROWS = 16

VMEM = pl.BlockSpec(memory_space=pltpu.VMEM)
ANY = pl.BlockSpec(memory_space=pl.ANY)
HBM = pl.BlockSpec(memory_space=pltpu.HBM)


def place():
    return lax.rem(lax.axis_index("tm"), GROUP)


def receiver(mine, k):
    return lax.rem(mine + k, GROUP)


def sender(mine, k):
    return lax.rem(mine + GROUP - k, GROUP)


def plane():
    return lax.axis_index("tm") // GROUP


def call(kernel, outs, scratch=(), ins=None, outs_in=None, flops=0, moved=0, exps=0, name=None):
    return pl.pallas_call(
        kernel,
        out_shape=outs,
        **({"in_specs": ins} if ins else {}),
        **({"out_specs": outs_in} if outs_in else {}),
        scratch_shapes=scratch,
        compiler_params=pltpu.CompilerParams(vmem_limit_bytes=32 * 2**20),
        cost_estimate=pl.CostEstimate(flops=flops, bytes_accessed=moved, transcendentals=exps),
        name=name,
    )


def product(a, b):
    return jnp.dot(a, b, preferred_element_type=jnp.float32)


def fetcher(sems):
    copies = []

    def fetch(source, target):
        copies.append(pltpu.make_async_copy(source, target, sems.at[len(copies)]))
        copies[-1].start()

    return copies, fetch


def split_kernel(audio, video, ids, *refs):
    packs, (ids_in, ids_wide, sems) = refs[:GROUP], refs[GROUP:]
    rows, width = audio.shape[0], packs[0].shape[1]
    mine = place()
    copies, fetch = fetcher(sems)
    fetch(ids, ids_in)
    for k in range(GROUP):
        at = pl.ds(pl.multiple_of(receiver(mine, k) * width, width), width)
        for i, stream in enumerate((audio, video)):
            fetch(stream.at[:, at], packs[k].at[i * rows : (i + 1) * rows])
    copies[0].wait()
    ids_wide[...] = jnp.zeros_like(ids_wide)
    ids_wide[: ids_in.shape[0]] = (ids_in[...] + 1).astype(jnp.float32)
    for k in range(GROUP):
        packs[k][2 * rows :] = ids_wide[...].astype(packs[k].dtype)
    for copy in copies[1:]:
        copy.wait()


def prepare_kernel(audio, video, query, key, *refs):
    sums, seconds, streams, firsts, sems = refs[-9:-7], refs[-7:-5], refs[-5:-3], refs[-3:-1], refs[-1]
    half = audio.shape[1]
    side = lax.axis_index("head")
    ours = pl.ds(pl.multiple_of(side * half, half), half)
    theirs = pl.ds(pl.multiple_of((1 - side) * half, half), half)
    copies, fetch = fetcher(sems)
    for i, (stream, weight) in enumerate(((audio, query), (video, key))):
        fetch(stream, streams[i])
        fetch(weight.at[ours], firsts[i])
    for i, weight in enumerate((query, key)):
        fetch(weight.at[theirs], seconds[i])
    for i in range(2):
        copies[2 * i].wait()
        copies[2 * i + 1].wait()
        sums[i][...] = product(streams[i][...], firsts[i][...])
    for copy in copies[4:]:
        copy.wait()


def project_kernel(scale, part, other, weight, *refs):
    pieces, full = refs[-GROUP - 1 : -1], refs[-1]
    width = pieces[0].shape[1]
    mine = place()
    full[...] = (part[...] + product(other[...], weight[...])).astype(jnp.bfloat16) * jnp.bfloat16(scale)
    for k in range(GROUP):
        pieces[k][...] = full[:, pl.ds(pl.multiple_of(receiver(mine, k) * width, width), width)]


def halo_kernel(ids_at, *refs):
    pieces, id_packs, outs = refs[:GROUP], refs[GROUP : 2 * GROUP], refs[-2:]
    rows = outs[0].shape[1] - (ID_ROWS if ids_at else 0)
    mine = place()
    odd = lax.rem(plane(), 2)
    for k in range(GROUP):
        block = sender(mine, k)
        for out, skip in zip(outs, ((GROUP - RADIUS) * (1 - odd), (GROUP - RADIUS) * odd)):
            spot = block - skip

            @pl.when((spot >= 0) & (spot < RADIUS))
            def _():
                out[spot, :rows] = pieces[k][:rows]
                if ids_at:
                    out[spot, rows:] = id_packs[k][ids_at:]


def join_kernel(*refs):
    pieces, out, sems = refs[:GROUP], refs[GROUP], refs[GROUP + 1]
    width = pieces[0].shape[1]
    mine = place()
    copies, fetch = fetcher(sems)
    for k in range(GROUP):
        fetch(pieces[k], out.at[:, pl.ds(pl.multiple_of(sender(mine, k) * width, width), width)])
    for copy in copies:
        copy.wait()


def marks_turned(lanes):
    lanes = lanes.astype(jnp.float32)
    width = lanes.shape[1]
    row = lax.broadcasted_iota(jnp.int32, (width, width), 0).astype(jnp.float32)
    return [
        jnp.where(row == lanes[part : part + 1], 1.0, 0.0).astype(jnp.bfloat16) for part in range(2)
    ]


def stacked_ask(block, turned):
    head = lax.broadcasted_iota(jnp.int32, block.shape, 1) // HEAD
    marks = jnp.concatenate([jnp.transpose(x) for x in turned], axis=0)
    beside = (marks - jnp.bfloat16(1.0)) * jnp.bfloat16(-NEG)
    return jnp.concatenate(
        [
            jnp.concatenate([jnp.where(head == h, block, jnp.zeros_like(block)), beside], axis=1)
            for h in range(block.shape[1] // HEAD)
        ],
        axis=0,
    )


def by_head(stacked, rows):
    out = stacked[:rows]
    head = lax.broadcasted_iota(jnp.int32, out.shape, 1) // HEAD
    for h in range(1, stacked.shape[0] // rows):
        out = jnp.where(head == h, stacked[h * rows : (h + 1) * rows], out)
    return out


def attend(scores, values):
    top = None
    for s in scores:
        for at in range(0, s.shape[1], values[0].shape[1] // 2):
            part = s[:, at : at + values[0].shape[1] // 2]
            top = part if top is None else jnp.maximum(top, part)
    peak = jnp.max(top, axis=1, keepdims=True)
    mixed = None
    for s, value in zip(scores, values):
        part = product(jnp.exp(s - peak).astype(jnp.bfloat16), value)
        mixed = part if mixed is None else mixed + part
    return peak, mixed


def set_up(packs, asked, keys, values, turned, beside, asks):
    rows, width = asks.shape[1] // 2, asks.shape[2] // 2
    mine = place()
    beside[:, width:] = jnp.ones((GROUP * rows, width), beside.dtype)
    for k in range(GROUP):
        b = sender(mine, k)

        def spot(at, size):
            return pl.ds(pl.multiple_of(b * rows + at, size), size)

        marks = marks_turned(packs[k][2 * rows :])
        asks[b] = stacked_ask(asked(k), marks)
        beside[spot(0, rows), :width] = values(k)
        key = keys(k)
        for part, x in enumerate(marks):
            at = spot(part * width, width)
            turned[:width, at] = jnp.transpose(key[part * width : (part + 1) * width])
            turned[width:, at] = x


def rows_kernel(*refs):
    packs, queries, keys = refs[:GROUP], refs[GROUP : 2 * GROUP], refs[2 * GROUP : 3 * GROUP]
    peaks, sums, turned, beside, asks = refs[-5:]
    rows, width = keys[0].shape
    set_up(
        packs,
        lambda k: queries[k][...],
        lambda k: keys[k][...],
        lambda k: packs[k][rows : 2 * rows],
        turned,
        beside,
        asks,
    )
    ahead = product(asks[0], turned[...])
    for b in range(GROUP):
        scores = ahead
        if b + 1 < GROUP:
            ahead = product(asks[b + 1], turned[...])
        peak, sums[b] = attend([scores], [beside[...]])
        peaks[b] = jnp.broadcast_to(peak, (peak.shape[0], width))


def lend_kernel(edge_b, edge_a, plane_turned, plane_beside, first, second, turned, ordered, results):
    rows, width = ordered.shape[2] - ID_ROWS, ordered.shape[3]
    odd = lax.rem(plane(), 2)
    ordered[1 - odd] = edge_a[...]
    ordered[odd] = edge_b[...]
    lane = lax.broadcasted_iota(jnp.int32, (rows, width), 1)
    blocks = [slice(0, (j + 1) * rows) for j in range(RADIUS)]
    blocks += [slice((j + 1) * rows, GROUP * rows) for j in range(RADIUS)]

    def scores_of(e):
        side, j = e // RADIUS, e % RADIUS
        marks = marks_turned(ordered[side, j, rows:])
        query = ordered[side, j, :rows]
        for part, x in enumerate(marks):
            at = slice(e * rows + part * width, e * rows + (part + 1) * width)
            turned[:width, at] = jnp.transpose(query[part * width : (part + 1) * width])
            turned[width:, at] = x
        return product(stacked_ask(query, marks), plane_turned[:, blocks[e]])

    ahead = scores_of(0)
    for e in range(2 * RADIUS):
        side, j = e // RADIUS, e % RADIUS
        scores = ahead
        if e + 1 < 2 * RADIUS:
            ahead = scores_of(e + 1)
        peak, mixed = attend([scores], [plane_beside[blocks[e]]])
        mean = by_head(mixed[:, :width], rows) / by_head(mixed[:, width:], rows)
        results[side, j, :rows] = mean.astype(results.dtype)
        logs = peak + jnp.log(mixed[:, width:])
        high = logs.astype(jnp.bfloat16)
        rest = logs - high.astype(jnp.float32)
        middle = rest.astype(jnp.bfloat16)
        low = (rest - middle.astype(jnp.float32)).astype(jnp.bfloat16)
        picked = jnp.zeros((rows, width), jnp.bfloat16)
        for h in range(width // HEAD):
            for n, piece in enumerate((high, middle, low)):
                picked = jnp.where(lane == 8 * h + n, piece[h * rows : (h + 1) * rows], picked)
        for part in range(rows // width):
            stats = jnp.transpose(picked[part * width : (part + 1) * width])
            at = rows + part * STAT_ROWS
            results[side, j, at : at + STAT_ROWS] = stats[:STAT_ROWS]
    first[...] = results[1 - odd]
    second[...] = results[odd]


def columns_kernel(receivers, *refs):
    refs = list(refs)
    take = lambda count: [refs.pop(0) for _ in range(count)]
    first = 0 not in receivers
    if first:
        packs, queries, keys, (edge_b, edge_a) = take(GROUP), take(GROUP), take(GROUP), take(2)
    (edge_turned,) = take(1)
    if not first:
        shared, _ = take(4), take(1)
    outs = take(len(receivers))
    turned, beside, asks, edge_beside = take(4) if first else shared
    rows, width = outs[0].shape
    mine = place()
    if first:
        odd = lax.rem(plane(), 2)
        set_up(
            packs,
            lambda k: keys[k][...],
            lambda k: queries[k][...],
            lambda k: packs[k][:rows],
            turned,
            beside,
            asks,
        )
        edge_beside[:, width:] = jnp.ones((edge_beside.shape[0], width), beside.dtype)
        for edge, base in ((edge_a, RADIUS * (1 - odd)), (edge_b, RADIUS * odd)):
            for j in range(RADIUS):
                at = pl.ds(pl.multiple_of((base + j) * rows, rows), rows)
                edge_beside[at, :width] = edge[j]
    near = [pl.ds(pl.multiple_of(receiver(mine, k) * rows, rows), RADIUS * rows) for k in receivers]

    def scores_of(n):
        ask = asks[receiver(mine, receivers[n])]
        return [product(ask, turned[...]), product(ask, edge_turned[:, near[n]])]

    ahead = scores_of(0)
    for n in range(len(receivers)):
        scores = ahead
        if n + 1 < len(receivers):
            ahead = scores_of(n + 1)
        _, mixed = attend(scores, [beside[...], edge_beside[near[n]]])
        mean = by_head(mixed[:, :width], rows) / by_head(mixed[:, width:], rows)
        outs[n][...] = mean.astype(outs[n].dtype)


def merge_kernel(back_a, back_b, peaks, sums, *refs):
    outs, (backs, whole) = refs[-GROUP - 2 : -2], refs[-2:]
    rows, width = outs[0].shape
    mine = place()
    odd = lax.rem(plane(), 2)
    backs[1 - odd] = back_a[...]
    backs[odd] = back_b[...]
    last = lax.axis_size("tm") // GROUP - 1
    absent = [jnp.where(plane() == end, NEG, 0.0) for end in (0, last)]

    def logs(side, j):
        squares = []
        for part in range(rows // width):
            at = rows + part * STAT_ROWS
            stats = backs[side, j, at : at + STAT_ROWS].astype(jnp.float32)
            heads = [
                stats[8 * h : 8 * h + 1] + stats[8 * h + 1 : 8 * h + 2] + stats[8 * h + 2 : 8 * h + 3]
                for h in range(width // HEAD)
            ]
            turned = jnp.transpose(
                jnp.concatenate([jnp.broadcast_to(x, (HEAD, width)) for x in heads], axis=0)
            )
            squares.append(turned)
        return jnp.concatenate(squares, axis=0) + absent[side]

    for b in range(GROUP):
        theirs = []
        if b < RADIUS:
            theirs.append((0, b))
        if b >= GROUP - RADIUS:
            theirs.append((1, b - (GROUP - RADIUS)))
        theirs = [(logs(*t), backs[t[0], t[1], :rows].astype(jnp.float32)) for t in theirs]
        old = by_head(peaks[b], rows)
        top = old
        for log, _ in theirs:
            top = jnp.maximum(top, log)
        factor = jnp.exp(old - top)
        value = by_head(sums[b, :, :width], rows) * factor
        total = by_head(sums[b, :, width:], rows) * factor
        for log, mean in theirs:
            weight = jnp.exp(log - top)
            value += weight * mean
            total += weight
        whole[b] = (value / total).astype(whole.dtype)
    for k in range(GROUP):
        outs[k][...] = whole[receiver(mine, k)]


def local(audio_frames, video_frames, recording, audio_query, video_key):
    rows, half = audio_frames.shape
    width = half // GROUP
    heads = width // HEAD
    length = lax.axis_size("tm")
    bf16, f32 = jnp.bfloat16, jnp.float32
    shape = jax.ShapeDtypeStruct
    assert length % (2 * GROUP) == 0

    def swapped(x):
        return lax.ppermute(x, "head", [(0, 1), (1, 0)])

    def traded(pieces):
        pairs = lambda k: [(i, i - i % GROUP + (i + k) % GROUP) for i in range(length)]
        return [pieces[0]] + [lax.ppermute(pieces[k], "tm", pairs(k)) for k in range(1, GROUP)]

    def crossed(sent, second):
        planes = range(second, length // GROUP - second)
        pairs = [(p, ((p + second) ^ 1) - second) for p in planes]
        return lax.ppermute(
            sent, "tm", [(p * GROUP + i, q * GROUP + i) for p, q in pairs for i in range(GROUP)]
        )

    part = shape((rows, half), f32)
    square = shape((half, half), bf16)
    piece = shape((rows, width), bf16)
    given = (audio_frames, video_frames, audio_query, video_key, recording.reshape(rows // width, width))
    audio_in, video_in, query_in, key_in, ids_in = (
        pltpu.with_memory_space_constraint(x, pltpu.HBM) for x in given
    )
    other_audio = swapped(audio_frames)
    other_video = swapped(video_frames)
    packs = call(
        split_kernel,
        [shape((2 * rows + ID_ROWS, width), bf16)] * GROUP,
        [pltpu.VMEM((rows // width, width), jnp.int32), pltpu.VMEM((ID_ROWS, width), f32)]
        + [pltpu.SemaphoreType.DMA((1 + 2 * GROUP,))],
        ins=[HBM] * 3,
        moved=8 * rows * half,
        name="split",
    )(audio_in, video_in, ids_in)
    packs = traded(packs)
    query_part, key_part, query_rest, key_rest = call(
        prepare_kernel,
        [part, part, square, square],
        [pltpu.VMEM((rows, half), bf16)] * 2
        + [pltpu.VMEM((half, half), bf16)] * 2
        + [pltpu.SemaphoreType.DMA((6,))],
        ins=[HBM] * 4 + [ANY],
        flops=4 * rows * half * half,
        moved=16 * half * half,
        name="prepare",
    )(audio_in, video_in, query_in, key_in, packs[1])

    def project(scale, *operands, after=()):
        return call(
            functools.partial(project_kernel, scale),
            [piece] * GROUP,
            [pltpu.VMEM((rows, half), bf16)],
            ins=[VMEM] * 3 + [ANY] * len(after),
            flops=2 * rows * half * half,
            moved=2 * half * half + 6 * rows * half * 2,
            name="project",
        )(*operands, *after)

    def halo(pieces, id_packs, *after):
        edge = shape((RADIUS, rows + (ID_ROWS if id_packs else 0), width), bf16)
        sent = call(
            functools.partial(halo_kernel, 2 * rows if id_packs else 0),
            [edge, edge],
            ins=[VMEM] * (GROUP + len(id_packs)) + [ANY] * len(after),
            moved=10 * rows * width * 2,
            name="halo",
        )(*pieces, *id_packs, *after)
        return [crossed(sent[i], i) for i in range(2)]

    queries = traded(project(HEAD**-0.5, query_part, other_audio, query_rest, after=packs[1:3]))
    keys = project(1.0, key_part, other_video, key_rest, after=())
    query_edges = halo(queries, packs, keys[0])
    keys = traded(keys)

    inside, around = GROUP * rows, 2 * RADIUS * rows
    turned, beside = shape((2 * width, inside), bf16), shape((inside, 2 * width), bf16)
    asks = shape((GROUP, heads * rows, 2 * width), bf16)
    peaks, sums, plane_turned, plane_beside = call(
        rows_kernel,
        [shape((GROUP, heads * rows, n * width), f32) for n in (1, 2)] + [turned, beside],
        [pltpu.VMEM(asks.shape, bf16)],
        flops=16 * GROUP * rows * inside * width,
        moved=8 * inside * width * 2,
        exps=2 * GROUP * rows * inside,
        name="rows",
    )(*packs, *queries, *keys)
    audio_edges = halo(packs, [], peaks)
    back = shape((RADIUS, rows + rows // width * STAT_ROWS, width), bf16)
    lent_a, lent_b, edge_turned = call(
        lend_kernel,
        [back, back, shape((2 * width, around), bf16)],
        [pltpu.VMEM((2, RADIUS, rows + ID_ROWS, width), bf16), pltpu.VMEM((2,) + back.shape, bf16)],
        flops=48 * RADIUS * GROUP * rows * rows * width,
        moved=8 * around * width * 2,
        exps=2 * RADIUS * GROUP * rows * rows,
        name="lend",
    )(*query_edges[::-1], plane_turned, plane_beside)
    backs = [crossed(x, i) for i, x in enumerate((lent_a, lent_b))]

    half_columns = dict(
        flops=56 * GROUP * rows * rows * width,
        moved=4 * around * width * 2,
        exps=7 * GROUP * rows * rows,
        name="columns",
    )
    shared = [turned, beside, asks, shape((around, 2 * width), bf16)]
    near, far = range(GROUP // 2), range(GROUP // 2, GROUP)
    *far_pieces, turned, beside, asks, edge_beside = call(
        functools.partial(columns_kernel, far), [piece] * len(far) + shared, **half_columns
    )(*packs, *queries, *keys, *audio_edges[::-1], edge_turned)
    audio_pieces = call(
        merge_kernel,
        [piece] * GROUP,
        [pltpu.VMEM((2,) + back.shape, bf16), pltpu.VMEM((GROUP, rows, width), bf16)],
        moved=16 * inside * width,
        exps=4 * inside * width,
        ins=[VMEM] * 4 + [ANY],
        name="merge",
    )(*backs, peaks, sums, far_pieces[0])
    audio_pieces = traded(audio_pieces)
    near_pieces = call(
        functools.partial(columns_kernel, near),
        [piece] * len(near),
        ins=[VMEM] * 5 + [ANY],
        **half_columns,
    )(edge_turned, turned, beside, asks, edge_beside, audio_pieces[0])
    video_pieces = traded([*near_pieces, *far_pieces])

    def join(pieces):
        return call(
            join_kernel,
            shape((rows, half), bf16),
            [pltpu.SemaphoreType.DMA((GROUP,))],
            outs_in=HBM,
            moved=2 * rows * half * 2,
            name="join",
        )(*pieces)

    video_attended = join(video_pieces)
    audio_attended = join(audio_pieces)
    return (audio_attended, video_attended)


def solution(mesh):
    return jax.shard_map(
        local,
        mesh=mesh,
        in_specs=(P("tm", "head"), P("tm", "head"), P("tm"), P(None, "head"), P(None, "head")),
        out_specs=(P("tm", "head"), P("tm", "head")),
        check_vma=False,
    )
```

```python
import functools

import jax
import jax.numpy as jnp
from jax import lax
from jax.experimental import pallas as pl
from jax.experimental.pallas import tpu as pltpu
from jax.sharding import PartitionSpec as P

HEAD = 64
RADIUS = 3
GROUP = 4
NEG = -1e30
ID_ROWS = 16
STAT_ROWS = 16

VMEM = pl.BlockSpec(memory_space=pltpu.VMEM)
ANY = pl.BlockSpec(memory_space=pl.ANY)
HBM = pl.BlockSpec(memory_space=pltpu.HBM)


def place():
    return lax.rem(lax.axis_index("tm"), GROUP)


def plane():
    return lax.axis_index("tm") // GROUP


def call(kernel, outs, scratch=(), ins=None, outs_in=None, flops=0, moved=0, exps=0, name=None):
    return pl.pallas_call(
        kernel,
        out_shape=outs,
        **({"in_specs": ins} if ins else {}),
        **({"out_specs": outs_in} if outs_in else {}),
        scratch_shapes=scratch,
        compiler_params=pltpu.CompilerParams(vmem_limit_bytes=32 * 2**20),
        cost_estimate=pl.CostEstimate(flops=flops, bytes_accessed=moved, transcendentals=exps),
        name=name,
    )


def product(a, b):
    return jnp.dot(a, b, preferred_element_type=jnp.float32)


def fetcher(sems):
    copies = []

    def fetch(source, target):
        copies.append(pltpu.make_async_copy(source, target, sems.at[len(copies)]))
        copies[-1].start()

    return copies, fetch


def split_kernel(audio, video, ids, *refs):
    packs, (ids_in, ids_wide, sems) = refs[:GROUP], refs[GROUP:]
    rows, width = audio.shape[0], packs[0].shape[1]
    mine = place()
    copies, fetch = fetcher(sems)
    fetch(ids, ids_in)
    for k in range(GROUP):
        at = pl.ds(pl.multiple_of((mine ^ k) * width, width), width)
        for i, stream in enumerate((audio, video)):
            fetch(stream.at[:, at], packs[k].at[i * rows : (i + 1) * rows])
    copies[0].wait()
    ids_wide[...] = jnp.zeros_like(ids_wide)
    ids_wide[: ids_in.shape[0]] = (ids_in[...] + 1).astype(jnp.float32)
    for k in range(GROUP):
        packs[k][2 * rows :] = ids_wide[...].astype(packs[k].dtype)
    for copy in copies[1:]:
        copy.wait()


def prepare_kernel(audio, video, query, key, *refs):
    sums, seconds, streams, firsts, sems = refs[-9:-7], refs[-7:-5], refs[-5:-3], refs[-3:-1], refs[-1]
    half = audio.shape[1]
    side = lax.axis_index("head")
    ours = pl.ds(pl.multiple_of(side * half, half), half)
    theirs = pl.ds(pl.multiple_of((1 - side) * half, half), half)
    copies, fetch = fetcher(sems)
    for i, (stream, weight) in enumerate(((audio, query), (video, key))):
        fetch(stream, streams[i])
        fetch(weight.at[ours], firsts[i])
    for i, weight in enumerate((query, key)):
        fetch(weight.at[theirs], seconds[i])
    for i in range(2):
        copies[2 * i].wait()
        copies[2 * i + 1].wait()
        sums[i][...] = product(streams[i][...], firsts[i][...])
    for copy in copies[4:]:
        copy.wait()


def project_kernel(scale, part, other, weight, *refs):
    pieces, full = refs[-GROUP - 1 : -1], refs[-1]
    width = pieces[0].shape[1]
    mine = place()
    full[...] = (part[...] + product(other[...], weight[...])).astype(jnp.bfloat16) * jnp.bfloat16(scale)
    for k in range(GROUP):
        pieces[k][...] = full[:, pl.ds(pl.multiple_of((mine ^ k) * width, width), width)]


def halo_kernel(ids_at, *refs):
    pieces, id_packs, outs = refs[:GROUP], refs[GROUP : 2 * GROUP], refs[-2:]
    rows = outs[0].shape[1] - (ID_ROWS if ids_at else 0)
    mine = place()
    odd = lax.rem(plane(), 2)
    for k in range(GROUP):
        block = mine ^ k
        for out, skip in zip(outs, ((GROUP - RADIUS) * (1 - odd), (GROUP - RADIUS) * odd)):
            spot = block - skip

            @pl.when((spot >= 0) & (spot < RADIUS))
            def _():
                out[spot, :rows] = pieces[k][:rows]
                if ids_at:
                    out[spot, rows:] = id_packs[k][ids_at:]


def join_kernel(*refs):
    pieces, out, sems = refs[:GROUP], refs[GROUP], refs[GROUP + 1]
    width = pieces[0].shape[1]
    mine = place()
    copies, fetch = fetcher(sems)
    for k in range(GROUP):
        fetch(pieces[k], out.at[:, pl.ds(pl.multiple_of((mine ^ k) * width, width), width)])
    for copy in copies:
        copy.wait()


def marks_turned(lanes):
    lanes = lanes.astype(jnp.float32)
    width = lanes.shape[1]
    row = lax.broadcasted_iota(jnp.int32, (width, width), 0).astype(jnp.float32)
    return [
        jnp.where(row == lanes[part : part + 1], 1.0, 0.0).astype(jnp.bfloat16) for part in range(2)
    ]


def stacked_ask(block, turned):
    head = lax.broadcasted_iota(jnp.int32, block.shape, 1) // HEAD
    marks = jnp.concatenate([jnp.transpose(x) for x in turned], axis=0)
    beside = (marks - jnp.bfloat16(1.0)) * jnp.bfloat16(-NEG)
    return jnp.concatenate(
        [
            jnp.concatenate([jnp.where(head == h, block, jnp.zeros_like(block)), beside], axis=1)
            for h in range(block.shape[1] // HEAD)
        ],
        axis=0,
    )


def by_head(stacked, rows):
    out = stacked[:rows]
    head = lax.broadcasted_iota(jnp.int32, out.shape, 1) // HEAD
    for h in range(1, stacked.shape[0] // rows):
        out = jnp.where(head == h, stacked[h * rows : (h + 1) * rows], out)
    return out


def attend(scores, values):
    top = None
    for s in scores:
        for at in range(0, s.shape[1], values[0].shape[1] // 2):
            part = s[:, at : at + values[0].shape[1] // 2]
            top = part if top is None else jnp.maximum(top, part)
    peak = jnp.max(top, axis=1, keepdims=True)
    mixed = None
    for s, value in zip(scores, values):
        part = product(jnp.exp(s - peak).astype(jnp.bfloat16), value)
        mixed = part if mixed is None else mixed + part
    return peak, mixed


def set_up(packs, asked, keys, values, turned, beside, asks):
    rows, width = asks.shape[1] // 2, asks.shape[2] // 2
    mine = place()
    beside[:, width:] = jnp.ones((GROUP * rows, width), beside.dtype)
    for k in range(GROUP):
        b = mine ^ k

        def spot(at, size):
            return pl.ds(pl.multiple_of(b * rows + at, size), size)

        marks = marks_turned(packs[k][2 * rows :])
        asks[b] = stacked_ask(asked(k), marks)
        beside[spot(0, rows), :width] = values(k)
        key = keys(k)
        for part, x in enumerate(marks):
            at = spot(part * width, width)
            turned[:width, at] = jnp.transpose(key[part * width : (part + 1) * width])
            turned[width:, at] = x


def rows_kernel(*refs):
    packs, queries, keys = refs[:GROUP], refs[GROUP : 2 * GROUP], refs[2 * GROUP : 3 * GROUP]
    peaks, sums, turned, beside, asks = refs[-5:]
    rows, width = keys[0].shape
    set_up(
        packs,
        lambda k: queries[k][...],
        lambda k: keys[k][...],
        lambda k: packs[k][rows : 2 * rows],
        turned,
        beside,
        asks,
    )
    ahead = product(asks[0], turned[...])
    for b in range(GROUP):
        scores = ahead
        if b + 1 < GROUP:
            ahead = product(asks[b + 1], turned[...])
        peak, mixed = attend([scores], [beside[...]])
        peaks[b] = by_head(jnp.broadcast_to(peak, (peak.shape[0], width)), rows)
        sums[b, 0] = by_head(mixed[:, :width], rows)
        sums[b, 1] = by_head(mixed[:, width:], rows)


def lend_kernel(edge_b, edge_a, plane_turned, plane_beside, first, second, turned, ordered, results):
    rows, width = ordered.shape[2] - ID_ROWS, ordered.shape[3]
    odd = lax.rem(plane(), 2)
    ordered[1 - odd] = edge_a[...]
    ordered[odd] = edge_b[...]
    lane = lax.broadcasted_iota(jnp.int32, (rows, width), 1)
    blocks = [slice(0, (j + 1) * rows) for j in range(RADIUS)]
    blocks += [slice((j + 1) * rows, GROUP * rows) for j in range(RADIUS)]

    def scores_of(e):
        side, j = e // RADIUS, e % RADIUS
        marks = marks_turned(ordered[side, j, rows:])
        query = ordered[side, j, :rows]
        for part, x in enumerate(marks):
            at = slice(e * rows + part * width, e * rows + (part + 1) * width)
            turned[:width, at] = jnp.transpose(query[part * width : (part + 1) * width])
            turned[width:, at] = x
        return product(stacked_ask(query, marks), plane_turned[:, blocks[e]])

    ahead = scores_of(0)
    for e in range(2 * RADIUS):
        side, j = e // RADIUS, e % RADIUS
        scores = ahead
        if e + 1 < 2 * RADIUS:
            ahead = scores_of(e + 1)
        peak, mixed = attend([scores], [plane_beside[blocks[e]]])
        total = by_head(mixed[:, width:], rows)
        results[side, j, :rows] = (by_head(mixed[:, :width], rows) / total).astype(results.dtype)
        logs = by_head(jnp.broadcast_to(peak, (peak.shape[0], width)), rows) + jnp.log(total)
        high = logs.astype(jnp.bfloat16).astype(jnp.float32)
        middle = (logs - high).astype(jnp.bfloat16).astype(jnp.float32)
        low = logs - high - middle
        picked = jnp.where(lane % HEAD == 0, high, jnp.where(lane % HEAD == 1, middle, low))
        for part in range(rows // width):
            flipped = jnp.transpose(picked[part * width : (part + 1) * width])
            stats = [flipped[h : h + STAT_ROWS // 2] for h in range(0, width, HEAD)]
            at = rows + part * STAT_ROWS
            results[side, j, at : at + STAT_ROWS] = jnp.concatenate(stats, axis=0).astype(
                results.dtype
            )
    first[...] = results[1 - odd]
    second[...] = results[odd]


def columns_kernel(receivers, *refs):
    refs = list(refs)
    take = lambda count: [refs.pop(0) for _ in range(count)]
    first = 0 not in receivers
    if first:
        packs, queries, keys, (edge_b, edge_a) = take(GROUP), take(GROUP), take(GROUP), take(2)
    (edge_turned,) = take(1)
    if not first:
        shared, _ = take(4), take(1)
    outs = take(len(receivers))
    turned, beside, asks, edge_beside = take(4) if first else shared
    rows, width = outs[0].shape
    mine = place()
    if first:
        odd = lax.rem(plane(), 2)
        set_up(
            packs,
            lambda k: keys[k][...],
            lambda k: queries[k][...],
            lambda k: packs[k][:rows],
            turned,
            beside,
            asks,
        )
        edge_beside[:, width:] = jnp.ones((edge_beside.shape[0], width), beside.dtype)
        for edge, base in ((edge_a, RADIUS * (1 - odd)), (edge_b, RADIUS * odd)):
            for j in range(RADIUS):
                at = pl.ds(pl.multiple_of((base + j) * rows, rows), rows)
                edge_beside[at, :width] = edge[j]
    near = [pl.ds(pl.multiple_of((mine ^ k) * rows, rows), RADIUS * rows) for k in receivers]

    def scores_of(n):
        ask = asks[mine ^ receivers[n]]
        return [product(ask, turned[...]), product(ask, edge_turned[:, near[n]])]

    ahead = scores_of(0)
    for n in range(len(receivers)):
        scores = ahead
        if n + 1 < len(receivers):
            ahead = scores_of(n + 1)
        _, mixed = attend(scores, [beside[...], edge_beside[near[n]]])
        mean = by_head(mixed[:, :width], rows) / by_head(mixed[:, width:], rows)
        outs[n][...] = mean.astype(outs[n].dtype)


def merge_kernel(back_a, back_b, peaks, sums, *refs):
    outs, (backs, whole) = refs[-GROUP - 2 : -2], refs[-2:]
    rows, width = outs[0].shape
    mine = place()
    odd = lax.rem(plane(), 2)
    backs[1 - odd] = back_a[...]
    backs[odd] = back_b[...]
    last = lax.axis_size("tm") // GROUP - 1
    absent = [jnp.where(plane() == end, NEG, 0.0) for end in (0, last)]

    def logs(side, j):
        squares = []
        for part in range(rows // width):
            at = rows + part * STAT_ROWS
            stats = backs[side, j, at : at + STAT_ROWS].astype(jnp.float32)
            heads = [
                stats[8 * h : 8 * h + 1] + stats[8 * h + 1 : 8 * h + 2] + stats[8 * h + 2 : 8 * h + 3]
                for h in range(width // HEAD)
            ]
            turned = jnp.transpose(
                jnp.concatenate([jnp.broadcast_to(x, (HEAD, width)) for x in heads], axis=0)
            )
            squares.append(turned)
        return jnp.concatenate(squares, axis=0) + absent[side]

    for b in range(GROUP):
        theirs = []
        if b < RADIUS:
            theirs.append((0, b))
        if b >= GROUP - RADIUS:
            theirs.append((1, b - (GROUP - RADIUS)))
        theirs = [(logs(*t), backs[t[0], t[1], :rows].astype(jnp.float32)) for t in theirs]
        old = peaks[b]
        top = old
        for log, _ in theirs:
            top = jnp.maximum(top, log)
        factor = jnp.exp(old - top)
        value = sums[b, 0] * factor
        total = sums[b, 1] * factor
        for log, mean in theirs:
            weight = jnp.exp(log - top)
            value += weight * mean
            total += weight
        whole[b] = (value / total).astype(whole.dtype)
    for k in range(GROUP):
        outs[k][...] = whole[mine ^ k]


def local(audio_frames, video_frames, recording, audio_query, video_key):
    rows, half = audio_frames.shape
    width = half // GROUP
    heads = width // HEAD
    length = lax.axis_size("tm")
    bf16, f32 = jnp.bfloat16, jnp.float32
    shape = jax.ShapeDtypeStruct
    assert length % (2 * GROUP) == 0

    def swapped(x):
        return lax.ppermute(x, "head", [(0, 1), (1, 0)])

    def traded(pieces):
        pairs = lambda k: [(i, i ^ k) for i in range(length)]
        return [pieces[0]] + [lax.ppermute(pieces[k], "tm", pairs(k)) for k in range(1, GROUP)]

    def crossed(sent, second):
        planes = range(second, length // GROUP - second)
        pairs = [(p, ((p + second) ^ 1) - second) for p in planes]
        return lax.ppermute(
            sent, "tm", [(p * GROUP + i, q * GROUP + i) for p, q in pairs for i in range(GROUP)]
        )

    part = shape((rows, half), f32)
    square = shape((half, half), bf16)
    piece = shape((rows, width), bf16)
    given = (audio_frames, video_frames, audio_query, video_key, recording.reshape(rows // width, width))
    audio_in, video_in, query_in, key_in, ids_in = (
        pltpu.with_memory_space_constraint(x, pltpu.HBM) for x in given
    )
    other_audio = swapped(audio_frames)
    other_video = swapped(video_frames)
    packs = call(
        split_kernel,
        [shape((2 * rows + ID_ROWS, width), bf16)] * GROUP,
        [pltpu.VMEM((rows // width, width), jnp.int32), pltpu.VMEM((ID_ROWS, width), f32)]
        + [pltpu.SemaphoreType.DMA((1 + 2 * GROUP,))],
        ins=[HBM] * 3,
        moved=8 * rows * half,
        name="split",
    )(audio_in, video_in, ids_in)
    packs = traded(packs)
    query_part, key_part, query_rest, key_rest = call(
        prepare_kernel,
        [part, part, square, square],
        [pltpu.VMEM((rows, half), bf16)] * 2
        + [pltpu.VMEM((half, half), bf16)] * 2
        + [pltpu.SemaphoreType.DMA((6,))],
        ins=[HBM] * 4 + [ANY],
        flops=4 * rows * half * half,
        moved=16 * half * half,
        name="prepare",
    )(audio_in, video_in, query_in, key_in, packs[1])

    def project(scale, *operands, after=()):
        return call(
            functools.partial(project_kernel, scale),
            [piece] * GROUP,
            [pltpu.VMEM((rows, half), bf16)],
            ins=[VMEM] * 3 + [ANY] * len(after),
            flops=2 * rows * half * half,
            moved=2 * half * half + 6 * rows * half * 2,
            name="project",
        )(*operands, *after)

    def halo(pieces, id_packs, *after):
        edge = shape((RADIUS, rows + (ID_ROWS if id_packs else 0), width), bf16)
        sent = call(
            functools.partial(halo_kernel, 2 * rows if id_packs else 0),
            [edge, edge],
            ins=[VMEM] * (GROUP + len(id_packs)) + [ANY] * len(after),
            moved=10 * rows * width * 2,
            name="halo",
        )(*pieces, *id_packs, *after)
        return [crossed(sent[i], i) for i in range(2)]

    queries = traded(project(HEAD**-0.5, query_part, other_audio, query_rest, after=packs[1:3]))
    keys = project(1.0, key_part, other_video, key_rest, after=())
    query_edges = halo(queries, packs, keys[0])
    keys = traded(keys)

    inside, around = GROUP * rows, 2 * RADIUS * rows
    turned, beside = shape((2 * width, inside), bf16), shape((inside, 2 * width), bf16)
    asks = shape((GROUP, heads * rows, 2 * width), bf16)
    peaks, sums, plane_turned, plane_beside = call(
        rows_kernel,
        [shape((GROUP, rows, width), f32), shape((GROUP, 2, rows, width), f32), turned, beside],
        [pltpu.VMEM(asks.shape, bf16)],
        flops=16 * GROUP * rows * inside * width,
        moved=8 * inside * width * 2,
        exps=2 * GROUP * rows * inside,
        name="rows",
    )(*packs, *queries, *keys)
    audio_edges = halo(packs, [])
    back = shape((RADIUS, rows + rows // width * STAT_ROWS, width), bf16)
    lent_a, lent_b, edge_turned = call(
        lend_kernel,
        [back, back, shape((2 * width, around), bf16)],
        [pltpu.VMEM((2, RADIUS, rows + ID_ROWS, width), bf16), pltpu.VMEM((2,) + back.shape, bf16)],
        flops=48 * RADIUS * GROUP * rows * rows * width,
        moved=8 * around * width * 2,
        exps=2 * RADIUS * GROUP * rows * rows,
        name="lend",
    )(*query_edges[::-1], plane_turned, plane_beside)
    backs = [crossed(x, i) for i, x in enumerate((lent_a, lent_b))]

    half_columns = dict(
        flops=56 * GROUP * rows * rows * width,
        moved=4 * around * width * 2,
        exps=7 * GROUP * rows * rows,
        name="columns",
    )
    shared = [turned, beside, asks, shape((around, 2 * width), bf16)]
    near, far = range(GROUP // 2), range(GROUP // 2, GROUP)
    *far_pieces, turned, beside, asks, edge_beside = call(
        functools.partial(columns_kernel, far), [piece] * len(far) + shared, **half_columns
    )(*packs, *queries, *keys, *audio_edges[::-1], edge_turned)
    audio_pieces = call(
        merge_kernel,
        [piece] * GROUP,
        [pltpu.VMEM((2,) + back.shape, bf16), pltpu.VMEM((GROUP, rows, width), bf16)],
        moved=16 * inside * width,
        exps=4 * inside * width,
        ins=[VMEM] * 4 + [ANY],
        name="merge",
    )(*backs, peaks, sums, far_pieces[0])
    audio_pieces = traded(audio_pieces)
    near_pieces = call(
        functools.partial(columns_kernel, near),
        [piece] * len(near),
        ins=[VMEM] * 5 + [ANY],
        **half_columns,
    )(edge_turned, turned, beside, asks, edge_beside, audio_pieces[0])
    video_pieces = traded([*near_pieces, *far_pieces])

    def join(pieces):
        return call(
            join_kernel,
            shape((rows, half), bf16),
            [pltpu.SemaphoreType.DMA((GROUP,))],
            outs_in=HBM,
            moved=2 * rows * half * 2,
            name="join",
        )(*pieces)

    video_attended = join(video_pieces)
    audio_attended = join(audio_pieces)
    return (audio_attended, video_attended)


def solution(mesh):
    return jax.shard_map(
        local,
        mesh=mesh,
        in_specs=(P("tm", "head"), P("tm", "head"), P("tm"), P(None, "head"), P(None, "head")),
        out_specs=(P("tm", "head"), P("tm", "head")),
        check_vma=False,
    )
```

```python
import functools

import jax
import jax.numpy as jnp
from jax import lax
from jax.experimental import pallas as pl
from jax.experimental.pallas import tpu as pltpu
from jax.sharding import PartitionSpec as P

HEAD = 64
RADIUS = 3
GROUP = 4
NEG = -1e30
ID_ROWS = 16
STAT_ROWS = 16

VMEM = pl.BlockSpec(memory_space=pltpu.VMEM)
ANY = pl.BlockSpec(memory_space=pl.ANY)
HBM = pl.BlockSpec(memory_space=pltpu.HBM)


def place():
    return lax.rem(lax.axis_index("tm"), GROUP)


def plane():
    return lax.axis_index("tm") // GROUP


def call(kernel, outs, scratch=(), ins=None, outs_in=None, flops=0, moved=0, exps=0, name=None):
    return pl.pallas_call(
        kernel,
        out_shape=outs,
        **({"in_specs": ins} if ins else {}),
        **({"out_specs": outs_in} if outs_in else {}),
        scratch_shapes=scratch,
        compiler_params=pltpu.CompilerParams(vmem_limit_bytes=32 * 2**20),
        cost_estimate=pl.CostEstimate(flops=flops, bytes_accessed=moved, transcendentals=exps),
        name=name,
    )


def product(a, b):
    return jnp.dot(a, b, preferred_element_type=jnp.float32)


def fetcher(sems):
    copies = []

    def fetch(source, target):
        copies.append(pltpu.make_async_copy(source, target, sems.at[len(copies)]))
        copies[-1].start()

    return copies, fetch


def split_kernel(audio, video, ids, *refs):
    packs, (ids_in, ids_wide, sems) = refs[:GROUP], refs[GROUP:]
    rows, width = audio.shape[0], packs[0].shape[1]
    mine = place()
    copies, fetch = fetcher(sems)
    fetch(ids, ids_in)
    for k in range(GROUP):
        at = pl.ds(pl.multiple_of((mine ^ k) * width, width), width)
        for i, stream in enumerate((audio, video)):
            fetch(stream.at[:, at], packs[k].at[i * rows : (i + 1) * rows])
    copies[0].wait()
    ids_wide[...] = jnp.zeros_like(ids_wide)
    ids_wide[: ids_in.shape[0]] = (ids_in[...] + 1).astype(jnp.float32)
    for k in range(GROUP):
        packs[k][2 * rows :] = ids_wide[...].astype(packs[k].dtype)
    for copy in copies[1:]:
        copy.wait()


def prepare_kernel(audio, video, query, key, *refs):
    sums, seconds, streams, firsts, sems = refs[-9:-7], refs[-7:-5], refs[-5:-3], refs[-3:-1], refs[-1]
    half = audio.shape[1]
    side = lax.axis_index("head")
    ours = pl.ds(pl.multiple_of(side * half, half), half)
    theirs = pl.ds(pl.multiple_of((1 - side) * half, half), half)
    copies, fetch = fetcher(sems)
    for i, (stream, weight) in enumerate(((audio, query), (video, key))):
        fetch(stream, streams[i])
        fetch(weight.at[ours], firsts[i])
    for i, weight in enumerate((query, key)):
        fetch(weight.at[theirs], seconds[i])
    for i in range(2):
        copies[2 * i].wait()
        copies[2 * i + 1].wait()
        sums[i][...] = product(streams[i][...], firsts[i][...])
    for copy in copies[4:]:
        copy.wait()


def project_kernel(scale, part, other, weight, *refs):
    pieces, full = refs[-GROUP - 1 : -1], refs[-1]
    width = pieces[0].shape[1]
    mine = place()
    full[...] = (part[...] + product(other[...], weight[...])).astype(jnp.bfloat16) * jnp.bfloat16(scale)
    for k in range(GROUP):
        pieces[k][...] = full[:, pl.ds(pl.multiple_of((mine ^ k) * width, width), width)]


def halo_kernel(second, ids_at, *refs):
    pieces, id_packs, out = refs[:GROUP], refs[GROUP : 2 * GROUP], refs[-1]
    rows = out.shape[1] - (ID_ROWS if ids_at else 0)
    mine = place()
    skip = (GROUP - RADIUS) * lax.rem(plane() + 1 + second, 2)
    for k in range(GROUP):
        spot = (mine ^ k) - skip

        @pl.when((spot >= 0) & (spot < RADIUS))
        def _():
            out[spot, :rows] = pieces[k][:rows]
            if ids_at:
                out[spot, rows:] = id_packs[k][ids_at:]


def join_kernel(*refs):
    pieces, out, sems = refs[:GROUP], refs[GROUP], refs[GROUP + 1]
    width = pieces[0].shape[1]
    mine = place()
    copies, fetch = fetcher(sems)
    for k in range(GROUP):
        fetch(pieces[k], out.at[:, pl.ds(pl.multiple_of((mine ^ k) * width, width), width)])
    for copy in copies:
        copy.wait()


def marks_turned(lanes):
    lanes = lanes.astype(jnp.float32)
    width = lanes.shape[1]
    row = lax.broadcasted_iota(jnp.int32, (width, width), 0).astype(jnp.float32)
    return [
        jnp.where(row == lanes[part : part + 1], 1.0, 0.0).astype(jnp.bfloat16) for part in range(2)
    ]


def stacked_ask(block, turned):
    head = lax.broadcasted_iota(jnp.int32, block.shape, 1) // HEAD
    marks = jnp.concatenate([jnp.transpose(x) for x in turned], axis=0)
    beside = (marks - jnp.bfloat16(1.0)) * jnp.bfloat16(-NEG)
    return jnp.concatenate(
        [
            jnp.concatenate([jnp.where(head == h, block, jnp.zeros_like(block)), beside], axis=1)
            for h in range(block.shape[1] // HEAD)
        ],
        axis=0,
    )


def by_head(stacked, rows):
    out = stacked[:rows]
    head = lax.broadcasted_iota(jnp.int32, out.shape, 1) // HEAD
    for h in range(1, stacked.shape[0] // rows):
        out = jnp.where(head == h, stacked[h * rows : (h + 1) * rows], out)
    return out


def attend(scores, values):
    top = None
    for s in scores:
        for at in range(0, s.shape[1], values[0].shape[1] // 2):
            part = s[:, at : at + values[0].shape[1] // 2]
            top = part if top is None else jnp.maximum(top, part)
    peak = jnp.max(top, axis=1, keepdims=True)
    mixed = None
    for s, value in zip(scores, values):
        part = product(jnp.exp(s - peak).astype(jnp.bfloat16), value)
        mixed = part if mixed is None else mixed + part
    return peak, mixed


def set_up(packs, asked, keys, values, turned, beside, asks):
    rows, width = asks.shape[1] // 2, asks.shape[2] // 2
    mine = place()
    beside[:, width:] = jnp.ones((GROUP * rows, width), beside.dtype)
    for k in range(GROUP):
        b = mine ^ k

        def spot(at, size):
            return pl.ds(pl.multiple_of(b * rows + at, size), size)

        marks = marks_turned(packs[k][2 * rows :])
        asks[b] = stacked_ask(asked(k), marks)
        beside[spot(0, rows), :width] = values(k)
        key = keys(k)
        for part, x in enumerate(marks):
            at = spot(part * width, width)
            turned[:width, at] = jnp.transpose(key[part * width : (part + 1) * width])
            turned[width:, at] = x


def rows_kernel(*refs):
    packs, queries, keys = refs[:GROUP], refs[GROUP : 2 * GROUP], refs[2 * GROUP : 3 * GROUP]
    peaks, sums, turned, beside, asks = refs[-5:]
    rows, width = keys[0].shape
    set_up(
        packs,
        lambda k: queries[k][...],
        lambda k: keys[k][...],
        lambda k: packs[k][rows : 2 * rows],
        turned,
        beside,
        asks,
    )
    ahead = product(asks[0], turned[...])
    for b in range(GROUP):
        scores = ahead
        if b + 1 < GROUP:
            ahead = product(asks[b + 1], turned[...])
        peak, mixed = attend([scores], [beside[...]])
        peaks[b] = by_head(jnp.broadcast_to(peak, (peak.shape[0], width)), rows)
        sums[b, 0] = by_head(mixed[:, :width], rows)
        sums[b, 1] = by_head(mixed[:, width:], rows)


def lend_kernel(second, edge, plane_turned, plane_beside, *refs):
    result = refs[-1]
    if second:
        last = lax.axis_size("tm") // GROUP - 1

        @pl.when((plane() > 0) & (plane() < last))
        def _():
            lend(second, edge, plane_turned, plane_beside, result)

    else:
        refs[1][...] = refs[0][...]
        lend(second, edge, plane_turned, plane_beside, result)


def lend(second, edge, plane_turned, plane_beside, result):
    rows, width = edge.shape[1] - ID_ROWS, edge.shape[2]
    above = lax.rem(plane() + 1 + second, 2)
    lane = lax.broadcasted_iota(jnp.int32, (rows, width), 1)

    def block_of(n):
        return n + above * (RADIUS - 1 - 2 * n)

    def near(n):
        return pl.ds(pl.multiple_of(above * (GROUP - 1 - n) * rows, rows), (n + 1) * rows)

    def scores_of(n):
        j = block_of(n)
        ask = stacked_ask(edge[j, :rows], marks_turned(edge[j, rows:]))
        return product(ask, plane_turned[:, near(n)])

    ahead = scores_of(0)
    for n in range(RADIUS):
        j = block_of(n)
        scores = ahead
        if n + 1 < RADIUS:
            ahead = scores_of(n + 1)
        peak, mixed = attend([scores], [plane_beside[near(n)]])
        total = by_head(mixed[:, width:], rows)
        result[j, :rows] = (by_head(mixed[:, :width], rows) / total).astype(result.dtype)
        logs = by_head(jnp.broadcast_to(peak, (peak.shape[0], width)), rows) + jnp.log(total)
        high = logs.astype(jnp.bfloat16).astype(jnp.float32)
        middle = (logs - high).astype(jnp.bfloat16).astype(jnp.float32)
        low = logs - high - middle
        picked = jnp.where(lane % HEAD == 0, high, jnp.where(lane % HEAD == 1, middle, low))
        for part in range(rows // width):
            flipped = jnp.transpose(picked[part * width : (part + 1) * width])
            stats = [flipped[h : h + STAT_ROWS // 2] for h in range(0, width, HEAD)]
            at = rows + part * STAT_ROWS
            result[j, at : at + STAT_ROWS] = jnp.concatenate(stats, axis=0).astype(
                result.dtype
            )


def columns_kernel(receivers, *refs):
    refs = list(refs)
    take = lambda count: [refs.pop(0) for _ in range(count)]
    first = 0 not in receivers
    if first:
        packs, queries, keys = take(GROUP), take(GROUP), take(GROUP)
        (ask_b, ask_a), (edge_b, edge_a) = take(2), take(2)
    else:
        shared, _ = take(5), take(1)
    outs = take(len(receivers))
    turned, beside, asks, edge_beside, edge_turned = take(5) if first else shared
    rows, width = outs[0].shape
    mine = place()
    if first:
        odd = lax.rem(plane(), 2)
        set_up(
            packs,
            lambda k: keys[k][...],
            lambda k: queries[k][...],
            lambda k: packs[k][:rows],
            turned,
            beside,
            asks,
        )
        edge_beside[:, width:] = jnp.ones((edge_beside.shape[0], width), beside.dtype)
        for ask, edge, base in ((ask_a, edge_a, RADIUS * (1 - odd)), (ask_b, edge_b, RADIUS * odd)):
            for j in range(RADIUS):

                def spot(at, size):
                    return pl.ds(pl.multiple_of((base + j) * rows + at, size), size)

                edge_beside[spot(0, rows), :width] = edge[j]
                for part, x in enumerate(marks_turned(ask[j, rows:])):
                    at = spot(part * width, width)
                    edge_turned[:width, at] = jnp.transpose(
                        ask[j, part * width : (part + 1) * width]
                    )
                    edge_turned[width:, at] = x
    near = [pl.ds(pl.multiple_of((mine ^ k) * rows, rows), RADIUS * rows) for k in receivers]

    def scores_of(n):
        ask = asks[mine ^ receivers[n]]
        return [product(ask, turned[...]), product(ask, edge_turned[:, near[n]])]

    ahead = scores_of(0)
    for n in range(len(receivers)):
        scores = ahead
        if n + 1 < len(receivers):
            ahead = scores_of(n + 1)
        _, mixed = attend(scores, [beside[...], edge_beside[near[n]]])
        mean = by_head(mixed[:, :width], rows) / by_head(mixed[:, width:], rows)
        outs[n][...] = mean.astype(outs[n].dtype)


def merge_kernel(back_a, back_b, peaks, sums, *refs):
    outs, (backs, whole) = refs[-GROUP - 2 : -2], refs[-2:]
    rows, width = outs[0].shape
    mine = place()
    odd = lax.rem(plane(), 2)
    backs[1 - odd] = back_a[...]
    backs[odd] = back_b[...]
    last = lax.axis_size("tm") // GROUP - 1
    absent = [jnp.where(plane() == end, NEG, 0.0) for end in (0, last)]

    def logs(side, j):
        squares = []
        for part in range(rows // width):
            at = rows + part * STAT_ROWS
            stats = backs[side, j, at : at + STAT_ROWS].astype(jnp.float32)
            heads = [
                stats[8 * h : 8 * h + 1] + stats[8 * h + 1 : 8 * h + 2] + stats[8 * h + 2 : 8 * h + 3]
                for h in range(width // HEAD)
            ]
            turned = jnp.transpose(
                jnp.concatenate([jnp.broadcast_to(x, (HEAD, width)) for x in heads], axis=0)
            )
            squares.append(turned)
        return jnp.concatenate(squares, axis=0) + absent[side]

    for b in range(GROUP):
        theirs = []
        if b < RADIUS:
            theirs.append((0, b))
        if b >= GROUP - RADIUS:
            theirs.append((1, b - (GROUP - RADIUS)))
        theirs = [(logs(*t), backs[t[0], t[1], :rows].astype(jnp.float32)) for t in theirs]
        old = peaks[b]
        top = old
        for log, _ in theirs:
            top = jnp.maximum(top, log)
        factor = jnp.exp(old - top)
        value = sums[b, 0] * factor
        total = sums[b, 1] * factor
        for log, mean in theirs:
            weight = jnp.exp(log - top)
            value += weight * mean
            total += weight
        whole[b] = (value / total).astype(whole.dtype)
    for k in range(GROUP):
        outs[k][...] = whole[mine ^ k]


def local(audio_frames, video_frames, recording, audio_query, video_key):
    rows, half = audio_frames.shape
    width = half // GROUP
    heads = width // HEAD
    length = lax.axis_size("tm")
    bf16, f32 = jnp.bfloat16, jnp.float32
    shape = jax.ShapeDtypeStruct
    assert length % (2 * GROUP) == 0

    def swapped(x):
        return lax.ppermute(x, "head", [(0, 1), (1, 0)])

    def traded(pieces):
        pairs = lambda k: [(i, i ^ k) for i in range(length)]
        return [pieces[0]] + [lax.ppermute(pieces[k], "tm", pairs(k)) for k in range(1, GROUP)]

    def crossed(sent, second):
        planes = range(second, length // GROUP - second)
        pairs = [(p, ((p + second) ^ 1) - second) for p in planes]
        return lax.ppermute(
            sent, "tm", [(p * GROUP + i, q * GROUP + i) for p, q in pairs for i in range(GROUP)]
        )

    part = shape((rows, half), f32)
    square = shape((half, half), bf16)
    piece = shape((rows, width), bf16)
    given = (audio_frames, video_frames, audio_query, video_key, recording.reshape(rows // width, width))
    audio_in, video_in, query_in, key_in, ids_in = (
        pltpu.with_memory_space_constraint(x, pltpu.HBM) for x in given
    )
    other_audio = swapped(audio_frames)
    other_video = swapped(video_frames)
    packs = call(
        split_kernel,
        [shape((2 * rows + ID_ROWS, width), bf16)] * GROUP,
        [pltpu.VMEM((rows // width, width), jnp.int32), pltpu.VMEM((ID_ROWS, width), f32)]
        + [pltpu.SemaphoreType.DMA((1 + 2 * GROUP,))],
        ins=[HBM] * 3,
        moved=8 * rows * half,
        name="split",
    )(audio_in, video_in, ids_in)
    packs = traded(packs)
    query_part, key_part, query_rest, key_rest = call(
        prepare_kernel,
        [part, part, square, square],
        [pltpu.VMEM((rows, half), bf16)] * 2
        + [pltpu.VMEM((half, half), bf16)] * 2
        + [pltpu.SemaphoreType.DMA((6,))],
        ins=[HBM] * 4 + [ANY],
        flops=4 * rows * half * half,
        moved=16 * half * half,
        name="prepare",
    )(audio_in, video_in, query_in, key_in, packs[1])

    def project(scale, *operands, after=()):
        return call(
            functools.partial(project_kernel, scale),
            [piece] * GROUP,
            [pltpu.VMEM((rows, half), bf16)],
            ins=[VMEM] * 3 + [ANY] * len(after),
            flops=2 * rows * half * half,
            moved=2 * half * half + 6 * rows * half * 2,
            name="project",
        )(*operands, *after)

    def halo(second, pieces, id_packs, *after):
        sent = call(
            functools.partial(halo_kernel, second, 2 * rows if id_packs else 0),
            shape((RADIUS, rows + (ID_ROWS if id_packs else 0), width), bf16),
            ins=[VMEM] * (GROUP + len(id_packs)) + [ANY] * len(after),
            moved=5 * rows * width * 2,
            name="halo",
        )(*pieces, *id_packs, *after)
        return crossed(sent, second)

    queries = traded(project(HEAD**-0.5, query_part, other_audio, query_rest, after=packs[1:3]))
    keys = project(1.0, key_part, other_video, key_rest, after=())
    query_edges = [halo(i, queries, packs, keys[0]) for i in range(2)]
    keys = traded(keys)

    inside, around = GROUP * rows, 2 * RADIUS * rows
    turned, beside = shape((2 * width, inside), bf16), shape((inside, 2 * width), bf16)
    asks = shape((GROUP, heads * rows, 2 * width), bf16)
    peaks, sums, plane_turned, plane_beside = call(
        rows_kernel,
        [shape((GROUP, rows, width), f32), shape((GROUP, 2, rows, width), f32), turned, beside],
        [pltpu.VMEM(asks.shape, bf16)],
        flops=16 * GROUP * rows * inside * width,
        moved=8 * inside * width * 2,
        exps=2 * GROUP * rows * inside,
        name="rows",
    )(*packs, *queries, *keys)
    audio_edges = [halo(0, packs, [], query_edges[1]), halo(1, packs, [])]
    back = shape((RADIUS, rows + rows // width * STAT_ROWS, width), bf16)
    lending = dict(
        flops=24 * RADIUS * GROUP * rows * rows * width,
        moved=4 * around * width * 2,
        exps=RADIUS * GROUP * rows * rows,
        name="lend",
    )
    lent_b = call(functools.partial(lend_kernel, 1), back, **lending)(
        query_edges[1], plane_turned, plane_beside
    )
    lent_b, lent_a = call(functools.partial(lend_kernel, 0), [back, back], **lending)(
        query_edges[0], plane_turned, plane_beside, lent_b
    )
    backs = [crossed(x, i) for i, x in enumerate((lent_a, lent_b))]

    half_columns = dict(
        flops=56 * GROUP * rows * rows * width,
        moved=4 * around * width * 2,
        exps=7 * GROUP * rows * rows,
        name="columns",
    )
    shared = [turned, beside, asks, shape((around, 2 * width), bf16), shape((2 * width, around), bf16)]
    near, far = range(GROUP // 2), range(GROUP // 2, GROUP)
    *far_pieces, turned, beside, asks, edge_beside, edge_turned = call(
        functools.partial(columns_kernel, far), [piece] * len(far) + shared, **half_columns
    )(*packs, *queries, *keys, *query_edges[::-1], *audio_edges[::-1])
    audio_pieces = call(
        merge_kernel,
        [piece] * GROUP,
        [pltpu.VMEM((2,) + back.shape, bf16), pltpu.VMEM((GROUP, rows, width), bf16)],
        moved=16 * inside * width,
        exps=4 * inside * width,
        ins=[VMEM] * 4 + [ANY],
        name="merge",
    )(*backs, peaks, sums, far_pieces[0])
    audio_pieces = traded(audio_pieces)
    near_pieces = call(
        functools.partial(columns_kernel, near),
        [piece] * len(near),
        ins=[VMEM] * 5 + [ANY],
        **half_columns,
    )(turned, beside, asks, edge_beside, edge_turned, audio_pieces[0])
    video_pieces = traded([*near_pieces, *far_pieces])

    def join(pieces):
        return call(
            join_kernel,
            shape((rows, half), bf16),
            [pltpu.SemaphoreType.DMA((GROUP,))],
            outs_in=HBM,
            moved=2 * rows * half * 2,
            name="join",
        )(*pieces)

    video_attended = join(video_pieces)
    audio_attended = join(audio_pieces)
    return (audio_attended, video_attended)


def solution(mesh):
    return jax.shard_map(
        local,
        mesh=mesh,
        in_specs=(P("tm", "head"), P("tm", "head"), P("tm"), P(None, "head"), P(None, "head")),
        out_specs=(P("tm", "head"), P("tm", "head")),
        check_vma=False,
    )
```

```python
import functools

import jax
import jax.numpy as jnp
from jax import lax
from jax.experimental import pallas as pl
from jax.experimental.pallas import tpu as pltpu
from jax.sharding import PartitionSpec as P

HEAD = 64
RADIUS = 3
GROUP = 4
NEG = -1e30
ID_ROWS = 16
STAT_ROWS = 16

VMEM = pl.BlockSpec(memory_space=pltpu.VMEM)
ANY = pl.BlockSpec(memory_space=pl.ANY)
HBM = pl.BlockSpec(memory_space=pltpu.HBM)


def place():
    return lax.rem(lax.axis_index("tm"), GROUP)


def plane():
    return lax.axis_index("tm") // GROUP


def call(kernel, outs, scratch=(), ins=None, outs_in=None, flops=0, moved=0, exps=0, name=None):
    return pl.pallas_call(
        kernel,
        out_shape=outs,
        **({"in_specs": ins} if ins else {}),
        **({"out_specs": outs_in} if outs_in else {}),
        scratch_shapes=scratch,
        compiler_params=pltpu.CompilerParams(vmem_limit_bytes=32 * 2**20),
        cost_estimate=pl.CostEstimate(flops=flops, bytes_accessed=moved, transcendentals=exps),
        name=name,
    )


def product(a, b):
    return jnp.dot(a, b, preferred_element_type=jnp.float32)


def fetcher(sems):
    copies = []

    def fetch(source, target):
        copies.append(pltpu.make_async_copy(source, target, sems.at[len(copies)]))
        copies[-1].start()

    return copies, fetch


def split_kernel(audio, video, ids, *refs):
    packs, (ids_in, ids_wide, sems) = refs[:GROUP], refs[GROUP:]
    rows, width = audio.shape[0], packs[0].shape[1]
    mine = place()
    copies, fetch = fetcher(sems)
    fetch(ids, ids_in)
    for k in range(GROUP):
        at = pl.ds(pl.multiple_of((mine ^ k) * width, width), width)
        for i, stream in enumerate((audio, video)):
            fetch(stream.at[:, at], packs[k].at[i * rows : (i + 1) * rows])
    copies[0].wait()
    ids_wide[...] = jnp.zeros_like(ids_wide)
    ids_wide[: ids_in.shape[0]] = (ids_in[...] + 1).astype(jnp.float32)
    for k in range(GROUP):
        packs[k][2 * rows :] = ids_wide[...].astype(packs[k].dtype)
    for copy in copies[1:]:
        copy.wait()


def prepare_kernel(audio, video, query, key, *refs):
    sums, seconds, streams, firsts, sems = refs[-9:-7], refs[-7:-5], refs[-5:-3], refs[-3:-1], refs[-1]
    half = audio.shape[1]
    side = lax.axis_index("head")
    ours = pl.ds(pl.multiple_of(side * half, half), half)
    theirs = pl.ds(pl.multiple_of((1 - side) * half, half), half)
    copies, fetch = fetcher(sems)
    for i, (stream, weight) in enumerate(((audio, query), (video, key))):
        fetch(stream, streams[i])
        fetch(weight.at[ours], firsts[i])
    for i, weight in enumerate((query, key)):
        fetch(weight.at[theirs], seconds[i])
    for i in range(2):
        copies[2 * i].wait()
        copies[2 * i + 1].wait()
        sums[i][...] = product(streams[i][...], firsts[i][...])
    for copy in copies[4:]:
        copy.wait()


def project_kernel(scale, part, other, weight, *refs):
    pieces, full = refs[-GROUP - 1 : -1], refs[-1]
    width = pieces[0].shape[1]
    mine = place()
    full[...] = (part[...] + product(other[...], weight[...])).astype(jnp.bfloat16) * jnp.bfloat16(scale)
    for k in range(GROUP):
        pieces[k][...] = full[:, pl.ds(pl.multiple_of((mine ^ k) * width, width), width)]


def halo_kernel(ids_at, *refs):
    pieces, id_packs, outs = refs[:GROUP], refs[GROUP : 2 * GROUP], refs[-2:]
    rows = outs[0].shape[1] - (ID_ROWS if ids_at else 0)
    mine = place()
    odd = lax.rem(plane(), 2)
    for k in range(GROUP):
        block = mine ^ k
        for out, skip in zip(outs, ((GROUP - RADIUS) * (1 - odd), (GROUP - RADIUS) * odd)):
            spot = block - skip

            @pl.when((spot >= 0) & (spot < RADIUS))
            def _():
                out[spot, :rows] = pieces[k][:rows]
                if ids_at:
                    out[spot, rows:] = id_packs[k][ids_at:]


def join_kernel(*refs):
    pieces, out, sems = refs[:GROUP], refs[GROUP], refs[GROUP + 1]
    width = pieces[0].shape[1]
    mine = place()
    copies, fetch = fetcher(sems)
    for k in range(GROUP):
        fetch(pieces[k], out.at[:, pl.ds(pl.multiple_of((mine ^ k) * width, width), width)])
    for copy in copies:
        copy.wait()


def marks_turned(lanes):
    lanes = lanes.astype(jnp.float32)
    width = lanes.shape[1]
    row = lax.broadcasted_iota(jnp.int32, (width, width), 0).astype(jnp.float32)
    return [
        jnp.where(row == lanes[part : part + 1], 1.0, 0.0).astype(jnp.bfloat16) for part in range(2)
    ]


def stacked_ask(block, turned):
    head = lax.broadcasted_iota(jnp.int32, block.shape, 1) // HEAD
    marks = jnp.concatenate([jnp.transpose(x) for x in turned], axis=0)
    beside = (marks - jnp.bfloat16(1.0)) * jnp.bfloat16(-NEG)
    return jnp.concatenate(
        [
            jnp.concatenate([jnp.where(head == h, block, jnp.zeros_like(block)), beside], axis=1)
            for h in range(block.shape[1] // HEAD)
        ],
        axis=0,
    )


def by_head(stacked, rows):
    out = stacked[:rows]
    head = lax.broadcasted_iota(jnp.int32, out.shape, 1) // HEAD
    for h in range(1, stacked.shape[0] // rows):
        out = jnp.where(head == h, stacked[h * rows : (h + 1) * rows], out)
    return out


def attend(scores, values):
    top = None
    for s in scores:
        for at in range(0, s.shape[1], values[0].shape[1] // 2):
            part = s[:, at : at + values[0].shape[1] // 2]
            top = part if top is None else jnp.maximum(top, part)
    peak = jnp.max(top, axis=1, keepdims=True)
    mixed = None
    for s, value in zip(scores, values):
        part = product(jnp.exp(s - peak).astype(jnp.bfloat16), value)
        mixed = part if mixed is None else mixed + part
    return peak, mixed


def set_up(packs, asked, keys, values, turned, beside, asks):
    rows, width = asks.shape[1] // 2, asks.shape[2] // 2
    mine = place()
    beside[:, width:] = jnp.ones((GROUP * rows, width), beside.dtype)
    for k in range(GROUP):
        b = mine ^ k

        def spot(at, size):
            return pl.ds(pl.multiple_of(b * rows + at, size), size)

        marks = marks_turned(packs[k][2 * rows :])
        asks[b] = stacked_ask(asked(k), marks)
        beside[spot(0, rows), :width] = values(k)
        key = keys(k)
        for part, x in enumerate(marks):
            at = spot(part * width, width)
            turned[:width, at] = jnp.transpose(key[part * width : (part + 1) * width])
            turned[width:, at] = x


def rows_kernel(*refs):
    packs, queries, keys = refs[:GROUP], refs[GROUP : 2 * GROUP], refs[2 * GROUP : 3 * GROUP]
    peaks, sums, turned, beside, asks = refs[-5:]
    rows, width = keys[0].shape
    set_up(
        packs,
        lambda k: queries[k][...],
        lambda k: keys[k][...],
        lambda k: packs[k][rows : 2 * rows],
        turned,
        beside,
        asks,
    )
    ahead = product(asks[0], turned[...])
    for b in range(GROUP):
        scores = ahead
        if b + 1 < GROUP:
            ahead = product(asks[b + 1], turned[...])
        peak, mixed = attend([scores], [beside[...]])
        peaks[b] = by_head(jnp.broadcast_to(peak, (peak.shape[0], width)), rows)
        sums[b, 0] = by_head(mixed[:, :width], rows)
        sums[b, 1] = by_head(mixed[:, width:], rows)


def lend_kernel(edge_b, edge_a, plane_turned, plane_beside, first, second, turned, ordered, results):
    rows, width = ordered.shape[2] - ID_ROWS, ordered.shape[3]
    odd = lax.rem(plane(), 2)
    ordered[1 - odd] = edge_a[...]
    ordered[odd] = edge_b[...]
    lane = lax.broadcasted_iota(jnp.int32, (rows, width), 1)
    blocks = [slice(0, (j + 1) * rows) for j in range(RADIUS)]
    blocks += [slice((j + 1) * rows, GROUP * rows) for j in range(RADIUS)]

    def scores_of(e):
        side, j = e // RADIUS, e % RADIUS
        marks = marks_turned(ordered[side, j, rows:])
        query = ordered[side, j, :rows]
        for part, x in enumerate(marks):
            at = slice(e * rows + part * width, e * rows + (part + 1) * width)
            turned[:width, at] = jnp.transpose(query[part * width : (part + 1) * width])
            turned[width:, at] = x
        return product(stacked_ask(query, marks), plane_turned[:, blocks[e]])

    ahead = scores_of(0)
    for e in range(2 * RADIUS):
        side, j = e // RADIUS, e % RADIUS
        scores = ahead
        if e + 1 < 2 * RADIUS:
            ahead = scores_of(e + 1)
        peak, mixed = attend([scores], [plane_beside[blocks[e]]])
        total = by_head(mixed[:, width:], rows)
        results[side, j, :rows] = (by_head(mixed[:, :width], rows) / total).astype(results.dtype)
        logs = by_head(jnp.broadcast_to(peak, (peak.shape[0], width)), rows) + jnp.log(total)
        high = logs.astype(jnp.bfloat16).astype(jnp.float32)
        middle = (logs - high).astype(jnp.bfloat16).astype(jnp.float32)
        low = logs - high - middle
        picked = jnp.where(lane % HEAD == 0, high, jnp.where(lane % HEAD == 1, middle, low))
        for part in range(rows // width):
            flipped = jnp.transpose(picked[part * width : (part + 1) * width])
            stats = [flipped[h : h + STAT_ROWS // 2] for h in range(0, width, HEAD)]
            at = rows + part * STAT_ROWS
            results[side, j, at : at + STAT_ROWS] = jnp.concatenate(stats, axis=0).astype(
                results.dtype
            )
    first[...] = results[1 - odd]
    second[...] = results[odd]


def columns_kernel(receivers, *refs):
    refs = list(refs)
    take = lambda count: [refs.pop(0) for _ in range(count)]
    first = 0 not in receivers
    if first:
        packs, queries, keys, (edge_b, edge_a) = take(GROUP), take(GROUP), take(GROUP), take(2)
    (edge_turned,) = take(1)
    if not first:
        shared, _ = take(4), take(1)
    outs = take(len(receivers))
    turned, beside, asks, edge_beside = take(4) if first else shared
    rows, width = outs[0].shape
    mine = place()
    if first:
        odd = lax.rem(plane(), 2)
        set_up(
            packs,
            lambda k: keys[k][...],
            lambda k: queries[k][...],
            lambda k: packs[k][:rows],
            turned,
            beside,
            asks,
        )
        edge_beside[:, width:] = jnp.ones((edge_beside.shape[0], width), beside.dtype)
        for edge, base in ((edge_a, RADIUS * (1 - odd)), (edge_b, RADIUS * odd)):
            for j in range(RADIUS):
                at = pl.ds(pl.multiple_of((base + j) * rows, rows), rows)
                edge_beside[at, :width] = edge[j]
    near = [pl.ds(pl.multiple_of((mine ^ k) * rows, rows), RADIUS * rows) for k in receivers]

    def scores_of(n):
        ask = asks[mine ^ receivers[n]]
        return [product(ask, turned[...]), product(ask, edge_turned[:, near[n]])]

    ahead = scores_of(0)
    for n in range(len(receivers)):
        scores = ahead
        if n + 1 < len(receivers):
            ahead = scores_of(n + 1)
        _, mixed = attend(scores, [beside[...], edge_beside[near[n]]])
        mean = by_head(mixed[:, :width], rows) / by_head(mixed[:, width:], rows)
        outs[n][...] = mean.astype(outs[n].dtype)


def merge_kernel(back_a, back_b, peaks, sums, *refs):
    outs, (backs, whole) = refs[-GROUP - 2 : -2], refs[-2:]
    rows, width = outs[0].shape
    mine = place()
    odd = lax.rem(plane(), 2)
    backs[1 - odd] = back_a[...]
    backs[odd] = back_b[...]
    last = lax.axis_size("tm") // GROUP - 1
    absent = [jnp.where(plane() == end, NEG, 0.0) for end in (0, last)]

    def logs(side, j):
        squares = []
        for part in range(rows // width):
            at = rows + part * STAT_ROWS
            stats = backs[side, j, at : at + STAT_ROWS].astype(jnp.float32)
            heads = [
                stats[8 * h : 8 * h + 1] + stats[8 * h + 1 : 8 * h + 2] + stats[8 * h + 2 : 8 * h + 3]
                for h in range(width // HEAD)
            ]
            turned = jnp.transpose(
                jnp.concatenate([jnp.broadcast_to(x, (HEAD, width)) for x in heads], axis=0)
            )
            squares.append(turned)
        return jnp.concatenate(squares, axis=0) + absent[side]

    for b in range(GROUP):
        theirs = []
        if b < RADIUS:
            theirs.append((0, b))
        if b >= GROUP - RADIUS:
            theirs.append((1, b - (GROUP - RADIUS)))
        theirs = [(logs(*t), backs[t[0], t[1], :rows].astype(jnp.float32)) for t in theirs]
        old = peaks[b]
        top = old
        for log, _ in theirs:
            top = jnp.maximum(top, log)
        factor = jnp.exp(old - top)
        value = sums[b, 0] * factor
        total = sums[b, 1] * factor
        for log, mean in theirs:
            weight = jnp.exp(log - top)
            value += weight * mean
            total += weight
        whole[b] = (value / total).astype(whole.dtype)
    for k in range(GROUP):
        outs[k][...] = whole[mine ^ k]


def local(audio_frames, video_frames, recording, audio_query, video_key):
    rows, half = audio_frames.shape
    width = half // GROUP
    heads = width // HEAD
    length = lax.axis_size("tm")
    bf16, f32 = jnp.bfloat16, jnp.float32
    shape = jax.ShapeDtypeStruct
    assert length % (2 * GROUP) == 0

    def swapped(x):
        return lax.ppermute(x, "head", [(0, 1), (1, 0)])

    def traded(pieces):
        pairs = lambda k: [(i, i ^ k) for i in range(length)]
        return [pieces[0]] + [lax.ppermute(pieces[k], "tm", pairs(k)) for k in range(1, GROUP)]

    def crossed(sent, second):
        planes = range(second, length // GROUP - second)
        pairs = [(p, ((p + second) ^ 1) - second) for p in planes]
        return lax.ppermute(
            sent, "tm", [(p * GROUP + i, q * GROUP + i) for p, q in pairs for i in range(GROUP)]
        )

    part = shape((rows, half), f32)
    square = shape((half, half), bf16)
    piece = shape((rows, width), bf16)
    given = (audio_frames, video_frames, audio_query, video_key, recording.reshape(rows // width, width))
    audio_in, video_in, query_in, key_in, ids_in = (
        pltpu.with_memory_space_constraint(x, pltpu.HBM) for x in given
    )
    other_audio = swapped(audio_frames)
    other_video = swapped(video_frames)
    packs = call(
        split_kernel,
        [shape((2 * rows + ID_ROWS, width), bf16)] * GROUP,
        [pltpu.VMEM((rows // width, width), jnp.int32), pltpu.VMEM((ID_ROWS, width), f32)]
        + [pltpu.SemaphoreType.DMA((1 + 2 * GROUP,))],
        ins=[HBM] * 3,
        moved=8 * rows * half,
        name="split",
    )(audio_in, video_in, ids_in)
    packs = traded(packs)
    query_part, key_part, query_rest, key_rest = call(
        prepare_kernel,
        [part, part, square, square],
        [pltpu.VMEM((rows, half), bf16)] * 2
        + [pltpu.VMEM((half, half), bf16)] * 2
        + [pltpu.SemaphoreType.DMA((6,))],
        ins=[HBM] * 4 + [ANY],
        flops=4 * rows * half * half,
        moved=16 * half * half,
        name="prepare",
    )(audio_in, video_in, query_in, key_in, packs[1])

    def project(scale, *operands, after=()):
        return call(
            functools.partial(project_kernel, scale),
            [piece] * GROUP,
            [pltpu.VMEM((rows, half), bf16)],
            ins=[VMEM] * 3 + [ANY] * len(after),
            flops=2 * rows * half * half,
            moved=2 * half * half + 6 * rows * half * 2,
            name="project",
        )(*operands, *after)

    def halo(pieces, id_packs, *after):
        edge = shape((RADIUS, rows + (ID_ROWS if id_packs else 0), width), bf16)
        sent = call(
            functools.partial(halo_kernel, 2 * rows if id_packs else 0),
            [edge, edge],
            ins=[VMEM] * (GROUP + len(id_packs)) + [ANY] * len(after),
            moved=10 * rows * width * 2,
            name="halo",
        )(*pieces, *id_packs, *after)
        return [crossed(sent[i], i) for i in range(2)]

    queries = traded(project(HEAD**-0.5, query_part, other_audio, query_rest, after=packs[1:3]))
    keys = project(1.0, key_part, other_video, key_rest, after=())
    query_edges = halo(queries, packs, keys[0])
    keys = traded(keys)

    inside, around = GROUP * rows, 2 * RADIUS * rows
    turned, beside = shape((2 * width, inside), bf16), shape((inside, 2 * width), bf16)
    asks = shape((GROUP, heads * rows, 2 * width), bf16)
    peaks, sums, plane_turned, plane_beside = call(
        rows_kernel,
        [shape((GROUP, rows, width), f32), shape((GROUP, 2, rows, width), f32), turned, beside],
        [pltpu.VMEM(asks.shape, bf16)],
        flops=16 * GROUP * rows * inside * width,
        moved=8 * inside * width * 2,
        exps=2 * GROUP * rows * inside,
        name="rows",
    )(*packs, *queries, *keys)
    audio_edges = [halo(packs, [], *[peaks])[0], halo(packs, [], *[])[1]]
    back = shape((RADIUS, rows + rows // width * STAT_ROWS, width), bf16)
    lent_a, lent_b, edge_turned = call(
        lend_kernel,
        [back, back, shape((2 * width, around), bf16)],
        [pltpu.VMEM((2, RADIUS, rows + ID_ROWS, width), bf16), pltpu.VMEM((2,) + back.shape, bf16)],
        flops=48 * RADIUS * GROUP * rows * rows * width,
        moved=8 * around * width * 2,
        exps=2 * RADIUS * GROUP * rows * rows,
        name="lend",
    )(*query_edges[::-1], plane_turned, plane_beside)
    backs = [crossed(x, i) for i, x in enumerate((lent_a, lent_b))]

    half_columns = dict(
        flops=56 * GROUP * rows * rows * width,
        moved=4 * around * width * 2,
        exps=7 * GROUP * rows * rows,
        name="columns",
    )
    shared = [turned, beside, asks, shape((around, 2 * width), bf16)]
    near, far = range(GROUP // 2), range(GROUP // 2, GROUP)
    *far_pieces, turned, beside, asks, edge_beside = call(
        functools.partial(columns_kernel, far), [piece] * len(far) + shared, **half_columns
    )(*packs, *queries, *keys, *audio_edges[::-1], edge_turned)
    audio_pieces = call(
        merge_kernel,
        [piece] * GROUP,
        [pltpu.VMEM((2,) + back.shape, bf16), pltpu.VMEM((GROUP, rows, width), bf16)],
        moved=16 * inside * width,
        exps=4 * inside * width,
        ins=[VMEM] * 4 + [ANY],
        name="merge",
    )(*backs, peaks, sums, far_pieces[0])
    audio_pieces = traded(audio_pieces)
    near_pieces = call(
        functools.partial(columns_kernel, near),
        [piece] * len(near),
        ins=[VMEM] * 5 + [ANY],
        **half_columns,
    )(edge_turned, turned, beside, asks, edge_beside, audio_pieces[0])
    video_pieces = traded([*near_pieces, *far_pieces])

    def join(pieces):
        return call(
            join_kernel,
            shape((rows, half), bf16),
            [pltpu.SemaphoreType.DMA((GROUP,))],
            outs_in=HBM,
            moved=2 * rows * half * 2,
            name="join",
        )(*pieces)

    video_attended = join(video_pieces)
    audio_attended = join(audio_pieces)
    return (audio_attended, video_attended)


def solution(mesh):
    return jax.shard_map(
        local,
        mesh=mesh,
        in_specs=(P("tm", "head"), P("tm", "head"), P("tm"), P(None, "head"), P(None, "head")),
        out_specs=(P("tm", "head"), P("tm", "head")),
        check_vma=False,
    )
```

```python
import functools

import jax
import jax.numpy as jnp
from jax import lax
from jax.experimental import pallas as pl
from jax.experimental.pallas import tpu as pltpu
from jax.sharding import PartitionSpec as P

HEAD = 64
RADIUS = 3
GROUP = 4
NEG = -1e30
ID_ROWS = 16
STAT_ROWS = 16

VMEM = pl.BlockSpec(memory_space=pltpu.VMEM)
ANY = pl.BlockSpec(memory_space=pl.ANY)
HBM = pl.BlockSpec(memory_space=pltpu.HBM)


def place():
    return lax.rem(lax.axis_index("tm"), GROUP)


def plane():
    return lax.axis_index("tm") // GROUP


def call(kernel, outs, scratch=(), ins=None, outs_in=None, flops=0, moved=0, exps=0, name=None):
    return pl.pallas_call(
        kernel,
        out_shape=outs,
        **({"in_specs": ins} if ins else {}),
        **({"out_specs": outs_in} if outs_in else {}),
        scratch_shapes=scratch,
        compiler_params=pltpu.CompilerParams(vmem_limit_bytes=32 * 2**20),
        cost_estimate=pl.CostEstimate(flops=flops, bytes_accessed=moved, transcendentals=exps),
        name=name,
    )


def product(a, b):
    return jnp.dot(a, b, preferred_element_type=jnp.float32)


def fetcher(sems):
    copies = []

    def fetch(source, target):
        copies.append(pltpu.make_async_copy(source, target, sems.at[len(copies)]))
        copies[-1].start()

    return copies, fetch


def split_kernel(audio, video, ids, *refs):
    packs, (ids_in, ids_wide, sems) = refs[:GROUP], refs[GROUP:]
    rows, width = audio.shape[0], packs[0].shape[1]
    mine = place()
    copies, fetch = fetcher(sems)
    fetch(ids, ids_in)
    for k in range(GROUP):
        at = pl.ds(pl.multiple_of((mine ^ k) * width, width), width)
        for i, stream in enumerate((audio, video)):
            fetch(stream.at[:, at], packs[k].at[i * rows : (i + 1) * rows])
    copies[0].wait()
    ids_wide[...] = jnp.zeros_like(ids_wide)
    ids_wide[: ids_in.shape[0]] = (ids_in[...] + 1).astype(jnp.float32)
    for k in range(GROUP):
        packs[k][2 * rows :] = ids_wide[...].astype(packs[k].dtype)
    for copy in copies[1:]:
        copy.wait()


def prepare_kernel(audio, video, query, key, *refs):
    sums, seconds, streams, firsts, sems = refs[-9:-7], refs[-7:-5], refs[-5:-3], refs[-3:-1], refs[-1]
    half = audio.shape[1]
    side = lax.axis_index("head")
    ours = pl.ds(pl.multiple_of(side * half, half), half)
    theirs = pl.ds(pl.multiple_of((1 - side) * half, half), half)
    copies, fetch = fetcher(sems)
    for i, (stream, weight) in enumerate(((audio, query), (video, key))):
        fetch(stream, streams[i])
        fetch(weight.at[ours], firsts[i])
    for i, weight in enumerate((query, key)):
        fetch(weight.at[theirs], seconds[i])
    for i in range(2):
        copies[2 * i].wait()
        copies[2 * i + 1].wait()
        sums[i][...] = product(streams[i][...], firsts[i][...])
    for copy in copies[4:]:
        copy.wait()


def project_kernel(scale, part, other, weight, *refs):
    pieces, full = refs[-GROUP - 1 : -1], refs[-1]
    width = pieces[0].shape[1]
    mine = place()
    full[...] = (part[...] + product(other[...], weight[...])).astype(jnp.bfloat16) * jnp.bfloat16(scale)
    for k in range(GROUP):
        pieces[k][...] = full[:, pl.ds(pl.multiple_of((mine ^ k) * width, width), width)]


def halo_kernel(seconds, ids_at, *refs):
    pieces, id_packs, outs = refs[:GROUP], refs[GROUP : 2 * GROUP], refs[-len(seconds) :]
    rows = outs[0].shape[1] - (ID_ROWS if ids_at else 0)
    mine = place()
    for out, second in zip(outs, seconds):
        skip = (GROUP - RADIUS) * lax.rem(plane() + 1 + second, 2)
        for k in range(GROUP):
            spot = (mine ^ k) - skip

            @pl.when((spot >= 0) & (spot < RADIUS))
            def _():
                out[spot, :rows] = pieces[k][:rows]
                if ids_at:
                    out[spot, rows:] = id_packs[k][ids_at:]


def join_kernel(*refs):
    pieces, out, sems = refs[:GROUP], refs[GROUP], refs[GROUP + 1]
    width = pieces[0].shape[1]
    mine = place()
    copies, fetch = fetcher(sems)
    for k in range(GROUP):
        fetch(pieces[k], out.at[:, pl.ds(pl.multiple_of((mine ^ k) * width, width), width)])
    for copy in copies:
        copy.wait()


def marks_turned(lanes):
    lanes = lanes.astype(jnp.float32)
    width = lanes.shape[1]
    row = lax.broadcasted_iota(jnp.int32, (width, width), 0).astype(jnp.float32)
    return [
        jnp.where(row == lanes[part : part + 1], 1.0, 0.0).astype(jnp.bfloat16) for part in range(2)
    ]


def stacked_ask(block, turned):
    head = lax.broadcasted_iota(jnp.int32, block.shape, 1) // HEAD
    marks = jnp.concatenate([jnp.transpose(x) for x in turned], axis=0)
    beside = (marks - jnp.bfloat16(1.0)) * jnp.bfloat16(-NEG)
    return jnp.concatenate(
        [
            jnp.concatenate([jnp.where(head == h, block, jnp.zeros_like(block)), beside], axis=1)
            for h in range(block.shape[1] // HEAD)
        ],
        axis=0,
    )


def by_head(stacked, rows):
    out = stacked[:rows]
    head = lax.broadcasted_iota(jnp.int32, out.shape, 1) // HEAD
    for h in range(1, stacked.shape[0] // rows):
        out = jnp.where(head == h, stacked[h * rows : (h + 1) * rows], out)
    return out


def attend(scores, values):
    top = None
    for s in scores:
        for at in range(0, s.shape[1], values[0].shape[1] // 2):
            part = s[:, at : at + values[0].shape[1] // 2]
            top = part if top is None else jnp.maximum(top, part)
    peak = jnp.max(top, axis=1, keepdims=True)
    mixed = None
    for s, value in zip(scores, values):
        part = product(jnp.exp(s - peak).astype(jnp.bfloat16), value)
        mixed = part if mixed is None else mixed + part
    return peak, mixed


def set_up(packs, asked, keys, values, turned, beside, asks):
    rows, width = asks.shape[1] // 2, asks.shape[2] // 2
    mine = place()
    beside[:, width:] = jnp.ones((GROUP * rows, width), beside.dtype)
    for k in range(GROUP):
        b = mine ^ k

        def spot(at, size):
            return pl.ds(pl.multiple_of(b * rows + at, size), size)

        marks = marks_turned(packs[k][2 * rows :])
        asks[b] = stacked_ask(asked(k), marks)
        beside[spot(0, rows), :width] = values(k)
        key = keys(k)
        for part, x in enumerate(marks):
            at = spot(part * width, width)
            turned[:width, at] = jnp.transpose(key[part * width : (part + 1) * width])
            turned[width:, at] = x


def rows_kernel(*refs):
    packs, queries, keys = refs[:GROUP], refs[GROUP : 2 * GROUP], refs[2 * GROUP : 3 * GROUP]
    peaks, sums, turned, beside, asks = refs[-5:]
    rows, width = keys[0].shape
    set_up(
        packs,
        lambda k: queries[k][...],
        lambda k: keys[k][...],
        lambda k: packs[k][rows : 2 * rows],
        turned,
        beside,
        asks,
    )
    ahead = product(asks[0], turned[...])
    for b in range(GROUP):
        scores = ahead
        if b + 1 < GROUP:
            ahead = product(asks[b + 1], turned[...])
        peak, mixed = attend([scores], [beside[...]])
        peaks[b] = by_head(jnp.broadcast_to(peak, (peak.shape[0], width)), rows)
        sums[b, 0] = by_head(mixed[:, :width], rows)
        sums[b, 1] = by_head(mixed[:, width:], rows)


def lend_kernel(edge_b, edge_a, plane_turned, plane_beside, first, second, turned, ordered, results):
    rows, width = ordered.shape[2] - ID_ROWS, ordered.shape[3]
    odd = lax.rem(plane(), 2)
    ordered[1 - odd] = edge_a[...]
    ordered[odd] = edge_b[...]
    lane = lax.broadcasted_iota(jnp.int32, (rows, width), 1)
    blocks = [slice(0, (j + 1) * rows) for j in range(RADIUS)]
    blocks += [slice((j + 1) * rows, GROUP * rows) for j in range(RADIUS)]

    def scores_of(e):
        side, j = e // RADIUS, e % RADIUS
        marks = marks_turned(ordered[side, j, rows:])
        query = ordered[side, j, :rows]
        for part, x in enumerate(marks):
            at = slice(e * rows + part * width, e * rows + (part + 1) * width)
            turned[:width, at] = jnp.transpose(query[part * width : (part + 1) * width])
            turned[width:, at] = x
        return product(stacked_ask(query, marks), plane_turned[:, blocks[e]])

    ahead = scores_of(0)
    for e in range(2 * RADIUS):
        side, j = e // RADIUS, e % RADIUS
        scores = ahead
        if e + 1 < 2 * RADIUS:
            ahead = scores_of(e + 1)
        peak, mixed = attend([scores], [plane_beside[blocks[e]]])
        total = by_head(mixed[:, width:], rows)
        results[side, j, :rows] = (by_head(mixed[:, :width], rows) / total).astype(results.dtype)
        logs = by_head(jnp.broadcast_to(peak, (peak.shape[0], width)), rows) + jnp.log(total)
        high = logs.astype(jnp.bfloat16).astype(jnp.float32)
        middle = (logs - high).astype(jnp.bfloat16).astype(jnp.float32)
        low = logs - high - middle
        picked = jnp.where(lane % HEAD == 0, high, jnp.where(lane % HEAD == 1, middle, low))
        for part in range(rows // width):
            flipped = jnp.transpose(picked[part * width : (part + 1) * width])
            stats = [flipped[h : h + STAT_ROWS // 2] for h in range(0, width, HEAD)]
            at = rows + part * STAT_ROWS
            results[side, j, at : at + STAT_ROWS] = jnp.concatenate(stats, axis=0).astype(
                results.dtype
            )
    first[...] = results[1 - odd]
    second[...] = results[odd]


def columns_kernel(receivers, *refs):
    refs = list(refs)
    take = lambda count: [refs.pop(0) for _ in range(count)]
    first = 0 not in receivers
    if first:
        packs, queries, keys, (edge_b, edge_a) = take(GROUP), take(GROUP), take(GROUP), take(2)
    (edge_turned,) = take(1)
    if not first:
        shared, _ = take(4), take(1)
    outs = take(len(receivers))
    turned, beside, asks, edge_beside = take(4) if first else shared
    rows, width = outs[0].shape
    mine = place()
    if first:
        odd = lax.rem(plane(), 2)
        set_up(
            packs,
            lambda k: keys[k][...],
            lambda k: queries[k][...],
            lambda k: packs[k][:rows],
            turned,
            beside,
            asks,
        )
        edge_beside[:, width:] = jnp.ones((edge_beside.shape[0], width), beside.dtype)
        for edge, base in ((edge_a, RADIUS * (1 - odd)), (edge_b, RADIUS * odd)):
            for j in range(RADIUS):
                at = pl.ds(pl.multiple_of((base + j) * rows, rows), rows)
                edge_beside[at, :width] = edge[j]
    near = [pl.ds(pl.multiple_of((mine ^ k) * rows, rows), RADIUS * rows) for k in receivers]

    def scores_of(n):
        ask = asks[mine ^ receivers[n]]
        return [product(ask, turned[...]), product(ask, edge_turned[:, near[n]])]

    ahead = scores_of(0)
    for n in range(len(receivers)):
        scores = ahead
        if n + 1 < len(receivers):
            ahead = scores_of(n + 1)
        _, mixed = attend(scores, [beside[...], edge_beside[near[n]]])
        mean = by_head(mixed[:, :width], rows) / by_head(mixed[:, width:], rows)
        outs[n][...] = mean.astype(outs[n].dtype)


def merge_kernel(back_a, back_b, peaks, sums, *refs):
    outs, (backs, whole) = refs[-GROUP - 2 : -2], refs[-2:]
    rows, width = outs[0].shape
    mine = place()
    odd = lax.rem(plane(), 2)
    backs[1 - odd] = back_a[...]
    backs[odd] = back_b[...]
    last = lax.axis_size("tm") // GROUP - 1
    absent = [jnp.where(plane() == end, NEG, 0.0) for end in (0, last)]

    def logs(side, j):
        squares = []
        for part in range(rows // width):
            at = rows + part * STAT_ROWS
            stats = backs[side, j, at : at + STAT_ROWS].astype(jnp.float32)
            heads = [
                stats[8 * h : 8 * h + 1] + stats[8 * h + 1 : 8 * h + 2] + stats[8 * h + 2 : 8 * h + 3]
                for h in range(width // HEAD)
            ]
            turned = jnp.transpose(
                jnp.concatenate([jnp.broadcast_to(x, (HEAD, width)) for x in heads], axis=0)
            )
            squares.append(turned)
        return jnp.concatenate(squares, axis=0) + absent[side]

    for b in range(GROUP):
        theirs = []
        if b < RADIUS:
            theirs.append((0, b))
        if b >= GROUP - RADIUS:
            theirs.append((1, b - (GROUP - RADIUS)))
        theirs = [(logs(*t), backs[t[0], t[1], :rows].astype(jnp.float32)) for t in theirs]
        old = peaks[b]
        top = old
        for log, _ in theirs:
            top = jnp.maximum(top, log)
        factor = jnp.exp(old - top)
        value = sums[b, 0] * factor
        total = sums[b, 1] * factor
        for log, mean in theirs:
            weight = jnp.exp(log - top)
            value += weight * mean
            total += weight
        whole[b] = (value / total).astype(whole.dtype)
    for k in range(GROUP):
        outs[k][...] = whole[mine ^ k]


def local(audio_frames, video_frames, recording, audio_query, video_key):
    rows, half = audio_frames.shape
    width = half // GROUP
    heads = width // HEAD
    length = lax.axis_size("tm")
    bf16, f32 = jnp.bfloat16, jnp.float32
    shape = jax.ShapeDtypeStruct
    assert length % (2 * GROUP) == 0

    def swapped(x):
        return lax.ppermute(x, "head", [(0, 1), (1, 0)])

    def traded(pieces):
        pairs = lambda k: [(i, i ^ k) for i in range(length)]
        return [pieces[0]] + [lax.ppermute(pieces[k], "tm", pairs(k)) for k in range(1, GROUP)]

    def crossed(sent, second):
        planes = range(second, length // GROUP - second)
        pairs = [(p, ((p + second) ^ 1) - second) for p in planes]
        return lax.ppermute(
            sent, "tm", [(p * GROUP + i, q * GROUP + i) for p, q in pairs for i in range(GROUP)]
        )

    part = shape((rows, half), f32)
    square = shape((half, half), bf16)
    piece = shape((rows, width), bf16)
    given = (audio_frames, video_frames, audio_query, video_key, recording.reshape(rows // width, width))
    audio_in, video_in, query_in, key_in, ids_in = (
        pltpu.with_memory_space_constraint(x, pltpu.HBM) for x in given
    )
    other_audio = swapped(audio_frames)
    other_video = swapped(video_frames)
    packs = call(
        split_kernel,
        [shape((2 * rows + ID_ROWS, width), bf16)] * GROUP,
        [pltpu.VMEM((rows // width, width), jnp.int32), pltpu.VMEM((ID_ROWS, width), f32)]
        + [pltpu.SemaphoreType.DMA((1 + 2 * GROUP,))],
        ins=[HBM] * 3,
        moved=8 * rows * half,
        name="split",
    )(audio_in, video_in, ids_in)
    packs = traded(packs)
    query_part, key_part, query_rest, key_rest = call(
        prepare_kernel,
        [part, part, square, square],
        [pltpu.VMEM((rows, half), bf16)] * 2
        + [pltpu.VMEM((half, half), bf16)] * 2
        + [pltpu.SemaphoreType.DMA((6,))],
        ins=[HBM] * 4 + [ANY],
        flops=4 * rows * half * half,
        moved=16 * half * half,
        name="prepare",
    )(audio_in, video_in, query_in, key_in, packs[1])

    def project(scale, *operands, after=()):
        return call(
            functools.partial(project_kernel, scale),
            [piece] * GROUP,
            [pltpu.VMEM((rows, half), bf16)],
            ins=[VMEM] * 3 + [ANY] * len(after),
            flops=2 * rows * half * half,
            moved=2 * half * half + 6 * rows * half * 2,
            name="project",
        )(*operands, *after)

    def halo(seconds, pieces, id_packs, *after):
        edge = shape((RADIUS, rows + (ID_ROWS if id_packs else 0), width), bf16)
        sent = call(
            functools.partial(halo_kernel, seconds, 2 * rows if id_packs else 0),
            [edge] * len(seconds),
            ins=[VMEM] * (GROUP + len(id_packs)) + [ANY] * len(after),
            moved=5 * len(seconds) * rows * width * 2,
            name="halo",
        )(*pieces, *id_packs, *after)
        return [crossed(x, second) for x, second in zip(sent, seconds)]

    queries = traded(project(HEAD**-0.5, query_part, other_audio, query_rest, after=packs[1:3]))
    keys = project(1.0, key_part, other_video, key_rest, after=())
    query_edges = halo((0, 1), queries, packs, keys[0])
    keys = traded(keys)

    inside, around = GROUP * rows, 2 * RADIUS * rows
    turned, beside = shape((2 * width, inside), bf16), shape((inside, 2 * width), bf16)
    asks = shape((GROUP, heads * rows, 2 * width), bf16)
    peaks, sums, plane_turned, plane_beside = call(
        rows_kernel,
        [shape((GROUP, rows, width), f32), shape((GROUP, 2, rows, width), f32), turned, beside],
        [pltpu.VMEM(asks.shape, bf16)],
        flops=16 * GROUP * rows * inside * width,
        moved=8 * inside * width * 2,
        exps=2 * GROUP * rows * inside,
        name="rows",
    )(*packs, *queries, *keys)
    audio_edges = halo((0,), packs, [], peaks) + halo((1,), packs, [])
    back = shape((RADIUS, rows + rows // width * STAT_ROWS, width), bf16)
    lent_a, lent_b, edge_turned = call(
        lend_kernel,
        [back, back, shape((2 * width, around), bf16)],
        [pltpu.VMEM((2, RADIUS, rows + ID_ROWS, width), bf16), pltpu.VMEM((2,) + back.shape, bf16)],
        flops=48 * RADIUS * GROUP * rows * rows * width,
        moved=8 * around * width * 2,
        exps=2 * RADIUS * GROUP * rows * rows,
        name="lend",
    )(*query_edges[::-1], plane_turned, plane_beside)
    backs = [crossed(x, i) for i, x in enumerate((lent_a, lent_b))]

    half_columns = dict(
        flops=56 * GROUP * rows * rows * width,
        moved=4 * around * width * 2,
        exps=7 * GROUP * rows * rows,
        name="columns",
    )
    shared = [turned, beside, asks, shape((around, 2 * width), bf16)]
    near, far = range(GROUP // 2), range(GROUP // 2, GROUP)
    *far_pieces, turned, beside, asks, edge_beside = call(
        functools.partial(columns_kernel, far), [piece] * len(far) + shared, **half_columns
    )(*packs, *queries, *keys, *audio_edges[::-1], edge_turned)
    audio_pieces = call(
        merge_kernel,
        [piece] * GROUP,
        [pltpu.VMEM((2,) + back.shape, bf16), pltpu.VMEM((GROUP, rows, width), bf16)],
        moved=16 * inside * width,
        exps=4 * inside * width,
        ins=[VMEM] * 4 + [ANY],
        name="merge",
    )(*backs, peaks, sums, far_pieces[0])
    audio_pieces = traded(audio_pieces)
    near_pieces = call(
        functools.partial(columns_kernel, near),
        [piece] * len(near),
        ins=[VMEM] * 5 + [ANY],
        **half_columns,
    )(edge_turned, turned, beside, asks, edge_beside, audio_pieces[0])
    video_pieces = traded([*near_pieces, *far_pieces])

    def join(pieces):
        return call(
            join_kernel,
            shape((rows, half), bf16),
            [pltpu.SemaphoreType.DMA((GROUP,))],
            outs_in=HBM,
            moved=2 * rows * half * 2,
            name="join",
        )(*pieces)

    video_attended = join(video_pieces)
    audio_attended = join(audio_pieces)
    return (audio_attended, video_attended)


def solution(mesh):
    return jax.shard_map(
        local,
        mesh=mesh,
        in_specs=(P("tm", "head"), P("tm", "head"), P("tm"), P(None, "head"), P(None, "head")),
        out_specs=(P("tm", "head"), P("tm", "head")),
        check_vma=False,
    )
```

```python
import functools

import jax
import jax.numpy as jnp
from jax import lax
from jax.experimental import pallas as pl
from jax.experimental.pallas import tpu as pltpu
from jax.sharding import PartitionSpec as P

HEAD = 64
RADIUS = 3
GROUP = 4
NEG = -1e30
ID_ROWS = 16
STAT_ROWS = 16

VMEM = pl.BlockSpec(memory_space=pltpu.VMEM)
ANY = pl.BlockSpec(memory_space=pl.ANY)
HBM = pl.BlockSpec(memory_space=pltpu.HBM)


def place():
    return lax.rem(lax.axis_index("tm"), GROUP)


def plane():
    return lax.axis_index("tm") // GROUP


def call(kernel, outs, scratch=(), ins=None, outs_in=None, flops=0, moved=0, exps=0, name=None):
    return pl.pallas_call(
        kernel,
        out_shape=outs,
        **({"in_specs": ins} if ins else {}),
        **({"out_specs": outs_in} if outs_in else {}),
        scratch_shapes=scratch,
        compiler_params=pltpu.CompilerParams(vmem_limit_bytes=32 * 2**20),
        cost_estimate=pl.CostEstimate(flops=flops, bytes_accessed=moved, transcendentals=exps),
        name=name,
    )


def product(a, b):
    return jnp.dot(a, b, preferred_element_type=jnp.float32)


def fetcher(sems):
    copies = []

    def fetch(source, target):
        copies.append(pltpu.make_async_copy(source, target, sems.at[len(copies)]))
        copies[-1].start()

    return copies, fetch


def split_kernel(audio, video, ids, *refs):
    packs, (ids_in, ids_wide, sems) = refs[:GROUP], refs[GROUP:]
    rows, width = audio.shape[0], packs[0].shape[1]
    mine = place()
    copies, fetch = fetcher(sems)
    fetch(ids, ids_in)
    for k in range(GROUP):
        at = pl.ds(pl.multiple_of((mine ^ k) * width, width), width)
        for i, stream in enumerate((audio, video)):
            fetch(stream.at[:, at], packs[k].at[i * rows : (i + 1) * rows])
    copies[0].wait()
    ids_wide[...] = jnp.zeros_like(ids_wide)
    ids_wide[: ids_in.shape[0]] = (ids_in[...] + 1).astype(jnp.float32)
    for k in range(GROUP):
        packs[k][2 * rows :] = ids_wide[...].astype(packs[k].dtype)
    for copy in copies[1:]:
        copy.wait()


def prepare_kernel(audio, video, query, key, *refs):
    sums, seconds, streams, firsts, sems = refs[-9:-7], refs[-7:-5], refs[-5:-3], refs[-3:-1], refs[-1]
    half = audio.shape[1]
    side = lax.axis_index("head")
    ours = pl.ds(pl.multiple_of(side * half, half), half)
    theirs = pl.ds(pl.multiple_of((1 - side) * half, half), half)
    copies, fetch = fetcher(sems)
    for i, (stream, weight) in enumerate(((audio, query), (video, key))):
        fetch(stream, streams[i])
        fetch(weight.at[ours], firsts[i])
    for i, weight in enumerate((query, key)):
        fetch(weight.at[theirs], seconds[i])
    for i in range(2):
        copies[2 * i].wait()
        copies[2 * i + 1].wait()
        sums[i][...] = product(streams[i][...], firsts[i][...])
    for copy in copies[4:]:
        copy.wait()


def project_kernel(scale, part, other, weight, *refs):
    pieces, full = refs[-GROUP - 1 : -1], refs[-1]
    width = pieces[0].shape[1]
    mine = place()
    full[...] = (part[...] + product(other[...], weight[...])).astype(jnp.bfloat16) * jnp.bfloat16(scale)
    for k in range(GROUP):
        pieces[k][...] = full[:, pl.ds(pl.multiple_of((mine ^ k) * width, width), width)]


def halo_kernel(seconds, ids_at, *refs):
    pieces, id_packs, outs = refs[:GROUP], refs[GROUP : 2 * GROUP], refs[-len(seconds) :]
    rows = outs[0].shape[1] - (ID_ROWS if ids_at else 0)
    mine = place()
    for out, second in zip(outs, seconds):
        skip = (GROUP - RADIUS) * lax.rem(plane() + 1 + second, 2)
        for k in range(GROUP):
            spot = (mine ^ k) - skip

            @pl.when((spot >= 0) & (spot < RADIUS))
            def _():
                out[spot, :rows] = pieces[k][:rows]
                if ids_at:
                    out[spot, rows:] = id_packs[k][ids_at:]


def join_kernel(*refs):
    pieces, outs, sems = refs[: 2 * GROUP], refs[2 * GROUP : 2 * GROUP + 2], refs[-1]
    width = pieces[0].shape[1]
    mine = place()
    copies, fetch = fetcher(sems)
    for i, out in enumerate(outs):
        for k in range(GROUP):
            at = pl.ds(pl.multiple_of((mine ^ k) * width, width), width)
            fetch(pieces[i * GROUP + k], out.at[:, at])
    for copy in copies:
        copy.wait()


def marks_turned(lanes):
    lanes = lanes.astype(jnp.float32)
    width = lanes.shape[1]
    row = lax.broadcasted_iota(jnp.int32, (width, width), 0).astype(jnp.float32)
    return [
        jnp.where(row == lanes[part : part + 1], 1.0, 0.0).astype(jnp.bfloat16) for part in range(2)
    ]


def stacked_ask(block, turned):
    head = lax.broadcasted_iota(jnp.int32, block.shape, 1) // HEAD
    marks = jnp.concatenate([jnp.transpose(x) for x in turned], axis=0)
    beside = (marks - jnp.bfloat16(1.0)) * jnp.bfloat16(-NEG)
    return jnp.concatenate(
        [
            jnp.concatenate([jnp.where(head == h, block, jnp.zeros_like(block)), beside], axis=1)
            for h in range(block.shape[1] // HEAD)
        ],
        axis=0,
    )


def by_head(stacked, rows):
    out = stacked[:rows]
    head = lax.broadcasted_iota(jnp.int32, out.shape, 1) // HEAD
    for h in range(1, stacked.shape[0] // rows):
        out = jnp.where(head == h, stacked[h * rows : (h + 1) * rows], out)
    return out


def attend(scores, values):
    top = None
    for s in scores:
        for at in range(0, s.shape[1], values[0].shape[1] // 2):
            part = s[:, at : at + values[0].shape[1] // 2]
            top = part if top is None else jnp.maximum(top, part)
    peak = jnp.max(top, axis=1, keepdims=True)
    mixed = None
    for s, value in zip(scores, values):
        part = product(jnp.exp(s - peak).astype(jnp.bfloat16), value)
        mixed = part if mixed is None else mixed + part
    return peak, mixed


def set_up(packs, asked, keys, values, turned, beside, asks):
    rows, width = asks.shape[1] // 2, asks.shape[2] // 2
    mine = place()
    beside[:, width:] = jnp.ones((GROUP * rows, width), beside.dtype)
    for k in range(GROUP):
        b = mine ^ k

        def spot(at, size):
            return pl.ds(pl.multiple_of(b * rows + at, size), size)

        marks = marks_turned(packs[k][2 * rows :])
        asks[b] = stacked_ask(asked(k), marks)
        beside[spot(0, rows), :width] = values(k)
        key = keys(k)
        for part, x in enumerate(marks):
            at = spot(part * width, width)
            turned[:width, at] = jnp.transpose(key[part * width : (part + 1) * width])
            turned[width:, at] = x


def rows_kernel(*refs):
    packs, queries, keys = refs[:GROUP], refs[GROUP : 2 * GROUP], refs[2 * GROUP : 3 * GROUP]
    peaks, sums, turned, beside, asks = refs[-5:]
    rows, width = keys[0].shape
    set_up(
        packs,
        lambda k: queries[k][...],
        lambda k: keys[k][...],
        lambda k: packs[k][rows : 2 * rows],
        turned,
        beside,
        asks,
    )
    ahead = product(asks[0], turned[...])
    for b in range(GROUP):
        scores = ahead
        if b + 1 < GROUP:
            ahead = product(asks[b + 1], turned[...])
        peak, mixed = attend([scores], [beside[...]])
        peaks[b] = by_head(jnp.broadcast_to(peak, (peak.shape[0], width)), rows)
        sums[b, 0] = by_head(mixed[:, :width], rows)
        sums[b, 1] = by_head(mixed[:, width:], rows)


def lend_kernel(edge_b, edge_a, plane_turned, plane_beside, first, second, turned, ordered, results):
    rows, width = ordered.shape[2] - ID_ROWS, ordered.shape[3]
    odd = lax.rem(plane(), 2)
    ordered[1 - odd] = edge_a[...]
    ordered[odd] = edge_b[...]
    lane = lax.broadcasted_iota(jnp.int32, (rows, width), 1)
    blocks = [slice(0, (j + 1) * rows) for j in range(RADIUS)]
    blocks += [slice((j + 1) * rows, GROUP * rows) for j in range(RADIUS)]

    def scores_of(e):
        side, j = e // RADIUS, e % RADIUS
        marks = marks_turned(ordered[side, j, rows:])
        query = ordered[side, j, :rows]
        for part, x in enumerate(marks):
            at = slice(e * rows + part * width, e * rows + (part + 1) * width)
            turned[:width, at] = jnp.transpose(query[part * width : (part + 1) * width])
            turned[width:, at] = x
        return product(stacked_ask(query, marks), plane_turned[:, blocks[e]])

    ahead = scores_of(0)
    for e in range(2 * RADIUS):
        side, j = e // RADIUS, e % RADIUS
        scores = ahead
        if e + 1 < 2 * RADIUS:
            ahead = scores_of(e + 1)
        peak, mixed = attend([scores], [plane_beside[blocks[e]]])
        total = by_head(mixed[:, width:], rows)
        results[side, j, :rows] = (by_head(mixed[:, :width], rows) / total).astype(results.dtype)
        logs = by_head(jnp.broadcast_to(peak, (peak.shape[0], width)), rows) + jnp.log(total)
        high = logs.astype(jnp.bfloat16).astype(jnp.float32)
        middle = (logs - high).astype(jnp.bfloat16).astype(jnp.float32)
        low = logs - high - middle
        picked = jnp.where(lane % HEAD == 0, high, jnp.where(lane % HEAD == 1, middle, low))
        for part in range(rows // width):
            flipped = jnp.transpose(picked[part * width : (part + 1) * width])
            stats = [flipped[h : h + STAT_ROWS // 2] for h in range(0, width, HEAD)]
            at = rows + part * STAT_ROWS
            results[side, j, at : at + STAT_ROWS] = jnp.concatenate(stats, axis=0).astype(
                results.dtype
            )
    first[...] = results[1 - odd]
    second[...] = results[odd]


def columns_kernel(receivers, *refs):
    refs = list(refs)
    take = lambda count: [refs.pop(0) for _ in range(count)]
    first = 0 not in receivers
    if first:
        packs, queries, keys, (edge_b, edge_a) = take(GROUP), take(GROUP), take(GROUP), take(2)
    (edge_turned,) = take(1)
    if not first:
        shared, _ = take(4), take(2)
    outs = take(len(receivers))
    turned, beside, asks, edge_beside = take(4) if first else shared
    rows, width = outs[0].shape
    mine = place()
    if first:
        odd = lax.rem(plane(), 2)
        set_up(
            packs,
            lambda k: keys[k][...],
            lambda k: queries[k][...],
            lambda k: packs[k][:rows],
            turned,
            beside,
            asks,
        )
        edge_beside[:, width:] = jnp.ones((edge_beside.shape[0], width), beside.dtype)
        for edge, base in ((edge_a, RADIUS * (1 - odd)), (edge_b, RADIUS * odd)):
            for j in range(RADIUS):
                at = pl.ds(pl.multiple_of((base + j) * rows, rows), rows)
                edge_beside[at, :width] = edge[j]
    near = [pl.ds(pl.multiple_of((mine ^ k) * rows, rows), RADIUS * rows) for k in receivers]

    def scores_of(n):
        ask = asks[mine ^ receivers[n]]
        return [product(ask, turned[...]), product(ask, edge_turned[:, near[n]])]

    ahead = scores_of(0)
    for n in range(len(receivers)):
        scores = ahead
        if n + 1 < len(receivers):
            ahead = scores_of(n + 1)
        _, mixed = attend(scores, [beside[...], edge_beside[near[n]]])
        mean = by_head(mixed[:, :width], rows) / by_head(mixed[:, width:], rows)
        outs[n][...] = mean.astype(outs[n].dtype)


def merge_kernel(back_a, back_b, peaks, sums, *refs):
    outs, (backs, whole) = refs[-GROUP - 2 : -2], refs[-2:]
    rows, width = outs[0].shape
    mine = place()
    odd = lax.rem(plane(), 2)
    backs[1 - odd] = back_a[...]
    backs[odd] = back_b[...]
    last = lax.axis_size("tm") // GROUP - 1
    absent = [jnp.where(plane() == end, NEG, 0.0) for end in (0, last)]

    def logs(side, j):
        squares = []
        for part in range(rows // width):
            at = rows + part * STAT_ROWS
            stats = backs[side, j, at : at + STAT_ROWS].astype(jnp.float32)
            heads = [
                stats[8 * h : 8 * h + 1] + stats[8 * h + 1 : 8 * h + 2] + stats[8 * h + 2 : 8 * h + 3]
                for h in range(width // HEAD)
            ]
            turned = jnp.transpose(
                jnp.concatenate([jnp.broadcast_to(x, (HEAD, width)) for x in heads], axis=0)
            )
            squares.append(turned)
        return jnp.concatenate(squares, axis=0) + absent[side]

    for b in range(GROUP):
        theirs = []
        if b < RADIUS:
            theirs.append((0, b))
        if b >= GROUP - RADIUS:
            theirs.append((1, b - (GROUP - RADIUS)))
        theirs = [(logs(*t), backs[t[0], t[1], :rows].astype(jnp.float32)) for t in theirs]
        old = peaks[b]
        top = old
        for log, _ in theirs:
            top = jnp.maximum(top, log)
        factor = jnp.exp(old - top)
        value = sums[b, 0] * factor
        total = sums[b, 1] * factor
        for log, mean in theirs:
            weight = jnp.exp(log - top)
            value += weight * mean
            total += weight
        whole[b] = (value / total).astype(whole.dtype)
    for k in range(GROUP):
        outs[k][...] = whole[mine ^ k]


def local(audio_frames, video_frames, recording, audio_query, video_key):
    rows, half = audio_frames.shape
    width = half // GROUP
    heads = width // HEAD
    length = lax.axis_size("tm")
    bf16, f32 = jnp.bfloat16, jnp.float32
    shape = jax.ShapeDtypeStruct
    assert length % (2 * GROUP) == 0

    def swapped(x):
        return lax.ppermute(x, "head", [(0, 1), (1, 0)])

    def traded(pieces):
        pairs = lambda k: [(i, i ^ k) for i in range(length)]
        return [
            lax.ppermute(x, "tm", pairs(k)) if k and x is not None else x for k, x in enumerate(pieces)
        ]

    def crossed(sent, second):
        planes = range(second, length // GROUP - second)
        pairs = [(p, ((p + second) ^ 1) - second) for p in planes]
        return lax.ppermute(
            sent, "tm", [(p * GROUP + i, q * GROUP + i) for p, q in pairs for i in range(GROUP)]
        )

    part = shape((rows, half), f32)
    square = shape((half, half), bf16)
    piece = shape((rows, width), bf16)
    given = (audio_frames, video_frames, audio_query, video_key, recording.reshape(rows // width, width))
    audio_in, video_in, query_in, key_in, ids_in = (
        pltpu.with_memory_space_constraint(x, pltpu.HBM) for x in given
    )
    other_audio = swapped(audio_frames)
    other_video = swapped(video_frames)
    packs = call(
        split_kernel,
        [shape((2 * rows + ID_ROWS, width), bf16)] * GROUP,
        [pltpu.VMEM((rows // width, width), jnp.int32), pltpu.VMEM((ID_ROWS, width), f32)]
        + [pltpu.SemaphoreType.DMA((1 + 2 * GROUP,))],
        ins=[HBM] * 3,
        moved=8 * rows * half,
        name="split",
    )(audio_in, video_in, ids_in)
    packs = traded(packs)
    query_part, key_part, query_rest, key_rest = call(
        prepare_kernel,
        [part, part, square, square],
        [pltpu.VMEM((rows, half), bf16)] * 2
        + [pltpu.VMEM((half, half), bf16)] * 2
        + [pltpu.SemaphoreType.DMA((6,))],
        ins=[HBM] * 4 + [ANY],
        flops=4 * rows * half * half,
        moved=16 * half * half,
        name="prepare",
    )(audio_in, video_in, query_in, key_in, packs[1])

    def project(scale, *operands, after=()):
        return call(
            functools.partial(project_kernel, scale),
            [piece] * GROUP,
            [pltpu.VMEM((rows, half), bf16)],
            ins=[VMEM] * 3 + [ANY] * len(after),
            flops=2 * rows * half * half,
            moved=2 * half * half + 6 * rows * half * 2,
            name="project",
        )(*operands, *after)

    def halo(seconds, pieces, id_packs, *after):
        edge = shape((RADIUS, rows + (ID_ROWS if id_packs else 0), width), bf16)
        sent = call(
            functools.partial(halo_kernel, seconds, 2 * rows if id_packs else 0),
            [edge] * len(seconds),
            ins=[VMEM] * (GROUP + len(id_packs)) + [ANY] * len(after),
            moved=5 * len(seconds) * rows * width * 2,
            name="halo",
        )(*pieces, *id_packs, *after)
        return [crossed(x, second) for x, second in zip(sent, seconds)]

    queries = traded(project(HEAD**-0.5, query_part, other_audio, query_rest, after=packs[1:3]))
    keys = project(1.0, key_part, other_video, key_rest, after=())
    query_edges = halo((0, 1), queries, packs, keys[0])
    keys = traded(keys)

    inside, around = GROUP * rows, 2 * RADIUS * rows
    turned, beside = shape((2 * width, inside), bf16), shape((inside, 2 * width), bf16)
    asks = shape((GROUP, heads * rows, 2 * width), bf16)
    peaks, sums, plane_turned, plane_beside = call(
        rows_kernel,
        [shape((GROUP, rows, width), f32), shape((GROUP, 2, rows, width), f32), turned, beside],
        [pltpu.VMEM(asks.shape, bf16)],
        flops=16 * GROUP * rows * inside * width,
        moved=8 * inside * width * 2,
        exps=2 * GROUP * rows * inside,
        name="rows",
    )(*packs, *queries, *keys)
    audio_edges = halo((0,), packs, [], peaks) + halo((1,), packs, [])
    back = shape((RADIUS, rows + rows // width * STAT_ROWS, width), bf16)
    lent_a, lent_b, edge_turned = call(
        lend_kernel,
        [back, back, shape((2 * width, around), bf16)],
        [pltpu.VMEM((2, RADIUS, rows + ID_ROWS, width), bf16), pltpu.VMEM((2,) + back.shape, bf16)],
        flops=48 * RADIUS * GROUP * rows * rows * width,
        moved=8 * around * width * 2,
        exps=2 * RADIUS * GROUP * rows * rows,
        name="lend",
    )(*query_edges[::-1], plane_turned, plane_beside)
    backs = [crossed(x, i) for i, x in enumerate((lent_a, lent_b))]

    half_columns = dict(
        flops=56 * GROUP * rows * rows * width,
        moved=4 * around * width * 2,
        exps=7 * GROUP * rows * rows,
        name="columns",
    )
    shared = [turned, beside, asks, shape((around, 2 * width), bf16)]
    near, far = range(GROUP // 2), range(GROUP // 2, GROUP)
    *far_pieces, turned, beside, asks, edge_beside = call(
        functools.partial(columns_kernel, far), [piece] * len(far) + shared, **half_columns
    )(*packs, *queries, *keys, *audio_edges[::-1], edge_turned)
    audio_pieces = call(
        merge_kernel,
        [piece] * GROUP,
        [pltpu.VMEM((2,) + back.shape, bf16), pltpu.VMEM((GROUP, rows, width), bf16)],
        moved=16 * inside * width,
        exps=4 * inside * width,
        ins=[VMEM] * 4 + [ANY],
        name="merge",
    )(*backs, peaks, sums, far_pieces[0])
    audio_pieces = traded(audio_pieces)
    far_pieces = traded([None, None, *far_pieces])[2:]
    near_pieces = call(
        functools.partial(columns_kernel, near),
        [piece] * len(near),
        ins=[VMEM] * 5 + [ANY] * 2,
        **half_columns,
    )(edge_turned, turned, beside, asks, edge_beside, far_pieces[0], audio_pieces[0])
    video_pieces = [*traded(near_pieces), *far_pieces]

    audio_attended, video_attended = call(
        join_kernel,
        [shape((rows, half), bf16)] * 2,
        [pltpu.SemaphoreType.DMA((2 * GROUP,))],
        outs_in=[HBM, HBM],
        moved=4 * rows * half * 2,
        name="join",
    )(*audio_pieces, *video_pieces)
    return (audio_attended, video_attended)


def solution(mesh):
    return jax.shard_map(
        local,
        mesh=mesh,
        in_specs=(P("tm", "head"), P("tm", "head"), P("tm"), P(None, "head"), P(None, "head")),
        out_specs=(P("tm", "head"), P("tm", "head")),
        check_vma=False,
    )
```

```python
import functools

import jax
import jax.numpy as jnp
from jax import lax
from jax.experimental import pallas as pl
from jax.experimental.pallas import tpu as pltpu
from jax.sharding import PartitionSpec as P

HEAD = 64
RADIUS = 3
GROUP = 4
NEG = -1e30
ID_ROWS = 16
STAT_ROWS = 16

VMEM = pl.BlockSpec(memory_space=pltpu.VMEM)
ANY = pl.BlockSpec(memory_space=pl.ANY)
HBM = pl.BlockSpec(memory_space=pltpu.HBM)


def place():
    return lax.rem(lax.axis_index("tm"), GROUP)


def plane():
    return lax.axis_index("tm") // GROUP


def call(kernel, outs, scratch=(), ins=None, outs_in=None, flops=0, moved=0, exps=0, name=None):
    return pl.pallas_call(
        kernel,
        out_shape=outs,
        **({"in_specs": ins} if ins else {}),
        **({"out_specs": outs_in} if outs_in else {}),
        scratch_shapes=scratch,
        compiler_params=pltpu.CompilerParams(vmem_limit_bytes=32 * 2**20),
        cost_estimate=pl.CostEstimate(flops=flops, bytes_accessed=moved, transcendentals=exps),
        name=name,
    )


def product(a, b):
    return jnp.dot(a, b, preferred_element_type=jnp.float32)


def fetcher(sems):
    copies = []

    def fetch(source, target):
        copies.append(pltpu.make_async_copy(source, target, sems.at[len(copies)]))
        copies[-1].start()

    return copies, fetch


def split_kernel(audio, video, ids, *refs):
    packs, (ids_in, ids_wide, sems) = refs[:GROUP], refs[GROUP:]
    rows, width = audio.shape[0], packs[0].shape[1]
    mine = place()
    copies, fetch = fetcher(sems)
    fetch(ids, ids_in)
    for k in range(GROUP):
        at = pl.ds(pl.multiple_of((mine ^ k) * width, width), width)
        for i, stream in enumerate((audio, video)):
            fetch(stream.at[:, at], packs[k].at[i * rows : (i + 1) * rows])
    copies[0].wait()
    ids_wide[...] = jnp.zeros_like(ids_wide)
    ids_wide[: ids_in.shape[0]] = (ids_in[...] + 1).astype(jnp.float32)
    for k in range(GROUP):
        packs[k][2 * rows :] = ids_wide[...].astype(packs[k].dtype)
    for copy in copies[1:]:
        copy.wait()


def prepare_kernel(audio, video, query, key, *refs):
    sums, seconds, streams, firsts, sems = refs[-9:-7], refs[-7:-5], refs[-5:-3], refs[-3:-1], refs[-1]
    half = audio.shape[1]
    side = lax.axis_index("head")
    ours = pl.ds(pl.multiple_of(side * half, half), half)
    theirs = pl.ds(pl.multiple_of((1 - side) * half, half), half)
    copies, fetch = fetcher(sems)
    for i, (stream, weight) in enumerate(((audio, query), (video, key))):
        fetch(stream, streams[i])
        fetch(weight.at[ours], firsts[i])
    for i, weight in enumerate((query, key)):
        fetch(weight.at[theirs], seconds[i])
    for i in range(2):
        copies[2 * i].wait()
        copies[2 * i + 1].wait()
        sums[i][...] = product(streams[i][...], firsts[i][...])
    for copy in copies[4:]:
        copy.wait()


def project_kernel(scale, part, other, weight, *refs):
    pieces, full = refs[-GROUP - 1 : -1], refs[-1]
    width = pieces[0].shape[1]
    mine = place()
    full[...] = (part[...] + product(other[...], weight[...])).astype(jnp.bfloat16) * jnp.bfloat16(scale)
    for k in range(GROUP):
        pieces[k][...] = full[:, pl.ds(pl.multiple_of((mine ^ k) * width, width), width)]


def halo_kernel(seconds, ids_at, *refs):
    pieces, id_packs, outs = refs[:GROUP], refs[GROUP : 2 * GROUP], refs[-len(seconds) :]
    rows = outs[0].shape[1] - (ID_ROWS if ids_at else 0)
    mine = place()
    for out, second in zip(outs, seconds):
        skip = (GROUP - RADIUS) * lax.rem(plane() + 1 + second, 2)
        for k in range(GROUP):
            spot = (mine ^ k) - skip

            @pl.when((spot >= 0) & (spot < RADIUS))
            def _():
                out[spot, :rows] = pieces[k][:rows]
                if ids_at:
                    out[spot, rows:] = id_packs[k][ids_at:]


def join_kernel(*refs):
    pieces, outs, sems = refs[: 2 * GROUP], refs[2 * GROUP : 2 * GROUP + 2], refs[-1]
    width = pieces[0].shape[1]
    mine = place()
    copies, fetch = fetcher(sems)
    for i, out in enumerate(outs):
        for k in range(GROUP):
            at = pl.ds(pl.multiple_of((mine ^ k) * width, width), width)
            fetch(pieces[i * GROUP + k], out.at[:, at])
    for copy in copies:
        copy.wait()


def marks_turned(lanes):
    lanes = lanes.astype(jnp.float32)
    width = lanes.shape[1]
    row = lax.broadcasted_iota(jnp.int32, (width, width), 0).astype(jnp.float32)
    return [
        jnp.where(row == lanes[part : part + 1], 1.0, 0.0).astype(jnp.bfloat16) for part in range(2)
    ]


def stacked_ask(block, turned):
    head = lax.broadcasted_iota(jnp.int32, block.shape, 1) // HEAD
    marks = jnp.concatenate([jnp.transpose(x) for x in turned], axis=0)
    beside = (marks - jnp.bfloat16(1.0)) * jnp.bfloat16(-NEG)
    return jnp.concatenate(
        [
            jnp.concatenate([jnp.where(head == h, block, jnp.zeros_like(block)), beside], axis=1)
            for h in range(block.shape[1] // HEAD)
        ],
        axis=0,
    )


def by_head(stacked, rows):
    out = stacked[:rows]
    head = lax.broadcasted_iota(jnp.int32, out.shape, 1) // HEAD
    for h in range(1, stacked.shape[0] // rows):
        out = jnp.where(head == h, stacked[h * rows : (h + 1) * rows], out)
    return out


def attend(scores, values):
    top = None
    for s in scores:
        for at in range(0, s.shape[1], values[0].shape[1] // 2):
            part = s[:, at : at + values[0].shape[1] // 2]
            top = part if top is None else jnp.maximum(top, part)
    peak = jnp.max(top, axis=1, keepdims=True)
    mixed = None
    for s, value in zip(scores, values):
        part = product(jnp.exp(s - peak).astype(jnp.bfloat16), value)
        mixed = part if mixed is None else mixed + part
    return peak, mixed


def set_up(packs, asked, keys, values, turned, beside, asks):
    rows, width = asks.shape[1] // 2, asks.shape[2] // 2
    mine = place()
    beside[:, width:] = jnp.ones((GROUP * rows, width), beside.dtype)
    for k in range(GROUP):
        b = mine ^ k

        def spot(at, size):
            return pl.ds(pl.multiple_of(b * rows + at, size), size)

        marks = marks_turned(packs[k][2 * rows :])
        asks[b] = stacked_ask(asked(k), marks)
        beside[spot(0, rows), :width] = values(k)
        key = keys(k)
        for part, x in enumerate(marks):
            at = spot(part * width, width)
            turned[:width, at] = jnp.transpose(key[part * width : (part + 1) * width])
            turned[width:, at] = x


def rows_kernel(*refs):
    packs, queries, keys = refs[:GROUP], refs[GROUP : 2 * GROUP], refs[2 * GROUP : 3 * GROUP]
    peaks, sums, turned, beside, asks = refs[-5:]
    rows, width = keys[0].shape
    set_up(
        packs,
        lambda k: queries[k][...],
        lambda k: keys[k][...],
        lambda k: packs[k][rows : 2 * rows],
        turned,
        beside,
        asks,
    )
    ahead = product(asks[0], turned[...])
    for b in range(GROUP):
        scores = ahead
        if b + 1 < GROUP:
            ahead = product(asks[b + 1], turned[...])
        peak, mixed = attend([scores], [beside[...]])
        peaks[b] = by_head(jnp.broadcast_to(peak, (peak.shape[0], width)), rows)
        sums[b, 0] = by_head(mixed[:, :width], rows)
        sums[b, 1] = by_head(mixed[:, width:], rows)


def lend_kernel(edge_b, edge_a, plane_turned, plane_beside, first, second, turned, ordered, results):
    rows, width = ordered.shape[2] - ID_ROWS, ordered.shape[3]
    odd = lax.rem(plane(), 2)
    ordered[1 - odd] = edge_a[...]
    ordered[odd] = edge_b[...]
    lane = lax.broadcasted_iota(jnp.int32, (rows, width), 1)
    blocks = [slice(0, (j + 1) * rows) for j in range(RADIUS)]
    blocks += [slice((j + 1) * rows, GROUP * rows) for j in range(RADIUS)]

    def scores_of(e):
        side, j = e // RADIUS, e % RADIUS
        marks = marks_turned(ordered[side, j, rows:])
        query = ordered[side, j, :rows]
        for part, x in enumerate(marks):
            at = slice(e * rows + part * width, e * rows + (part + 1) * width)
            turned[:width, at] = jnp.transpose(query[part * width : (part + 1) * width])
            turned[width:, at] = x
        return product(stacked_ask(query, marks), plane_turned[:, blocks[e]])

    ahead = scores_of(0)
    for e in range(2 * RADIUS):
        side, j = e // RADIUS, e % RADIUS
        scores = ahead
        if e + 1 < 2 * RADIUS:
            ahead = scores_of(e + 1)
        peak, mixed = attend([scores], [plane_beside[blocks[e]]])
        total = by_head(mixed[:, width:], rows)
        results[side, j, :rows] = (by_head(mixed[:, :width], rows) / total).astype(results.dtype)
        logs = by_head(jnp.broadcast_to(peak, (peak.shape[0], width)), rows) + jnp.log(total)
        high = logs.astype(jnp.bfloat16).astype(jnp.float32)
        middle = (logs - high).astype(jnp.bfloat16).astype(jnp.float32)
        low = logs - high - middle
        stats = 0.0
        for part in range(rows // width):
            at = slice(part * width, (part + 1) * width)
            picked = jnp.zeros((width, width), jnp.float32)
            for n, piece in enumerate((high, middle, low)):
                picked = jnp.where(lane[:width] % HEAD == 3 * part + n, piece[at], picked)
            flipped = jnp.transpose(picked)
            stats += jnp.concatenate(
                [flipped[h : h + STAT_ROWS // 2] for h in range(0, width, HEAD)], axis=0
            )
        results[side, j, rows:] = stats.astype(results.dtype)
    first[...] = results[1 - odd]
    second[...] = results[odd]


def columns_kernel(receivers, *refs):
    refs = list(refs)
    take = lambda count: [refs.pop(0) for _ in range(count)]
    first = 0 not in receivers
    if first:
        packs, queries, keys, (edge_b, edge_a) = take(GROUP), take(GROUP), take(GROUP), take(2)
    (edge_turned,) = take(1)
    if not first:
        shared, _ = take(4), take(2)
    outs = take(len(receivers))
    turned, beside, asks, edge_beside = take(4) if first else shared
    rows, width = outs[0].shape
    mine = place()
    if first:
        odd = lax.rem(plane(), 2)
        set_up(
            packs,
            lambda k: keys[k][...],
            lambda k: queries[k][...],
            lambda k: packs[k][:rows],
            turned,
            beside,
            asks,
        )
        edge_beside[:, width:] = jnp.ones((edge_beside.shape[0], width), beside.dtype)
        for edge, base in ((edge_a, RADIUS * (1 - odd)), (edge_b, RADIUS * odd)):
            for j in range(RADIUS):
                at = pl.ds(pl.multiple_of((base + j) * rows, rows), rows)
                edge_beside[at, :width] = edge[j]
    near = [pl.ds(pl.multiple_of((mine ^ k) * rows, rows), RADIUS * rows) for k in receivers]

    def scores_of(n):
        ask = asks[mine ^ receivers[n]]
        return [product(ask, turned[...]), product(ask, edge_turned[:, near[n]])]

    ahead = scores_of(0)
    for n in range(len(receivers)):
        scores = ahead
        if n + 1 < len(receivers):
            ahead = scores_of(n + 1)
        _, mixed = attend(scores, [beside[...], edge_beside[near[n]]])
        mean = by_head(mixed[:, :width], rows) / by_head(mixed[:, width:], rows)
        outs[n][...] = mean.astype(outs[n].dtype)


def merge_kernel(back_a, back_b, peaks, sums, *refs):
    outs, (backs, whole) = refs[-GROUP - 2 : -2], refs[-2:]
    rows, width = outs[0].shape
    mine = place()
    odd = lax.rem(plane(), 2)
    backs[1 - odd] = back_a[...]
    backs[odd] = back_b[...]
    last = lax.axis_size("tm") // GROUP - 1
    absent = [jnp.where(plane() == end, NEG, 0.0) for end in (0, last)]

    def logs(side, j):
        squares = []
        for part in range(rows // width):
            stats = backs[side, j, rows:].astype(jnp.float32)
            heads = []
            for h in range(width // HEAD):
                at = 8 * h + 3 * part
                heads.append(stats[at : at + 1] + stats[at + 1 : at + 2] + stats[at + 2 : at + 3])
            turned = jnp.transpose(
                jnp.concatenate([jnp.broadcast_to(x, (HEAD, width)) for x in heads], axis=0)
            )
            squares.append(turned)
        return jnp.concatenate(squares, axis=0) + absent[side]

    for b in range(GROUP):
        theirs = []
        if b < RADIUS:
            theirs.append((0, b))
        if b >= GROUP - RADIUS:
            theirs.append((1, b - (GROUP - RADIUS)))
        theirs = [(logs(*t), backs[t[0], t[1], :rows].astype(jnp.float32)) for t in theirs]
        old = peaks[b]
        top = old
        for log, _ in theirs:
            top = jnp.maximum(top, log)
        factor = jnp.exp(old - top)
        value = sums[b, 0] * factor
        total = sums[b, 1] * factor
        for log, mean in theirs:
            weight = jnp.exp(log - top)
            value += weight * mean
            total += weight
        whole[b] = (value / total).astype(whole.dtype)
    for k in range(GROUP):
        outs[k][...] = whole[mine ^ k]


def local(audio_frames, video_frames, recording, audio_query, video_key):
    rows, half = audio_frames.shape
    width = half // GROUP
    heads = width // HEAD
    length = lax.axis_size("tm")
    bf16, f32 = jnp.bfloat16, jnp.float32
    shape = jax.ShapeDtypeStruct
    assert length % (2 * GROUP) == 0

    def swapped(x):
        return lax.ppermute(x, "head", [(0, 1), (1, 0)])

    def traded(pieces):
        pairs = lambda k: [(i, i ^ k) for i in range(length)]
        return [
            lax.ppermute(x, "tm", pairs(k)) if k and x is not None else x for k, x in enumerate(pieces)
        ]

    def crossed(sent, second):
        planes = range(second, length // GROUP - second)
        pairs = [(p, ((p + second) ^ 1) - second) for p in planes]
        return lax.ppermute(
            sent, "tm", [(p * GROUP + i, q * GROUP + i) for p, q in pairs for i in range(GROUP)]
        )

    part = shape((rows, half), f32)
    square = shape((half, half), bf16)
    piece = shape((rows, width), bf16)
    given = (audio_frames, video_frames, audio_query, video_key, recording.reshape(rows // width, width))
    audio_in, video_in, query_in, key_in, ids_in = (
        pltpu.with_memory_space_constraint(x, pltpu.HBM) for x in given
    )
    other_audio = swapped(audio_frames)
    other_video = swapped(video_frames)
    packs = call(
        split_kernel,
        [shape((2 * rows + ID_ROWS, width), bf16)] * GROUP,
        [pltpu.VMEM((rows // width, width), jnp.int32), pltpu.VMEM((ID_ROWS, width), f32)]
        + [pltpu.SemaphoreType.DMA((1 + 2 * GROUP,))],
        ins=[HBM] * 3,
        moved=8 * rows * half,
        name="split",
    )(audio_in, video_in, ids_in)
    packs = traded(packs)
    query_part, key_part, query_rest, key_rest = call(
        prepare_kernel,
        [part, part, square, square],
        [pltpu.VMEM((rows, half), bf16)] * 2
        + [pltpu.VMEM((half, half), bf16)] * 2
        + [pltpu.SemaphoreType.DMA((6,))],
        ins=[HBM] * 4 + [ANY],
        flops=4 * rows * half * half,
        moved=16 * half * half,
        name="prepare",
    )(audio_in, video_in, query_in, key_in, packs[1])

    def project(scale, *operands, after=()):
        return call(
            functools.partial(project_kernel, scale),
            [piece] * GROUP,
            [pltpu.VMEM((rows, half), bf16)],
            ins=[VMEM] * 3 + [ANY] * len(after),
            flops=2 * rows * half * half,
            moved=2 * half * half + 6 * rows * half * 2,
            name="project",
        )(*operands, *after)

    def halo(seconds, pieces, id_packs, *after):
        edge = shape((RADIUS, rows + (ID_ROWS if id_packs else 0), width), bf16)
        sent = call(
            functools.partial(halo_kernel, seconds, 2 * rows if id_packs else 0),
            [edge] * len(seconds),
            ins=[VMEM] * (GROUP + len(id_packs)) + [ANY] * len(after),
            moved=5 * len(seconds) * rows * width * 2,
            name="halo",
        )(*pieces, *id_packs, *after)
        return [crossed(x, second) for x, second in zip(sent, seconds)]

    queries = traded(project(HEAD**-0.5, query_part, other_audio, query_rest, after=packs[1:3]))
    keys = project(1.0, key_part, other_video, key_rest, after=())
    query_edges = halo((0, 1), queries, packs, keys[0])
    keys = traded(keys)

    inside, around = GROUP * rows, 2 * RADIUS * rows
    turned, beside = shape((2 * width, inside), bf16), shape((inside, 2 * width), bf16)
    asks = shape((GROUP, heads * rows, 2 * width), bf16)
    peaks, sums, plane_turned, plane_beside = call(
        rows_kernel,
        [shape((GROUP, rows, width), f32), shape((GROUP, 2, rows, width), f32), turned, beside],
        [pltpu.VMEM(asks.shape, bf16)],
        flops=16 * GROUP * rows * inside * width,
        moved=8 * inside * width * 2,
        exps=2 * GROUP * rows * inside,
        name="rows",
    )(*packs, *queries, *keys)
    audio_edges = halo((0,), packs, [], peaks) + halo((1,), packs, [])
    back = shape((RADIUS, rows + STAT_ROWS, width), bf16)
    lent_a, lent_b, edge_turned = call(
        lend_kernel,
        [back, back, shape((2 * width, around), bf16)],
        [pltpu.VMEM((2, RADIUS, rows + ID_ROWS, width), bf16), pltpu.VMEM((2,) + back.shape, bf16)],
        flops=48 * RADIUS * GROUP * rows * rows * width,
        moved=8 * around * width * 2,
        exps=2 * RADIUS * GROUP * rows * rows,
        name="lend",
    )(*query_edges[::-1], plane_turned, plane_beside)
    backs = [crossed(x, i) for i, x in enumerate((lent_a, lent_b))]

    half_columns = dict(
        flops=56 * GROUP * rows * rows * width,
        moved=4 * around * width * 2,
        exps=7 * GROUP * rows * rows,
        name="columns",
    )
    shared = [turned, beside, asks, shape((around, 2 * width), bf16)]
    near, far = range(GROUP // 2), range(GROUP // 2, GROUP)
    *far_pieces, turned, beside, asks, edge_beside = call(
        functools.partial(columns_kernel, far), [piece] * len(far) + shared, **half_columns
    )(*packs, *queries, *keys, *audio_edges[::-1], edge_turned)
    audio_pieces = call(
        merge_kernel,
        [piece] * GROUP,
        [pltpu.VMEM((2,) + back.shape, bf16), pltpu.VMEM((GROUP, rows, width), bf16)],
        moved=16 * inside * width,
        exps=4 * inside * width,
        ins=[VMEM] * 4 + [ANY],
        name="merge",
    )(*backs, peaks, sums, far_pieces[0])
    audio_pieces = traded(audio_pieces)
    far_pieces = traded([None, None, *far_pieces])[2:]
    near_pieces = call(
        functools.partial(columns_kernel, near),
        [piece] * len(near),
        ins=[VMEM] * 5 + [ANY] * 2,
        **half_columns,
    )(edge_turned, turned, beside, asks, edge_beside, far_pieces[0], audio_pieces[0])
    video_pieces = [*traded(near_pieces), *far_pieces]

    audio_attended, video_attended = call(
        join_kernel,
        [shape((rows, half), bf16)] * 2,
        [pltpu.SemaphoreType.DMA((2 * GROUP,))],
        outs_in=[HBM, HBM],
        moved=4 * rows * half * 2,
        name="join",
    )(*audio_pieces, *video_pieces)
    return (audio_attended, video_attended)


def solution(mesh):
    return jax.shard_map(
        local,
        mesh=mesh,
        in_specs=(P("tm", "head"), P("tm", "head"), P("tm"), P(None, "head"), P(None, "head")),
        out_specs=(P("tm", "head"), P("tm", "head")),
        check_vma=False,
    )
```

```python
import functools

import jax
import jax.numpy as jnp
from jax import lax
from jax.experimental import pallas as pl
from jax.experimental.pallas import tpu as pltpu
from jax.sharding import PartitionSpec as P

HEAD = 64
RADIUS = 3
GROUP = 4
NEG = -1e30
ID_ROWS = 16
STAT_ROWS = 16

VMEM = pl.BlockSpec(memory_space=pltpu.VMEM)
ANY = pl.BlockSpec(memory_space=pl.ANY)
HBM = pl.BlockSpec(memory_space=pltpu.HBM)


def place():
    return lax.rem(lax.axis_index("tm"), GROUP)


def plane():
    return lax.axis_index("tm") // GROUP


def call(kernel, outs, scratch=(), ins=None, outs_in=None, flops=0, moved=0, exps=0, name=None):
    return pl.pallas_call(
        kernel,
        out_shape=outs,
        **({"in_specs": ins} if ins else {}),
        **({"out_specs": outs_in} if outs_in else {}),
        scratch_shapes=scratch,
        compiler_params=pltpu.CompilerParams(vmem_limit_bytes=32 * 2**20),
        cost_estimate=pl.CostEstimate(flops=flops, bytes_accessed=moved, transcendentals=exps),
        name=name,
    )


def product(a, b):
    return jnp.dot(a, b, preferred_element_type=jnp.float32)


def fetcher(sems):
    copies = []

    def fetch(source, target):
        copies.append(pltpu.make_async_copy(source, target, sems.at[len(copies)]))
        copies[-1].start()

    return copies, fetch


def split_kernel(audio, video, ids, *refs):
    packs, (ids_in, ids_wide, sems) = refs[:GROUP], refs[GROUP:]
    rows, width = audio.shape[0], packs[0].shape[1]
    mine = place()
    copies, fetch = fetcher(sems)
    fetch(ids, ids_in)
    for k in range(GROUP):
        at = pl.ds(pl.multiple_of((mine ^ k) * width, width), width)
        for i, stream in enumerate((audio, video)):
            fetch(stream.at[:, at], packs[k].at[i * rows : (i + 1) * rows])
    copies[0].wait()
    ids_wide[...] = jnp.zeros_like(ids_wide)
    ids_wide[: ids_in.shape[0]] = (ids_in[...] + 1).astype(jnp.float32)
    for k in range(GROUP):
        packs[k][2 * rows :] = ids_wide[...].astype(packs[k].dtype)
    for copy in copies[1:]:
        copy.wait()


def prepare_kernel(audio, video, query, key, *refs):
    sums, seconds, streams, firsts, sems = refs[-9:-7], refs[-7:-5], refs[-5:-3], refs[-3:-1], refs[-1]
    half = audio.shape[1]
    side = lax.axis_index("head")
    ours = pl.ds(pl.multiple_of(side * half, half), half)
    theirs = pl.ds(pl.multiple_of((1 - side) * half, half), half)
    copies, fetch = fetcher(sems)
    for i, (stream, weight) in enumerate(((audio, query), (video, key))):
        fetch(stream, streams[i])
        fetch(weight.at[ours], firsts[i])
    for i, weight in enumerate((query, key)):
        fetch(weight.at[theirs], seconds[i])
    for i in range(2):
        copies[2 * i].wait()
        copies[2 * i + 1].wait()
        sums[i][...] = product(streams[i][...], firsts[i][...])
    for copy in copies[4:]:
        copy.wait()


def project_kernel(scale, part, other, weight, *refs):
    pieces, full = refs[-GROUP - 1 : -1], refs[-1]
    width = pieces[0].shape[1]
    mine = place()
    full[...] = (part[...] + product(other[...], weight[...])).astype(jnp.bfloat16) * jnp.bfloat16(scale)
    for k in range(GROUP):
        pieces[k][...] = full[:, pl.ds(pl.multiple_of((mine ^ k) * width, width), width)]


def halo_kernel(seconds, ids_at, *refs):
    pieces, id_packs, outs = refs[:GROUP], refs[GROUP : 2 * GROUP], refs[-len(seconds) :]
    rows = outs[0].shape[1] - (ID_ROWS if ids_at else 0)
    mine = place()
    for out, second in zip(outs, seconds):
        skip = (GROUP - RADIUS) * lax.rem(plane() + 1 + second, 2)
        for k in range(GROUP):
            spot = (mine ^ k) - skip

            @pl.when((spot >= 0) & (spot < RADIUS))
            def _():
                out[spot, :rows] = pieces[k][:rows]
                if ids_at:
                    out[spot, rows:] = id_packs[k][ids_at:]


def join_kernel(*refs):
    pieces, outs, sems = refs[: 2 * GROUP], refs[2 * GROUP : 2 * GROUP + 2], refs[-1]
    width = pieces[0].shape[1]
    mine = place()
    copies, fetch = fetcher(sems)
    for i, out in enumerate(outs):
        for k in range(GROUP):
            at = pl.ds(pl.multiple_of((mine ^ k) * width, width), width)
            fetch(pieces[i * GROUP + k], out.at[:, at])
    for copy in copies:
        copy.wait()


def marks_turned(lanes):
    lanes = lanes.astype(jnp.float32)
    width = lanes.shape[1]
    row = lax.broadcasted_iota(jnp.int32, (width, width), 0).astype(jnp.float32)
    return [
        jnp.where(row == lanes[part : part + 1], 1.0, 0.0).astype(jnp.bfloat16) for part in range(2)
    ]


def stacked_ask(block, turned):
    head = lax.broadcasted_iota(jnp.int32, block.shape, 1) // HEAD
    marks = jnp.concatenate([jnp.transpose(x) for x in turned], axis=0)
    beside = (marks - jnp.bfloat16(1.0)) * jnp.bfloat16(-NEG)
    return jnp.concatenate(
        [
            jnp.concatenate([jnp.where(head == h, block, jnp.zeros_like(block)), beside], axis=1)
            for h in range(block.shape[1] // HEAD)
        ],
        axis=0,
    )


def by_head(stacked, rows):
    out = stacked[:rows]
    head = lax.broadcasted_iota(jnp.int32, out.shape, 1) // HEAD
    for h in range(1, stacked.shape[0] // rows):
        out = jnp.where(head == h, stacked[h * rows : (h + 1) * rows], out)
    return out


def attend(scores, values):
    top = None
    for s in scores:
        for at in range(0, s.shape[1], values[0].shape[1] // 2):
            part = s[:, at : at + values[0].shape[1] // 2]
            top = part if top is None else jnp.maximum(top, part)
    peak = jnp.max(top, axis=1, keepdims=True)
    mixed = None
    for s, value in zip(scores, values):
        part = product(jnp.exp(s - peak).astype(jnp.bfloat16), value)
        mixed = part if mixed is None else mixed + part
    return peak, mixed


def set_up(packs, asked, keys, values, turned, beside, asks):
    rows, width = asks.shape[1] // 2, asks.shape[2] // 2
    mine = place()
    beside[:, width:] = jnp.ones((GROUP * rows, width), beside.dtype)
    for k in range(GROUP):
        b = mine ^ k

        def spot(at, size):
            return pl.ds(pl.multiple_of(b * rows + at, size), size)

        marks = marks_turned(packs[k][2 * rows :])
        asks[b] = stacked_ask(asked(k), marks)
        beside[spot(0, rows), :width] = values(k)
        key = keys(k)
        for part, x in enumerate(marks):
            at = spot(part * width, width)
            turned[:width, at] = jnp.transpose(key[part * width : (part + 1) * width])
            turned[width:, at] = x


def rows_kernel(*refs):
    packs, queries, keys = refs[:GROUP], refs[GROUP : 2 * GROUP], refs[2 * GROUP : 3 * GROUP]
    peaks, sums, turned, beside, asks = refs[-5:]
    rows, width = keys[0].shape
    set_up(
        packs,
        lambda k: queries[k][...],
        lambda k: keys[k][...],
        lambda k: packs[k][rows : 2 * rows],
        turned,
        beside,
        asks,
    )
    ahead = product(asks[0], turned[...])
    for b in range(GROUP):
        scores = ahead
        if b + 1 < GROUP:
            ahead = product(asks[b + 1], turned[...])
        peak, mixed = attend([scores], [beside[...]])
        peaks[b] = by_head(jnp.broadcast_to(peak, (peak.shape[0], width)), rows)
        sums[b, 0] = by_head(mixed[:, :width], rows)
        sums[b, 1] = by_head(mixed[:, width:], rows)


def lend_kernel(edge_b, edge_a, plane_turned, plane_beside, first, second, turned, ordered, results):
    rows, width = ordered.shape[2] - ID_ROWS, ordered.shape[3]
    odd = lax.rem(plane(), 2)
    ordered[1 - odd] = edge_a[...]
    ordered[odd] = edge_b[...]
    lane = lax.broadcasted_iota(jnp.int32, (rows, width), 1)
    blocks = [slice(0, (j + 1) * rows) for j in range(RADIUS)]
    blocks += [slice((j + 1) * rows, GROUP * rows) for j in range(RADIUS)]

    def ask_of(e):
        side, j = e // RADIUS, e % RADIUS
        marks = marks_turned(ordered[side, j, rows:])
        query = ordered[side, j, :rows]
        for part, x in enumerate(marks):
            at = slice(e * rows + part * width, e * rows + (part + 1) * width)
            turned[:width, at] = jnp.transpose(query[part * width : (part + 1) * width])
            turned[width:, at] = x
        return stacked_ask(query, marks)

    asks = [ask_of(e) for e in range(2 * RADIUS)]

    def scores_of(e):
        return product(asks[e], plane_turned[:, blocks[e]])

    ahead = scores_of(0)
    for e in range(2 * RADIUS):
        side, j = e // RADIUS, e % RADIUS
        scores = ahead
        if e + 1 < 2 * RADIUS:
            ahead = scores_of(e + 1)
        peak, mixed = attend([scores], [plane_beside[blocks[e]]])
        total = by_head(mixed[:, width:], rows)
        results[side, j, :rows] = (by_head(mixed[:, :width], rows) / total).astype(results.dtype)
        logs = by_head(jnp.broadcast_to(peak, (peak.shape[0], width)), rows) + jnp.log(total)
        high = logs.astype(jnp.bfloat16).astype(jnp.float32)
        middle = (logs - high).astype(jnp.bfloat16).astype(jnp.float32)
        low = logs - high - middle
        stats = 0.0
        for part in range(rows // width):
            at = slice(part * width, (part + 1) * width)
            picked = jnp.zeros((width, width), jnp.float32)
            for n, piece in enumerate((high, middle, low)):
                picked = jnp.where(lane[:width] % HEAD == 3 * part + n, piece[at], picked)
            flipped = jnp.transpose(picked)
            stats += jnp.concatenate(
                [flipped[h : h + STAT_ROWS // 2] for h in range(0, width, HEAD)], axis=0
            )
        results[side, j, rows:] = stats.astype(results.dtype)
    first[...] = results[1 - odd]
    second[...] = results[odd]


def columns_kernel(receivers, *refs):
    refs = list(refs)
    take = lambda count: [refs.pop(0) for _ in range(count)]
    first = 0 not in receivers
    if first:
        packs, queries, keys, (edge_b, edge_a) = take(GROUP), take(GROUP), take(GROUP), take(2)
    (edge_turned,) = take(1)
    if not first:
        shared, _ = take(4), take(2)
    outs = take(len(receivers))
    turned, beside, asks, edge_beside = take(4) if first else shared
    rows, width = outs[0].shape
    mine = place()
    if first:
        odd = lax.rem(plane(), 2)
        set_up(
            packs,
            lambda k: keys[k][...],
            lambda k: queries[k][...],
            lambda k: packs[k][:rows],
            turned,
            beside,
            asks,
        )
        edge_beside[:, width:] = jnp.ones((edge_beside.shape[0], width), beside.dtype)
        for edge, base in ((edge_a, RADIUS * (1 - odd)), (edge_b, RADIUS * odd)):
            for j in range(RADIUS):
                at = pl.ds(pl.multiple_of((base + j) * rows, rows), rows)
                edge_beside[at, :width] = edge[j]
    near = [pl.ds(pl.multiple_of((mine ^ k) * rows, rows), RADIUS * rows) for k in receivers]

    def scores_of(n):
        ask = asks[mine ^ receivers[n]]
        return [product(ask, turned[...]), product(ask, edge_turned[:, near[n]])]

    ahead = scores_of(0)
    for n in range(len(receivers)):
        scores = ahead
        if n + 1 < len(receivers):
            ahead = scores_of(n + 1)
        _, mixed = attend(scores, [beside[...], edge_beside[near[n]]])
        mean = by_head(mixed[:, :width], rows) / by_head(mixed[:, width:], rows)
        outs[n][...] = mean.astype(outs[n].dtype)


def merge_kernel(back_a, back_b, peaks, sums, *refs):
    outs, (backs, whole) = refs[-GROUP - 2 : -2], refs[-2:]
    rows, width = outs[0].shape
    mine = place()
    odd = lax.rem(plane(), 2)
    backs[1 - odd] = back_a[...]
    backs[odd] = back_b[...]
    last = lax.axis_size("tm") // GROUP - 1
    absent = [jnp.where(plane() == end, NEG, 0.0) for end in (0, last)]

    def logs(side, j):
        squares = []
        for part in range(rows // width):
            stats = backs[side, j, rows:].astype(jnp.float32)
            heads = []
            for h in range(width // HEAD):
                at = 8 * h + 3 * part
                heads.append(stats[at : at + 1] + stats[at + 1 : at + 2] + stats[at + 2 : at + 3])
            turned = jnp.transpose(
                jnp.concatenate([jnp.broadcast_to(x, (HEAD, width)) for x in heads], axis=0)
            )
            squares.append(turned)
        return jnp.concatenate(squares, axis=0) + absent[side]

    for b in range(GROUP):
        theirs = []
        if b < RADIUS:
            theirs.append((0, b))
        if b >= GROUP - RADIUS:
            theirs.append((1, b - (GROUP - RADIUS)))
        theirs = [(logs(*t), backs[t[0], t[1], :rows].astype(jnp.float32)) for t in theirs]
        old = peaks[b]
        top = old
        for log, _ in theirs:
            top = jnp.maximum(top, log)
        factor = jnp.exp(old - top)
        value = sums[b, 0] * factor
        total = sums[b, 1] * factor
        for log, mean in theirs:
            weight = jnp.exp(log - top)
            value += weight * mean
            total += weight
        whole[b] = (value / total).astype(whole.dtype)
    for k in range(GROUP):
        outs[k][...] = whole[mine ^ k]


def local(audio_frames, video_frames, recording, audio_query, video_key):
    rows, half = audio_frames.shape
    width = half // GROUP
    heads = width // HEAD
    length = lax.axis_size("tm")
    bf16, f32 = jnp.bfloat16, jnp.float32
    shape = jax.ShapeDtypeStruct
    assert length % (2 * GROUP) == 0

    def swapped(x):
        return lax.ppermute(x, "head", [(0, 1), (1, 0)])

    def traded(pieces):
        pairs = lambda k: [(i, i ^ k) for i in range(length)]
        return [
            lax.ppermute(x, "tm", pairs(k)) if k and x is not None else x for k, x in enumerate(pieces)
        ]

    def crossed(sent, second):
        planes = range(second, length // GROUP - second)
        pairs = [(p, ((p + second) ^ 1) - second) for p in planes]
        return lax.ppermute(
            sent, "tm", [(p * GROUP + i, q * GROUP + i) for p, q in pairs for i in range(GROUP)]
        )

    part = shape((rows, half), f32)
    square = shape((half, half), bf16)
    piece = shape((rows, width), bf16)
    given = (audio_frames, video_frames, audio_query, video_key, recording.reshape(rows // width, width))
    audio_in, video_in, query_in, key_in, ids_in = (
        pltpu.with_memory_space_constraint(x, pltpu.HBM) for x in given
    )
    other_audio = swapped(audio_frames)
    other_video = swapped(video_frames)
    packs = call(
        split_kernel,
        [shape((2 * rows + ID_ROWS, width), bf16)] * GROUP,
        [pltpu.VMEM((rows // width, width), jnp.int32), pltpu.VMEM((ID_ROWS, width), f32)]
        + [pltpu.SemaphoreType.DMA((1 + 2 * GROUP,))],
        ins=[HBM] * 3,
        moved=8 * rows * half,
        name="split",
    )(audio_in, video_in, ids_in)
    packs = traded(packs)
    query_part, key_part, query_rest, key_rest = call(
        prepare_kernel,
        [part, part, square, square],
        [pltpu.VMEM((rows, half), bf16)] * 2
        + [pltpu.VMEM((half, half), bf16)] * 2
        + [pltpu.SemaphoreType.DMA((6,))],
        ins=[HBM] * 4 + [ANY],
        flops=4 * rows * half * half,
        moved=16 * half * half,
        name="prepare",
    )(audio_in, video_in, query_in, key_in, packs[1])

    def project(scale, *operands, after=()):
        return call(
            functools.partial(project_kernel, scale),
            [piece] * GROUP,
            [pltpu.VMEM((rows, half), bf16)],
            ins=[VMEM] * 3 + [ANY] * len(after),
            flops=2 * rows * half * half,
            moved=2 * half * half + 6 * rows * half * 2,
            name="project",
        )(*operands, *after)

    def halo(seconds, pieces, id_packs, *after):
        edge = shape((RADIUS, rows + (ID_ROWS if id_packs else 0), width), bf16)
        sent = call(
            functools.partial(halo_kernel, seconds, 2 * rows if id_packs else 0),
            [edge] * len(seconds),
            ins=[VMEM] * (GROUP + len(id_packs)) + [ANY] * len(after),
            moved=5 * len(seconds) * rows * width * 2,
            name="halo",
        )(*pieces, *id_packs, *after)
        return [crossed(x, second) for x, second in zip(sent, seconds)]

    queries = traded(project(HEAD**-0.5, query_part, other_audio, query_rest, after=packs[1:3]))
    keys = project(1.0, key_part, other_video, key_rest, after=())
    query_edges = halo((0, 1), queries, packs, keys[0])
    keys = traded(keys)

    inside, around = GROUP * rows, 2 * RADIUS * rows
    turned, beside = shape((2 * width, inside), bf16), shape((inside, 2 * width), bf16)
    asks = shape((GROUP, heads * rows, 2 * width), bf16)
    peaks, sums, plane_turned, plane_beside = call(
        rows_kernel,
        [shape((GROUP, rows, width), f32), shape((GROUP, 2, rows, width), f32), turned, beside],
        [pltpu.VMEM(asks.shape, bf16)],
        flops=16 * GROUP * rows * inside * width,
        moved=8 * inside * width * 2,
        exps=2 * GROUP * rows * inside,
        name="rows",
    )(*packs, *queries, *keys)
    audio_edges = halo((0,), packs, [], peaks) + halo((1,), packs, [])
    back = shape((RADIUS, rows + STAT_ROWS, width), bf16)
    lent_a, lent_b, edge_turned = call(
        lend_kernel,
        [back, back, shape((2 * width, around), bf16)],
        [pltpu.VMEM((2, RADIUS, rows + ID_ROWS, width), bf16), pltpu.VMEM((2,) + back.shape, bf16)],
        flops=48 * RADIUS * GROUP * rows * rows * width,
        moved=8 * around * width * 2,
        exps=2 * RADIUS * GROUP * rows * rows,
        name="lend",
    )(*query_edges[::-1], plane_turned, plane_beside)
    backs = [crossed(x, i) for i, x in enumerate((lent_a, lent_b))]

    half_columns = dict(
        flops=56 * GROUP * rows * rows * width,
        moved=4 * around * width * 2,
        exps=7 * GROUP * rows * rows,
        name="columns",
    )
    shared = [turned, beside, asks, shape((around, 2 * width), bf16)]
    near, far = range(GROUP // 2), range(GROUP // 2, GROUP)
    *far_pieces, turned, beside, asks, edge_beside = call(
        functools.partial(columns_kernel, far), [piece] * len(far) + shared, **half_columns
    )(*packs, *queries, *keys, *audio_edges[::-1], edge_turned)
    audio_pieces = call(
        merge_kernel,
        [piece] * GROUP,
        [pltpu.VMEM((2,) + back.shape, bf16), pltpu.VMEM((GROUP, rows, width), bf16)],
        moved=16 * inside * width,
        exps=4 * inside * width,
        ins=[VMEM] * 4 + [ANY],
        name="merge",
    )(*backs, peaks, sums, far_pieces[0])
    audio_pieces = traded(audio_pieces)
    far_pieces = traded([None, None, *far_pieces])[2:]
    near_pieces = call(
        functools.partial(columns_kernel, near),
        [piece] * len(near),
        ins=[VMEM] * 5 + [ANY] * 2,
        **half_columns,
    )(edge_turned, turned, beside, asks, edge_beside, far_pieces[0], audio_pieces[0])
    video_pieces = [*traded(near_pieces), *far_pieces]

    audio_attended, video_attended = call(
        join_kernel,
        [shape((rows, half), bf16)] * 2,
        [pltpu.SemaphoreType.DMA((2 * GROUP,))],
        outs_in=[HBM, HBM],
        moved=4 * rows * half * 2,
        name="join",
    )(*audio_pieces, *video_pieces)
    return (audio_attended, video_attended)


def solution(mesh):
    return jax.shard_map(
        local,
        mesh=mesh,
        in_specs=(P("tm", "head"), P("tm", "head"), P("tm"), P(None, "head"), P(None, "head")),
        out_specs=(P("tm", "head"), P("tm", "head")),
        check_vma=False,
    )
```
